32 devices in a mesh: rows: 8 (over z, core), heads: 4 (over y, x).
Axes of the slice: x: 2, y: 2, z: 4, core: 2. Of those that a mesh axis runs over, the one named last changes fastest.
Arguments:
- tokens: bfloat16 [16384, 1024], P(('rows', 'heads')), may hold values from -6 to 6
- memory: bfloat16 [16384, 1024], P(('rows', 'heads')), may hold values from -6 to 6
- cotangent: bfloat16 [16384, 1024], P(('rows', 'heads')), may hold values from -6 to 6
- dec_seg: int32 [16384], P('rows'), may hold values from 0 to 3, as said below
- mem_seg: int32 [16384], P('rows'), may hold values from 0 to 3, as said below
- w_self: bfloat16 [3, 1024, 1024], P(None, None, 'heads'), may hold values from -0.1875 to 0.1875
- w_self_out: bfloat16 [1024, 1024], P('heads'), may hold values from -1.5 to 1.5
- w_cross_q: bfloat16 [1024, 1024], P(None, 'heads'), may hold values from -0.1875 to 0.1875
- w_cross_kv: bfloat16 [2, 1024, 1024], P(None, None, 'heads'), may hold values from -0.1875 to 0.1875
- w_cross_out: bfloat16 [1024, 1024], P('heads'), may hold values from -1.5 to 1.5
- fc_in: bfloat16 [1024, 4096], P(None, 'heads'), may hold values from -0.1875 to 0.1875
- fc_out: bfloat16 [4096, 1024], P('heads'), may hold values from -0.09375 to 0.09375
- ad_down: bfloat16 [1024, 512], P(None, 'heads'), may hold values from -0.1875 to 0.1875
- ad_up: bfloat16 [512, 1024], P('heads'), may hold values from -0.0625 to 0.0625
- prefix: bfloat16 [2, 30, 1024], P(None, None, 'heads'), may hold values from -6 to 6
- ln_gain: float32 [3, 1024], replicated, may hold values from 0.5 to 1.5
- ln_bias: float32 [3, 1024], replicated, may hold values from -1.2 to 1.2
Outputs:
- output: bfloat16 [16384, 1024], P(('rows', 'heads'))
- grad_input: float32 [16384, 1024], P(('rows', 'heads'))
- grad_memory: float32 [16384, 1024], P(('rows', 'heads'))
- grad_prefix: float32 [2, 30, 1024], P(None, None, 'heads')
- grad_down: float32 [1024, 512], P(None, 'heads')
- grad_up: float32 [512, 1024], P('heads')
The draws below stay inside these ranges and needn't reach their ends.
Inputs may be any that keep to these rules, and one draw needn't show every extreme that they name: `dec_seg`: within each decoder sequence of 1024 tokens the document numbers start at 0, never fall, take every value 0 to 3, and no document is empty. `mem_seg`: within each memory of 1024 rows the document numbers start at 0, never fall, take every value 0 to 3, and no document is empty; so every decoder token has memory rows of its own document.
All inputs are finite; a program needn't handle non-finite values.
Results may differ from the reference program's by a relative error of at most 0.024.
The reference program's roundings to bfloat16 on the way count: a program that leaves them out, or rounds other values in their place, can miss the bound.
Values may be sent and summed in bfloat16 or wider, within the bound.
A program may use at most 128 MiB of HBM per device.

```python
import jax
import jax.numpy as jnp
from jax import lax

D = 1024
H = 16
HD = 64
FF = 4096
AD = 512
PREFIX = 30
SEQ = 1024
MLEN = 1024
DOCS = 4
TOKENS = 16384
MTOK = 16384


def cut_segments(key, length, whole):
    row_count = whole // length
    key_list = jax.random.split(key, row_count)

    def single_row(subkey):
        shuffled = jax.random.permutation(subkey, length - 1) + 1
        boundaries = shuffled[:DOCS - 1].astype(jnp.int32)
        positions = jnp.arange(length, dtype=jnp.int32)
        return jnp.sum((positions[:, None] >= boundaries[None, :]).astype(jnp.int32), axis=1)
    return jax.vmap(single_row)(key_list).reshape(whole).astype(jnp.int32)


def draw_dec_seg(key, part):
    return cut_segments(jax.random.fold_in(key, 11), SEQ, TOKENS)


def draw_mem_seg(key, part):
    return cut_segments(jax.random.fold_in(key, 12), MLEN, MTOK)


def level_of(rng, shape, shards, low, high):
    def one(position, parts):
        steps = jax.random.uniform(jax.random.fold_in(jax.random.fold_in(rng, 6), position), (parts,), jnp.float32, low / len(shards), high / len(shards))
        return jnp.repeat(jnp.exp(steps), shape[position] // parts).reshape((-1,) + (1,) * (len(shape) - position - 1))

    loudness = one(*shards[0])
    for cut in shards[1:]:
        loudness = loudness * one(*cut)
    return loudness


def normal_values(stream_key, dims, scale, reach, cuts=(), kind=jnp.bfloat16):
    values = jax.random.normal(stream_key, dims, jnp.float32) * scale
    if len(cuts) > 0:
        values = level_of(stream_key, dims, cuts, -0.22, 0.18) * values
    return jnp.clip(values, min=-reach, max=reach).astype(kind)


def setup_inputs(seed: int = 0) -> dict:
    keys = jax.random.split(jax.random.key(seed), 18)
    tokens = normal_values(keys[0], (TOKENS, D), 1.0, 6.0, ((0, 32),))
    memory = normal_values(keys[1], (MTOK, D), 1.0, 6.0, ((0, 32),))
    cotangent = normal_values(keys[2], (TOKENS, D), 1.0, 6.0, ((0, 32),))
    dec_seg = draw_dec_seg(jax.random.fold_in(keys[17], 71), 0)
    mem_seg = draw_mem_seg(jax.random.fold_in(keys[17], 71), 0)
    w_self = normal_values(keys[5], (3, D, D), D ** -0.5, 0.1875, ((2, 4),))
    w_self_out = normal_values(keys[6], (D, D), (max(D // 64, 4)) ** -0.5, 1.5, ((0, 4),))
    w_cross_q = normal_values(keys[7], (D, D), D ** -0.5, 0.1875, ((1, 4),))
    w_cross_kv = normal_values(keys[8], (2, D, D), D ** -0.5, 0.1875, ((2, 4),))
    w_cross_out = normal_values(keys[9], (D, D), (max(D // 64, 4)) ** -0.5, 1.5, ((0, 4),))
    fc_in = normal_values(keys[10], (D, FF), D ** -0.5, 0.1875, ((1, 4),))
    fc_out = normal_values(keys[11], (FF, D), FF ** -0.5, 0.09375, ((0, 4),))
    ad_down = normal_values(keys[12], (D, AD), D ** -0.5, 0.1875, ((1, 4),))
    ad_up = normal_values(keys[13], (AD, D), (16 * AD) ** -0.5, 0.0625, ((0, 4),))
    prefix = normal_values(keys[14], (2, PREFIX, D), 1.0, 6.0, ((2, 4),))
    ln_gain = jnp.clip(1.0 + 0.1 * jax.random.normal(keys[15], (3, D), jnp.float32), 0.5, 1.5)
    ln_bias = normal_values(keys[16], (3, D), 0.2, 1.2, (), jnp.float32)
    return dict(tokens=tokens, memory=memory, cotangent=cotangent, dec_seg=dec_seg, mem_seg=mem_seg, w_self=w_self, w_self_out=w_self_out, w_cross_q=w_cross_q, w_cross_kv=w_cross_kv, w_cross_out=w_cross_out, fc_in=fc_in, fc_out=fc_out, ad_down=ad_down, ad_up=ad_up, prefix=prefix, ln_gain=ln_gain, ln_bias=ln_bias)


@jax.custom_vjp
def low(v):
    return lax.optimization_barrier(v.astype(jnp.bfloat16)).astype(jnp.float32)

@jax.custom_vjp
def low_back(v):
    return v

def low_keep(v):
    return (low(v), None)

def low_pass(kept, grad):
    return (grad,)

def back_keep(v):
    return (v, None)

def back_low(kept, grad):
    return (low(grad),)
low.defvjp(low_keep, low_pass)
low_back.defvjp(back_keep, back_low)
epsilon = 1e-05
adapter_scale = 4.0

def round_both(value):
    return low_back(low(value))

def matmul(left, right):
    return jnp.dot(left, right, precision=lax.Precision.HIGHEST, preferred_element_type=jnp.float32)

def product(form, left, right):
    return jnp.einsum(form, left, right, precision=lax.Precision.HIGHEST, preferred_element_type=jnp.float32)

def split_heads(arrays):
    return arrays.reshape(arrays.shape[0], H, HD).transpose(1, 0, 2)

def merge_heads(arrays):
    return arrays.transpose(1, 0, 2).reshape(arrays.shape[1], H * HD)

def layer_norm(resid, gain, shift):
    average = lax.optimization_barrier(jnp.mean(resid, axis=-1, keepdims=True))
    centered = resid - average
    variance = lax.optimization_barrier(jnp.mean(centered * centered, axis=-1, keepdims=True))
    return centered * lax.rsqrt(variance + epsilon) * gain + shift

def masked_softmax(scores, allowed):
    kept = jnp.where(allowed, scores, jnp.zeros_like(scores))
    floor_value = lax.optimization_barrier(jnp.min(kept, axis=-1, keepdims=True))
    row_max = lax.optimization_barrier(jnp.max(jnp.where(allowed, kept, floor_value), axis=-1, keepdims=True))
    weights = jnp.where(allowed, jnp.exp(kept - row_max), jnp.zeros_like(kept))
    return weights / lax.optimization_barrier(jnp.sum(weights, axis=-1, keepdims=True))

def attention(queries, key_rows, value_rows, allowed):
    qk_scale = HD ** (-0.5)
    scores = low_back(product('hqe,hke->hqk', queries, key_rows) * qk_scale)
    probs = low(masked_softmax(scores, allowed[None]))
    return round_both(merge_heads(product('hqk,hke->hqe', probs, value_rows)))

def sequence_layer(weights, seg_dec, seg_mem, inputs, memory_rows, prefix_arg, down_arg, up_arg):
    w_self, w_self_out, w_cross_q, w_cross_kv, w_cross_out, fc_in, fc_out, ln_gain, ln_bias = weights
    queries = split_heads(round_both(matmul(inputs, w_self[0])))
    key_rows = jnp.concatenate([split_heads(prefix_arg[0]), split_heads(round_both(matmul(inputs, w_self[1])))], axis=1)
    value_rows = jnp.concatenate([split_heads(prefix_arg[1]), split_heads(round_both(matmul(inputs, w_self[2])))], axis=1)
    positions = jnp.arange(SEQ, dtype=jnp.int32)
    causal = (seg_dec[:, None] == seg_dec[None, :]) & (positions[None, :] <= positions[:, None])
    allowed = jnp.concatenate([jnp.ones((SEQ, PREFIX), dtype=jnp.bool_), causal], axis=1)
    attended = low_back(matmul(attention(queries, key_rows, value_rows, allowed), w_self_out))
    hidden_one = layer_norm(inputs + attended, ln_gain[0], ln_bias[0])
    hidden_low_one = low(hidden_one)
    cross_queries = split_heads(round_both(matmul(hidden_low_one, w_cross_q)))
    cross_keys = split_heads(round_both(matmul(memory_rows, w_cross_kv[0])))
    cross_values = split_heads(round_both(matmul(memory_rows, w_cross_kv[1])))
    cross_allowed = seg_dec[:, None] == seg_mem[None, :]
    crossed = low_back(matmul(attention(cross_queries, cross_keys, cross_values, cross_allowed), w_cross_out))
    hidden_two = layer_norm(hidden_one + crossed, ln_gain[1], ln_bias[1])
    hidden_low_two = low(hidden_two)
    pre_gelu = low_back(matmul(hidden_low_two, fc_in))
    activated = low(jax.nn.gelu(pre_gelu, approximate=False))
    pre_relu = low_back(matmul(hidden_low_two, down_arg))
    adapted = low(pre_relu * jax.nn.sigmoid(pre_relu))
    branch = low_back(matmul(activated, fc_out) + adapter_scale * matmul(adapted, up_arg))
    return layer_norm(hidden_two + branch, ln_gain[2], ln_bias[2])

def widen(arrays):
    return arrays.astype(jnp.float32)

def reference(tokens, memory, cotangent, dec_seg, mem_seg, w_self, w_self_out, w_cross_q, w_cross_kv, w_cross_out, fc_in, fc_out, ad_down, ad_up, prefix, ln_gain, ln_bias):
    weights = tuple((widen(arrays) for arrays in (w_self, w_self_out, w_cross_q, w_cross_kv, w_cross_out, fc_in, fc_out, ln_gain, ln_bias)))
    seq_count = tokens.shape[0] // SEQ
    inputs = widen(tokens).reshape(seq_count, SEQ, D)
    memory_rows = widen(memory).reshape(seq_count, MLEN, D)
    grad_rows = widen(cotangent).reshape(seq_count, SEQ, D)
    seg_dec = dec_seg.astype(jnp.int32).reshape(seq_count, SEQ)
    seg_mem = mem_seg.astype(jnp.int32).reshape(seq_count, MLEN)
    prefix_wide = widen(prefix)
    down_wide = widen(ad_down)
    up_wide = widen(ad_up)

    def sequence_step(running, packed):
        inputs_one, memory_one, grad_one, seg_one, mem_one = packed

        def layer_apply(inputs_arg, memory_arg, prefix_arg, down_arg, up_arg):
            return sequence_layer(weights, seg_one, mem_one, inputs_arg, memory_arg, prefix_arg, down_arg, up_arg)
        result, pullback = jax.vjp(layer_apply, inputs_one, memory_one, prefix_wide, down_wide, up_wide)
        grad_in, grad_mem, grad_pre, grad_dn, grad_upw = pullback(grad_one)
        return ((running[0] + grad_pre, running[1] + grad_dn, running[2] + grad_upw), (result.astype(jnp.bfloat16), grad_in, grad_mem))
    initial = (jnp.zeros_like(prefix_wide), jnp.zeros_like(down_wide), jnp.zeros_like(up_wide))
    totals, stacked = lax.scan(sequence_step, initial, (inputs, memory_rows, grad_rows, seg_dec, seg_mem))
    output = stacked[0].reshape(seq_count * SEQ, D)
    grad_input = stacked[1].reshape(seq_count * SEQ, D)
    grad_memory = stacked[2].reshape(seq_count * MLEN, D)
    return (output, grad_input, grad_memory, totals[0], totals[1], totals[2])
```

```python
import functools
import math

import jax
import jax.numpy as jnp
from jax import lax
from jax.experimental import pallas as pl
from jax.experimental.pallas import tpu as pltpu
from jax.sharding import PartitionSpec as P

HD = 64
SEQ = 1024
MLEN = 1024


epsilon = 1e-05
adapter_scale = 4.0
masked_score = -1e30


def dot_right(left, right):
    return lax.dot_general(
        left, right, (((1,), (1,)), ((), ())), preferred_element_type=jnp.float32
    )


def dot_left(left, right):
    return lax.dot_general(
        left, right, (((0,), (0,)), ((), ())), preferred_element_type=jnp.float32
    )


def norm_parts(resid):
    average = jnp.mean(resid, axis=-1, keepdims=True)
    centered = resid - average
    inv_scale = lax.rsqrt(jnp.mean(centered * centered, axis=-1, keepdims=True) + epsilon)
    return (centered * inv_scale, inv_scale)


def norm_forward(resid, gain, shift):
    normed, inv_scale = norm_parts(resid)
    return normed * gain + shift


def norm_backward(resid, gain, grad_out):
    normed, inv_scale = norm_parts(resid)
    scaled = grad_out * gain
    return inv_scale * (
        scaled
        - jnp.mean(scaled, axis=-1, keepdims=True)
        - normed * jnp.mean(scaled * normed, axis=-1, keepdims=True)
    )


def gelu_slope(pre_gelu):
    return (
        0.5 * (1.0 + lax.erf(pre_gelu * 0.7071067811865476))
        + pre_gelu * jnp.exp(-0.5 * pre_gelu * pre_gelu) * 0.3989422804014327
    )


def silu_slope(pre_relu):
    sigma = jax.nn.sigmoid(pre_relu)
    return sigma * (1.0 + pre_relu * (1.0 - sigma))


def to_heads(arrays, heads_here):
    return arrays.reshape(arrays.shape[0], arrays.shape[1], heads_here, HD).transpose(0, 2, 1, 3)


def from_heads(arrays):
    return arrays.transpose(0, 2, 1, 3).reshape(
        arrays.shape[0] * arrays.shape[2], arrays.shape[1] * arrays.shape[3]
    )


def join_blocks(stacked):
    moved = jnp.moveaxis(stacked, 0, 1)
    return moved.reshape((moved.shape[0], moved.shape[1] * moved.shape[2]) + moved.shape[3:])


def block_mask(row_segs, key_segs, offset, causal):
    allowed = row_segs[:, None] == key_segs[None, :]
    if causal:
        row_places = offset + lax.iota(jnp.int32, row_segs.shape[0])
        key_places = lax.iota(jnp.int32, key_segs.shape[0])
        allowed = allowed & (key_places[None, :] <= row_places[:, None])
    return allowed


def block_scores(queries, key_rows, allowed, prefix_keys):
    qk_scale = HD ** (-0.5)
    token_scores = (
        jnp.einsum("hqe,hke->hqk", queries, key_rows, preferred_element_type=jnp.float32) * qk_scale
    )
    token_scores = jnp.where(allowed[None], token_scores, masked_score)
    if prefix_keys is None:
        return (token_scores, None)
    prefix_scores = (
        jnp.einsum("hqe,hpe->hqp", queries, prefix_keys, preferred_element_type=jnp.float32)
        * qk_scale
    )
    return (token_scores, prefix_scores)


def attend_block(queries, key_rows, value_rows, allowed, prefix_keys, prefix_values):
    token_scores, prefix_scores = block_scores(queries, key_rows, allowed, prefix_keys)
    row_max = jnp.max(token_scores, axis=-1, keepdims=True)
    if prefix_scores is not None:
        row_max = jnp.maximum(row_max, jnp.max(prefix_scores, axis=-1, keepdims=True))
    token_weights = jnp.exp(token_scores - row_max)
    row_total = jnp.sum(token_weights, axis=-1, keepdims=True)
    if prefix_scores is not None:
        prefix_weights = jnp.exp(prefix_scores - row_max)
        row_total = row_total + jnp.sum(prefix_weights, axis=-1, keepdims=True)
    context = jnp.einsum(
        "hqk,hke->hqe",
        (token_weights / row_total).astype(jnp.bfloat16),
        value_rows,
        preferred_element_type=jnp.float32,
    )
    if prefix_scores is not None:
        context = context + jnp.einsum(
            "hqp,hpe->hqe",
            (prefix_weights / row_total).astype(jnp.bfloat16),
            prefix_values,
            preferred_element_type=jnp.float32,
        )
    return (context.astype(jnp.bfloat16), row_max + jnp.log(row_total))


def attend_back(
    queries, key_rows, value_rows, allowed, prefix_keys, prefix_values, log_total, context_grad
):
    qk_scale = HD ** (-0.5)
    token_scores, prefix_scores = block_scores(queries, key_rows, allowed, prefix_keys)
    token_probs = jnp.exp(token_scores - log_total)
    token_dprob = jnp.einsum(
        "hqe,hke->hqk", context_grad, value_rows, preferred_element_type=jnp.float32
    )
    inner = jnp.sum(token_probs * token_dprob, axis=-1, keepdims=True)
    if prefix_scores is not None:
        prefix_probs = jnp.exp(prefix_scores - log_total)
        prefix_dprob = jnp.einsum(
            "hqe,hpe->hqp", context_grad, prefix_values, preferred_element_type=jnp.float32
        )
        inner = inner + jnp.sum(prefix_probs * prefix_dprob, axis=-1, keepdims=True)
    token_dscore = (token_probs * (token_dprob - inner)).astype(jnp.bfloat16)
    query_grad = jnp.einsum(
        "hqk,hke->hqe", token_dscore, key_rows, preferred_element_type=jnp.float32
    )
    key_grad = (
        jnp.einsum("hqk,hqe->hke", token_dscore, queries, preferred_element_type=jnp.float32)
        * qk_scale
    )
    value_grad = jnp.einsum(
        "hqk,hqe->hke",
        token_probs.astype(jnp.bfloat16),
        context_grad,
        preferred_element_type=jnp.float32,
    )
    if prefix_scores is None:
        return (query_grad * qk_scale, (key_grad, value_grad))
    prefix_dscore = (prefix_probs * (prefix_dprob - inner)).astype(jnp.bfloat16)
    query_grad = query_grad + jnp.einsum(
        "hqp,hpe->hqe", prefix_dscore, prefix_keys, preferred_element_type=jnp.float32
    )
    prefix_key_grad = (
        jnp.einsum("hqp,hqe->hpe", prefix_dscore, queries, preferred_element_type=jnp.float32)
        * qk_scale
    )
    prefix_value_grad = jnp.einsum(
        "hqp,hqe->hpe",
        prefix_probs.astype(jnp.bfloat16),
        context_grad,
        preferred_element_type=jnp.float32,
    )
    return (query_grad * qk_scale, (key_grad, value_grad, prefix_key_grad, prefix_value_grad))


def sequence_forward(
    queries, key_rows, value_rows, row_segs, key_segs, prefix_keys, prefix_values, causal
):
    seq_width = queries.shape[1]
    block_rows = min(512, seq_width)

    def one_block(block_index):
        offset = block_index * block_rows
        allowed = block_mask(
            lax.dynamic_slice_in_dim(row_segs, offset, block_rows, 0), key_segs, offset, causal
        )
        query_part = lax.dynamic_slice_in_dim(queries, offset, block_rows, 1)
        return attend_block(query_part, key_rows, value_rows, allowed, prefix_keys, prefix_values)

    context, log_total = lax.map(one_block, jnp.arange(seq_width // block_rows, dtype=jnp.int32))
    return (join_blocks(context), join_blocks(log_total))


def sequence_backward(
    queries,
    key_rows,
    value_rows,
    row_segs,
    key_segs,
    prefix_keys,
    prefix_values,
    causal,
    log_total,
    context_grad,
):
    seq_width = queries.shape[1]
    block_rows = min(512, seq_width)
    key_zero = jnp.zeros(key_rows.shape, jnp.float32)
    initial = (key_zero, key_zero)
    if prefix_keys is not None:
        prefix_zero = jnp.zeros(prefix_keys.shape, jnp.float32)
        initial = initial + (prefix_zero, prefix_zero)

    def one_block(running, block_index):
        offset = block_index * block_rows
        allowed = block_mask(
            lax.dynamic_slice_in_dim(row_segs, offset, block_rows, 0), key_segs, offset, causal
        )
        query_part = lax.dynamic_slice_in_dim(queries, offset, block_rows, 1)
        total_part = lax.dynamic_slice_in_dim(log_total, offset, block_rows, 1)
        grad_part = lax.dynamic_slice_in_dim(context_grad, offset, block_rows, 1)
        query_grad, block_grads = attend_back(
            query_part,
            key_rows,
            value_rows,
            allowed,
            prefix_keys,
            prefix_values,
            total_part,
            grad_part,
        )
        return (tuple((summed + added for summed, added in zip(running, block_grads))), query_grad)

    running, query_grad = lax.scan(
        one_block, initial, jnp.arange(seq_width // block_rows, dtype=jnp.int32)
    )
    outputs = (
        join_blocks(query_grad).astype(jnp.bfloat16),
        running[0].astype(jnp.bfloat16),
        running[1].astype(jnp.bfloat16),
    )
    return outputs + running[2:]


def gather_rows(row_share):
    return lax.all_gather(row_share, "heads", axis=0, tiled=True)


def gather_grads(row_share):
    return lax.all_gather(row_share, "heads", axis=0, tiled=True)


def sum_rows(partial_value):
    return lax.psum_scatter(partial_value, "heads", scatter_dimension=0, tiled=True)


def sum_grads(partial_value):
    return lax.psum_scatter(partial_value, "heads", scatter_dimension=0, tiled=True)


def body(
    tokens,
    memory,
    cotangent,
    dec_seg,
    mem_seg,
    w_self,
    w_self_out,
    w_cross_q,
    w_cross_kv,
    w_cross_out,
    fc_in,
    fc_out,
    ad_down,
    ad_up,
    prefix,
    ln_gain,
    ln_bias,
):
    local_width = w_self.shape[2]
    heads_here = local_width // HD
    seg_dec = dec_seg.reshape(-1, SEQ)
    seg_mem = mem_seg.reshape(-1, MLEN)
    seq_count = seg_dec.shape[0]
    prefix_heads = to_heads(prefix, heads_here)
    prefix_keys = prefix_heads[0]
    prefix_values = prefix_heads[1]
    gathered_x = gather_rows(tokens)
    self_proj = jnp.einsum(
        "td,cdn->ctn", gathered_x, w_self, preferred_element_type=jnp.float32
    ).astype(jnp.bfloat16)
    self_proj = self_proj.reshape(3, seq_count, SEQ, local_width)
    self_queries = to_heads(self_proj[0], heads_here)
    self_keys = to_heads(self_proj[1], heads_here)
    self_values = to_heads(self_proj[2], heads_here)

    def self_forward(packed):
        return sequence_forward(
            packed[0], packed[1], packed[2], packed[3], packed[3], prefix_keys, prefix_values, True
        )

    self_context, self_total = lax.map(
        self_forward, (self_queries, self_keys, self_values, seg_dec)
    )
    attn_partial = jnp.dot(from_heads(self_context), w_self_out, preferred_element_type=jnp.float32)
    resid_one = tokens.astype(jnp.float32) + sum_rows(attn_partial)
    hidden_one = norm_forward(resid_one, ln_gain[0], ln_bias[0])
    gathered_one = gather_rows(hidden_one.astype(jnp.bfloat16))
    gathered_mem = lax.all_gather(memory, "heads", axis=0, tiled=True)
    cross_rows = jnp.dot(gathered_one, w_cross_q, preferred_element_type=jnp.float32).astype(
        jnp.bfloat16
    )
    cross_proj = jnp.einsum(
        "td,cdn->ctn", gathered_mem, w_cross_kv, preferred_element_type=jnp.float32
    ).astype(jnp.bfloat16)
    cross_queries = to_heads(cross_rows.reshape(seq_count, SEQ, local_width), heads_here)
    cross_proj = cross_proj.reshape(2, seq_count, MLEN, local_width)
    cross_keys = to_heads(cross_proj[0], heads_here)
    cross_values = to_heads(cross_proj[1], heads_here)

    def cross_forward(packed):
        return sequence_forward(
            packed[0], packed[1], packed[2], packed[3], packed[4], None, None, False
        )

    cross_context, cross_total = lax.map(
        cross_forward, (cross_queries, cross_keys, cross_values, seg_dec, seg_mem)
    )
    cross_partial = jnp.dot(
        from_heads(cross_context), w_cross_out, preferred_element_type=jnp.float32
    )
    resid_two = hidden_one + sum_rows(cross_partial)
    hidden_two = norm_forward(resid_two, ln_gain[1], ln_bias[1])
    hidden_low = hidden_two.astype(jnp.bfloat16)
    full_in, full_out, full_down, full_up = (fc_in, fc_out, ad_down, ad_up)
    ffn_rows = gather_rows(hidden_low)
    pre_gelu = jnp.dot(ffn_rows, full_in, preferred_element_type=jnp.float32)
    activated = jax.nn.gelu(pre_gelu, approximate=False).astype(jnp.bfloat16)
    pre_relu = jnp.dot(ffn_rows, full_down, preferred_element_type=jnp.float32)
    adapted = (pre_relu * jax.nn.sigmoid(pre_relu)).astype(jnp.bfloat16)
    branch = jnp.dot(
        activated, full_out, preferred_element_type=jnp.float32
    ) + adapter_scale * jnp.dot(adapted, full_up, preferred_element_type=jnp.float32)
    resid_three = hidden_two + sum_rows(branch)
    output = norm_forward(resid_three, ln_gain[2], ln_bias[2]).astype(jnp.bfloat16)
    grad_three = norm_backward(resid_three, ln_gain[2], cotangent.astype(jnp.float32))
    grad_branch = grad_three.astype(jnp.bfloat16)
    branch_rows = gather_grads(grad_branch)
    grad_gelu = (dot_right(branch_rows, full_out) * gelu_slope(pre_gelu)).astype(jnp.bfloat16)
    grad_relu = (adapter_scale * dot_right(branch_rows, full_up) * silu_slope(pre_relu)).astype(
        jnp.bfloat16
    )
    up_grad = adapter_scale * dot_left(adapted, branch_rows)
    down_grad = dot_left(ffn_rows, grad_relu)
    hidden_partial = dot_right(grad_gelu, full_in) + dot_right(grad_relu, full_down)
    grad_two_in = grad_three + sum_grads(hidden_partial)
    down_grad, up_grad = (
        lax.psum(down_grad.astype(jnp.bfloat16), "rows").astype(jnp.float32),
        lax.psum(up_grad.astype(jnp.bfloat16), "rows").astype(jnp.float32),
    )
    grad_two = norm_backward(resid_two, ln_gain[1], grad_two_in)
    cross_out_rows = gather_grads(grad_two.astype(jnp.bfloat16))
    cross_dctx = dot_right(cross_out_rows, w_cross_out).astype(jnp.bfloat16)
    cross_dctx = to_heads(cross_dctx.reshape(seq_count, SEQ, local_width), heads_here)

    def cross_back(packed):
        return sequence_backward(
            packed[0],
            packed[1],
            packed[2],
            packed[3],
            packed[4],
            None,
            None,
            False,
            packed[5],
            packed[6],
        )

    cross_qgrad, cross_kgrad, cross_vgrad = lax.map(
        cross_back,
        (cross_queries, cross_keys, cross_values, seg_dec, seg_mem, cross_total, cross_dctx),
    )
    memory_kv = jnp.stack([from_heads(cross_kgrad), from_heads(cross_vgrad)])
    one_partial = dot_right(from_heads(cross_qgrad), w_cross_q)
    grad_one_in = grad_two + sum_grads(one_partial)
    memory_partial = jnp.einsum(
        "ctn,cdn->td", memory_kv, w_cross_kv, preferred_element_type=jnp.float32
    )
    grad_memory = lax.psum_scatter(
        memory_partial.astype(jnp.bfloat16), "heads", scatter_dimension=0, tiled=True
    ).astype(jnp.float32)
    grad_one = norm_backward(resid_one, ln_gain[0], grad_one_in)
    attn_rows = gather_grads(grad_one.astype(jnp.bfloat16))
    self_dctx = dot_right(attn_rows, w_self_out).astype(jnp.bfloat16)
    self_dctx = to_heads(self_dctx.reshape(seq_count, SEQ, local_width), heads_here)

    def self_back(running, packed):
        query_grad, key_grad, value_grad, pkey_grad, pvalue_grad = sequence_backward(
            packed[0],
            packed[1],
            packed[2],
            packed[3],
            packed[3],
            prefix_keys,
            prefix_values,
            True,
            packed[4],
            packed[5],
        )
        return (
            (running[0] + pkey_grad, running[1] + pvalue_grad),
            (query_grad, key_grad, value_grad),
        )

    zero_grad = jnp.zeros(prefix_keys.shape, jnp.float32)
    prefix_sums, self_grads = lax.scan(
        self_back,
        (zero_grad, zero_grad),
        (self_queries, self_keys, self_values, seg_dec, self_total, self_dctx),
    )
    self_stack = jnp.stack(
        [from_heads(self_grads[0]), from_heads(self_grads[1]), from_heads(self_grads[2])]
    )
    input_partial = jnp.einsum(
        "ctn,cdn->td", self_stack, w_self, preferred_element_type=jnp.float32
    )
    grad_input = grad_one + sum_grads(input_partial)
    prefix_grad = (
        jnp.stack([prefix_sums[0], prefix_sums[1]])
        .transpose(0, 2, 1, 3)
        .reshape(2, prefix.shape[1], local_width)
    )
    prefix_grad = lax.psum(prefix_grad, "rows")
    return (output, grad_input, grad_memory, prefix_grad, down_grad, up_grad)


QB = 256
KB = 256
LOG2E = math.log2(math.e)
NEG = -1e30
WIDTHS = (256, 384, 512, 768, 1024)


def nt(a, b):
    return lax.dot_general(a, b, (((1,), (1,)), ((), ())), preferred_element_type=jnp.float32)


def nn(a, b):
    return lax.dot_general(a, b, (((1,), (0,)), ((), ())), preferred_element_type=jnp.float32)


def half_lanes(v, h):
    lane = lax.broadcasted_iota(jnp.int32, v.shape, 1)
    keep = (lane < 64) if h == 0 else (lane >= 64)
    return jnp.where(keep, v, jnp.zeros_like(v))


def prefix_rows(scores):
    row = lax.broadcasted_iota(jnp.int32, scores.shape, 0)
    return jnp.where(lax.rem(row, 64) < 30, scores, NEG)


def fwd_kernel(has_prefix, win, q_ref, k_ref, v_ref, lo_ref, hi_ref, *rest):
    if has_prefix:
        kp_ref, vp_ref, ctx_ref, lse_ref, vt_ref = rest
    else:
        ctx_ref, lse_ref, vt_ref = rest
    scale = 0.125 * LOG2E
    vt_ref[...] = v_ref[...].astype(jnp.float32).T.astype(jnp.bfloat16)
    if has_prefix:
        vpt = vp_ref[0].astype(jnp.float32).T.astype(jnp.bfloat16)

    def one(qi, _):
        q0 = pl.multiple_of(qi * QB, QB)
        q = q_ref[pl.ds(q0, QB), :]
        lo = lo_ref[:, pl.ds(q0, QB)]
        hi = hi_ref[:, pl.ds(q0, QB)]
        st = pl.multiple_of(win[qi, 0], 128)

        def run(width):
            k = k_ref[pl.ds(st, width), :]
            pos = st + lax.broadcasted_iota(jnp.int32, (width, QB), 0)
            mask = (pos >= lo) & (pos <= hi)
            if has_prefix:
                sp = prefix_rows(nt(kp_ref[0], q) * scale)
            outs, tops, sums = [], [], []
            for h in range(2):
                s = nt(k, half_lanes(q, h)) * scale
                s = jnp.where(mask, s, NEG)
                m = jnp.max(s, axis=0, keepdims=True)
                if has_prefix:
                    m = jnp.maximum(m, jnp.max(sp[h * 64 : h * 64 + 32], axis=0, keepdims=True))
                e = jnp.exp2(s - m)
                l = jnp.sum(e, axis=0, keepdims=True)
                vt = vt_ref[h * 64 : h * 64 + 64, pl.ds(st, width)]
                outs.append(nn(vt, e.astype(jnp.bfloat16)))
                tops.append(m)
                sums.append(l)
            if has_prefix:
                mm = jnp.concatenate([jnp.broadcast_to(t, (64, QB)) for t in tops], axis=0)
                ep = jnp.exp2(sp - mm)
                sums = [
                    sums[h] + jnp.sum(ep[h * 64 : h * 64 + 32], axis=0, keepdims=True)
                    for h in range(2)
                ]
                extra = nn(vpt, ep.astype(jnp.bfloat16))
                outs = [outs[h] + extra[h * 64 : h * 64 + 64] for h in range(2)]
            both = jnp.concatenate([outs[h] * (1.0 / sums[h]) for h in range(2)], axis=0)
            ctx_ref[pl.ds(q0, QB), :] = both.T.astype(jnp.bfloat16)
            for h in range(2):
                lse_ref[0, h : h + 1, pl.ds(q0, QB)] = tops[h] + jnp.log2(sums[h])

        for index, width in enumerate(WIDTHS):
            pl.when(win[qi, 1] == index)(functools.partial(run, width))
        return 0

    lax.fori_loop(0, SEQ // QB, one, 0)


def bwd_kernel(has_prefix, win, q_ref, k_ref, v_ref, lo_ref, hi_ref, ctx_ref, dctx_ref, lse_ref, *rest):
    if has_prefix:
        kp_ref, vp_ref, dq_ref, dk_ref, dv_ref, dpre_ref, kt_ref, dk_acc, dv_acc, dq_acc, dpre_acc = rest
    else:
        dq_ref, dk_ref, dv_ref, kt_ref, dk_acc, dv_acc, dq_acc = rest
    scale = 0.125 * LOG2E
    kt_ref[...] = k_ref[...].astype(jnp.float32).T.astype(jnp.bfloat16)
    dk_acc[...] = jnp.zeros_like(dk_acc)
    dv_acc[...] = jnp.zeros_like(dv_acc)
    if has_prefix:
        dpre_acc[...] = jnp.zeros_like(dpre_acc)
        kpt = kp_ref[0].astype(jnp.float32).T.astype(jnp.bfloat16)

    def one(qi, _):
        q0 = pl.multiple_of(qi * QB, QB)
        q = q_ref[pl.ds(q0, QB), :]
        dctx = dctx_ref[pl.ds(q0, QB), :]
        lo = lo_ref[:, pl.ds(q0, QB)]
        hi = hi_ref[:, pl.ds(q0, QB)]
        prod = (dctx.astype(jnp.float32) * ctx_ref[pl.ds(q0, QB), :].astype(jnp.float32)).T
        inner = [jnp.sum(prod[h * 64 : h * 64 + 64], axis=0, keepdims=True) for h in range(2)]
        lse = [lse_ref[0, h : h + 1, pl.ds(q0, QB)] for h in range(2)]
        qh = [half_lanes(q, h) for h in range(2)]
        dh = [half_lanes(dctx, h) for h in range(2)]
        if has_prefix:
            sp = prefix_rows(nt(kp_ref[0], q) * scale)
            rows = lambda pair: jnp.concatenate([jnp.broadcast_to(t, (64, QB)) for t in pair], axis=0)
            pp = jnp.exp2(sp - rows(lse))
            dpp = nt(vp_ref[0], dctx)
            dsp = (pp * (dpp - rows(inner))).astype(jnp.bfloat16)
            dpre_acc[0] += nn(dsp, q)
            dpre_acc[1] += nn(pp.astype(jnp.bfloat16), dctx)
            dq_acc[...] = nn(kpt, dsp)
        else:
            dq_acc[...] = jnp.zeros_like(dq_acc)

        def chunk(ki, _):
            k0 = pl.multiple_of(ki * KB, KB)
            k = k_ref[pl.ds(k0, KB), :]
            v = v_ref[pl.ds(k0, KB), :]
            pos = k0 + lax.broadcasted_iota(jnp.int32, (KB, QB), 0)
            mask = (pos >= lo) & (pos <= hi)
            ps, dss = [], []
            for h in range(2):
                s = nt(k, qh[h]) * scale
                p = jnp.exp2(jnp.where(mask, s, NEG) - lse[h])
                dp = nt(v, dh[h])
                ds = (p * (dp - inner[h])).astype(jnp.bfloat16)
                ps.append(p.astype(jnp.bfloat16))
                dss.append(ds)
                dq_acc[h * 64 : h * 64 + 64, :] += nn(kt_ref[h * 64 : h * 64 + 64, pl.ds(k0, KB)], ds)
            dv_acc[pl.ds(k0, KB), :] += nn(ps[0], dh[0]) + nn(ps[1], dh[1])
            dk_acc[pl.ds(k0, KB), :] += nn(dss[0], qh[0]) + nn(dss[1], qh[1])
            return 0

        lax.fori_loop(win[qi, 2], win[qi, 3], chunk, 0)
        dq_ref[pl.ds(q0, QB), :] = (dq_acc[...].T * 0.125).astype(jnp.bfloat16)
        return 0

    lax.fori_loop(0, SEQ // QB, one, 0)
    dk_ref[...] = (dk_acc[...] * 0.125).astype(jnp.bfloat16)
    dv_ref[...] = dv_acc[...].astype(jnp.bfloat16)
    if has_prefix:
        lane = lax.broadcasted_iota(jnp.int32, (32, 128), 1)
        for i, factor in ((0, 0.125), (1, 1.0)):
            dpre_ref[0, i] = jnp.where(lane < 64, dpre_acc[i, 0:32], dpre_acc[i, 64:96]) * factor


def row_spec():
    return pl.BlockSpec((1, SEQ), lambda j, *_: (0, 0))


def col_spec(offset):
    return pl.BlockSpec((SEQ, 128), lambda j, *_: (0, offset + j))


def pre_spec():
    return pl.BlockSpec((1, 128, 128), lambda j, *_: (j, 0, 0))


def lse_spec():
    return pl.BlockSpec((1, 8, SEQ), lambda j, *_: (j, 0, 0))


def attend_fwd(q, k, v, offs, lo, hi, win, prefix_kv=None):
    pairs = 4
    in_specs = [col_spec(offs[0]), col_spec(offs[1]), col_spec(offs[2]), row_spec(), row_spec()]
    args = [q, k, v, lo, hi]
    if prefix_kv is not None:
        in_specs += [pre_spec(), pre_spec()]
        args += list(prefix_kv)
    return pl.pallas_call(
        functools.partial(fwd_kernel, prefix_kv is not None),
        grid_spec=pltpu.PrefetchScalarGridSpec(
            num_scalar_prefetch=1,
            grid=(pairs,),
            in_specs=in_specs,
            out_specs=[col_spec(0), lse_spec()],
            scratch_shapes=[pltpu.VMEM((128, SEQ), jnp.bfloat16)],
        ),
        out_shape=[
            jax.ShapeDtypeStruct((SEQ, 128 * pairs), jnp.bfloat16),
            jax.ShapeDtypeStruct((pairs, 8, SEQ), jnp.float32),
        ],
        compiler_params=pltpu.CompilerParams(vmem_limit_bytes=40 * 2**20),
        cost_estimate=pl.CostEstimate(flops=2 * 2 * 8 * SEQ * SEQ * 64, bytes_accessed=6 * 2**20, transcendentals=8 * SEQ * SEQ),
        name="attend_forward",
    )(win, *args)


def attend_bwd(q, k, v, offs, lo, hi, win, ctx, dctx, lse, prefix_kv=None):
    pairs = 4
    in_specs = [col_spec(offs[0]), col_spec(offs[1]), col_spec(offs[2]), row_spec(), row_spec(), col_spec(0), col_spec(0), lse_spec()]
    args = [q, k, v, lo, hi, ctx, dctx, lse]
    wide = jax.ShapeDtypeStruct((SEQ, 128 * pairs), jnp.bfloat16)
    out_specs = [col_spec(0)] * 3
    out_shape = [wide] * 3
    if prefix_kv is not None:
        in_specs += [pre_spec(), pre_spec()]
        args += list(prefix_kv)
        out_specs = out_specs + [pl.BlockSpec((1, 2, 32, 128), lambda j, *_: (j, 0, 0, 0))]
        out_shape = out_shape + [jax.ShapeDtypeStruct((pairs, 2, 32, 128), jnp.float32)]
    return pl.pallas_call(
        functools.partial(bwd_kernel, prefix_kv is not None),
        grid_spec=pltpu.PrefetchScalarGridSpec(
            num_scalar_prefetch=1,
            grid=(pairs,),
            in_specs=in_specs,
            out_specs=out_specs,
            scratch_shapes=[
                pltpu.VMEM((128, SEQ), jnp.bfloat16),
                pltpu.VMEM((SEQ, 128), jnp.float32),
                pltpu.VMEM((SEQ, 128), jnp.float32),
                pltpu.VMEM((128, QB), jnp.float32),
            ]
            + ([pltpu.VMEM((2, 128, 128), jnp.float32)] if prefix_kv is not None else []),
        ),
        out_shape=out_shape,
        compiler_params=pltpu.CompilerParams(vmem_limit_bytes=40 * 2**20),
        cost_estimate=pl.CostEstimate(flops=5 * 2 * 8 * SEQ * SEQ * 64, bytes_accessed=10 * 2**20, transcendentals=8 * SEQ * SEQ),
        name="attend_backward",
    )(win, *args)


def windows(lo, hi):
    first = lo.reshape(-1, QB)[:, 0]
    last = hi.reshape(-1, QB)[:, -1]
    start = first // 128 * 128
    need = last + 1 - start
    variant = sum((need > width).astype(jnp.int32) for width in WIDTHS[:-1])
    width = jnp.full_like(variant, WIDTHS[0])
    for index in range(1, len(WIDTHS)):
        width = jnp.where(variant == index, WIDTHS[index], width)
    start = jnp.minimum(start, SEQ - width)
    return jnp.stack([start, variant, first // KB, last // KB + 1], axis=1).astype(jnp.int32)


AXES = ("rows", "heads")


def fast_fits(mesh):
    rows, heads = mesh.shape["rows"], mesh.shape["heads"]
    return heads == 4 and rows % 2 == 0 and (rows & (rows - 1)) == 0


def pairs_of(rows, move):
    def number(z, c, y, x):
        return (z * 2 + c) * 4 + y * 2 + x

    found = []
    for z in range(rows // 2):
        for c in range(2):
            for y in range(2):
                for x in range(2):
                    found.append((number(z, c, y, x), number(*move(z, c, y, x))))
    return found


class Moves:
    def __init__(self, rows):
        def perm(move):
            table = pairs_of(rows, move)
            return lambda value: lax.ppermute(value, AXES, table)

        self.core = perm(lambda z, c, y, x: (z, 1 - c, y, x))
        self.x = perm(lambda z, c, y, x: (z, c, y, 1 - x))
        self.y = perm(lambda z, c, y, x: (z, c, 1 - y, x))
        self.swap = perm(lambda z, c, y, x: (z, x, y, c))
        self.z = []
        step = 1
        while step < rows // 2:
            self.z.append(perm(lambda z, c, y, x, step=step: (z ^ step, c, y, x)))
            step *= 2


def fast_body(
    rows,
    tokens,
    memory,
    cotangent,
    dec_seg,
    mem_seg,
    w_self,
    w_self_out,
    w_cross_q,
    w_cross_kv,
    w_cross_out,
    fc_in,
    fc_out,
    ad_down,
    ad_up,
    prefix,
    ln_gain,
    ln_bias,
):
    bf16 = jnp.bfloat16
    f32 = jnp.float32
    move = Moves(rows)
    core = lax.axis_index("rows") % 2
    x_place = lax.axis_index("heads") % 2
    y_place = lax.axis_index("heads") // 2

    def half(value, axis):
        size = value.shape[axis] // 2
        return lax.dynamic_slice_in_dim(value, core * size, size, axis)

    def own_rows(value):
        size = value.shape[0] // 2
        return lax.dynamic_slice_in_dim(value, core * size, size, 0)

    def other_rows(value):
        size = value.shape[0] // 2
        return lax.dynamic_slice_in_dim(value, (1 - core) * size, size, 0)

    def whole(mine, others):
        return jnp.where(
            core == 0,
            jnp.concatenate([mine, others], axis=0),
            jnp.concatenate([others, mine], axis=0),
        )

    def four(value, axis, through_x):
        from_x = move.x(value)
        from_y = move.y(value)
        from_d = move.x(from_y) if through_x else move.y(from_x)
        return jnp.concatenate([value, from_x, from_y, from_d], axis=axis)

    tok = move.swap(tokens)
    tok_all = whole(tok, move.core(tok))
    self_w = four(half(w_self, 2), 2, False)
    prefix_all = four(half(prefix, 2), 2, False)
    mem_rows = move.swap(memory)
    mem_all = whole(mem_rows, move.core(mem_rows))
    self_out_m = four(half(w_self_out, 0), 0, True)
    self_out_o = move.core(self_out_m)
    cross_q_m = four(half(w_cross_q, 1), 1, True)
    cross_q_o = move.core(cross_q_m)
    cross_kv = four(half(w_cross_kv, 2), 2, False)
    cross_out_m = four(half(w_cross_out, 0), 0, True)
    cross_out_o = move.core(cross_out_m)
    cot = move.swap(cotangent).astype(f32)
    fc_in_m = four(half(fc_in, 1), 1, False)
    fc_in_o = move.core(fc_in_m)
    down_m = four(half(ad_down.T, 0), 0, False)
    down_o = move.core(down_m)
    fc_out_m = four(half(fc_out, 0), 0, True)
    fc_out_o = move.core(fc_out_m)
    up_m = four(half(ad_up, 0), 0, False)
    up_o = move.core(up_m)

    def chip_seg(seg):
        both = jnp.where(core == x_place, seg, move.core(seg))
        return lax.dynamic_slice_in_dim(both, y_place * SEQ, SEQ, 0)

    seg = chip_seg(dec_seg)
    mseg = chip_seg(mem_seg)
    self_lo = jnp.sum(seg[None, :] < seg[:, None], axis=1, dtype=jnp.int32)
    self_hi = lax.iota(jnp.int32, SEQ)
    cross_lo = jnp.sum(mseg[None, :] < seg[:, None], axis=1, dtype=jnp.int32)
    cross_hi = jnp.sum(mseg[None, :] <= seg[:, None], axis=1, dtype=jnp.int32) - 1
    self_win = windows(self_lo, self_hi)
    cross_win = windows(cross_lo, cross_hi)
    self_lo, self_hi = self_lo[None], self_hi[None]
    cross_lo, cross_hi = cross_lo[None], cross_hi[None]

    count = prefix.shape[1]
    blocks = prefix_all.reshape(2, count, 4, 2, HD)
    placed = jnp.zeros((2, 4, 2, HD, 2, HD), bf16)
    for head in range(2):
        placed = placed.at[:, :, head, :count, head, :].set(blocks[:, :, :, head].transpose(0, 2, 1, 3))
    placed = placed.reshape(2, 4, 128, 128)
    prefix_kv = (placed[0], placed[1])

    def dot(left, right):
        return jnp.dot(left, right, preferred_element_type=f32)

    width = self_w.shape[2]
    qkv = jnp.concatenate([dot(tok_all, self_w[i]).astype(bf16) for i in range(3)], axis=1)
    groups = width // 128
    self_offs = (0, groups, 2 * groups)
    self_ctx, self_lse = attend_fwd(qkv, qkv, qkv, self_offs, self_lo, self_hi, self_win, prefix_kv)
    got = move.core(other_rows(self_ctx))
    resid_one = tok.astype(f32) + dot(own_rows(self_ctx), self_out_m) + dot(got, self_out_o)
    hidden_one = norm_forward(resid_one, ln_gain[0], ln_bias[0])
    low_one = hidden_one.astype(bf16)

    kv = jnp.concatenate([dot(mem_all, cross_kv[i]).astype(bf16) for i in range(2)], axis=1)
    q_send = dot(low_one, cross_q_o).astype(bf16)
    cross_q = whole(dot(low_one, cross_q_m).astype(bf16), move.core(q_send))
    cross_offs = (0, 0, groups)
    cross_ctx, cross_lse = attend_fwd(cross_q, kv, kv, cross_offs, cross_lo, cross_hi, cross_win)
    got = move.core(other_rows(cross_ctx))
    resid_two = hidden_one + dot(own_rows(cross_ctx), cross_out_m) + dot(got, cross_out_o)
    hidden_two = norm_forward(resid_two, ln_gain[1], ln_bias[1])
    low_two = hidden_two.astype(bf16)

    pre_m = dot(low_two, fc_in_m)
    pre_o = dot(low_two, fc_in_o)
    act_m = jax.nn.gelu(pre_m, approximate=False).astype(bf16)
    act_o = jax.nn.gelu(pre_o, approximate=False).astype(bf16)
    relu_m = dot_right(low_two, down_m)
    relu_o = dot_right(low_two, down_o)
    ada_m = (relu_m * jax.nn.sigmoid(relu_m)).astype(bf16)
    ada_o = (relu_o * jax.nn.sigmoid(relu_o)).astype(bf16)
    branch = dot(act_m, fc_out_m) + dot(act_o, fc_out_o)
    branch = branch + adapter_scale * (dot(ada_m, up_m) + dot(ada_o, up_o))
    resid_three = hidden_two + branch
    output = move.swap(norm_forward(resid_three, ln_gain[2], ln_bias[2]).astype(bf16))
    grad_three = norm_backward(resid_three, ln_gain[2], cot)
    grad_branch = grad_three.astype(bf16)
    gelu_m = (dot_right(grad_branch, fc_out_m) * gelu_slope(pre_m)).astype(bf16)
    gelu_o = (dot_right(grad_branch, fc_out_o) * gelu_slope(pre_o)).astype(bf16)
    grelu_m = (adapter_scale * dot_right(grad_branch, up_m) * silu_slope(relu_m)).astype(bf16)
    grelu_o = (adapter_scale * dot_right(grad_branch, up_o) * silu_slope(relu_o)).astype(bf16)
    grad_two_in = grad_three + dot_right(gelu_m, fc_in_m) + dot_right(gelu_o, fc_in_o)
    grad_two_in = grad_two_in + dot(grelu_m, down_m) + dot(grelu_o, down_o)
    grad_two = norm_backward(resid_two, ln_gain[1], grad_two_in)

    def unit_grads(grelu, ada):
        return jnp.concatenate(
            [dot_left(grelu, low_two), adapter_scale * dot_left(ada, grad_branch)], axis=1
        )

    unit_mine = unit_grads(grelu_m, ada_m) + move.core(unit_grads(grelu_o, ada_o).astype(bf16)).astype(f32)
    units = unit_mine.shape[0] // 4
    pieces = [unit_mine[i * units : (i + 1) * units] for i in range(4)]
    low_pieces = [piece.astype(bf16) for piece in pieces]
    unit_sum = (
        pieces[0]
        + move.x(low_pieces[1]).astype(f32)
        + move.y(low_pieces[2]).astype(f32)
        + move.x(move.y(low_pieces[3])).astype(f32)
    )
    for step in move.z:
        unit_sum = unit_sum + step(unit_sum.astype(bf16)).astype(f32)
    unit_all = whole(unit_sum, move.core(unit_sum.astype(bf16)).astype(f32))
    features = low_two.shape[1]
    down_grad = unit_all[:, :features].T
    up_grad = unit_all[:, features:]

    low_grad_two = grad_two.astype(bf16)
    d_send = dot_right(low_grad_two, cross_out_o).astype(bf16)
    cross_dctx = whole(dot_right(low_grad_two, cross_out_m).astype(bf16), move.core(d_send))
    cross_dq, cross_dk, cross_dv = attend_bwd(
        cross_q, kv, kv, cross_offs, cross_lo, cross_hi, cross_win, cross_ctx, cross_dctx, cross_lse
    )
    got = move.core(other_rows(cross_dq))
    grad_one_in = grad_two + dot_right(own_rows(cross_dq), cross_q_m) + dot_right(got, cross_q_o)
    memory_part = dot_right(cross_dk, cross_kv[0]) + dot_right(cross_dv, cross_kv[1])
    memory_sum = own_rows(memory_part) + move.core(other_rows(memory_part).astype(bf16)).astype(f32)
    grad_memory = move.swap(memory_sum.astype(bf16)).astype(f32)
    grad_one = norm_backward(resid_one, ln_gain[0], grad_one_in)

    low_grad_one = grad_one.astype(bf16)
    d_send = dot_right(low_grad_one, self_out_o).astype(bf16)
    self_dctx = whole(dot_right(low_grad_one, self_out_m).astype(bf16), move.core(d_send))
    self_dq, self_dk, self_dv, prefix_blocks = attend_bwd(
        qkv, qkv, qkv, self_offs, self_lo, self_hi, self_win, self_ctx, self_dctx, self_lse, prefix_kv
    )
    input_part = dot_right(self_dq, self_w[0]) + dot_right(self_dk, self_w[1]) + dot_right(self_dv, self_w[2])
    input_sum = own_rows(input_part) + move.core(other_rows(input_part).astype(bf16)).astype(f32) + grad_one
    grad_input = move.swap(input_sum.astype(bf16)).astype(f32)

    prefix_sum = (
        prefix_blocks[0]
        + move.x(prefix_blocks[1])
        + move.y(prefix_blocks[2])
        + move.x(move.y(prefix_blocks[3]))
    )
    for step in move.z:
        prefix_sum = prefix_sum + step(prefix_sum)
    prefix_other = move.core(prefix_sum)
    prefix_grad = jnp.where(
        core == 0,
        jnp.concatenate([prefix_sum, prefix_other], axis=2),
        jnp.concatenate([prefix_other, prefix_sum], axis=2),
    )[:, :count]
    return (output, grad_input, grad_memory, prefix_grad, down_grad, up_grad)


def solution(mesh):
    in_specs = (
        P(("rows", "heads"), None),
        P(("rows", "heads"), None),
        P(("rows", "heads"), None),
        P("rows"),
        P("rows"),
        P(None, None, "heads"),
        P("heads", None),
        P(None, "heads"),
        P(None, None, "heads"),
        P("heads", None),
        P(None, "heads"),
        P("heads", None),
        P(None, "heads"),
        P("heads", None),
        P(None, None, "heads"),
        P(),
        P(),
    )
    out_specs = (
        P(("rows", "heads"), None),
        P(("rows", "heads"), None),
        P(("rows", "heads"), None),
        P(None, None, "heads"),
        P(None, "heads"),
        P("heads", None),
    )
    chosen = functools.partial(fast_body, mesh.shape["rows"]) if fast_fits(mesh) else body
    return jax.shard_map(chosen, mesh=mesh, in_specs=in_specs, out_specs=out_specs, check_vma=False)
```

```python
import functools
import math
import typing

import jax
import jax.numpy as jnp
from jax import lax
from jax.experimental import pallas as pl
from jax.experimental.pallas import tpu as pltpu
from jax.sharding import PartitionSpec as P

HD = 64
SEQ = 1024
MLEN = 1024


epsilon = 1e-05
adapter_scale = 4.0
masked_score = -1e30


def dot_right(left, right):
    return lax.dot_general(
        left, right, (((1,), (1,)), ((), ())), preferred_element_type=jnp.float32
    )


def dot_left(left, right):
    return lax.dot_general(
        left, right, (((0,), (0,)), ((), ())), preferred_element_type=jnp.float32
    )


def norm_parts(resid):
    average = jnp.mean(resid, axis=-1, keepdims=True)
    centered = resid - average
    inv_scale = lax.rsqrt(jnp.mean(centered * centered, axis=-1, keepdims=True) + epsilon)
    return (centered * inv_scale, inv_scale)


def norm_forward(resid, gain, shift):
    normed, inv_scale = norm_parts(resid)
    return normed * gain + shift


def norm_backward(resid, gain, grad_out):
    normed, inv_scale = norm_parts(resid)
    scaled = grad_out * gain
    return inv_scale * (
        scaled
        - jnp.mean(scaled, axis=-1, keepdims=True)
        - normed * jnp.mean(scaled * normed, axis=-1, keepdims=True)
    )


def gelu_slope(pre_gelu):
    return (
        0.5 * (1.0 + lax.erf(pre_gelu * 0.7071067811865476))
        + pre_gelu * jnp.exp(-0.5 * pre_gelu * pre_gelu) * 0.3989422804014327
    )


def silu_slope(pre_relu):
    sigma = jax.nn.sigmoid(pre_relu)
    return sigma * (1.0 + pre_relu * (1.0 - sigma))


def to_heads(arrays, heads_here):
    return arrays.reshape(arrays.shape[0], arrays.shape[1], heads_here, HD).transpose(0, 2, 1, 3)


def from_heads(arrays):
    return arrays.transpose(0, 2, 1, 3).reshape(
        arrays.shape[0] * arrays.shape[2], arrays.shape[1] * arrays.shape[3]
    )


def join_blocks(stacked):
    moved = jnp.moveaxis(stacked, 0, 1)
    return moved.reshape((moved.shape[0], moved.shape[1] * moved.shape[2]) + moved.shape[3:])


def block_mask(row_segs, key_segs, offset, causal):
    allowed = row_segs[:, None] == key_segs[None, :]
    if causal:
        row_places = offset + lax.iota(jnp.int32, row_segs.shape[0])
        key_places = lax.iota(jnp.int32, key_segs.shape[0])
        allowed = allowed & (key_places[None, :] <= row_places[:, None])
    return allowed


def block_scores(queries, key_rows, allowed, prefix_keys):
    qk_scale = HD ** (-0.5)
    token_scores = (
        jnp.einsum("hqe,hke->hqk", queries, key_rows, preferred_element_type=jnp.float32) * qk_scale
    )
    token_scores = jnp.where(allowed[None], token_scores, masked_score)
    if prefix_keys is None:
        return (token_scores, None)
    prefix_scores = (
        jnp.einsum("hqe,hpe->hqp", queries, prefix_keys, preferred_element_type=jnp.float32)
        * qk_scale
    )
    return (token_scores, prefix_scores)


def attend_block(queries, key_rows, value_rows, allowed, prefix_keys, prefix_values):
    token_scores, prefix_scores = block_scores(queries, key_rows, allowed, prefix_keys)
    row_max = jnp.max(token_scores, axis=-1, keepdims=True)
    if prefix_scores is not None:
        row_max = jnp.maximum(row_max, jnp.max(prefix_scores, axis=-1, keepdims=True))
    token_weights = jnp.exp(token_scores - row_max)
    row_total = jnp.sum(token_weights, axis=-1, keepdims=True)
    if prefix_scores is not None:
        prefix_weights = jnp.exp(prefix_scores - row_max)
        row_total = row_total + jnp.sum(prefix_weights, axis=-1, keepdims=True)
    context = jnp.einsum(
        "hqk,hke->hqe",
        (token_weights / row_total).astype(jnp.bfloat16),
        value_rows,
        preferred_element_type=jnp.float32,
    )
    if prefix_scores is not None:
        context = context + jnp.einsum(
            "hqp,hpe->hqe",
            (prefix_weights / row_total).astype(jnp.bfloat16),
            prefix_values,
            preferred_element_type=jnp.float32,
        )
    return (context.astype(jnp.bfloat16), row_max + jnp.log(row_total))


def attend_back(
    queries, key_rows, value_rows, allowed, prefix_keys, prefix_values, log_total, context_grad
):
    qk_scale = HD ** (-0.5)
    token_scores, prefix_scores = block_scores(queries, key_rows, allowed, prefix_keys)
    token_probs = jnp.exp(token_scores - log_total)
    token_dprob = jnp.einsum(
        "hqe,hke->hqk", context_grad, value_rows, preferred_element_type=jnp.float32
    )
    inner = jnp.sum(token_probs * token_dprob, axis=-1, keepdims=True)
    if prefix_scores is not None:
        prefix_probs = jnp.exp(prefix_scores - log_total)
        prefix_dprob = jnp.einsum(
            "hqe,hpe->hqp", context_grad, prefix_values, preferred_element_type=jnp.float32
        )
        inner = inner + jnp.sum(prefix_probs * prefix_dprob, axis=-1, keepdims=True)
    token_dscore = (token_probs * (token_dprob - inner)).astype(jnp.bfloat16)
    query_grad = jnp.einsum(
        "hqk,hke->hqe", token_dscore, key_rows, preferred_element_type=jnp.float32
    )
    key_grad = (
        jnp.einsum("hqk,hqe->hke", token_dscore, queries, preferred_element_type=jnp.float32)
        * qk_scale
    )
    value_grad = jnp.einsum(
        "hqk,hqe->hke",
        token_probs.astype(jnp.bfloat16),
        context_grad,
        preferred_element_type=jnp.float32,
    )
    if prefix_scores is None:
        return (query_grad * qk_scale, (key_grad, value_grad))
    prefix_dscore = (prefix_probs * (prefix_dprob - inner)).astype(jnp.bfloat16)
    query_grad = query_grad + jnp.einsum(
        "hqp,hpe->hqe", prefix_dscore, prefix_keys, preferred_element_type=jnp.float32
    )
    prefix_key_grad = (
        jnp.einsum("hqp,hqe->hpe", prefix_dscore, queries, preferred_element_type=jnp.float32)
        * qk_scale
    )
    prefix_value_grad = jnp.einsum(
        "hqp,hqe->hpe",
        prefix_probs.astype(jnp.bfloat16),
        context_grad,
        preferred_element_type=jnp.float32,
    )
    return (query_grad * qk_scale, (key_grad, value_grad, prefix_key_grad, prefix_value_grad))


def sequence_forward(
    queries, key_rows, value_rows, row_segs, key_segs, prefix_keys, prefix_values, causal
):
    seq_width = queries.shape[1]
    block_rows = min(512, seq_width)

    def one_block(block_index):
        offset = block_index * block_rows
        allowed = block_mask(
            lax.dynamic_slice_in_dim(row_segs, offset, block_rows, 0), key_segs, offset, causal
        )
        query_part = lax.dynamic_slice_in_dim(queries, offset, block_rows, 1)
        return attend_block(query_part, key_rows, value_rows, allowed, prefix_keys, prefix_values)

    context, log_total = lax.map(one_block, jnp.arange(seq_width // block_rows, dtype=jnp.int32))
    return (join_blocks(context), join_blocks(log_total))


def sequence_backward(
    queries,
    key_rows,
    value_rows,
    row_segs,
    key_segs,
    prefix_keys,
    prefix_values,
    causal,
    log_total,
    context_grad,
):
    seq_width = queries.shape[1]
    block_rows = min(512, seq_width)
    key_zero = jnp.zeros(key_rows.shape, jnp.float32)
    initial = (key_zero, key_zero)
    if prefix_keys is not None:
        prefix_zero = jnp.zeros(prefix_keys.shape, jnp.float32)
        initial = initial + (prefix_zero, prefix_zero)

    def one_block(running, block_index):
        offset = block_index * block_rows
        allowed = block_mask(
            lax.dynamic_slice_in_dim(row_segs, offset, block_rows, 0), key_segs, offset, causal
        )
        query_part = lax.dynamic_slice_in_dim(queries, offset, block_rows, 1)
        total_part = lax.dynamic_slice_in_dim(log_total, offset, block_rows, 1)
        grad_part = lax.dynamic_slice_in_dim(context_grad, offset, block_rows, 1)
        query_grad, block_grads = attend_back(
            query_part,
            key_rows,
            value_rows,
            allowed,
            prefix_keys,
            prefix_values,
            total_part,
            grad_part,
        )
        return (tuple((summed + added for summed, added in zip(running, block_grads))), query_grad)

    running, query_grad = lax.scan(
        one_block, initial, jnp.arange(seq_width // block_rows, dtype=jnp.int32)
    )
    outputs = (
        join_blocks(query_grad).astype(jnp.bfloat16),
        running[0].astype(jnp.bfloat16),
        running[1].astype(jnp.bfloat16),
    )
    return outputs + running[2:]


def gather_rows(row_share):
    return lax.all_gather(row_share, "heads", axis=0, tiled=True)


def gather_grads(row_share):
    return lax.all_gather(row_share, "heads", axis=0, tiled=True)


def sum_rows(partial_value):
    return lax.psum_scatter(partial_value, "heads", scatter_dimension=0, tiled=True)


def sum_grads(partial_value):
    return lax.psum_scatter(partial_value, "heads", scatter_dimension=0, tiled=True)


def body(
    tokens,
    memory,
    cotangent,
    dec_seg,
    mem_seg,
    w_self,
    w_self_out,
    w_cross_q,
    w_cross_kv,
    w_cross_out,
    fc_in,
    fc_out,
    ad_down,
    ad_up,
    prefix,
    ln_gain,
    ln_bias,
):
    local_width = w_self.shape[2]
    heads_here = local_width // HD
    seg_dec = dec_seg.reshape(-1, SEQ)
    seg_mem = mem_seg.reshape(-1, MLEN)
    seq_count = seg_dec.shape[0]
    prefix_heads = to_heads(prefix, heads_here)
    prefix_keys = prefix_heads[0]
    prefix_values = prefix_heads[1]
    gathered_x = gather_rows(tokens)
    self_proj = jnp.einsum(
        "td,cdn->ctn", gathered_x, w_self, preferred_element_type=jnp.float32
    ).astype(jnp.bfloat16)
    self_proj = self_proj.reshape(3, seq_count, SEQ, local_width)
    self_queries = to_heads(self_proj[0], heads_here)
    self_keys = to_heads(self_proj[1], heads_here)
    self_values = to_heads(self_proj[2], heads_here)

    def self_forward(packed):
        return sequence_forward(
            packed[0], packed[1], packed[2], packed[3], packed[3], prefix_keys, prefix_values, True
        )

    self_context, self_total = lax.map(
        self_forward, (self_queries, self_keys, self_values, seg_dec)
    )
    attn_partial = jnp.dot(from_heads(self_context), w_self_out, preferred_element_type=jnp.float32)
    resid_one = tokens.astype(jnp.float32) + sum_rows(attn_partial)
    hidden_one = norm_forward(resid_one, ln_gain[0], ln_bias[0])
    gathered_one = gather_rows(hidden_one.astype(jnp.bfloat16))
    gathered_mem = lax.all_gather(memory, "heads", axis=0, tiled=True)
    cross_rows = jnp.dot(gathered_one, w_cross_q, preferred_element_type=jnp.float32).astype(
        jnp.bfloat16
    )
    cross_proj = jnp.einsum(
        "td,cdn->ctn", gathered_mem, w_cross_kv, preferred_element_type=jnp.float32
    ).astype(jnp.bfloat16)
    cross_queries = to_heads(cross_rows.reshape(seq_count, SEQ, local_width), heads_here)
    cross_proj = cross_proj.reshape(2, seq_count, MLEN, local_width)
    cross_keys = to_heads(cross_proj[0], heads_here)
    cross_values = to_heads(cross_proj[1], heads_here)

    def cross_forward(packed):
        return sequence_forward(
            packed[0], packed[1], packed[2], packed[3], packed[4], None, None, False
        )

    cross_context, cross_total = lax.map(
        cross_forward, (cross_queries, cross_keys, cross_values, seg_dec, seg_mem)
    )
    cross_partial = jnp.dot(
        from_heads(cross_context), w_cross_out, preferred_element_type=jnp.float32
    )
    resid_two = hidden_one + sum_rows(cross_partial)
    hidden_two = norm_forward(resid_two, ln_gain[1], ln_bias[1])
    hidden_low = hidden_two.astype(jnp.bfloat16)
    full_in, full_out, full_down, full_up = (fc_in, fc_out, ad_down, ad_up)
    ffn_rows = gather_rows(hidden_low)
    pre_gelu = jnp.dot(ffn_rows, full_in, preferred_element_type=jnp.float32)
    activated = jax.nn.gelu(pre_gelu, approximate=False).astype(jnp.bfloat16)
    pre_relu = jnp.dot(ffn_rows, full_down, preferred_element_type=jnp.float32)
    adapted = (pre_relu * jax.nn.sigmoid(pre_relu)).astype(jnp.bfloat16)
    branch = jnp.dot(
        activated, full_out, preferred_element_type=jnp.float32
    ) + adapter_scale * jnp.dot(adapted, full_up, preferred_element_type=jnp.float32)
    resid_three = hidden_two + sum_rows(branch)
    output = norm_forward(resid_three, ln_gain[2], ln_bias[2]).astype(jnp.bfloat16)
    grad_three = norm_backward(resid_three, ln_gain[2], cotangent.astype(jnp.float32))
    grad_branch = grad_three.astype(jnp.bfloat16)
    branch_rows = gather_grads(grad_branch)
    grad_gelu = (dot_right(branch_rows, full_out) * gelu_slope(pre_gelu)).astype(jnp.bfloat16)
    grad_relu = (adapter_scale * dot_right(branch_rows, full_up) * silu_slope(pre_relu)).astype(
        jnp.bfloat16
    )
    up_grad = adapter_scale * dot_left(adapted, branch_rows)
    down_grad = dot_left(ffn_rows, grad_relu)
    hidden_partial = dot_right(grad_gelu, full_in) + dot_right(grad_relu, full_down)
    grad_two_in = grad_three + sum_grads(hidden_partial)
    down_grad, up_grad = (
        lax.psum(down_grad.astype(jnp.bfloat16), "rows").astype(jnp.float32),
        lax.psum(up_grad.astype(jnp.bfloat16), "rows").astype(jnp.float32),
    )
    grad_two = norm_backward(resid_two, ln_gain[1], grad_two_in)
    cross_out_rows = gather_grads(grad_two.astype(jnp.bfloat16))
    cross_dctx = dot_right(cross_out_rows, w_cross_out).astype(jnp.bfloat16)
    cross_dctx = to_heads(cross_dctx.reshape(seq_count, SEQ, local_width), heads_here)

    def cross_back(packed):
        return sequence_backward(
            packed[0],
            packed[1],
            packed[2],
            packed[3],
            packed[4],
            None,
            None,
            False,
            packed[5],
            packed[6],
        )

    cross_qgrad, cross_kgrad, cross_vgrad = lax.map(
        cross_back,
        (cross_queries, cross_keys, cross_values, seg_dec, seg_mem, cross_total, cross_dctx),
    )
    memory_kv = jnp.stack([from_heads(cross_kgrad), from_heads(cross_vgrad)])
    one_partial = dot_right(from_heads(cross_qgrad), w_cross_q)
    grad_one_in = grad_two + sum_grads(one_partial)
    memory_partial = jnp.einsum(
        "ctn,cdn->td", memory_kv, w_cross_kv, preferred_element_type=jnp.float32
    )
    grad_memory = lax.psum_scatter(
        memory_partial.astype(jnp.bfloat16), "heads", scatter_dimension=0, tiled=True
    ).astype(jnp.float32)
    grad_one = norm_backward(resid_one, ln_gain[0], grad_one_in)
    attn_rows = gather_grads(grad_one.astype(jnp.bfloat16))
    self_dctx = dot_right(attn_rows, w_self_out).astype(jnp.bfloat16)
    self_dctx = to_heads(self_dctx.reshape(seq_count, SEQ, local_width), heads_here)

    def self_back(running, packed):
        query_grad, key_grad, value_grad, pkey_grad, pvalue_grad = sequence_backward(
            packed[0],
            packed[1],
            packed[2],
            packed[3],
            packed[3],
            prefix_keys,
            prefix_values,
            True,
            packed[4],
            packed[5],
        )
        return (
            (running[0] + pkey_grad, running[1] + pvalue_grad),
            (query_grad, key_grad, value_grad),
        )

    zero_grad = jnp.zeros(prefix_keys.shape, jnp.float32)
    prefix_sums, self_grads = lax.scan(
        self_back,
        (zero_grad, zero_grad),
        (self_queries, self_keys, self_values, seg_dec, self_total, self_dctx),
    )
    self_stack = jnp.stack(
        [from_heads(self_grads[0]), from_heads(self_grads[1]), from_heads(self_grads[2])]
    )
    input_partial = jnp.einsum(
        "ctn,cdn->td", self_stack, w_self, preferred_element_type=jnp.float32
    )
    grad_input = grad_one + sum_grads(input_partial)
    prefix_grad = (
        jnp.stack([prefix_sums[0], prefix_sums[1]])
        .transpose(0, 2, 1, 3)
        .reshape(2, prefix.shape[1], local_width)
    )
    prefix_grad = lax.psum(prefix_grad, "rows")
    return (output, grad_input, grad_memory, prefix_grad, down_grad, up_grad)


QB = 256
KB = 256
LOG2E = math.log2(math.e)
NEG = -1e30


def nt(a, b):
    return lax.dot_general(a, b, (((1,), (1,)), ((), ())), preferred_element_type=jnp.float32)


def nn(a, b):
    return lax.dot_general(a, b, (((1,), (0,)), ((), ())), preferred_element_type=jnp.float32)


def tn(a, b):
    return lax.dot_general(a, b, (((0,), (0,)), ((), ())), preferred_element_type=jnp.float32)


def half_lanes(v, h):
    lane = lax.broadcasted_iota(jnp.int32, v.shape, 1)
    keep = (lane < 64) if h == 0 else (lane >= 64)
    return jnp.where(keep, v, jnp.zeros_like(v))


def prefix_rows(scores):
    row = lax.broadcasted_iota(jnp.int32, scores.shape, 0)
    return jnp.where(lax.rem(row, 64) < 30, scores, NEG)


MESH = pl.DeviceIdType.MESH
TILE = 256

TOK, TOK_C, MEM, MEM_C, COT, SEG, MSEG, SO_C, CO_C, CQ_C, Q_C = range(11)
A_X, A_Y, A_D = 11, 15, 19
R_X, R_Y, R_D = 23, 25, 27
C_X, C_Y, C_D = 29, 32, 35
SELF_CTX, CROSS_CTX = 38, 42
FEED_I, FEED_O, FEED_A = 46, 53, 60
SLOTS = 67
OWN, KEEP = 7, 24
LOCAL_SLOTS = 44


def prefix_block(rows):
    nothing = jnp.zeros_like(rows)
    return jnp.concatenate([half_lanes(rows, 0), nothing, half_lanes(rows, 1), nothing], axis=0)


def attend_tile(q, k, vt, mask, kp, vpt):
    scale = 0.125 * LOG2E
    rows = q.shape[0]
    if kp is not None:
        sp = prefix_rows(nt(kp, q) * scale)
    outs, tops, sums = [], [], []
    for h in range(2):
        s = jnp.where(mask, nt(k, half_lanes(q, h)) * scale, NEG)
        m = jnp.max(s, axis=0, keepdims=True)
        if kp is not None:
            m = jnp.maximum(m, jnp.max(sp[h * 64 : h * 64 + 32], axis=0, keepdims=True))
        e = jnp.exp2(s - m)
        outs.append(nn(vt[h * 64 : h * 64 + 64], e.astype(jnp.bfloat16)))
        sums.append(jnp.sum(e, axis=0, keepdims=True))
        tops.append(m)
    if kp is not None:
        mm = jnp.concatenate([jnp.broadcast_to(t, (64, rows)) for t in tops], axis=0)
        ep = jnp.exp2(sp - mm)
        sums = [sums[h] + jnp.sum(ep[h * 64 : h * 64 + 32], axis=0, keepdims=True) for h in range(2)]
        extra = nn(vpt, ep.astype(jnp.bfloat16))
        outs = [outs[h] + extra[h * 64 : h * 64 + 64] for h in range(2)]
    both = jnp.concatenate([outs[h] * (1.0 / sums[h]) for h in range(2)], axis=0)
    return both.T.astype(jnp.bfloat16), [tops[h] + jnp.log2(sums[h]) for h in range(2)]


def forward_kernel(
    tokens, memory, cotangent, seg, mseg, prefix, w_self, w_so, w_cq, w_ckv, w_co, fc_in, fc_out, ad, gain, bias,
    o_wself, o_qkv, o_sctx, o_slse, o_pre, o_wso_m, o_wso_o, o_wkv, o_wq_m, o_wq_o, o_wco_m, o_wco_o,
    o_q, o_kv, o_cctx, o_clse, o_resid1, o_resid2, o_bounds, o_tok, o_cot, fin, fout, fad,
    wself, qkv, sctx, slse, pre, wso_m, wso_o, wkv, wq_m, wq_o, wco_m, wco_o,
    q_all, kv, cctx, clse, resid1, resid2, bounds, tok, mem, sctx_o, cctx_o, q_send, hidden, low_one, vt, seg_v, mseg_v,
    send, recv, local,
):
    row = lax.axis_index("rows")
    head = lax.axis_index("heads")
    c, z = lax.rem(row, 2), lax.div(row, 2)
    x, y = lax.rem(head, 2), lax.div(head, 2)
    odd = lax.rem(z, 2)
    to_x = (row, 2 * y + 1 - x)
    to_y = (row, 2 * (1 - y) + x)
    to_d = (row, 2 * (1 - y) + 1 - x)
    to_z = (2 * (z + 1 - 2 * odd) + c, head)
    to_c = (2 * z + 1 - c, head)
    to_s = (2 * z + x, 2 * y + c)
    stays = c == x
    moves = c != x

    barrier = pltpu.get_barrier_semaphore()
    for device in (to_x, to_y, to_d, to_z, to_c):
        pl.semaphore_signal(barrier, inc=1, device_id=device, device_id_type=MESH)

    @pl.when(moves)
    def _():
        pl.semaphore_signal(barrier, inc=1, device_id=to_s, device_id_type=MESH)

    pl.semaphore_wait(barrier, 5 + moves.astype(jnp.int32))

    def there(slot, src, dst, device):
        return pltpu.make_async_remote_copy(
            src_ref=src, dst_ref=dst, send_sem=send.at[slot], recv_sem=recv.at[slot], device_id=device, device_id_type=MESH
        )

    def here(slot, src, dst):
        return pltpu.make_async_copy(src, dst, local.at[slot])

    half = tok.shape[0] // 2
    mine = pl.ds(pl.multiple_of(c * half, half), half)
    others = pl.ds(pl.multiple_of((1 - c) * half, half), half)
    partner_rows = pl.ds(pl.multiple_of(x * half, half), half)
    lanes = pl.ds(pl.multiple_of(c * 128, 128), 128)
    other_lanes = pl.ds(pl.multiple_of((1 - c) * 128, 128), 128)

    pending = []

    def go(copy):
        copy.start()
        pending.append(copy)
        return copy

    def swap_start(slot, src, target, dst_there, dst_here):
        pl.when(moves)(lambda: there(slot, src, target.at[dst_there], to_s).start())
        pl.when(stays)(lambda: here(slot, src, target.at[dst_here]).start())

    def swap_wait(slot, src, target, dst_here):
        pl.when(moves)(lambda: there(slot, src, target.at[dst_here], to_s).wait())
        pl.when(stays)(lambda: here(slot, src, target.at[dst_here]).wait())

    def seg_start(slot, src, dst):
        @pl.when(stays)
        def _():
            here(slot, src.at[y], dst).start()
            there(slot, src.at[y], dst, to_c).start()

    def seg_wait(slot, src, dst):
        @pl.when(stays)
        def _():
            here(slot, src.at[y], dst).wait()
            there(slot, src.at[y], dst, to_c).wait_send()

        pl.when(moves)(lambda: there(slot, src.at[y], dst, to_c).wait_recv())

    swap_start(TOK, tokens, tok, partner_rows, mine)
    own_a = [here(OWN + i, w_self.at[i, :, lanes], wself.at[0, :, pl.ds(128 * i, 128)]) for i in range(3)]
    own_a.append(here(OWN + 3, prefix.at[:, :, lanes], pre.at[0]))
    for copy in own_a:
        copy.start()

    def send_a(base, piece, device):
        out = [
            there(base + i, w_self.at[i, :, lanes], wself.at[piece, :, pl.ds(128 * i, 128)], device) for i in range(3)
        ]
        return out + [there(base + 3, prefix.at[:, :, lanes], pre.at[piece], device)]

    ax, ay = send_a(A_X, 1, to_x), send_a(A_Y, 2, to_y)
    for copy in ax + ay:
        go(copy)
    ad_ = [there(A_D + i, wself.at[1, :, pl.ds(128 * i, 128)], wself.at[3, :, pl.ds(128 * i, 128)], to_y) for i in range(3)]
    ad_.append(there(A_D + 3, pre.at[1], pre.at[3], to_y))

    seg_start(SEG, seg, seg_v)
    seg_start(MSEG, mseg, mseg_v)
    rows_c = pl.ds(pl.multiple_of(c * 128, 128), 128)
    rows_o = pl.ds(pl.multiple_of((1 - c) * 128, 128), 128)
    own_b = [
        here(OWN + 4, w_so.at[rows_c], wso_m.at[pl.ds(0, 128)]),
        here(OWN + 5, w_so.at[rows_o], wso_o.at[pl.ds(0, 128)]),
        here(OWN + 6, w_co.at[rows_c], wco_m.at[pl.ds(0, 128)]),
        here(OWN + 7, w_co.at[rows_o], wco_o.at[pl.ds(0, 128)]),
        here(OWN + 8, w_cq.at[:, lanes], wq_m.at[:, pl.ds(0, 128)]),
        here(OWN + 9, w_cq.at[:, other_lanes], wq_o.at[:, pl.ds(0, 128)]),
        here(OWN + 10, w_ckv.at[0, :, lanes], wkv.at[0, :, pl.ds(0, 128)]),
        here(OWN + 11, w_ckv.at[1, :, lanes], wkv.at[0, :, pl.ds(128, 128)]),
    ]
    for copy in own_b:
        copy.start()

    def send_r(base, piece, device):
        place = pl.ds(128 * piece, 128)
        return [
            there(base, w_so.at[rows_c], wso_m.at[place], device),
            there(base + 1, w_co.at[rows_c], wco_m.at[place], device),
        ]

    rx, ry, rd = send_r(R_X, 1, to_x), send_r(R_Y, 2, to_y), send_r(R_D, 3, to_d)

    def send_c(base, piece, device):
        return [
            there(base, w_cq.at[:, lanes], wq_m.at[:, pl.ds(128 * piece, 128)], device),
            there(base + 1, w_ckv.at[0, :, lanes], wkv.at[piece, :, pl.ds(0, 128)], device),
            there(base + 2, w_ckv.at[1, :, lanes], wkv.at[piece, :, pl.ds(128, 128)], device),
        ]

    cx, cy = send_c(C_X, 1, to_x), send_c(C_Y, 2, to_y)
    cd = [
        there(C_D, wq_m.at[:, pl.ds(128, 128)], wq_m.at[:, pl.ds(384, 128)], to_y),
        there(C_D + 1, wkv.at[1, :, pl.ds(0, 128)], wkv.at[3, :, pl.ds(0, 128)], to_y),
        there(C_D + 2, wkv.at[1, :, pl.ds(128, 128)], wkv.at[3, :, pl.ds(128, 128)], to_y),
    ]

    hid = fc_in.shape[1]
    units = ad.shape[1]
    at_cols = lambda start, size: (slice(None), pl.ds(pl.multiple_of(start, 256), size))
    at_rows = lambda start, size: (pl.ds(pl.multiple_of(start, 256), size), slice(None))
    at_units = lambda start, size: (slice(None), pl.ds(pl.multiple_of(start, 32), size), slice(None))
    def part(ref, lead, index):
        return ref.at[index] if lead is None else ref.at[(lead,) + index]

    class Feed:
        def __init__(self, base, src, dst, size, at, through_x):
            quarter = at(c * (size // 2) + odd * (size // 4), size // 4)
            half_of = (slice(None),) + at(c * (size // 2), size // 2)
            self.x = there(base, part(src, None, quarter), part(dst, 0, quarter), to_x)
            self.y = there(base + 1, part(src, None, quarter), part(dst, 1, quarter), to_y)
            if through_x:
                self.d = there(base + 2, part(dst, 1, quarter), part(dst, 2, quarter), to_x)
            else:
                self.d = there(base + 2, part(dst, 0, quarter), part(dst, 2, quarter), to_y)
            self.zx, self.zy, self.zd = [
                there(base + 3 + i, part(dst, i, quarter), part(dst, i, quarter), to_z) for i in range(3)
            ]
            self.c = there(base + 6, dst.at[half_of], dst.at[half_of], to_c)

    fi = Feed(FEED_I, fc_in, fin, hid, at_cols, True)
    fo = Feed(FEED_O, fc_out, fout, hid, at_rows, False)
    fa = Feed(FEED_A, ad, fad, units, at_units, False)

    swap_wait(TOK, tokens, tok, mine)
    tok_c = go(there(TOK_C, tok.at[mine], tok.at[mine], to_c))
    saves = []

    def keep(src, dst):
        copy = here(KEEP + len(saves), src, dst)
        copy.start()
        saves.append(copy)

    keep(tok.at[mine], o_tok)
    seg_wait(SEG, seg, seg_v)
    seg_wait(MSEG, mseg, mseg_v)
    dec, men = seg_v[...], mseg_v[...]

    def below(values, d):
        return jnp.sum((values < d).astype(jnp.int32), axis=1, keepdims=True)

    def pick(counts):
        out = jnp.broadcast_to(counts[0], dec.shape)
        for d in range(1, 4):
            out = jnp.where(dec == d, counts[d], out)
        return out

    zero = jnp.zeros((1, 1), jnp.int32)
    full = jnp.full((1, 1), MLEN, jnp.int32)
    self_lo = pick([zero] + [below(dec, d) for d in range(1, 4)])
    mem_counts = [zero] + [below(men, d) for d in range(1, 4)] + [full]
    bounds[...] = jnp.concatenate(
        [self_lo, lax.broadcasted_iota(jnp.int32, dec.shape, 1), pick(mem_counts[:4]), pick(mem_counts[1:]) - 1]
        + [jnp.zeros_like(dec)] * 4,
        axis=0,
    )
    keep(bounds, o_bounds)
    for copy in own_a:
        copy.wait()
    tok_c.wait_recv()

    def first_piece(p, _):
        @pl.when(p == 1)
        def _():
            for copy in ax:
                copy.wait_recv()
            for copy in ad_ + rx + rd:
                copy.start()
            swap_start(MEM, memory, mem, partner_rows, mine)
            for copy in cx:
                copy.start()

        @pl.when(p == 2)
        def _():
            for copy in ay:
                copy.wait_recv()
            for copy in ry + [fi.y, fi.x] + cy:
                copy.start()

        @pl.when(p == 3)
        def _():
            for copy in ad_:
                copy.wait_recv()

        def rows_of(t, _):
            rows = pl.ds(pl.multiple_of(t * TILE, TILE), TILE)
            qkv[p, rows, :] = nn(tok[rows, :], wself[p]).astype(jnp.bfloat16)
            return 0

        lax.fori_loop(0, SEQ // TILE, rows_of, 0)
        vt[...] = qkv[p, :, 256:384].astype(jnp.float32).T.astype(jnp.bfloat16)
        kp = prefix_block(pre[p, 0])
        vpt = prefix_block(pre[p, 1]).astype(jnp.float32).T.astype(jnp.bfloat16)
        place = pl.ds(pl.multiple_of(p * 128, 128), 128)
        for qi in range(SEQ // QB):
            width = (qi + 1) * QB
            span = slice(qi * QB, (qi + 1) * QB)
            pos = lax.broadcasted_iota(jnp.int32, (width, QB), 0)
            mask = (pos >= bounds[0:1, span]) & (pos <= bounds[1:2, span])
            out, lse = attend_tile(qkv[p, span, 0:128], qkv[p, 0:width, 128:256], vt[:, 0:width], mask, kp, vpt)
            sctx[span, place] = out
            for h in range(2):
                slse[p, h : h + 1, span] = lse[h]
        there(SELF_CTX + p, sctx.at[others, place], sctx_o.at[:, place], to_c).start()
        return 0

    lax.fori_loop(0, 4, first_piece, 0)
    pending.extend(ad_ + rx + rd + cx + ry + cy + [fi.x, fi.y])
    for i in range(4):
        copy = there(SELF_CTX + i, sctx.at[others, pl.ds(128 * i, 128)], sctx_o.at[:, pl.ds(128 * i, 128)], to_c)
        pending.append(copy)
    sctx_in = pending[-4:]
    keep(qkv, o_qkv)
    keep(wself, o_wself)
    keep(sctx, o_sctx)
    keep(slse, o_slse)
    keep(pre, o_pre)

    for copy in rx + ry + rd:
        copy.wait_recv()
    for copy in own_b:
        copy.wait()
    foreign = pl.ds(128, 384)
    so_c = go(there(SO_C, wso_m.at[foreign], wso_o.at[foreign], to_c))
    co_c = go(there(CO_C, wco_m.at[foreign], wco_o.at[foreign], to_c))
    fi.y.wait_recv()
    go(fi.d)
    go(fi.zy)
    for copy in sctx_in + [so_c]:
        copy.wait_recv()
    keep(wso_m, o_wso_m)
    keep(wso_o, o_wso_o)

    def out_rows(t, resid_before, ctx_m, ctx_o, w_m, w_o):
        rows = pl.ds(pl.multiple_of(t * TILE, TILE), TILE)
        rows_all = pl.ds(pl.multiple_of(c * half + t * TILE, TILE), TILE)
        return rows, rows_all, resid_before + nn(ctx_m[rows_all, :], w_m[...]) + nn(ctx_o[rows, :], w_o[...])

    def out_one(t, _):
        rows_all = pl.ds(pl.multiple_of(c * half + t * TILE, TILE), TILE)
        rows, _, resid = out_rows(t, tok[rows_all, :].astype(jnp.float32), sctx, sctx_o, wso_m, wso_o)
        resid1[rows, :] = resid
        normed = norm_forward(resid, gain[0:1, :], bias[0:1, :])
        hidden[rows, :] = normed
        low_one[rows, :] = normed.astype(jnp.bfloat16)
        return 0

    lax.fori_loop(0, half // TILE, out_one, 0)
    keep(resid1, o_resid1)

    fi.x.wait_recv()
    go(fi.zx)
    for copy in cx:
        copy.wait_recv()
    for copy in cd:
        go(copy)
    go(fo.x)
    go(fa.x)
    swap_wait(MEM, memory, mem, mine)
    mem_c = go(there(MEM_C, mem.at[mine], mem.at[mine], to_c))
    for copy in cy:
        copy.wait_recv()
    go(fo.y)
    go(fa.y)
    for copy in cd:
        copy.wait_recv()
    cq_c = go(there(CQ_C, wq_m.at[:, foreign], wq_o.at[:, foreign], to_c))
    mem_c.wait_recv()

    def kv_rows(step, _):
        p, t = lax.div(step, SEQ // TILE), lax.rem(step, SEQ // TILE)
        rows = pl.ds(pl.multiple_of(t * TILE, TILE), TILE)
        kv[p, rows, :] = nn(mem[rows, :], wkv[p]).astype(jnp.bfloat16)
        return 0

    lax.fori_loop(0, 4 * (MLEN // TILE), kv_rows, 0)
    keep(kv, o_kv)
    keep(wkv, o_wkv)
    fi.d.wait_recv()
    go(fi.zd)
    cq_c.wait_recv()
    keep(wq_m, o_wq_m)
    keep(wq_o, o_wq_o)

    def q_rows(t, _):
        rows = pl.ds(pl.multiple_of(t * TILE, TILE), TILE)
        rows_all = pl.ds(pl.multiple_of(c * half + t * TILE, TILE), TILE)
        q_send[rows, :] = nn(low_one[rows, :], wq_o[...]).astype(jnp.bfloat16)
        q_all[rows_all, :] = nn(low_one[rows, :], wq_m[...]).astype(jnp.bfloat16)
        return 0

    lax.fori_loop(0, half // TILE, q_rows, 0)
    q_c = go(there(Q_C, q_send, q_all.at[mine], to_c))
    q_c.wait_recv()
    keep(q_all, o_q)

    def second_piece(p, _):
        @pl.when(p == 2)
        def _():
            fo.x.wait_recv()
            fa.x.wait_recv()
            for copy in (fo.d, fa.d, fo.zx, fa.zx):
                copy.start()

        vt[...] = kv[p, :, 128:256].astype(jnp.float32).T.astype(jnp.bfloat16)
        place = pl.ds(pl.multiple_of(p * 128, 128), 128)

        def block(qi, _):
            span = pl.ds(pl.multiple_of(qi * QB, QB), QB)
            pos = lax.broadcasted_iota(jnp.int32, (MLEN, QB), 0)
            mask = (pos >= bounds[2:3, span]) & (pos <= bounds[3:4, span])
            out, lse = attend_tile(q_all[span, place], kv[p, :, 0:128], vt[...], mask, None, None)
            cctx[span, place] = out
            for h in range(2):
                clse[p, h : h + 1, span] = lse[h]
            return 0

        lax.fori_loop(0, SEQ // QB, block, 0)
        there(CROSS_CTX + p, cctx.at[others, place], cctx_o.at[:, place], to_c).start()
        return 0

    lax.fori_loop(0, 4, second_piece, 0)
    pending.extend([fo.d, fa.d, fo.zx, fa.zx])
    for i in range(4):
        copy = there(CROSS_CTX + i, cctx.at[others, pl.ds(128 * i, 128)], cctx_o.at[:, pl.ds(128 * i, 128)], to_c)
        pending.append(copy)
    cctx_in = pending[-4:]
    keep(cctx, o_cctx)
    keep(clse, o_clse)
    for copy in (fo.y, fa.y):
        copy.wait_recv()
    go(fo.zy)
    go(fa.zy)
    swap_start(COT, cotangent, o_cot, slice(None), slice(None))
    for copy in (fi.zx, fi.zy, fi.zd):
        copy.wait_recv()
    go(fi.c)
    for copy in cctx_in + [co_c]:
        copy.wait_recv()
    keep(wco_m, o_wco_m)
    keep(wco_o, o_wco_o)

    def out_two(t, _):
        rows = pl.ds(pl.multiple_of(t * TILE, TILE), TILE)
        rows, _, resid = out_rows(t, hidden[rows, :], cctx, cctx_o, wco_m, wco_o)
        resid2[rows, :] = resid
        return 0

    lax.fori_loop(0, half // TILE, out_two, 0)
    keep(resid2, o_resid2)
    for copy in (fo.d, fa.d):
        copy.wait_recv()
    go(fo.zd)
    go(fa.zd)
    for group in (fo, fa):
        for copy in (group.zx, group.zy, group.zd):
            copy.wait_recv()
    go(fo.c)
    go(fa.c)
    for group in (fi, fo, fa):
        group.c.wait_recv()
    swap_wait(COT, cotangent, o_cot, slice(None))
    for copy in pending:
        copy.wait_send()
    for copy in saves:
        copy.wait()


class Held(typing.NamedTuple):
    wself: jax.Array
    qkv: jax.Array
    sctx: jax.Array
    slse: jax.Array
    pre: jax.Array
    wso_m: jax.Array
    wso_o: jax.Array
    wkv: jax.Array
    wq_m: jax.Array
    wq_o: jax.Array
    wco_m: jax.Array
    wco_o: jax.Array
    q: jax.Array
    kv: jax.Array
    cctx: jax.Array
    clse: jax.Array
    resid1: jax.Array
    resid2: jax.Array
    bounds: jax.Array
    tok: jax.Array
    cot: jax.Array
    fin: jax.Array
    fout: jax.Array
    fad: jax.Array


def forward_call(tokens, memory, cotangent, seg, mseg, prefix, w_self, w_so, w_cq, w_ckv, w_co, fc_in, fc_out, ad, gain, bias):
    bf16, f32 = jnp.bfloat16, jnp.float32
    half, deep = tokens.shape
    shape = jax.ShapeDtypeStruct
    held = dict(
        wself=((4, deep, 384), bf16),
        qkv=((4, SEQ, 384), bf16),
        sctx=((SEQ, 512), bf16),
        slse=((4, 8, SEQ), f32),
        pre=((4, 2, 32, 128), bf16),
        wso_m=((512, deep), bf16),
        wso_o=((512, deep), bf16),
        wkv=((4, deep, 256), bf16),
        wq_m=((deep, 512), bf16),
        wq_o=((deep, 512), bf16),
        wco_m=((512, deep), bf16),
        wco_o=((512, deep), bf16),
        q=((SEQ, 512), bf16),
        kv=((4, MLEN, 256), bf16),
        cctx=((SEQ, 512), bf16),
        clse=((4, 8, SEQ), f32),
        resid1=((half, deep), f32),
        resid2=((half, deep), f32),
        bounds=((8, SEQ), jnp.int32),
    )
    outs = [shape(*value) for value in held.values()]
    outs += [shape((half, deep), bf16), shape((half, deep), bf16)]
    outs += [shape((3,) + fc_in.shape, bf16), shape((3,) + fc_out.shape, bf16), shape((3,) + ad.shape, bf16)]
    scratch = [pltpu.VMEM(*value) for value in held.values()] + [
        pltpu.VMEM((SEQ, deep), bf16),
        pltpu.VMEM((MLEN, deep), bf16),
        pltpu.VMEM((half, 512), bf16),
        pltpu.VMEM((half, 512), bf16),
        pltpu.VMEM((half, 512), bf16),
        pltpu.VMEM((half, deep), f32),
        pltpu.VMEM((half, deep), bf16),
        pltpu.VMEM((128, SEQ), bf16),
        pltpu.VMEM((1, SEQ), jnp.int32),
        pltpu.VMEM((1, SEQ), jnp.int32),
        pltpu.SemaphoreType.DMA((SLOTS,)),
        pltpu.SemaphoreType.DMA((SLOTS,)),
        pltpu.SemaphoreType.DMA((LOCAL_SLOTS,)),
    ]
    anywhere = pl.BlockSpec(memory_space=pl.ANY)
    vmem = pl.BlockSpec(memory_space=pltpu.VMEM)
    results = pl.pallas_call(
        forward_kernel,
        out_shape=outs,
        in_specs=[anywhere] * 14 + [vmem] * 2,
        out_specs=[anywhere] * len(outs),
        scratch_shapes=scratch,
        compiler_params=pltpu.CompilerParams(
            collective_id=0, has_side_effects=True, vmem_limit_bytes=58 * 2**20
        ),
        name="layer_forward",
    )(tokens, memory, cotangent, seg, mseg, prefix, w_self, w_so, w_cq, w_ckv, w_co, fc_in, fc_out, ad, gain, bias)
    return Held(*results)


def backward_kernel(has_prefix, first_bound, bounds_s, *refs):
    if has_prefix:
        qkv_ref, bounds, ctx_ref, dctx_ref, lse_ref, pre_ref, dqkv_ref, dpre_ref, kt_ref, dk_acc, dv_acc, dq_acc, dpre_acc = refs
        q_at = lambda rows: qkv_ref[0, rows, 0:128]
        k_at = lambda rows: qkv_ref[0, rows, 128:256]
        v_at = lambda rows: qkv_ref[0, rows, 256:384]
    else:
        q_ref, kv_ref, bounds, ctx_ref, dctx_ref, lse_ref, dq_ref, dkv_ref, kt_ref, dk_acc, dv_acc, dq_acc = refs
        q_at = lambda rows: q_ref[rows, :]
        k_at = lambda rows: kv_ref[0, rows, 0:128]
        v_at = lambda rows: kv_ref[0, rows, 128:256]
    scale = 0.125 * LOG2E
    kt_ref[...] = k_at(slice(None)).astype(jnp.float32).T.astype(jnp.bfloat16)
    dk_acc[...] = jnp.zeros_like(dk_acc)
    dv_acc[...] = jnp.zeros_like(dv_acc)
    if has_prefix:
        dpre_acc[...] = jnp.zeros_like(dpre_acc)
        kp = prefix_block(pre_ref[0, 0])
        vp = prefix_block(pre_ref[0, 1])
        kpt = kp.astype(jnp.float32).T.astype(jnp.bfloat16)

    def one(qi, _):
        q0 = pl.multiple_of(qi * QB, QB)
        span = pl.ds(q0, QB)
        q = q_at(span)
        dctx = dctx_ref[span, :]
        lo = bounds[first_bound : first_bound + 1, span]
        hi = bounds[first_bound + 1 : first_bound + 2, span]
        prod = (dctx.astype(jnp.float32) * ctx_ref[span, :].astype(jnp.float32)).T
        inner = [jnp.sum(prod[h * 64 : h * 64 + 64], axis=0, keepdims=True) for h in range(2)]
        lse = [lse_ref[0, h : h + 1, span] for h in range(2)]
        qh = [half_lanes(q, h) for h in range(2)]
        dh = [half_lanes(dctx, h) for h in range(2)]
        if has_prefix:
            sp = prefix_rows(nt(kp, q) * scale)
            rows = lambda pair: jnp.concatenate([jnp.broadcast_to(t, (64, QB)) for t in pair], axis=0)
            pp = jnp.exp2(sp - rows(lse))
            dpp = nt(vp, dctx)
            dsp = (pp * (dpp - rows(inner))).astype(jnp.bfloat16)
            dpre_acc[0] += nn(dsp, q)
            dpre_acc[1] += nn(pp.astype(jnp.bfloat16), dctx)
            dq_acc[...] = nn(kpt, dsp)
        else:
            dq_acc[...] = jnp.zeros_like(dq_acc)

        def chunk(ki, _):
            k0 = pl.multiple_of(ki * KB, KB)
            keys = pl.ds(k0, KB)
            k = k_at(keys)
            v = v_at(keys)
            pos = k0 + lax.broadcasted_iota(jnp.int32, (KB, QB), 0)
            mask = (pos >= lo) & (pos <= hi)
            ps, dss = [], []
            for h in range(2):
                s = nt(k, qh[h]) * scale
                p = jnp.exp2(jnp.where(mask, s, NEG) - lse[h])
                dp = nt(v, dh[h])
                ds = (p * (dp - inner[h])).astype(jnp.bfloat16)
                ps.append(p.astype(jnp.bfloat16))
                dss.append(ds)
                dq_acc[h * 64 : h * 64 + 64, :] += nn(kt_ref[h * 64 : h * 64 + 64, keys], ds)
            dv_acc[keys, :] += nn(ps[0], dh[0]) + nn(ps[1], dh[1])
            dk_acc[keys, :] += nn(dss[0], qh[0]) + nn(dss[1], qh[1])
            return 0

        lowest = lax.div(bounds_s[first_bound, q0], KB)
        highest = lax.div(bounds_s[first_bound + 1, q0 + QB - 1], KB) + 1
        lax.fori_loop(lowest, highest, chunk, 0)
        dq = (dq_acc[...].T * 0.125).astype(jnp.bfloat16)
        if has_prefix:
            dqkv_ref[0, span, 0:128] = dq
        else:
            dq_ref[span, :] = dq
        return 0

    lax.fori_loop(0, SEQ // QB, one, 0)
    dk = (dk_acc[...] * 0.125).astype(jnp.bfloat16)
    dv = dv_acc[...].astype(jnp.bfloat16)
    if has_prefix:
        dqkv_ref[0, :, 128:256] = dk
        dqkv_ref[0, :, 256:384] = dv
        lane = lax.broadcasted_iota(jnp.int32, (32, 128), 1)
        for i, factor in ((0, 0.125), (1, 1.0)):
            dpre_ref[0, i] = jnp.where(lane < 64, dpre_acc[i, 0:32], dpre_acc[i, 64:96]) * factor
    else:
        dkv_ref[0, :, 0:128] = dk
        dkv_ref[0, :, 128:256] = dv


def backward_call(has_prefix, arrays, bounds, ctx, dctx, lse, pre=None):
    col = pl.BlockSpec((SEQ, 128), lambda j, *_: (0, j))
    piece = lambda width: pl.BlockSpec((1, SEQ, width), lambda j, *_: (j, 0, 0))
    shape = jax.ShapeDtypeStruct
    bf16, f32 = jnp.bfloat16, jnp.float32
    if has_prefix:
        in_specs = [piece(384)]
        out_specs = [piece(384), pl.BlockSpec((1, 2, 32, 128), lambda j, *_: (j, 0, 0, 0))]
        out_shape = [shape((4, SEQ, 384), bf16), shape((4, 2, 32, 128), f32)]
    else:
        in_specs = [col, piece(256)]
        out_specs = [col, piece(256)]
        out_shape = [shape((SEQ, 512), bf16), shape((4, SEQ, 256), bf16)]
    in_specs += [
        pl.BlockSpec((8, SEQ), lambda j, *_: (0, 0)),
        col,
        col,
        pl.BlockSpec((1, 8, SEQ), lambda j, *_: (j, 0, 0)),
    ]
    args = list(arrays) + [bounds, ctx, dctx, lse]
    scratch = [
        pltpu.VMEM((128, SEQ), bf16),
        pltpu.VMEM((SEQ, 128), f32),
        pltpu.VMEM((SEQ, 128), f32),
        pltpu.VMEM((128, QB), f32),
    ]
    if has_prefix:
        in_specs.append(pl.BlockSpec((1, 2, 32, 128), lambda j, *_: (j, 0, 0, 0)))
        args.append(pre)
        scratch.append(pltpu.VMEM((2, 128, 128), f32))
    return pl.pallas_call(
        functools.partial(backward_kernel, has_prefix, 0 if has_prefix else 2),
        grid_spec=pltpu.PrefetchScalarGridSpec(
            num_scalar_prefetch=1, grid=(4,), in_specs=in_specs, out_specs=out_specs, scratch_shapes=scratch
        ),
        out_shape=out_shape,
        compiler_params=pltpu.CompilerParams(vmem_limit_bytes=40 * 2**20),
        cost_estimate=pl.CostEstimate(flops=10 * 8 * SEQ * SEQ * 64, bytes_accessed=10 * 2**20, transcendentals=8 * SEQ * SEQ),
        name="self_backward" if has_prefix else "cross_backward",
    )(bounds, *args)


HIDDEN = 512


def feed_kernel(
    resid2, cot, gain, bias, wco_m, wco_o, fc_in, fin, fc_out, fout, ad, fad,
    out, grad_two, units, dctx_m, dctx_s,
    win, wout, down, up, slope, low, hidden, acc, gate, ada, branch_low, sem,
):
    bf16 = jnp.bfloat16
    per = fc_in.shape[1] // HIDDEN
    steps = 4 * per
    group = ad.shape[1]
    loads = []
    for j in range(steps):
        piece, part = divmod(j, per)
        cols = pl.ds(part * HIDDEN, HIDDEN)
        src = fc_in.at[:, cols] if piece == 0 else fin.at[piece - 1, :, cols]
        loads.append(pltpu.make_async_copy(src, win.at[j], sem.at[0, j]))
        src = fc_out.at[cols] if piece == 0 else fout.at[piece - 1, cols]
        loads.append(pltpu.make_async_copy(src, wout.at[j], sem.at[1, j]))
    ad_loads = []
    for piece in range(4):
        for i, dst in enumerate((down, up)):
            src = ad.at[i] if piece == 0 else fad.at[piece - 1, i]
            ad_loads.append(pltpu.make_async_copy(src, dst.at[pl.ds(group * piece, group)], sem.at[2, 2 * piece + i]))
    for copy in loads + ad_loads:
        copy.start()

    rows_all = resid2.shape[0]
    tiles = rows_all // TILE
    at = lambda t: pl.ds(pl.multiple_of(t * TILE, TILE), TILE)

    def begin(t, _):
        rows = at(t)
        normed = norm_forward(resid2[rows, :], gain[1:2, :], bias[1:2, :])
        hidden[rows, :] = normed
        low[rows, :] = normed.astype(bf16)
        return 0

    lax.fori_loop(0, tiles, begin, 0)
    for copy in ad_loads:
        copy.wait()
    pre = nt(low[...], down[...])
    sigma = jax.nn.sigmoid(pre)
    gate[...] = sigma * (1.0 + pre * (1.0 - sigma))
    ada[...] = (pre * sigma).astype(bf16)
    acc[...] = adapter_scale * nn(ada[...], up[...])

    def ahead(j, _):
        for i, buf in enumerate((win, wout)):
            pltpu.make_async_copy(buf.at[j], buf.at[j], sem.at[i, j]).wait()
        pre = nn(low[...], win[j])
        phi = 0.5 * (1.0 + lax.erf(pre * 0.7071067811865476))
        slope[j] = phi + pre * jnp.exp(-0.5 * pre * pre) * 0.3989422804014327
        acc[...] += nn((pre * phi).astype(bf16), wout[j])
        return 0

    lax.fori_loop(0, steps, ahead, 0)

    def middle(t, _):
        rows = at(t)
        resid = hidden[rows, :] + acc[rows, :]
        normed, inv = norm_parts(resid)
        out[rows, :] = (normed * gain[2:3, :] + bias[2:3, :]).astype(bf16)
        scaled = cot[rows, :].astype(jnp.float32) * gain[2:3, :]
        grad = inv * (
            scaled
            - jnp.mean(scaled, axis=-1, keepdims=True)
            - normed * jnp.mean(scaled * normed, axis=-1, keepdims=True)
        )
        acc[rows, :] = grad
        branch_low[rows, :] = grad.astype(bf16)
        return 0

    lax.fori_loop(0, tiles, middle, 0)
    grelu = (adapter_scale * nt(branch_low[...], up[...]) * gate[...]).astype(bf16)
    features = low.shape[1]
    units[:, 0:features] = tn(grelu, low[...])
    units[:, features : 2 * features] = adapter_scale * tn(ada[...], branch_low[...])
    acc[...] += nn(grelu, down[...])

    def behind(j, _):
        grad = (nt(branch_low[...], wout[j]) * slope[j]).astype(bf16)
        acc[...] += nt(grad, win[j])
        return 0

    lax.fori_loop(0, steps, behind, 0)

    def finish(t, _):
        rows = at(t)
        grad = norm_backward(resid2[rows, :], gain[1:2, :], acc[rows, :])
        grad_two[rows, :] = grad
        small = grad.astype(bf16)
        dctx_m[rows, :] = nt(small, wco_m[...]).astype(bf16)
        dctx_s[rows, :] = nt(small, wco_o[...]).astype(bf16)
        return 0

    lax.fori_loop(0, tiles, finish, 0)


def feed_call(resid2, cot, gain, bias, wco_m, wco_o, fc_in, fin, fc_out, fout, ad, fad):
    bf16, f32 = jnp.bfloat16, jnp.float32
    rows, deep = resid2.shape
    shape = jax.ShapeDtypeStruct
    anywhere = pl.BlockSpec(memory_space=pl.ANY)
    vmem = pl.BlockSpec(memory_space=pltpu.VMEM)
    steps = 4 * fc_in.shape[1] // HIDDEN
    units = 4 * ad.shape[1]
    return pl.pallas_call(
        feed_kernel,
        out_shape=[
            shape((rows, deep), bf16),
            shape((rows, deep), f32),
            shape((units, 2 * deep), f32),
            shape((rows, 512), bf16),
            shape((rows, 512), bf16),
        ],
        in_specs=[vmem] * 6 + [anywhere] * 6,
        out_specs=[vmem] * 5,
        scratch_shapes=[
            pltpu.VMEM((steps, deep, HIDDEN), bf16),
            pltpu.VMEM((steps, HIDDEN, deep), bf16),
            pltpu.VMEM((units, deep), bf16),
            pltpu.VMEM((units, deep), bf16),
            pltpu.VMEM((steps, rows, HIDDEN), f32),
            pltpu.VMEM((rows, deep), bf16),
            pltpu.VMEM((rows, deep), f32),
            pltpu.VMEM((rows, deep), f32),
            pltpu.VMEM((rows, units), f32),
            pltpu.VMEM((rows, units), bf16),
            pltpu.VMEM((rows, deep), bf16),
            pltpu.SemaphoreType.DMA((3, 8)),
        ],
        compiler_params=pltpu.CompilerParams(vmem_limit_bytes=60 * 2**20),
        name="feed_forward",
    )(resid2, cot, gain, bias, wco_m, wco_o, fc_in, fin, fc_out, fout, ad, fad)


AXES = ("rows", "heads")


def fast_fits(mesh):
    rows, heads = mesh.shape["rows"], mesh.shape["heads"]
    return heads == 4 and rows % 4 == 0 and (rows & (rows - 1)) == 0


def pairs_of(rows, move):
    def number(z, c, y, x):
        return (z * 2 + c) * 4 + y * 2 + x

    found = []
    for z in range(rows // 2):
        for c in range(2):
            for y in range(2):
                for x in range(2):
                    found.append((number(z, c, y, x), number(*move(z, c, y, x))))
    return found


class Moves:
    def __init__(self, rows):
        def perm(move):
            table = pairs_of(rows, move)
            return lambda value: lax.ppermute(value, AXES, table)

        self.core = perm(lambda z, c, y, x: (z, 1 - c, y, x))
        self.x = perm(lambda z, c, y, x: (z, c, y, 1 - x))
        self.y = perm(lambda z, c, y, x: (z, c, 1 - y, x))
        self.d = perm(lambda z, c, y, x: (z, c, 1 - y, 1 - x))
        crossing = [pair for pair in pairs_of(rows, lambda z, c, y, x: (z, x, y, c)) if pair[0] != pair[1]]

        def swap(value):
            stays = lax.axis_index("rows") % 2 == lax.axis_index("heads") % 2
            return jnp.where(stays, value, lax.ppermute(value, AXES, crossing))

        self.swap = swap
        self.z = []
        step = 1
        while step < rows // 2:
            self.z.append(perm(lambda z, c, y, x, step=step: (z ^ step, c, y, x)))
            step *= 2


def fast_body(
    rows,
    tokens,
    memory,
    cotangent,
    dec_seg,
    mem_seg,
    w_self,
    w_self_out,
    w_cross_q,
    w_cross_kv,
    w_cross_out,
    fc_in,
    fc_out,
    ad_down,
    ad_up,
    prefix,
    ln_gain,
    ln_bias,
):
    bf16 = jnp.bfloat16
    f32 = jnp.float32
    move = Moves(rows)
    core = lax.axis_index("rows") % 2
    count = prefix.shape[1]
    ad = jnp.stack([ad_down.T, ad_up])
    held = forward_call(
        tokens,
        memory,
        cotangent,
        dec_seg.reshape(2, 1, SEQ),
        mem_seg.reshape(2, 1, MLEN),
        jnp.pad(prefix, ((0, 0), (0, 32 - count), (0, 0))),
        w_self,
        w_self_out,
        w_cross_q,
        w_cross_kv,
        w_cross_out,
        fc_in,
        fc_out,
        ad,
        ln_gain,
        ln_bias,
    )
    half = tokens.shape[0]

    def own_rows(value):
        return lax.dynamic_slice_in_dim(value, core * half, half, 0)

    def other_rows(value):
        return lax.dynamic_slice_in_dim(value, (1 - core) * half, half, 0)

    def whole(mine, others):
        return jnp.where(
            core == 0,
            jnp.concatenate([mine, others], axis=0),
            jnp.concatenate([others, mine], axis=0),
        )

    def after(value, *earlier):
        return lax.optimization_barrier((value,) + earlier)[0]

    out, grad_two, unit_grads, dctx_m, dctx_s = feed_call(
        held.resid2, held.cot, ln_gain, ln_bias, held.wco_m, held.wco_o,
        fc_in, held.fin, fc_out, held.fout, ad, held.fad,
    )
    output = move.swap(out)
    units = ad.shape[1] // 2
    unit_grads = unit_grads.reshape(4, 2, units, -1)
    unit_mine = lax.dynamic_index_in_dim(unit_grads, core, 1, keepdims=False)
    unit_other = lax.dynamic_index_in_dim(unit_grads, 1 - core, 1, keepdims=False)
    unit_mine = unit_mine + move.core(unit_other.astype(bf16)).astype(f32)
    low_pieces = unit_mine.astype(bf16)
    unit_sum = (
        unit_mine[0]
        + move.x(low_pieces[1]).astype(f32)
        + move.y(low_pieces[2]).astype(f32)
        + move.d(low_pieces[3]).astype(f32)
    )

    cross_dctx = whole(dctx_m, move.core(dctx_s))
    cross_dctx = after(cross_dctx, unit_sum)
    cross_dq, cross_dkv = backward_call(
        False, (held.q, held.kv), held.bounds, held.cctx, cross_dctx, held.clse
    )
    got = move.core(other_rows(cross_dq))
    resid_one = held.resid1
    grad_one_in = grad_two + dot_right(own_rows(cross_dq), held.wq_m) + dot_right(got, held.wq_o)
    memory_part = sum(dot_right(cross_dkv[i], held.wkv[i]) for i in range(4))
    memory_sum = own_rows(memory_part) + move.core(other_rows(memory_part).astype(bf16)).astype(f32)
    grad_memory = move.swap(memory_sum.astype(bf16)).astype(f32)
    grad_one = norm_backward(resid_one, ln_gain[0], grad_one_in)

    low_grad_one = grad_one.astype(bf16)
    d_send = dot_right(low_grad_one, held.wso_o).astype(bf16)
    self_dctx = whole(dot_right(low_grad_one, held.wso_m).astype(bf16), move.core(d_send))
    self_dqkv, prefix_blocks = backward_call(
        True, (held.qkv,), held.bounds, held.sctx, self_dctx, held.slse, held.pre
    )
    input_part = sum(dot_right(self_dqkv[i], held.wself[i]) for i in range(4))
    input_sum = own_rows(input_part) + move.core(other_rows(input_part).astype(bf16)).astype(f32) + grad_one
    grad_input = move.swap(input_sum.astype(bf16)).astype(f32)
    unit_sum = after(unit_sum, self_dqkv)
    for step in move.z:
        unit_sum = unit_sum + step(unit_sum.astype(bf16)).astype(f32)
    unit_all = whole(unit_sum, move.core(unit_sum.astype(bf16)).astype(f32))
    features = tokens.shape[1]
    down_grad = unit_all[:, :features].T
    up_grad = unit_all[:, features:]

    prefix_sum = (
        prefix_blocks[0]
        + move.x(prefix_blocks[1])
        + move.y(prefix_blocks[2])
        + move.d(prefix_blocks[3])
    )
    for step in move.z:
        prefix_sum = prefix_sum + step(prefix_sum)
    prefix_other = move.core(prefix_sum)
    prefix_grad = jnp.where(
        core == 0,
        jnp.concatenate([prefix_sum, prefix_other], axis=2),
        jnp.concatenate([prefix_other, prefix_sum], axis=2),
    )[:, :count]
    return (output, grad_input, grad_memory, prefix_grad, down_grad, up_grad)


def solution(mesh):
    in_specs = (
        P(("rows", "heads"), None),
        P(("rows", "heads"), None),
        P(("rows", "heads"), None),
        P("rows"),
        P("rows"),
        P(None, None, "heads"),
        P("heads", None),
        P(None, "heads"),
        P(None, None, "heads"),
        P("heads", None),
        P(None, "heads"),
        P("heads", None),
        P(None, "heads"),
        P("heads", None),
        P(None, None, "heads"),
        P(),
        P(),
    )
    out_specs = (
        P(("rows", "heads"), None),
        P(("rows", "heads"), None),
        P(("rows", "heads"), None),
        P(None, None, "heads"),
        P(None, "heads"),
        P("heads", None),
    )
    chosen = functools.partial(fast_body, mesh.shape["rows"]) if fast_fits(mesh) else body
    return jax.shard_map(chosen, mesh=mesh, in_specs=in_specs, out_specs=out_specs, check_vma=False)
```

```python
import functools
import math
import typing

import jax
import jax.numpy as jnp
from jax import lax
from jax.experimental import pallas as pl
from jax.experimental.pallas import tpu as pltpu
from jax.sharding import PartitionSpec as P

HD = 64
SEQ = 1024
MLEN = 1024


epsilon = 1e-05
adapter_scale = 4.0
masked_score = -1e30


def dot_right(left, right):
    return lax.dot_general(
        left, right, (((1,), (1,)), ((), ())), preferred_element_type=jnp.float32
    )


def dot_left(left, right):
    return lax.dot_general(
        left, right, (((0,), (0,)), ((), ())), preferred_element_type=jnp.float32
    )


def norm_parts(resid):
    average = jnp.mean(resid, axis=-1, keepdims=True)
    centered = resid - average
    inv_scale = lax.rsqrt(jnp.mean(centered * centered, axis=-1, keepdims=True) + epsilon)
    return (centered * inv_scale, inv_scale)


def norm_forward(resid, gain, shift):
    normed, inv_scale = norm_parts(resid)
    return normed * gain + shift


def norm_backward(resid, gain, grad_out):
    normed, inv_scale = norm_parts(resid)
    scaled = grad_out * gain
    return inv_scale * (
        scaled
        - jnp.mean(scaled, axis=-1, keepdims=True)
        - normed * jnp.mean(scaled * normed, axis=-1, keepdims=True)
    )


def gelu_slope(pre_gelu):
    return (
        0.5 * (1.0 + lax.erf(pre_gelu * 0.7071067811865476))
        + pre_gelu * jnp.exp(-0.5 * pre_gelu * pre_gelu) * 0.3989422804014327
    )


def silu_slope(pre_relu):
    sigma = jax.nn.sigmoid(pre_relu)
    return sigma * (1.0 + pre_relu * (1.0 - sigma))


def to_heads(arrays, heads_here):
    return arrays.reshape(arrays.shape[0], arrays.shape[1], heads_here, HD).transpose(0, 2, 1, 3)


def from_heads(arrays):
    return arrays.transpose(0, 2, 1, 3).reshape(
        arrays.shape[0] * arrays.shape[2], arrays.shape[1] * arrays.shape[3]
    )


def join_blocks(stacked):
    moved = jnp.moveaxis(stacked, 0, 1)
    return moved.reshape((moved.shape[0], moved.shape[1] * moved.shape[2]) + moved.shape[3:])


def block_mask(row_segs, key_segs, offset, causal):
    allowed = row_segs[:, None] == key_segs[None, :]
    if causal:
        row_places = offset + lax.iota(jnp.int32, row_segs.shape[0])
        key_places = lax.iota(jnp.int32, key_segs.shape[0])
        allowed = allowed & (key_places[None, :] <= row_places[:, None])
    return allowed


def block_scores(queries, key_rows, allowed, prefix_keys):
    qk_scale = HD ** (-0.5)
    token_scores = (
        jnp.einsum("hqe,hke->hqk", queries, key_rows, preferred_element_type=jnp.float32) * qk_scale
    )
    token_scores = jnp.where(allowed[None], token_scores, masked_score)
    if prefix_keys is None:
        return (token_scores, None)
    prefix_scores = (
        jnp.einsum("hqe,hpe->hqp", queries, prefix_keys, preferred_element_type=jnp.float32)
        * qk_scale
    )
    return (token_scores, prefix_scores)


def attend_block(queries, key_rows, value_rows, allowed, prefix_keys, prefix_values):
    token_scores, prefix_scores = block_scores(queries, key_rows, allowed, prefix_keys)
    row_max = jnp.max(token_scores, axis=-1, keepdims=True)
    if prefix_scores is not None:
        row_max = jnp.maximum(row_max, jnp.max(prefix_scores, axis=-1, keepdims=True))
    token_weights = jnp.exp(token_scores - row_max)
    row_total = jnp.sum(token_weights, axis=-1, keepdims=True)
    if prefix_scores is not None:
        prefix_weights = jnp.exp(prefix_scores - row_max)
        row_total = row_total + jnp.sum(prefix_weights, axis=-1, keepdims=True)
    context = jnp.einsum(
        "hqk,hke->hqe",
        (token_weights / row_total).astype(jnp.bfloat16),
        value_rows,
        preferred_element_type=jnp.float32,
    )
    if prefix_scores is not None:
        context = context + jnp.einsum(
            "hqp,hpe->hqe",
            (prefix_weights / row_total).astype(jnp.bfloat16),
            prefix_values,
            preferred_element_type=jnp.float32,
        )
    return (context.astype(jnp.bfloat16), row_max + jnp.log(row_total))


def attend_back(
    queries, key_rows, value_rows, allowed, prefix_keys, prefix_values, log_total, context_grad
):
    qk_scale = HD ** (-0.5)
    token_scores, prefix_scores = block_scores(queries, key_rows, allowed, prefix_keys)
    token_probs = jnp.exp(token_scores - log_total)
    token_dprob = jnp.einsum(
        "hqe,hke->hqk", context_grad, value_rows, preferred_element_type=jnp.float32
    )
    inner = jnp.sum(token_probs * token_dprob, axis=-1, keepdims=True)
    if prefix_scores is not None:
        prefix_probs = jnp.exp(prefix_scores - log_total)
        prefix_dprob = jnp.einsum(
            "hqe,hpe->hqp", context_grad, prefix_values, preferred_element_type=jnp.float32
        )
        inner = inner + jnp.sum(prefix_probs * prefix_dprob, axis=-1, keepdims=True)
    token_dscore = (token_probs * (token_dprob - inner)).astype(jnp.bfloat16)
    query_grad = jnp.einsum(
        "hqk,hke->hqe", token_dscore, key_rows, preferred_element_type=jnp.float32
    )
    key_grad = (
        jnp.einsum("hqk,hqe->hke", token_dscore, queries, preferred_element_type=jnp.float32)
        * qk_scale
    )
    value_grad = jnp.einsum(
        "hqk,hqe->hke",
        token_probs.astype(jnp.bfloat16),
        context_grad,
        preferred_element_type=jnp.float32,
    )
    if prefix_scores is None:
        return (query_grad * qk_scale, (key_grad, value_grad))
    prefix_dscore = (prefix_probs * (prefix_dprob - inner)).astype(jnp.bfloat16)
    query_grad = query_grad + jnp.einsum(
        "hqp,hpe->hqe", prefix_dscore, prefix_keys, preferred_element_type=jnp.float32
    )
    prefix_key_grad = (
        jnp.einsum("hqp,hqe->hpe", prefix_dscore, queries, preferred_element_type=jnp.float32)
        * qk_scale
    )
    prefix_value_grad = jnp.einsum(
        "hqp,hqe->hpe",
        prefix_probs.astype(jnp.bfloat16),
        context_grad,
        preferred_element_type=jnp.float32,
    )
    return (query_grad * qk_scale, (key_grad, value_grad, prefix_key_grad, prefix_value_grad))


def sequence_forward(
    queries, key_rows, value_rows, row_segs, key_segs, prefix_keys, prefix_values, causal
):
    seq_width = queries.shape[1]
    block_rows = min(512, seq_width)

    def one_block(block_index):
        offset = block_index * block_rows
        allowed = block_mask(
            lax.dynamic_slice_in_dim(row_segs, offset, block_rows, 0), key_segs, offset, causal
        )
        query_part = lax.dynamic_slice_in_dim(queries, offset, block_rows, 1)
        return attend_block(query_part, key_rows, value_rows, allowed, prefix_keys, prefix_values)

    context, log_total = lax.map(one_block, jnp.arange(seq_width // block_rows, dtype=jnp.int32))
    return (join_blocks(context), join_blocks(log_total))


def sequence_backward(
    queries,
    key_rows,
    value_rows,
    row_segs,
    key_segs,
    prefix_keys,
    prefix_values,
    causal,
    log_total,
    context_grad,
):
    seq_width = queries.shape[1]
    block_rows = min(512, seq_width)
    key_zero = jnp.zeros(key_rows.shape, jnp.float32)
    initial = (key_zero, key_zero)
    if prefix_keys is not None:
        prefix_zero = jnp.zeros(prefix_keys.shape, jnp.float32)
        initial = initial + (prefix_zero, prefix_zero)

    def one_block(running, block_index):
        offset = block_index * block_rows
        allowed = block_mask(
            lax.dynamic_slice_in_dim(row_segs, offset, block_rows, 0), key_segs, offset, causal
        )
        query_part = lax.dynamic_slice_in_dim(queries, offset, block_rows, 1)
        total_part = lax.dynamic_slice_in_dim(log_total, offset, block_rows, 1)
        grad_part = lax.dynamic_slice_in_dim(context_grad, offset, block_rows, 1)
        query_grad, block_grads = attend_back(
            query_part,
            key_rows,
            value_rows,
            allowed,
            prefix_keys,
            prefix_values,
            total_part,
            grad_part,
        )
        return (tuple((summed + added for summed, added in zip(running, block_grads))), query_grad)

    running, query_grad = lax.scan(
        one_block, initial, jnp.arange(seq_width // block_rows, dtype=jnp.int32)
    )
    outputs = (
        join_blocks(query_grad).astype(jnp.bfloat16),
        running[0].astype(jnp.bfloat16),
        running[1].astype(jnp.bfloat16),
    )
    return outputs + running[2:]


def gather_rows(row_share):
    return lax.all_gather(row_share, "heads", axis=0, tiled=True)


def gather_grads(row_share):
    return lax.all_gather(row_share, "heads", axis=0, tiled=True)


def sum_rows(partial_value):
    return lax.psum_scatter(partial_value, "heads", scatter_dimension=0, tiled=True)


def sum_grads(partial_value):
    return lax.psum_scatter(partial_value, "heads", scatter_dimension=0, tiled=True)


def body(
    tokens,
    memory,
    cotangent,
    dec_seg,
    mem_seg,
    w_self,
    w_self_out,
    w_cross_q,
    w_cross_kv,
    w_cross_out,
    fc_in,
    fc_out,
    ad_down,
    ad_up,
    prefix,
    ln_gain,
    ln_bias,
):
    local_width = w_self.shape[2]
    heads_here = local_width // HD
    seg_dec = dec_seg.reshape(-1, SEQ)
    seg_mem = mem_seg.reshape(-1, MLEN)
    seq_count = seg_dec.shape[0]
    prefix_heads = to_heads(prefix, heads_here)
    prefix_keys = prefix_heads[0]
    prefix_values = prefix_heads[1]
    gathered_x = gather_rows(tokens)
    self_proj = jnp.einsum(
        "td,cdn->ctn", gathered_x, w_self, preferred_element_type=jnp.float32
    ).astype(jnp.bfloat16)
    self_proj = self_proj.reshape(3, seq_count, SEQ, local_width)
    self_queries = to_heads(self_proj[0], heads_here)
    self_keys = to_heads(self_proj[1], heads_here)
    self_values = to_heads(self_proj[2], heads_here)

    def self_forward(packed):
        return sequence_forward(
            packed[0], packed[1], packed[2], packed[3], packed[3], prefix_keys, prefix_values, True
        )

    self_context, self_total = lax.map(
        self_forward, (self_queries, self_keys, self_values, seg_dec)
    )
    attn_partial = jnp.dot(from_heads(self_context), w_self_out, preferred_element_type=jnp.float32)
    resid_one = tokens.astype(jnp.float32) + sum_rows(attn_partial)
    hidden_one = norm_forward(resid_one, ln_gain[0], ln_bias[0])
    gathered_one = gather_rows(hidden_one.astype(jnp.bfloat16))
    gathered_mem = lax.all_gather(memory, "heads", axis=0, tiled=True)
    cross_rows = jnp.dot(gathered_one, w_cross_q, preferred_element_type=jnp.float32).astype(
        jnp.bfloat16
    )
    cross_proj = jnp.einsum(
        "td,cdn->ctn", gathered_mem, w_cross_kv, preferred_element_type=jnp.float32
    ).astype(jnp.bfloat16)
    cross_queries = to_heads(cross_rows.reshape(seq_count, SEQ, local_width), heads_here)
    cross_proj = cross_proj.reshape(2, seq_count, MLEN, local_width)
    cross_keys = to_heads(cross_proj[0], heads_here)
    cross_values = to_heads(cross_proj[1], heads_here)

    def cross_forward(packed):
        return sequence_forward(
            packed[0], packed[1], packed[2], packed[3], packed[4], None, None, False
        )

    cross_context, cross_total = lax.map(
        cross_forward, (cross_queries, cross_keys, cross_values, seg_dec, seg_mem)
    )
    cross_partial = jnp.dot(
        from_heads(cross_context), w_cross_out, preferred_element_type=jnp.float32
    )
    resid_two = hidden_one + sum_rows(cross_partial)
    hidden_two = norm_forward(resid_two, ln_gain[1], ln_bias[1])
    hidden_low = hidden_two.astype(jnp.bfloat16)
    full_in, full_out, full_down, full_up = (fc_in, fc_out, ad_down, ad_up)
    ffn_rows = gather_rows(hidden_low)
    pre_gelu = jnp.dot(ffn_rows, full_in, preferred_element_type=jnp.float32)
    activated = jax.nn.gelu(pre_gelu, approximate=False).astype(jnp.bfloat16)
    pre_relu = jnp.dot(ffn_rows, full_down, preferred_element_type=jnp.float32)
    adapted = (pre_relu * jax.nn.sigmoid(pre_relu)).astype(jnp.bfloat16)
    branch = jnp.dot(
        activated, full_out, preferred_element_type=jnp.float32
    ) + adapter_scale * jnp.dot(adapted, full_up, preferred_element_type=jnp.float32)
    resid_three = hidden_two + sum_rows(branch)
    output = norm_forward(resid_three, ln_gain[2], ln_bias[2]).astype(jnp.bfloat16)
    grad_three = norm_backward(resid_three, ln_gain[2], cotangent.astype(jnp.float32))
    grad_branch = grad_three.astype(jnp.bfloat16)
    branch_rows = gather_grads(grad_branch)
    grad_gelu = (dot_right(branch_rows, full_out) * gelu_slope(pre_gelu)).astype(jnp.bfloat16)
    grad_relu = (adapter_scale * dot_right(branch_rows, full_up) * silu_slope(pre_relu)).astype(
        jnp.bfloat16
    )
    up_grad = adapter_scale * dot_left(adapted, branch_rows)
    down_grad = dot_left(ffn_rows, grad_relu)
    hidden_partial = dot_right(grad_gelu, full_in) + dot_right(grad_relu, full_down)
    grad_two_in = grad_three + sum_grads(hidden_partial)
    down_grad, up_grad = (
        lax.psum(down_grad.astype(jnp.bfloat16), "rows").astype(jnp.float32),
        lax.psum(up_grad.astype(jnp.bfloat16), "rows").astype(jnp.float32),
    )
    grad_two = norm_backward(resid_two, ln_gain[1], grad_two_in)
    cross_out_rows = gather_grads(grad_two.astype(jnp.bfloat16))
    cross_dctx = dot_right(cross_out_rows, w_cross_out).astype(jnp.bfloat16)
    cross_dctx = to_heads(cross_dctx.reshape(seq_count, SEQ, local_width), heads_here)

    def cross_back(packed):
        return sequence_backward(
            packed[0],
            packed[1],
            packed[2],
            packed[3],
            packed[4],
            None,
            None,
            False,
            packed[5],
            packed[6],
        )

    cross_qgrad, cross_kgrad, cross_vgrad = lax.map(
        cross_back,
        (cross_queries, cross_keys, cross_values, seg_dec, seg_mem, cross_total, cross_dctx),
    )
    memory_kv = jnp.stack([from_heads(cross_kgrad), from_heads(cross_vgrad)])
    one_partial = dot_right(from_heads(cross_qgrad), w_cross_q)
    grad_one_in = grad_two + sum_grads(one_partial)
    memory_partial = jnp.einsum(
        "ctn,cdn->td", memory_kv, w_cross_kv, preferred_element_type=jnp.float32
    )
    grad_memory = lax.psum_scatter(
        memory_partial.astype(jnp.bfloat16), "heads", scatter_dimension=0, tiled=True
    ).astype(jnp.float32)
    grad_one = norm_backward(resid_one, ln_gain[0], grad_one_in)
    attn_rows = gather_grads(grad_one.astype(jnp.bfloat16))
    self_dctx = dot_right(attn_rows, w_self_out).astype(jnp.bfloat16)
    self_dctx = to_heads(self_dctx.reshape(seq_count, SEQ, local_width), heads_here)

    def self_back(running, packed):
        query_grad, key_grad, value_grad, pkey_grad, pvalue_grad = sequence_backward(
            packed[0],
            packed[1],
            packed[2],
            packed[3],
            packed[3],
            prefix_keys,
            prefix_values,
            True,
            packed[4],
            packed[5],
        )
        return (
            (running[0] + pkey_grad, running[1] + pvalue_grad),
            (query_grad, key_grad, value_grad),
        )

    zero_grad = jnp.zeros(prefix_keys.shape, jnp.float32)
    prefix_sums, self_grads = lax.scan(
        self_back,
        (zero_grad, zero_grad),
        (self_queries, self_keys, self_values, seg_dec, self_total, self_dctx),
    )
    self_stack = jnp.stack(
        [from_heads(self_grads[0]), from_heads(self_grads[1]), from_heads(self_grads[2])]
    )
    input_partial = jnp.einsum(
        "ctn,cdn->td", self_stack, w_self, preferred_element_type=jnp.float32
    )
    grad_input = grad_one + sum_grads(input_partial)
    prefix_grad = (
        jnp.stack([prefix_sums[0], prefix_sums[1]])
        .transpose(0, 2, 1, 3)
        .reshape(2, prefix.shape[1], local_width)
    )
    prefix_grad = lax.psum(prefix_grad, "rows")
    return (output, grad_input, grad_memory, prefix_grad, down_grad, up_grad)


QB = 256
KB = 256
LOG2E = math.log2(math.e)
NEG = -1e30


def nt(a, b):
    return lax.dot_general(a, b, (((1,), (1,)), ((), ())), preferred_element_type=jnp.float32)


def nn(a, b):
    return lax.dot_general(a, b, (((1,), (0,)), ((), ())), preferred_element_type=jnp.float32)


def tn(a, b):
    return lax.dot_general(a, b, (((0,), (0,)), ((), ())), preferred_element_type=jnp.float32)


def half_lanes(v, h):
    lane = lax.broadcasted_iota(jnp.int32, v.shape, 1)
    keep = (lane < 64) if h == 0 else (lane >= 64)
    return jnp.where(keep, v, jnp.zeros_like(v))


def prefix_rows(scores):
    row = lax.broadcasted_iota(jnp.int32, scores.shape, 0)
    return jnp.where(lax.rem(row, 64) < 30, scores, NEG)


MESH = pl.DeviceIdType.MESH
TILE = 256

TOK, TOK_C, MEM, MEM_C = 112, 113, 114, 115
SELF_PIECE, OUT_ONE, CROSS_Q, CROSS_PIECE, OUT_TWO = 128, 132, 133, 134, 138
SLOTS, LOCAL_SLOTS = 128, 48
GROUPS = ((1, 0), (1, 0), (1, 0), (0, 1), (1, 1), (0, 0), (1, 0))
SCHEDULE = (16, 17, 65, 64, 20, 33, 32, 68, 97, 112, 35, 67, 36, 19, 114, 113, 18, 100, 49, 128, 0, 115, 21, 1, 22, 96, 3, 2, 4, 129, 48, 34, 98, 5, 130, 80, 37, 131, 81, 99, 38, 132, 133, 101, 134, 66, 50, 82, 135, 69, 102, 136, 70, 137, 86, 138)


class Place:
    def __init__(self):
        self.row, self.head = lax.axis_index("rows"), lax.axis_index("heads")
        self.c, self.z = lax.rem(self.row, 2), lax.div(self.row, 2)
        self.x, self.y = lax.rem(self.head, 2), lax.div(self.head, 2)
        self.odd = lax.rem(self.z, 2)
        c, x, y, z = self.c, self.x, self.y, self.z
        self.to_x = (self.row, 2 * y + 1 - x)
        self.to_y = (self.row, 2 * (1 - y) + x)
        self.to_d = (self.row, 2 * (1 - y) + 1 - x)
        self.to_z = (2 * (z + 1 - 2 * self.odd) + c, self.head)
        self.to_c = (2 * z + 1 - c, self.head)
        self.to_s = (2 * z + x, 2 * y + c)

    def greet(self, devices, swaps):
        barrier = pltpu.get_barrier_semaphore()
        for device in devices:
            pl.semaphore_signal(barrier, inc=1, device_id=device, device_id_type=MESH)
        count = len(devices)
        if swaps:
            moves = self.c != self.x

            @pl.when(moves)
            def _():
                pl.semaphore_signal(barrier, inc=1, device_id=self.to_s, device_id_type=MESH)

            count = count + moves.astype(jnp.int32)
        pl.semaphore_wait(barrier, count)


def prefix_block(rows):
    nothing = jnp.zeros_like(rows)
    return jnp.concatenate([half_lanes(rows, 0), nothing, half_lanes(rows, 1), nothing], axis=0)


def attend_tile(q, k, vt, mask, kp, vpt):
    scale = 0.125 * LOG2E
    rows = q.shape[0]
    if kp is not None:
        sp = prefix_rows(nt(kp, q) * scale)
    outs, tops, sums = [], [], []
    for h in range(2):
        s = jnp.where(mask, nt(k, half_lanes(q, h)) * scale, NEG)
        m = jnp.max(s, axis=0, keepdims=True)
        if kp is not None:
            m = jnp.maximum(m, jnp.max(sp[h * 64 : h * 64 + 32], axis=0, keepdims=True))
        e = jnp.exp2(s - m)
        outs.append(nn(vt[h * 64 : h * 64 + 64], e.astype(jnp.bfloat16)))
        sums.append(jnp.sum(e, axis=0, keepdims=True))
        tops.append(m)
    if kp is not None:
        mm = jnp.concatenate([jnp.broadcast_to(t, (64, rows)) for t in tops], axis=0)
        ep = jnp.exp2(sp - mm)
        sums = [sums[h] + jnp.sum(ep[h * 64 : h * 64 + 32], axis=0, keepdims=True) for h in range(2)]
        extra = nn(vpt, ep.astype(jnp.bfloat16))
        outs = [outs[h] + extra[h * 64 : h * 64 + 64] for h in range(2)]
    both = jnp.concatenate([outs[h] * (1.0 / sums[h]) for h in range(2)], axis=0)
    return both.T.astype(jnp.bfloat16), [tops[h] + jnp.log2(sums[h]) for h in range(2)]


def forward_kernel(
    tokens, memory, seg, mseg, prefix, w_self, w_so, w_cq, w_ckv, w_co, fc_in, fc_out, ad, gain, bias,
    o_wself, o_qkv, o_sctx, o_slse, o_pre, o_wso_m, o_wso_o, o_wkv, o_wq_m, o_wq_o, o_wco_m, o_wco_o,
    o_q, o_kv, o_cctx, o_clse, o_resid1, o_resid2, o_bounds, fin, fout, fad,
    wself, qkv, sctx, slse, pre, wso_m, wso_o, wkv, wq_m, wq_o, wco_m, wco_o,
    q_all, kv, cctx, clse, resid1, resid2, bounds, tok, mem, sctx_o, cctx_o, q_send, hidden, low_one, vt, seg_v, mseg_v,
    send, recv, local,
):
    place_of = Place()
    c, x, y, odd = place_of.c, place_of.x, place_of.y, place_of.odd
    to_x, to_y, to_z, to_c, to_s = place_of.to_x, place_of.to_y, place_of.to_z, place_of.to_c, place_of.to_s
    stays, moves = c == x, c != x
    place_of.greet((to_x, to_y, to_z, to_c), True)

    taken = []

    def there(src, dst, device):
        slot = len(taken)
        taken.append(slot)
        return pltpu.make_async_remote_copy(
            src_ref=src, dst_ref=dst, send_sem=send.at[slot], recv_sem=recv.at[slot], device_id=device, device_id_type=MESH
        )

    used = []

    def here(src, dst):
        slot = len(used)
        used.append(slot)
        return pltpu.make_async_copy(src, dst, local.at[slot])

    deep = w_self.shape[1]
    half = tok.shape[0] // 2
    step = lambda start, size, unit: pl.ds(pl.multiple_of(start, unit), size)
    mine = step(c * half, half, half)
    others = step((1 - c) * half, half, half)
    lanes = step(c * 128, 128, 128)
    other_lanes = step((1 - c) * 128, 128, 128)
    rows_c, rows_o = lanes, other_lanes
    foreign = pl.ds(128, 384)
    hid = fc_in.shape[1]
    units = ad.shape[1]
    pending = []

    def swap_of(src, target):
        away = there(src, target.at[step(x * half, half, half)], to_s)
        home = here(src, target.at[mine])
        back = there(target.at[mine], target.at[mine], to_c)

        def start():
            pl.when(moves)(away.start)
            pl.when(stays)(home.start)

        def wait():
            pl.when(moves)(away.wait)
            pl.when(stays)(home.wait)

        return start, wait, back

    def seg_of(src, dst):
        home = here(src.at[y], dst)
        away = there(src.at[y], dst, to_c)

        def start():
            pl.when(stays)(home.start)
            pl.when(stays)(away.start)

        def wait():
            pl.when(stays)(home.wait)
            pl.when(stays)(away.wait_send)
            pl.when(moves)(away.wait_recv)

        return start, wait

    def deep_rows(shared):
        return step(odd * (deep // 2), deep // 2, deep // 2) if shared else pl.ds(0, deep)

    def thin_rows(piece, shared):
        return step(128 * piece + odd * 64, 64, 64) if shared else pl.ds(128 * piece, 128)

    def thin_own(shared):
        return step(128 * c + odd * 64, 64, 64) if shared else rows_c

    def span(size, shared):
        return step(c * (size // 2) + odd * (size // 4), size // 4, size // 4) if shared else step(c * (size // 2), size // 2, size // 2)

    lane_of = lambda i: pl.ds(128 * i, 128)

    def group_a(shared):
        rows = deep_rows(shared)
        first = lambda piece: [(w_self.at[i, rows, lanes], wself.at[piece, rows, lane_of(i)]) for i in range(3)] + [
            (prefix.at[:, :, lanes], pre.at[piece])
        ]
        return first, lambda piece: [wself.at[piece, rows], pre.at[piece]], 1, []

    def group_thin(src, dst_m, dst_o, shared):
        first = lambda piece: [(src.at[thin_own(shared)], dst_m.at[thin_rows(piece, shared)])]
        return first, lambda piece: [dst_m.at[thin_rows(piece, shared)]], 1, [(dst_m.at[foreign], dst_o.at[foreign])]

    def group_q(shared):
        rows = deep_rows(shared)
        first = lambda piece: [(w_cq.at[rows, lanes], wq_m.at[rows, lane_of(piece)])]
        return first, lambda piece: [wq_m.at[rows, lane_of(piece)]], 1, [(wq_m.at[:, foreign], wq_o.at[:, foreign])]

    def group_v(shared):
        rows = deep_rows(shared)
        first = lambda piece: [(w_ckv.at[i, rows, lanes], wkv.at[piece, rows, lane_of(i)]) for i in range(2)]
        return first, lambda piece: [wkv.at[piece, rows]], 1, []

    def group_i(shared):
        cols = span(hid, shared)
        both = fin.at[:, :, span(hid, False)]
        first = lambda piece: [(fc_in.at[:, cols], fin.at[piece - 1, :, cols])]
        return first, lambda piece: [fin.at[piece - 1, :, cols]], 1, [(both, both)]

    def group_o(shared):
        rows, some = span(hid, shared), span(units, shared)
        both, both_units = fout.at[:, span(hid, False)], fad.at[:, :, span(units, False)]
        first = lambda piece: [(fc_out.at[rows], fout.at[piece - 1, rows]), (ad.at[:, some], fad.at[piece - 1, :, some])]
        hold = lambda piece: [fout.at[piece - 1, rows], fad.at[piece - 1, :, some]]
        return first, hold, 2, [(both, both), (both_units, both_units)]

    makers = [
        group_a,
        functools.partial(group_thin, w_so, wso_m, wso_o),
        group_q,
        group_v,
        functools.partial(group_thin, w_co, wco_m, wco_o),
        group_i,
        group_o,
    ]
    copies, needs = {}, {}
    for index, (make, (shared, through_x)) in enumerate(zip(makers, GROUPS)):
        first, hold, shared_count, cross = make(bool(shared))
        base = 16 * index
        copies[base] = [there(src, dst, to_x) for src, dst in first(1)]
        copies[base + 1] = [there(src, dst, to_y) for src, dst in first(2)]
        near, device = (2, to_x) if through_x else (1, to_y)
        copies[base + 2] = [there(src, dst, device) for src, dst in zip(hold(near), hold(3))]
        needs[base], needs[base + 1], needs[base + 2] = [], [], [base + near - 1]
        arrived = [base, base + 1, base + 2]
        if shared:
            for i in range(3):
                copies[base + 3 + i] = [there(ref, ref, to_z) for ref in hold(i + 1)[:shared_count]]
                needs[base + 3 + i] = [base + i]
                arrived.append(base + 3 + i)
        if cross:
            copies[base + 6] = [there(src, dst, to_c) for src, dst in cross]
            needs[base + 6] = arrived
    tok_start, tok_wait, tok_back = swap_of(tokens, tok)
    mem_start, mem_wait, mem_back = swap_of(memory, mem)
    copies[TOK_C], copies[MEM_C] = [tok_back], [mem_back]
    needs[TOK_C], needs[MEM_C] = [TOK], [MEM]
    seg_start, seg_wait = seg_of(seg, seg_v)
    mseg_start, mseg_wait = seg_of(mseg, mseg_v)
    sctx_out = [there(sctx.at[others, lane_of(i)], sctx_o.at[:, lane_of(i)], to_c) for i in range(4)]
    cctx_out = [there(cctx.at[others, lane_of(i)], cctx_o.at[:, lane_of(i)], to_c) for i in range(4)]
    q_out = there(q_send, q_all.at[mine], to_c)

    landed = set()

    def wait_for(op):
        if op in landed:
            return
        landed.add(op)
        if op == TOK:
            tok_wait()
        elif op == MEM:
            mem_wait()
        elif op in copies:
            for copy in copies[op]:
                copy.wait_recv()

    def launch(op):
        if op == TOK:
            tok_start()
        elif op == MEM:
            mem_start()
        else:
            for need in needs[op]:
                wait_for(need)
            for copy in copies[op]:
                copy.start()
                pending.append(copy)

    saves = []

    def keep(src, dst):
        copy = here(src, dst)
        copy.start()
        saves.append(copy)

    own_a = [here(w_self.at[i, :, lanes], wself.at[0, :, lane_of(i)]) for i in range(3)]
    own_a.append(here(prefix.at[:, :, lanes], pre.at[0]))
    own_b = [
        here(w_so.at[rows_c], wso_m.at[lane_of(0)]),
        here(w_so.at[rows_o], wso_o.at[lane_of(0)]),
        here(w_co.at[rows_c], wco_m.at[lane_of(0)]),
        here(w_co.at[rows_o], wco_o.at[lane_of(0)]),
        here(w_cq.at[:, lanes], wq_m.at[:, lane_of(0)]),
        here(w_cq.at[:, other_lanes], wq_o.at[:, lane_of(0)]),
        here(w_ckv.at[0, :, lanes], wkv.at[0, :, lane_of(0)]),
        here(w_ckv.at[1, :, lanes], wkv.at[0, :, lane_of(1)]),
    ]

    def bounds_of():
        seg_wait()
        mseg_wait()
        dec, men = seg_v[...], mseg_v[...]

        def below(values, d):
            return jnp.sum((values < d).astype(jnp.int32), axis=1, keepdims=True)

        def pick(counts):
            out = jnp.broadcast_to(counts[0], dec.shape)
            for d in range(1, 4):
                out = jnp.where(dec == d, counts[d], out)
            return out

        zero = jnp.zeros((1, 1), jnp.int32)
        full = jnp.full((1, 1), MLEN, jnp.int32)
        self_lo = pick([zero] + [below(dec, d) for d in range(1, 4)])
        mem_counts = [zero] + [below(men, d) for d in range(1, 4)] + [full]
        bounds[...] = jnp.concatenate(
            [self_lo, lax.broadcasted_iota(jnp.int32, dec.shape, 1), pick(mem_counts[:4]), pick(mem_counts[1:]) - 1]
            + [jnp.zeros_like(dec)] * 4,
            axis=0,
        )
        keep(bounds, o_bounds)

    def weight_needs(base, piece):
        found = [base + piece - 1, base + 2 + piece]
        return [op for op in found if op in copies]

    def project(dst, p, source, weight):
        def rows_of(t, _):
            rows = step(t * TILE, TILE, TILE)
            dst[p, rows, :] = nn(source[rows, :], weight[p]).astype(jnp.bfloat16)
            return 0

        lax.fori_loop(0, SEQ // TILE, rows_of, 0)

    def self_piece(p):
        project(qkv, p, tok, wself)
        vt[...] = qkv[p, :, 256:384].astype(jnp.float32).T.astype(jnp.bfloat16)
        kp = prefix_block(pre[p, 0])
        vpt = prefix_block(pre[p, 1]).astype(jnp.float32).T.astype(jnp.bfloat16)
        place = step(p * 128, 128, 128)
        for qi in range(SEQ // QB):
            width = (qi + 1) * QB
            rows = slice(qi * QB, (qi + 1) * QB)
            pos = lax.broadcasted_iota(jnp.int32, (width, QB), 0)
            mask = (pos >= bounds[0:1, rows]) & (pos <= bounds[1:2, rows])
            out, lse = attend_tile(qkv[p, rows, 0:128], qkv[p, 0:width, 128:256], vt[:, 0:width], mask, kp, vpt)
            sctx[rows, place] = out
            for h in range(2):
                slse[p, h : h + 1, rows] = lse[h]

    def cross_piece(p):
        project(kv, p, mem, wkv)
        vt[...] = kv[p, :, 128:256].astype(jnp.float32).T.astype(jnp.bfloat16)
        place = step(p * 128, 128, 128)

        def block(qi, _):
            rows = step(qi * QB, QB, QB)
            pos = lax.broadcasted_iota(jnp.int32, (MLEN, QB), 0)
            mask = (pos >= bounds[2:3, rows]) & (pos <= bounds[3:4, rows])
            out, lse = attend_tile(q_all[rows, place], kv[p, :, 0:128], vt[...], mask, None, None)
            cctx[rows, place] = out
            for h in range(2):
                clse[p, h : h + 1, rows] = lse[h]
            return 0

        lax.fori_loop(0, SEQ // QB, block, 0)

    def with_out(t, resid_before, ctx_m, ctx_o, w_m, w_o):
        rows = step(t * TILE, TILE, TILE)
        rows_all = step(c * half + t * TILE, TILE, TILE)
        return resid_before + nn(ctx_m[rows_all, :], w_m[...]) + nn(ctx_o[rows, :], w_o[...])

    def out_one(t, _):
        rows = step(t * TILE, TILE, TILE)
        rows_all = step(c * half + t * TILE, TILE, TILE)
        resid = with_out(t, tok[rows_all, :].astype(jnp.float32), sctx, sctx_o, wso_m, wso_o)
        resid1[rows, :] = resid
        normed = norm_forward(resid, gain[0:1, :], bias[0:1, :])
        hidden[rows, :] = normed
        low_one[rows, :] = normed.astype(jnp.bfloat16)
        return 0

    def out_two(t, _):
        rows = step(t * TILE, TILE, TILE)
        resid2[rows, :] = with_out(t, hidden[rows, :], cctx, cctx_o, wco_m, wco_o)
        return 0

    def q_rows(t, _):
        rows = step(t * TILE, TILE, TILE)
        rows_all = step(c * half + t * TILE, TILE, TILE)
        q_send[rows, :] = nn(low_one[rows, :], wq_o[...]).astype(jnp.bfloat16)
        q_all[rows_all, :] = nn(low_one[rows, :], wq_m[...]).astype(jnp.bfloat16)
        return 0

    def split_at(order, first, count):
        places = [order.index(first + k) for k in range(count)]
        starts = [0] + [place + 1 for place in places]
        return [order[a:b] for a, b in zip(starts, places)], order[places[-1] + 1 :]

    def pieces_loop(segments, ready, work, sends):
        def body(p, _):
            for k, segment in enumerate(segments):

                @pl.when(p == k)
                def _():
                    for op in segment:
                        launch(op)
                    ready(k)

            work(p)
            for k, copy in enumerate(sends):
                pl.when(p == k)(copy.start)
            return 0

        lax.fori_loop(0, len(segments), body, 0)
        pending.extend(sends)

    for copy in own_a[:3]:
        copy.start()
    own_a[3].start()
    seg_start()
    mseg_start()
    segments, rest = split_at(list(SCHEDULE), SELF_PIECE, 4)
    for op in segments[0]:
        launch(op)
    for copy in own_b:
        copy.start()
    bounds_of()
    for copy in own_a:
        copy.wait()
    segments[0] = []

    def self_ready(k):
        if k == 0:
            wait_for(TOK_C)
        else:
            for op in weight_needs(0, k):
                wait_for(op)

    pieces_loop(segments, self_ready, self_piece, sctx_out)
    for src, dst in ((qkv, o_qkv), (wself, o_wself), (sctx, o_sctx), (slse, o_slse), (pre, o_pre)):
        keep(src, dst)
    for copy in own_b:
        copy.wait()
    before, rest = split_at(rest, OUT_ONE, 1)
    for op in before[0]:
        launch(op)
    for copy in sctx_out:
        copy.wait_recv()
    wait_for(16 + 6)
    lax.fori_loop(0, half // TILE, out_one, 0)
    for src, dst in ((resid1, o_resid1), (wso_m, o_wso_m), (wso_o, o_wso_o)):
        keep(src, dst)
    before, rest = split_at(rest, CROSS_Q, 1)
    for op in before[0]:
        launch(op)
    wait_for(32 + 6)
    lax.fori_loop(0, half // TILE, q_rows, 0)
    q_out.start()
    pending.append(q_out)
    for src, dst in ((wq_m, o_wq_m), (wq_o, o_wq_o)):
        keep(src, dst)
    segments, rest = split_at(rest, CROSS_PIECE, 4)

    def cross_ready(k):
        if k == 0:
            wait_for(MEM_C)
            q_out.wait_recv()
        else:
            for op in weight_needs(48, k):
                wait_for(op)

    pieces_loop(segments, cross_ready, cross_piece, cctx_out)
    for src, dst in ((q_all, o_q), (kv, o_kv), (wkv, o_wkv), (cctx, o_cctx), (clse, o_clse)):
        keep(src, dst)
    before, rest = split_at(rest, OUT_TWO, 1)
    for op in before[0]:
        launch(op)
    for copy in cctx_out:
        copy.wait_recv()
    wait_for(64 + 6)
    lax.fori_loop(0, half // TILE, out_two, 0)
    for src, dst in ((resid2, o_resid2), (wco_m, o_wco_m), (wco_o, o_wco_o)):
        keep(src, dst)
    for op in rest:
        launch(op)
    for op in list(copies):
        wait_for(op)
    for copy in pending:
        copy.wait_send()
    for copy in saves:
        copy.wait()


class Held(typing.NamedTuple):
    wself: jax.Array
    qkv: jax.Array
    sctx: jax.Array
    slse: jax.Array
    pre: jax.Array
    wso_m: jax.Array
    wso_o: jax.Array
    wkv: jax.Array
    wq_m: jax.Array
    wq_o: jax.Array
    wco_m: jax.Array
    wco_o: jax.Array
    q: jax.Array
    kv: jax.Array
    cctx: jax.Array
    clse: jax.Array
    resid1: jax.Array
    resid2: jax.Array
    bounds: jax.Array
    fin: jax.Array
    fout: jax.Array
    fad: jax.Array


def forward_call(tokens, memory, seg, mseg, prefix, w_self, w_so, w_cq, w_ckv, w_co, fc_in, fc_out, ad, gain, bias):
    bf16, f32 = jnp.bfloat16, jnp.float32
    half, deep = tokens.shape
    shape = jax.ShapeDtypeStruct
    held = dict(
        wself=((4, deep, 384), bf16),
        qkv=((4, SEQ, 384), bf16),
        sctx=((SEQ, 512), bf16),
        slse=((4, 8, SEQ), f32),
        pre=((4, 2, 32, 128), bf16),
        wso_m=((512, deep), bf16),
        wso_o=((512, deep), bf16),
        wkv=((4, deep, 256), bf16),
        wq_m=((deep, 512), bf16),
        wq_o=((deep, 512), bf16),
        wco_m=((512, deep), bf16),
        wco_o=((512, deep), bf16),
        q=((SEQ, 512), bf16),
        kv=((4, MLEN, 256), bf16),
        cctx=((SEQ, 512), bf16),
        clse=((4, 8, SEQ), f32),
        resid1=((half, deep), f32),
        resid2=((half, deep), f32),
        bounds=((8, SEQ), jnp.int32),
    )
    outs = [shape(*value) for value in held.values()]
    outs += [shape((3,) + fc_in.shape, bf16), shape((3,) + fc_out.shape, bf16), shape((3,) + ad.shape, bf16)]
    scratch = [pltpu.VMEM(*value) for value in held.values()] + [
        pltpu.VMEM((SEQ, deep), bf16),
        pltpu.VMEM((MLEN, deep), bf16),
        pltpu.VMEM((half, 512), bf16),
        pltpu.VMEM((half, 512), bf16),
        pltpu.VMEM((half, 512), bf16),
        pltpu.VMEM((half, deep), f32),
        pltpu.VMEM((half, deep), bf16),
        pltpu.VMEM((128, SEQ), bf16),
        pltpu.VMEM((1, SEQ), jnp.int32),
        pltpu.VMEM((1, SEQ), jnp.int32),
        pltpu.SemaphoreType.DMA((SLOTS,)),
        pltpu.SemaphoreType.DMA((SLOTS,)),
        pltpu.SemaphoreType.DMA((LOCAL_SLOTS,)),
    ]
    anywhere = pl.BlockSpec(memory_space=pl.ANY)
    vmem = pl.BlockSpec(memory_space=pltpu.VMEM)
    results = pl.pallas_call(
        forward_kernel,
        out_shape=outs,
        in_specs=[anywhere] * 13 + [vmem] * 2,
        out_specs=[anywhere] * len(outs),
        scratch_shapes=scratch,
        compiler_params=pltpu.CompilerParams(
            collective_id=0, has_side_effects=True, vmem_limit_bytes=58 * 2**20
        ),
        name="layer_forward",
    )(tokens, memory, seg, mseg, prefix, w_self, w_so, w_cq, w_ckv, w_co, fc_in, fc_out, ad, gain, bias)
    return Held(*results)


def backward_kernel(has_prefix, first_bound, bounds_s, *refs):
    if has_prefix:
        qkv_ref, bounds, ctx_ref, dctx_ref, lse_ref, pre_ref, dqkv_ref, dpre_ref, kt_ref, dk_acc, dv_acc, dq_acc, dpre_acc = refs
        q_at = lambda rows: qkv_ref[0, rows, 0:128]
        k_at = lambda rows: qkv_ref[0, rows, 128:256]
        v_at = lambda rows: qkv_ref[0, rows, 256:384]
    else:
        q_ref, kv_ref, bounds, ctx_ref, dctx_ref, lse_ref, dq_ref, dkv_ref, kt_ref, dk_acc, dv_acc, dq_acc = refs
        q_at = lambda rows: q_ref[rows, :]
        k_at = lambda rows: kv_ref[0, rows, 0:128]
        v_at = lambda rows: kv_ref[0, rows, 128:256]
    scale = 0.125 * LOG2E
    kt_ref[...] = k_at(slice(None)).astype(jnp.float32).T.astype(jnp.bfloat16)
    dk_acc[...] = jnp.zeros_like(dk_acc)
    dv_acc[...] = jnp.zeros_like(dv_acc)
    if has_prefix:
        dpre_acc[...] = jnp.zeros_like(dpre_acc)
        kp = prefix_block(pre_ref[0, 0])
        vp = prefix_block(pre_ref[0, 1])
        kpt = kp.astype(jnp.float32).T.astype(jnp.bfloat16)

    def one(qi, _):
        q0 = pl.multiple_of(qi * QB, QB)
        span = pl.ds(q0, QB)
        q = q_at(span)
        dctx = dctx_ref[span, :]
        lo = bounds[first_bound : first_bound + 1, span]
        hi = bounds[first_bound + 1 : first_bound + 2, span]
        prod = (dctx.astype(jnp.float32) * ctx_ref[span, :].astype(jnp.float32)).T
        inner = [jnp.sum(prod[h * 64 : h * 64 + 64], axis=0, keepdims=True) for h in range(2)]
        lse = [lse_ref[0, h : h + 1, span] for h in range(2)]
        qh = [half_lanes(q, h) for h in range(2)]
        dh = [half_lanes(dctx, h) for h in range(2)]
        if has_prefix:
            sp = prefix_rows(nt(kp, q) * scale)
            rows = lambda pair: jnp.concatenate([jnp.broadcast_to(t, (64, QB)) for t in pair], axis=0)
            pp = jnp.exp2(sp - rows(lse))
            dpp = nt(vp, dctx)
            dsp = (pp * (dpp - rows(inner))).astype(jnp.bfloat16)
            dpre_acc[0] += nn(dsp, q)
            dpre_acc[1] += nn(pp.astype(jnp.bfloat16), dctx)
            dq_acc[...] = nn(kpt, dsp)
        else:
            dq_acc[...] = jnp.zeros_like(dq_acc)

        def chunk(ki, _):
            k0 = pl.multiple_of(ki * KB, KB)
            keys = pl.ds(k0, KB)
            k = k_at(keys)
            v = v_at(keys)
            pos = k0 + lax.broadcasted_iota(jnp.int32, (KB, QB), 0)
            mask = (pos >= lo) & (pos <= hi)
            ps, dss = [], []
            for h in range(2):
                s = nt(k, qh[h]) * scale
                p = jnp.exp2(jnp.where(mask, s, NEG) - lse[h])
                dp = nt(v, dh[h])
                ds = (p * (dp - inner[h])).astype(jnp.bfloat16)
                ps.append(p.astype(jnp.bfloat16))
                dss.append(ds)
                dq_acc[h * 64 : h * 64 + 64, :] += nn(kt_ref[h * 64 : h * 64 + 64, keys], ds)
            dv_acc[keys, :] += nn(ps[0], dh[0]) + nn(ps[1], dh[1])
            dk_acc[keys, :] += nn(dss[0], qh[0]) + nn(dss[1], qh[1])
            return 0

        lowest = lax.div(bounds_s[first_bound, q0], KB)
        highest = lax.div(bounds_s[first_bound + 1, q0 + QB - 1], KB) + 1
        lax.fori_loop(lowest, highest, chunk, 0)
        dq = (dq_acc[...].T * 0.125).astype(jnp.bfloat16)
        if has_prefix:
            dqkv_ref[0, span, 0:128] = dq
        else:
            dq_ref[span, :] = dq
        return 0

    lax.fori_loop(0, SEQ // QB, one, 0)
    dk = (dk_acc[...] * 0.125).astype(jnp.bfloat16)
    dv = dv_acc[...].astype(jnp.bfloat16)
    if has_prefix:
        dqkv_ref[0, :, 128:256] = dk
        dqkv_ref[0, :, 256:384] = dv
        lane = lax.broadcasted_iota(jnp.int32, (32, 128), 1)
        for i, factor in ((0, 0.125), (1, 1.0)):
            dpre_ref[0, i] = jnp.where(lane < 64, dpre_acc[i, 0:32], dpre_acc[i, 64:96]) * factor
    else:
        dkv_ref[0, :, 0:128] = dk
        dkv_ref[0, :, 128:256] = dv


def backward_call(has_prefix, arrays, bounds, ctx, dctx, lse, pre=None):
    col = pl.BlockSpec((SEQ, 128), lambda j, *_: (0, j))
    piece = lambda width: pl.BlockSpec((1, SEQ, width), lambda j, *_: (j, 0, 0))
    shape = jax.ShapeDtypeStruct
    bf16, f32 = jnp.bfloat16, jnp.float32
    if has_prefix:
        in_specs = [piece(384)]
        out_specs = [piece(384), pl.BlockSpec((1, 2, 32, 128), lambda j, *_: (j, 0, 0, 0))]
        out_shape = [shape((4, SEQ, 384), bf16), shape((4, 2, 32, 128), f32)]
    else:
        in_specs = [col, piece(256)]
        out_specs = [col, piece(256)]
        out_shape = [shape((SEQ, 512), bf16), shape((4, SEQ, 256), bf16)]
    in_specs += [
        pl.BlockSpec((8, SEQ), lambda j, *_: (0, 0)),
        col,
        col,
        pl.BlockSpec((1, 8, SEQ), lambda j, *_: (j, 0, 0)),
    ]
    args = list(arrays) + [bounds, ctx, dctx, lse]
    scratch = [
        pltpu.VMEM((128, SEQ), bf16),
        pltpu.VMEM((SEQ, 128), f32),
        pltpu.VMEM((SEQ, 128), f32),
        pltpu.VMEM((128, QB), f32),
    ]
    if has_prefix:
        in_specs.append(pl.BlockSpec((1, 2, 32, 128), lambda j, *_: (j, 0, 0, 0)))
        args.append(pre)
        scratch.append(pltpu.VMEM((2, 128, 128), f32))
    return pl.pallas_call(
        functools.partial(backward_kernel, has_prefix, 0 if has_prefix else 2),
        grid_spec=pltpu.PrefetchScalarGridSpec(
            num_scalar_prefetch=1, grid=(4,), in_specs=in_specs, out_specs=out_specs, scratch_shapes=scratch
        ),
        out_shape=out_shape,
        compiler_params=pltpu.CompilerParams(vmem_limit_bytes=40 * 2**20),
        cost_estimate=pl.CostEstimate(flops=10 * 8 * SEQ * SEQ * 64, bytes_accessed=10 * 2**20, transcendentals=8 * SEQ * SEQ),
        name="self_backward" if has_prefix else "cross_backward",
    )(bounds, *args)


HIDDEN = 512


def feed_kernel(
    resid2, cot, gain, bias, wco_m, wco_o, fc_in, fin, fc_out, fout, ad, fad,
    out, grad_two, units, dctx_m, dctx_s,
    win, wout, down, up, slope, low, hidden, acc, gate, ada, branch_low, sem,
):
    bf16 = jnp.bfloat16
    per = fc_in.shape[1] // HIDDEN
    steps = 4 * per
    group = ad.shape[1]
    loads = []
    for j in range(steps):
        piece, part = divmod(j, per)
        cols = pl.ds(part * HIDDEN, HIDDEN)
        src = fc_in.at[:, cols] if piece == 0 else fin.at[piece - 1, :, cols]
        loads.append(pltpu.make_async_copy(src, win.at[j], sem.at[0, j]))
        src = fc_out.at[cols] if piece == 0 else fout.at[piece - 1, cols]
        loads.append(pltpu.make_async_copy(src, wout.at[j], sem.at[1, j]))
    ad_loads = []
    for piece in range(4):
        for i, dst in enumerate((down, up)):
            src = ad.at[i] if piece == 0 else fad.at[piece - 1, i]
            ad_loads.append(pltpu.make_async_copy(src, dst.at[pl.ds(group * piece, group)], sem.at[2, 2 * piece + i]))
    for copy in loads + ad_loads:
        copy.start()

    rows_all = resid2.shape[0]
    tiles = rows_all // TILE
    at = lambda t: pl.ds(pl.multiple_of(t * TILE, TILE), TILE)

    def begin(t, _):
        rows = at(t)
        normed = norm_forward(resid2[rows, :], gain[1:2, :], bias[1:2, :])
        hidden[rows, :] = normed
        low[rows, :] = normed.astype(bf16)
        return 0

    lax.fori_loop(0, tiles, begin, 0)
    for copy in ad_loads:
        copy.wait()
    pre = nt(low[...], down[...])
    sigma = jax.nn.sigmoid(pre)
    gate[...] = sigma * (1.0 + pre * (1.0 - sigma))
    ada[...] = (pre * sigma).astype(bf16)
    acc[...] = adapter_scale * nn(ada[...], up[...])

    def ahead(j, _):
        for i, buf in enumerate((win, wout)):
            pltpu.make_async_copy(buf.at[j], buf.at[j], sem.at[i, j]).wait()
        pre = nn(low[...], win[j])
        phi = 0.5 * (1.0 + lax.erf(pre * 0.7071067811865476))
        slope[j] = phi + pre * jnp.exp(-0.5 * pre * pre) * 0.3989422804014327
        acc[...] += nn((pre * phi).astype(bf16), wout[j])
        return 0

    lax.fori_loop(0, steps, ahead, 0)

    def middle(t, _):
        rows = at(t)
        resid = hidden[rows, :] + acc[rows, :]
        normed, inv = norm_parts(resid)
        out[rows, :] = (normed * gain[2:3, :] + bias[2:3, :]).astype(bf16)
        scaled = cot[rows, :].astype(jnp.float32) * gain[2:3, :]
        grad = inv * (
            scaled
            - jnp.mean(scaled, axis=-1, keepdims=True)
            - normed * jnp.mean(scaled * normed, axis=-1, keepdims=True)
        )
        acc[rows, :] = grad
        branch_low[rows, :] = grad.astype(bf16)
        return 0

    lax.fori_loop(0, tiles, middle, 0)
    grelu = (adapter_scale * nt(branch_low[...], up[...]) * gate[...]).astype(bf16)
    features = low.shape[1]
    units[:, 0:features] = tn(grelu, low[...])
    units[:, features : 2 * features] = adapter_scale * tn(ada[...], branch_low[...])
    acc[...] += nn(grelu, down[...])

    def behind(j, _):
        grad = (nt(branch_low[...], wout[j]) * slope[j]).astype(bf16)
        acc[...] += nt(grad, win[j])
        return 0

    lax.fori_loop(0, steps, behind, 0)

    def finish(t, _):
        rows = at(t)
        grad = norm_backward(resid2[rows, :], gain[1:2, :], acc[rows, :])
        grad_two[rows, :] = grad
        small = grad.astype(bf16)
        dctx_m[rows, :] = nt(small, wco_m[...]).astype(bf16)
        dctx_s[rows, :] = nt(small, wco_o[...]).astype(bf16)
        return 0

    lax.fori_loop(0, tiles, finish, 0)


def feed_call(resid2, cot, gain, bias, wco_m, wco_o, fc_in, fin, fc_out, fout, ad, fad):
    bf16, f32 = jnp.bfloat16, jnp.float32
    rows, deep = resid2.shape
    shape = jax.ShapeDtypeStruct
    anywhere = pl.BlockSpec(memory_space=pl.ANY)
    vmem = pl.BlockSpec(memory_space=pltpu.VMEM)
    steps = 4 * fc_in.shape[1] // HIDDEN
    units = 4 * ad.shape[1]
    return pl.pallas_call(
        feed_kernel,
        out_shape=[
            shape((rows, deep), bf16),
            shape((rows, deep), f32),
            shape((units, 2 * deep), f32),
            shape((rows, 512), bf16),
            shape((rows, 512), bf16),
        ],
        in_specs=[vmem] * 6 + [anywhere] * 6,
        out_specs=[vmem] * 5,
        scratch_shapes=[
            pltpu.VMEM((steps, deep, HIDDEN), bf16),
            pltpu.VMEM((steps, HIDDEN, deep), bf16),
            pltpu.VMEM((units, deep), bf16),
            pltpu.VMEM((units, deep), bf16),
            pltpu.VMEM((steps, rows, HIDDEN), f32),
            pltpu.VMEM((rows, deep), bf16),
            pltpu.VMEM((rows, deep), f32),
            pltpu.VMEM((rows, deep), f32),
            pltpu.VMEM((rows, units), f32),
            pltpu.VMEM((rows, units), bf16),
            pltpu.VMEM((rows, deep), bf16),
            pltpu.SemaphoreType.DMA((3, 8)),
        ],
        compiler_params=pltpu.CompilerParams(vmem_limit_bytes=60 * 2**20),
        name="feed_forward",
    )(resid2, cot, gain, bias, wco_m, wco_o, fc_in, fin, fc_out, fout, ad, fad)


AXES = ("rows", "heads")


def fast_fits(mesh):
    rows, heads = mesh.shape["rows"], mesh.shape["heads"]
    return heads == 4 and rows % 4 == 0 and (rows & (rows - 1)) == 0


def pairs_of(rows, move):
    def number(z, c, y, x):
        return (z * 2 + c) * 4 + y * 2 + x

    found = []
    for z in range(rows // 2):
        for c in range(2):
            for y in range(2):
                for x in range(2):
                    found.append((number(z, c, y, x), number(*move(z, c, y, x))))
    return found


class Moves:
    def __init__(self, rows):
        def perm(move):
            table = pairs_of(rows, move)
            return lambda value: lax.ppermute(value, AXES, table)

        self.core = perm(lambda z, c, y, x: (z, 1 - c, y, x))
        self.x = perm(lambda z, c, y, x: (z, c, y, 1 - x))
        self.y = perm(lambda z, c, y, x: (z, c, 1 - y, x))
        self.d = perm(lambda z, c, y, x: (z, c, 1 - y, 1 - x))
        crossing = [pair for pair in pairs_of(rows, lambda z, c, y, x: (z, x, y, c)) if pair[0] != pair[1]]

        def swap(value):
            stays = lax.axis_index("rows") % 2 == lax.axis_index("heads") % 2
            return jnp.where(stays, value, lax.ppermute(value, AXES, crossing))

        self.swap = swap
        self.z = []
        step = 1
        while step < rows // 2:
            self.z.append(perm(lambda z, c, y, x, step=step: (z ^ step, c, y, x)))
            step *= 2


def fast_body(
    rows,
    tokens,
    memory,
    cotangent,
    dec_seg,
    mem_seg,
    w_self,
    w_self_out,
    w_cross_q,
    w_cross_kv,
    w_cross_out,
    fc_in,
    fc_out,
    ad_down,
    ad_up,
    prefix,
    ln_gain,
    ln_bias,
):
    bf16 = jnp.bfloat16
    f32 = jnp.float32
    move = Moves(rows)
    core = lax.axis_index("rows") % 2
    count = prefix.shape[1]
    ad = jnp.stack([ad_down.T, ad_up])
    held = forward_call(
        tokens,
        memory,
        dec_seg.reshape(2, 1, SEQ),
        mem_seg.reshape(2, 1, MLEN),
        jnp.pad(prefix, ((0, 0), (0, 32 - count), (0, 0))),
        w_self,
        w_self_out,
        w_cross_q,
        w_cross_kv,
        w_cross_out,
        fc_in,
        fc_out,
        ad,
        ln_gain,
        ln_bias,
    )
    half = tokens.shape[0]

    def own_rows(value):
        return lax.dynamic_slice_in_dim(value, core * half, half, 0)

    def other_rows(value):
        return lax.dynamic_slice_in_dim(value, (1 - core) * half, half, 0)

    def whole(mine, others):
        return jnp.where(
            core == 0,
            jnp.concatenate([mine, others], axis=0),
            jnp.concatenate([others, mine], axis=0),
        )

    def after(value, *earlier):
        return lax.optimization_barrier((value,) + earlier)[0]

    out, grad_two, unit_grads, dctx_m, dctx_s = feed_call(
        held.resid2, move.swap(cotangent), ln_gain, ln_bias, held.wco_m, held.wco_o,
        fc_in, held.fin, fc_out, held.fout, ad, held.fad,
    )
    output = move.swap(out)
    units = ad.shape[1] // 2
    unit_grads = unit_grads.reshape(4, 2, units, -1)
    unit_mine = lax.dynamic_index_in_dim(unit_grads, core, 1, keepdims=False)
    unit_other = lax.dynamic_index_in_dim(unit_grads, 1 - core, 1, keepdims=False)
    unit_mine = unit_mine + move.core(unit_other.astype(bf16)).astype(f32)
    low_pieces = unit_mine.astype(bf16)
    unit_sum = (
        unit_mine[0]
        + move.x(low_pieces[1]).astype(f32)
        + move.y(low_pieces[2]).astype(f32)
        + move.d(low_pieces[3]).astype(f32)
    )

    cross_dctx = whole(dctx_m, move.core(dctx_s))
    cross_dctx = after(cross_dctx, unit_sum)
    cross_dq, cross_dkv = backward_call(
        False, (held.q, held.kv), held.bounds, held.cctx, cross_dctx, held.clse
    )
    got = move.core(other_rows(cross_dq))
    resid_one = held.resid1
    grad_one_in = grad_two + dot_right(own_rows(cross_dq), held.wq_m) + dot_right(got, held.wq_o)
    memory_part = sum(dot_right(cross_dkv[i], held.wkv[i]) for i in range(4))
    memory_sum = own_rows(memory_part) + move.core(other_rows(memory_part).astype(bf16)).astype(f32)
    grad_memory = move.swap(memory_sum.astype(bf16)).astype(f32)
    grad_one = norm_backward(resid_one, ln_gain[0], grad_one_in)

    low_grad_one = grad_one.astype(bf16)
    d_send = dot_right(low_grad_one, held.wso_o).astype(bf16)
    self_dctx = whole(dot_right(low_grad_one, held.wso_m).astype(bf16), move.core(d_send))
    self_dqkv, prefix_blocks = backward_call(
        True, (held.qkv,), held.bounds, held.sctx, self_dctx, held.slse, held.pre
    )
    input_part = sum(dot_right(self_dqkv[i], held.wself[i]) for i in range(4))
    input_sum = own_rows(input_part) + move.core(other_rows(input_part).astype(bf16)).astype(f32) + grad_one
    grad_input = move.swap(input_sum.astype(bf16)).astype(f32)
    unit_sum = after(unit_sum, self_dqkv)
    for step in move.z:
        unit_sum = unit_sum + step(unit_sum.astype(bf16)).astype(f32)
    unit_all = whole(unit_sum, move.core(unit_sum.astype(bf16)).astype(f32))
    features = tokens.shape[1]
    down_grad = unit_all[:, :features].T
    up_grad = unit_all[:, features:]

    prefix_sum = (
        prefix_blocks[0]
        + move.x(prefix_blocks[1])
        + move.y(prefix_blocks[2])
        + move.d(prefix_blocks[3])
    )
    for step in move.z:
        prefix_sum = prefix_sum + step(prefix_sum)
    prefix_other = move.core(prefix_sum)
    prefix_grad = jnp.where(
        core == 0,
        jnp.concatenate([prefix_sum, prefix_other], axis=2),
        jnp.concatenate([prefix_other, prefix_sum], axis=2),
    )[:, :count]
    return (output, grad_input, grad_memory, prefix_grad, down_grad, up_grad)


def solution(mesh):
    in_specs = (
        P(("rows", "heads"), None),
        P(("rows", "heads"), None),
        P(("rows", "heads"), None),
        P("rows"),
        P("rows"),
        P(None, None, "heads"),
        P("heads", None),
        P(None, "heads"),
        P(None, None, "heads"),
        P("heads", None),
        P(None, "heads"),
        P("heads", None),
        P(None, "heads"),
        P("heads", None),
        P(None, None, "heads"),
        P(),
        P(),
    )
    out_specs = (
        P(("rows", "heads"), None),
        P(("rows", "heads"), None),
        P(("rows", "heads"), None),
        P(None, None, "heads"),
        P(None, "heads"),
        P("heads", None),
    )
    chosen = functools.partial(fast_body, mesh.shape["rows"]) if fast_fits(mesh) else body
    return jax.shard_map(chosen, mesh=mesh, in_specs=in_specs, out_specs=out_specs, check_vma=False)
```

```python
import functools
import math
import typing

import jax
import jax.numpy as jnp
from jax import lax
from jax.experimental import pallas as pl
from jax.experimental.pallas import tpu as pltpu
from jax.sharding import PartitionSpec as P

HD = 64
SEQ = 1024
MLEN = 1024


epsilon = 1e-05
adapter_scale = 4.0
masked_score = -1e30


def dot_right(left, right):
    return lax.dot_general(
        left, right, (((1,), (1,)), ((), ())), preferred_element_type=jnp.float32
    )


def dot_left(left, right):
    return lax.dot_general(
        left, right, (((0,), (0,)), ((), ())), preferred_element_type=jnp.float32
    )


def norm_parts(resid):
    average = jnp.mean(resid, axis=-1, keepdims=True)
    centered = resid - average
    inv_scale = lax.rsqrt(jnp.mean(centered * centered, axis=-1, keepdims=True) + epsilon)
    return (centered * inv_scale, inv_scale)


def norm_forward(resid, gain, shift):
    normed, inv_scale = norm_parts(resid)
    return normed * gain + shift


def norm_backward(resid, gain, grad_out):
    normed, inv_scale = norm_parts(resid)
    scaled = grad_out * gain
    return inv_scale * (
        scaled
        - jnp.mean(scaled, axis=-1, keepdims=True)
        - normed * jnp.mean(scaled * normed, axis=-1, keepdims=True)
    )


def gelu_slope(pre_gelu):
    return (
        0.5 * (1.0 + lax.erf(pre_gelu * 0.7071067811865476))
        + pre_gelu * jnp.exp(-0.5 * pre_gelu * pre_gelu) * 0.3989422804014327
    )


def silu_slope(pre_relu):
    sigma = jax.nn.sigmoid(pre_relu)
    return sigma * (1.0 + pre_relu * (1.0 - sigma))


def to_heads(arrays, heads_here):
    return arrays.reshape(arrays.shape[0], arrays.shape[1], heads_here, HD).transpose(0, 2, 1, 3)


def from_heads(arrays):
    return arrays.transpose(0, 2, 1, 3).reshape(
        arrays.shape[0] * arrays.shape[2], arrays.shape[1] * arrays.shape[3]
    )


def join_blocks(stacked):
    moved = jnp.moveaxis(stacked, 0, 1)
    return moved.reshape((moved.shape[0], moved.shape[1] * moved.shape[2]) + moved.shape[3:])


def block_mask(row_segs, key_segs, offset, causal):
    allowed = row_segs[:, None] == key_segs[None, :]
    if causal:
        row_places = offset + lax.iota(jnp.int32, row_segs.shape[0])
        key_places = lax.iota(jnp.int32, key_segs.shape[0])
        allowed = allowed & (key_places[None, :] <= row_places[:, None])
    return allowed


def block_scores(queries, key_rows, allowed, prefix_keys):
    qk_scale = HD ** (-0.5)
    token_scores = (
        jnp.einsum("hqe,hke->hqk", queries, key_rows, preferred_element_type=jnp.float32) * qk_scale
    )
    token_scores = jnp.where(allowed[None], token_scores, masked_score)
    if prefix_keys is None:
        return (token_scores, None)
    prefix_scores = (
        jnp.einsum("hqe,hpe->hqp", queries, prefix_keys, preferred_element_type=jnp.float32)
        * qk_scale
    )
    return (token_scores, prefix_scores)


def attend_block(queries, key_rows, value_rows, allowed, prefix_keys, prefix_values):
    token_scores, prefix_scores = block_scores(queries, key_rows, allowed, prefix_keys)
    row_max = jnp.max(token_scores, axis=-1, keepdims=True)
    if prefix_scores is not None:
        row_max = jnp.maximum(row_max, jnp.max(prefix_scores, axis=-1, keepdims=True))
    token_weights = jnp.exp(token_scores - row_max)
    row_total = jnp.sum(token_weights, axis=-1, keepdims=True)
    if prefix_scores is not None:
        prefix_weights = jnp.exp(prefix_scores - row_max)
        row_total = row_total + jnp.sum(prefix_weights, axis=-1, keepdims=True)
    context = jnp.einsum(
        "hqk,hke->hqe",
        (token_weights / row_total).astype(jnp.bfloat16),
        value_rows,
        preferred_element_type=jnp.float32,
    )
    if prefix_scores is not None:
        context = context + jnp.einsum(
            "hqp,hpe->hqe",
            (prefix_weights / row_total).astype(jnp.bfloat16),
            prefix_values,
            preferred_element_type=jnp.float32,
        )
    return (context.astype(jnp.bfloat16), row_max + jnp.log(row_total))


def attend_back(
    queries, key_rows, value_rows, allowed, prefix_keys, prefix_values, log_total, context_grad
):
    qk_scale = HD ** (-0.5)
    token_scores, prefix_scores = block_scores(queries, key_rows, allowed, prefix_keys)
    token_probs = jnp.exp(token_scores - log_total)
    token_dprob = jnp.einsum(
        "hqe,hke->hqk", context_grad, value_rows, preferred_element_type=jnp.float32
    )
    inner = jnp.sum(token_probs * token_dprob, axis=-1, keepdims=True)
    if prefix_scores is not None:
        prefix_probs = jnp.exp(prefix_scores - log_total)
        prefix_dprob = jnp.einsum(
            "hqe,hpe->hqp", context_grad, prefix_values, preferred_element_type=jnp.float32
        )
        inner = inner + jnp.sum(prefix_probs * prefix_dprob, axis=-1, keepdims=True)
    token_dscore = (token_probs * (token_dprob - inner)).astype(jnp.bfloat16)
    query_grad = jnp.einsum(
        "hqk,hke->hqe", token_dscore, key_rows, preferred_element_type=jnp.float32
    )
    key_grad = (
        jnp.einsum("hqk,hqe->hke", token_dscore, queries, preferred_element_type=jnp.float32)
        * qk_scale
    )
    value_grad = jnp.einsum(
        "hqk,hqe->hke",
        token_probs.astype(jnp.bfloat16),
        context_grad,
        preferred_element_type=jnp.float32,
    )
    if prefix_scores is None:
        return (query_grad * qk_scale, (key_grad, value_grad))
    prefix_dscore = (prefix_probs * (prefix_dprob - inner)).astype(jnp.bfloat16)
    query_grad = query_grad + jnp.einsum(
        "hqp,hpe->hqe", prefix_dscore, prefix_keys, preferred_element_type=jnp.float32
    )
    prefix_key_grad = (
        jnp.einsum("hqp,hqe->hpe", prefix_dscore, queries, preferred_element_type=jnp.float32)
        * qk_scale
    )
    prefix_value_grad = jnp.einsum(
        "hqp,hqe->hpe",
        prefix_probs.astype(jnp.bfloat16),
        context_grad,
        preferred_element_type=jnp.float32,
    )
    return (query_grad * qk_scale, (key_grad, value_grad, prefix_key_grad, prefix_value_grad))


def sequence_forward(
    queries, key_rows, value_rows, row_segs, key_segs, prefix_keys, prefix_values, causal
):
    seq_width = queries.shape[1]
    block_rows = min(512, seq_width)

    def one_block(block_index):
        offset = block_index * block_rows
        allowed = block_mask(
            lax.dynamic_slice_in_dim(row_segs, offset, block_rows, 0), key_segs, offset, causal
        )
        query_part = lax.dynamic_slice_in_dim(queries, offset, block_rows, 1)
        return attend_block(query_part, key_rows, value_rows, allowed, prefix_keys, prefix_values)

    context, log_total = lax.map(one_block, jnp.arange(seq_width // block_rows, dtype=jnp.int32))
    return (join_blocks(context), join_blocks(log_total))


def sequence_backward(
    queries,
    key_rows,
    value_rows,
    row_segs,
    key_segs,
    prefix_keys,
    prefix_values,
    causal,
    log_total,
    context_grad,
):
    seq_width = queries.shape[1]
    block_rows = min(512, seq_width)
    key_zero = jnp.zeros(key_rows.shape, jnp.float32)
    initial = (key_zero, key_zero)
    if prefix_keys is not None:
        prefix_zero = jnp.zeros(prefix_keys.shape, jnp.float32)
        initial = initial + (prefix_zero, prefix_zero)

    def one_block(running, block_index):
        offset = block_index * block_rows
        allowed = block_mask(
            lax.dynamic_slice_in_dim(row_segs, offset, block_rows, 0), key_segs, offset, causal
        )
        query_part = lax.dynamic_slice_in_dim(queries, offset, block_rows, 1)
        total_part = lax.dynamic_slice_in_dim(log_total, offset, block_rows, 1)
        grad_part = lax.dynamic_slice_in_dim(context_grad, offset, block_rows, 1)
        query_grad, block_grads = attend_back(
            query_part,
            key_rows,
            value_rows,
            allowed,
            prefix_keys,
            prefix_values,
            total_part,
            grad_part,
        )
        return (tuple((summed + added for summed, added in zip(running, block_grads))), query_grad)

    running, query_grad = lax.scan(
        one_block, initial, jnp.arange(seq_width // block_rows, dtype=jnp.int32)
    )
    outputs = (
        join_blocks(query_grad).astype(jnp.bfloat16),
        running[0].astype(jnp.bfloat16),
        running[1].astype(jnp.bfloat16),
    )
    return outputs + running[2:]


def gather_rows(row_share):
    return lax.all_gather(row_share, "heads", axis=0, tiled=True)


def gather_grads(row_share):
    return lax.all_gather(row_share, "heads", axis=0, tiled=True)


def sum_rows(partial_value):
    return lax.psum_scatter(partial_value, "heads", scatter_dimension=0, tiled=True)


def sum_grads(partial_value):
    return lax.psum_scatter(partial_value, "heads", scatter_dimension=0, tiled=True)


def body(
    tokens,
    memory,
    cotangent,
    dec_seg,
    mem_seg,
    w_self,
    w_self_out,
    w_cross_q,
    w_cross_kv,
    w_cross_out,
    fc_in,
    fc_out,
    ad_down,
    ad_up,
    prefix,
    ln_gain,
    ln_bias,
):
    local_width = w_self.shape[2]
    heads_here = local_width // HD
    seg_dec = dec_seg.reshape(-1, SEQ)
    seg_mem = mem_seg.reshape(-1, MLEN)
    seq_count = seg_dec.shape[0]
    prefix_heads = to_heads(prefix, heads_here)
    prefix_keys = prefix_heads[0]
    prefix_values = prefix_heads[1]
    gathered_x = gather_rows(tokens)
    self_proj = jnp.einsum(
        "td,cdn->ctn", gathered_x, w_self, preferred_element_type=jnp.float32
    ).astype(jnp.bfloat16)
    self_proj = self_proj.reshape(3, seq_count, SEQ, local_width)
    self_queries = to_heads(self_proj[0], heads_here)
    self_keys = to_heads(self_proj[1], heads_here)
    self_values = to_heads(self_proj[2], heads_here)

    def self_forward(packed):
        return sequence_forward(
            packed[0], packed[1], packed[2], packed[3], packed[3], prefix_keys, prefix_values, True
        )

    self_context, self_total = lax.map(
        self_forward, (self_queries, self_keys, self_values, seg_dec)
    )
    attn_partial = jnp.dot(from_heads(self_context), w_self_out, preferred_element_type=jnp.float32)
    resid_one = tokens.astype(jnp.float32) + sum_rows(attn_partial)
    hidden_one = norm_forward(resid_one, ln_gain[0], ln_bias[0])
    gathered_one = gather_rows(hidden_one.astype(jnp.bfloat16))
    gathered_mem = lax.all_gather(memory, "heads", axis=0, tiled=True)
    cross_rows = jnp.dot(gathered_one, w_cross_q, preferred_element_type=jnp.float32).astype(
        jnp.bfloat16
    )
    cross_proj = jnp.einsum(
        "td,cdn->ctn", gathered_mem, w_cross_kv, preferred_element_type=jnp.float32
    ).astype(jnp.bfloat16)
    cross_queries = to_heads(cross_rows.reshape(seq_count, SEQ, local_width), heads_here)
    cross_proj = cross_proj.reshape(2, seq_count, MLEN, local_width)
    cross_keys = to_heads(cross_proj[0], heads_here)
    cross_values = to_heads(cross_proj[1], heads_here)

    def cross_forward(packed):
        return sequence_forward(
            packed[0], packed[1], packed[2], packed[3], packed[4], None, None, False
        )

    cross_context, cross_total = lax.map(
        cross_forward, (cross_queries, cross_keys, cross_values, seg_dec, seg_mem)
    )
    cross_partial = jnp.dot(
        from_heads(cross_context), w_cross_out, preferred_element_type=jnp.float32
    )
    resid_two = hidden_one + sum_rows(cross_partial)
    hidden_two = norm_forward(resid_two, ln_gain[1], ln_bias[1])
    hidden_low = hidden_two.astype(jnp.bfloat16)
    full_in, full_out, full_down, full_up = (fc_in, fc_out, ad_down, ad_up)
    ffn_rows = gather_rows(hidden_low)
    pre_gelu = jnp.dot(ffn_rows, full_in, preferred_element_type=jnp.float32)
    activated = jax.nn.gelu(pre_gelu, approximate=False).astype(jnp.bfloat16)
    pre_relu = jnp.dot(ffn_rows, full_down, preferred_element_type=jnp.float32)
    adapted = (pre_relu * jax.nn.sigmoid(pre_relu)).astype(jnp.bfloat16)
    branch = jnp.dot(
        activated, full_out, preferred_element_type=jnp.float32
    ) + adapter_scale * jnp.dot(adapted, full_up, preferred_element_type=jnp.float32)
    resid_three = hidden_two + sum_rows(branch)
    output = norm_forward(resid_three, ln_gain[2], ln_bias[2]).astype(jnp.bfloat16)
    grad_three = norm_backward(resid_three, ln_gain[2], cotangent.astype(jnp.float32))
    grad_branch = grad_three.astype(jnp.bfloat16)
    branch_rows = gather_grads(grad_branch)
    grad_gelu = (dot_right(branch_rows, full_out) * gelu_slope(pre_gelu)).astype(jnp.bfloat16)
    grad_relu = (adapter_scale * dot_right(branch_rows, full_up) * silu_slope(pre_relu)).astype(
        jnp.bfloat16
    )
    up_grad = adapter_scale * dot_left(adapted, branch_rows)
    down_grad = dot_left(ffn_rows, grad_relu)
    hidden_partial = dot_right(grad_gelu, full_in) + dot_right(grad_relu, full_down)
    grad_two_in = grad_three + sum_grads(hidden_partial)
    down_grad, up_grad = (
        lax.psum(down_grad.astype(jnp.bfloat16), "rows").astype(jnp.float32),
        lax.psum(up_grad.astype(jnp.bfloat16), "rows").astype(jnp.float32),
    )
    grad_two = norm_backward(resid_two, ln_gain[1], grad_two_in)
    cross_out_rows = gather_grads(grad_two.astype(jnp.bfloat16))
    cross_dctx = dot_right(cross_out_rows, w_cross_out).astype(jnp.bfloat16)
    cross_dctx = to_heads(cross_dctx.reshape(seq_count, SEQ, local_width), heads_here)

    def cross_back(packed):
        return sequence_backward(
            packed[0],
            packed[1],
            packed[2],
            packed[3],
            packed[4],
            None,
            None,
            False,
            packed[5],
            packed[6],
        )

    cross_qgrad, cross_kgrad, cross_vgrad = lax.map(
        cross_back,
        (cross_queries, cross_keys, cross_values, seg_dec, seg_mem, cross_total, cross_dctx),
    )
    memory_kv = jnp.stack([from_heads(cross_kgrad), from_heads(cross_vgrad)])
    one_partial = dot_right(from_heads(cross_qgrad), w_cross_q)
    grad_one_in = grad_two + sum_grads(one_partial)
    memory_partial = jnp.einsum(
        "ctn,cdn->td", memory_kv, w_cross_kv, preferred_element_type=jnp.float32
    )
    grad_memory = lax.psum_scatter(
        memory_partial.astype(jnp.bfloat16), "heads", scatter_dimension=0, tiled=True
    ).astype(jnp.float32)
    grad_one = norm_backward(resid_one, ln_gain[0], grad_one_in)
    attn_rows = gather_grads(grad_one.astype(jnp.bfloat16))
    self_dctx = dot_right(attn_rows, w_self_out).astype(jnp.bfloat16)
    self_dctx = to_heads(self_dctx.reshape(seq_count, SEQ, local_width), heads_here)

    def self_back(running, packed):
        query_grad, key_grad, value_grad, pkey_grad, pvalue_grad = sequence_backward(
            packed[0],
            packed[1],
            packed[2],
            packed[3],
            packed[3],
            prefix_keys,
            prefix_values,
            True,
            packed[4],
            packed[5],
        )
        return (
            (running[0] + pkey_grad, running[1] + pvalue_grad),
            (query_grad, key_grad, value_grad),
        )

    zero_grad = jnp.zeros(prefix_keys.shape, jnp.float32)
    prefix_sums, self_grads = lax.scan(
        self_back,
        (zero_grad, zero_grad),
        (self_queries, self_keys, self_values, seg_dec, self_total, self_dctx),
    )
    self_stack = jnp.stack(
        [from_heads(self_grads[0]), from_heads(self_grads[1]), from_heads(self_grads[2])]
    )
    input_partial = jnp.einsum(
        "ctn,cdn->td", self_stack, w_self, preferred_element_type=jnp.float32
    )
    grad_input = grad_one + sum_grads(input_partial)
    prefix_grad = (
        jnp.stack([prefix_sums[0], prefix_sums[1]])
        .transpose(0, 2, 1, 3)
        .reshape(2, prefix.shape[1], local_width)
    )
    prefix_grad = lax.psum(prefix_grad, "rows")
    return (output, grad_input, grad_memory, prefix_grad, down_grad, up_grad)


QB = 256
KB = 256
LOG2E = math.log2(math.e)
NEG = -1e30


def nt(a, b):
    return lax.dot_general(a, b, (((1,), (1,)), ((), ())), preferred_element_type=jnp.float32)


def nn(a, b):
    return lax.dot_general(a, b, (((1,), (0,)), ((), ())), preferred_element_type=jnp.float32)


def tn(a, b):
    return lax.dot_general(a, b, (((0,), (0,)), ((), ())), preferred_element_type=jnp.float32)


def half_lanes(v, h):
    lane = lax.broadcasted_iota(jnp.int32, v.shape, 1)
    keep = (lane < 64) if h == 0 else (lane >= 64)
    return jnp.where(keep, v, jnp.zeros_like(v))


def prefix_rows(scores):
    row = lax.broadcasted_iota(jnp.int32, scores.shape, 0)
    return jnp.where(lax.rem(row, 64) < 30, scores, NEG)


MESH = pl.DeviceIdType.MESH
TILE = 256

TOK, TOK_C, MEM, MEM_C = 112, 113, 114, 115
SELF_PIECE, OUT_ONE, CROSS_Q, CROSS_PIECE, OUT_TWO = 128, 132, 133, 134, 138
SLOTS, LOCAL_SLOTS = 128, 48
GROUPS = ((1, 0), (1, 0), (1, 0), (0, 1), (1, 1), (0, 0), (1, 0))
SCHEDULE = (16, 17, 65, 64, 20, 33, 32, 68, 97, 112, 35, 67, 36, 19, 114, 113, 18, 100, 49, 128, 0, 115, 21, 1, 22, 96, 3, 2, 4, 129, 48, 34, 98, 5, 130, 80, 37, 131, 81, 99, 38, 132, 133, 101, 134, 66, 50, 82, 135, 69, 102, 136, 70, 137, 86, 138)


class Place:
    def __init__(self):
        self.row, self.head = lax.axis_index("rows"), lax.axis_index("heads")
        self.c, self.z = lax.rem(self.row, 2), lax.div(self.row, 2)
        self.x, self.y = lax.rem(self.head, 2), lax.div(self.head, 2)
        self.odd = lax.rem(self.z, 2)
        c, x, y, z = self.c, self.x, self.y, self.z
        self.to_x = (self.row, 2 * y + 1 - x)
        self.to_y = (self.row, 2 * (1 - y) + x)
        self.to_d = (self.row, 2 * (1 - y) + 1 - x)
        self.to_z = (2 * (z + 1 - 2 * self.odd) + c, self.head)
        self.to_c = (2 * z + 1 - c, self.head)
        self.to_s = (2 * z + x, 2 * y + c)

    def greet(self, devices, swaps):
        barrier = pltpu.get_barrier_semaphore()
        for device in devices:
            pl.semaphore_signal(barrier, inc=1, device_id=device, device_id_type=MESH)
        count = len(devices)
        if swaps:
            moves = self.c != self.x

            @pl.when(moves)
            def _():
                pl.semaphore_signal(barrier, inc=1, device_id=self.to_s, device_id_type=MESH)

            count = count + moves.astype(jnp.int32)
        pl.semaphore_wait(barrier, count)


def prefix_block(rows):
    nothing = jnp.zeros_like(rows)
    return jnp.concatenate([half_lanes(rows, 0), nothing, half_lanes(rows, 1), nothing], axis=0)


def attend_tile(q, k, vt, mask, kp, vpt):
    scale = 0.125 * LOG2E
    rows = q.shape[0]
    if kp is not None:
        sp = prefix_rows(nt(kp, q) * scale)
    outs, tops, sums = [], [], []
    for h in range(2):
        s = jnp.where(mask, nt(k, half_lanes(q, h)) * scale, NEG)
        m = jnp.max(s, axis=0, keepdims=True)
        if kp is not None:
            m = jnp.maximum(m, jnp.max(sp[h * 64 : h * 64 + 32], axis=0, keepdims=True))
        e = jnp.exp2(s - m)
        outs.append(nn(vt[h * 64 : h * 64 + 64], e.astype(jnp.bfloat16)))
        sums.append(jnp.sum(e, axis=0, keepdims=True))
        tops.append(m)
    if kp is not None:
        mm = jnp.concatenate([jnp.broadcast_to(t, (64, rows)) for t in tops], axis=0)
        ep = jnp.exp2(sp - mm)
        sums = [sums[h] + jnp.sum(ep[h * 64 : h * 64 + 32], axis=0, keepdims=True) for h in range(2)]
        extra = nn(vpt, ep.astype(jnp.bfloat16))
        outs = [outs[h] + extra[h * 64 : h * 64 + 64] for h in range(2)]
    both = jnp.concatenate([outs[h] * (1.0 / sums[h]) for h in range(2)], axis=0)
    return both.T.astype(jnp.bfloat16), [tops[h] + jnp.log2(sums[h]) for h in range(2)]


def forward_kernel(
    tokens, memory, seg, mseg, prefix, w_self, w_so, w_cq, w_ckv, w_co, fc_in, fc_out, ad, gain, bias,
    o_wself, o_qkv, o_sctx, o_slse, o_pre, o_wso_m, o_wso_o, o_wkv, o_wq_m, o_wq_o, o_wco_m, o_wco_o,
    o_q, o_kv, o_cctx, o_clse, o_resid1, o_resid2, o_bounds, fin, fout, fad,
    wself, qkv, sctx, slse, pre, wso_m, wso_o, wkv, wq_m, wq_o, wco_m, wco_o,
    q_all, kv, cctx, clse, resid1, resid2, bounds, tok, mem, sctx_o, cctx_o, q_send, hidden, low_one, vt, seg_v, mseg_v,
    send, recv, local,
):
    place_of = Place()
    c, x, y, odd = place_of.c, place_of.x, place_of.y, place_of.odd
    to_x, to_y, to_z, to_c, to_s = place_of.to_x, place_of.to_y, place_of.to_z, place_of.to_c, place_of.to_s
    stays, moves = c == x, c != x
    place_of.greet((to_x, to_y, to_z, to_c), True)

    taken = []

    def there(src, dst, device):
        slot = len(taken)
        taken.append(slot)
        return pltpu.make_async_remote_copy(
            src_ref=src, dst_ref=dst, send_sem=send.at[slot], recv_sem=recv.at[slot], device_id=device, device_id_type=MESH
        )

    used = []

    def here(src, dst):
        slot = len(used)
        used.append(slot)
        return pltpu.make_async_copy(src, dst, local.at[slot])

    deep = w_self.shape[1]
    half = tok.shape[0] // 2
    step = lambda start, size, unit: pl.ds(pl.multiple_of(start, unit), size)
    mine = step(c * half, half, half)
    others = step((1 - c) * half, half, half)
    lanes = step(c * 128, 128, 128)
    other_lanes = step((1 - c) * 128, 128, 128)
    rows_c, rows_o = lanes, other_lanes
    foreign = pl.ds(128, 384)
    hid = fc_in.shape[1]
    units = ad.shape[1]
    pending = []

    def swap_of(src, target):
        away = there(src, target.at[step(x * half, half, half)], to_s)
        home = here(src, target.at[mine])
        back = there(target.at[mine], target.at[mine], to_c)

        def start():
            pl.when(moves)(away.start)
            pl.when(stays)(home.start)

        def wait():
            pl.when(moves)(away.wait)
            pl.when(stays)(home.wait)

        return start, wait, back

    def seg_of(src, dst):
        home = here(src.at[y], dst)
        away = there(src.at[y], dst, to_c)

        def start():
            pl.when(stays)(home.start)
            pl.when(stays)(away.start)

        def wait():
            pl.when(stays)(home.wait)
            pl.when(stays)(away.wait_send)
            pl.when(moves)(away.wait_recv)

        return start, wait

    def deep_rows(shared):
        return step(odd * (deep // 2), deep // 2, deep // 2) if shared else pl.ds(0, deep)

    def thin_rows(piece, shared):
        return step(128 * piece + odd * 64, 64, 64) if shared else pl.ds(128 * piece, 128)

    def thin_own(shared):
        return step(128 * c + odd * 64, 64, 64) if shared else rows_c

    def span(size, shared):
        return step(c * (size // 2) + odd * (size // 4), size // 4, size // 4) if shared else step(c * (size // 2), size // 2, size // 2)

    lane_of = lambda i: pl.ds(128 * i, 128)

    def group_a(shared):
        rows = deep_rows(shared)
        first = lambda piece: [(w_self.at[i, rows, lanes], wself.at[piece, rows, lane_of(i)]) for i in range(3)] + [
            (prefix.at[:, :, lanes], pre.at[piece])
        ]
        return first, lambda piece: [wself.at[piece, rows], pre.at[piece]], 1, []

    def group_thin(src, dst_m, dst_o, shared):
        first = lambda piece: [(src.at[thin_own(shared)], dst_m.at[thin_rows(piece, shared)])]
        return first, lambda piece: [dst_m.at[thin_rows(piece, shared)]], 1, [(dst_m.at[foreign], dst_o.at[foreign])]

    def group_q(shared):
        rows = deep_rows(shared)
        first = lambda piece: [(w_cq.at[rows, lanes], wq_m.at[rows, lane_of(piece)])]
        return first, lambda piece: [wq_m.at[rows, lane_of(piece)]], 1, [(wq_m.at[:, foreign], wq_o.at[:, foreign])]

    def group_v(shared):
        rows = deep_rows(shared)
        first = lambda piece: [(w_ckv.at[i, rows, lanes], wkv.at[piece, rows, lane_of(i)]) for i in range(2)]
        return first, lambda piece: [wkv.at[piece, rows]], 1, []

    def group_i(shared):
        cols = span(hid, shared)
        both = fin.at[:, :, span(hid, False)]
        first = lambda piece: [(fc_in.at[:, cols], fin.at[piece - 1, :, cols])]
        return first, lambda piece: [fin.at[piece - 1, :, cols]], 1, [(both, both)]

    def group_o(shared):
        rows, some = span(hid, shared), span(units, shared)
        both, both_units = fout.at[:, span(hid, False)], fad.at[:, :, span(units, False)]
        first = lambda piece: [(fc_out.at[rows], fout.at[piece - 1, rows]), (ad.at[:, some], fad.at[piece - 1, :, some])]
        hold = lambda piece: [fout.at[piece - 1, rows], fad.at[piece - 1, :, some]]
        return first, hold, 2, [(both, both), (both_units, both_units)]

    makers = [
        group_a,
        functools.partial(group_thin, w_so, wso_m, wso_o),
        group_q,
        group_v,
        functools.partial(group_thin, w_co, wco_m, wco_o),
        group_i,
        group_o,
    ]
    copies, needs = {}, {}
    for index, (make, (shared, through_x)) in enumerate(zip(makers, GROUPS)):
        first, hold, shared_count, cross = make(bool(shared))
        base = 16 * index
        copies[base] = [there(src, dst, to_x) for src, dst in first(1)]
        copies[base + 1] = [there(src, dst, to_y) for src, dst in first(2)]
        near, device = (2, to_x) if through_x else (1, to_y)
        copies[base + 2] = [there(src, dst, device) for src, dst in zip(hold(near), hold(3))]
        needs[base], needs[base + 1], needs[base + 2] = [], [], [base + near - 1]
        arrived = [base, base + 1, base + 2]
        if shared:
            for i in range(3):
                copies[base + 3 + i] = [there(ref, ref, to_z) for ref in hold(i + 1)[:shared_count]]
                needs[base + 3 + i] = [base + i]
                arrived.append(base + 3 + i)
        if cross:
            copies[base + 6] = [there(src, dst, to_c) for src, dst in cross]
            needs[base + 6] = arrived
    tok_start, tok_wait, tok_back = swap_of(tokens, tok)
    mem_start, mem_wait, mem_back = swap_of(memory, mem)
    copies[TOK_C], copies[MEM_C] = [tok_back], [mem_back]
    needs[TOK_C], needs[MEM_C] = [TOK], [MEM]
    seg_start, seg_wait = seg_of(seg, seg_v)
    mseg_start, mseg_wait = seg_of(mseg, mseg_v)
    sctx_out = [there(sctx.at[others, lane_of(i)], sctx_o.at[:, lane_of(i)], to_c) for i in range(4)]
    cctx_out = [there(cctx.at[others, lane_of(i)], cctx_o.at[:, lane_of(i)], to_c) for i in range(4)]
    q_out = there(q_send, q_all.at[mine], to_c)

    landed = set()

    def wait_for(op):
        if op in landed:
            return
        landed.add(op)
        if op == TOK:
            tok_wait()
        elif op == MEM:
            mem_wait()
        elif op in copies:
            for copy in copies[op]:
                copy.wait_recv()

    def launch(op):
        if op == TOK:
            tok_start()
        elif op == MEM:
            mem_start()
        else:
            for need in needs[op]:
                wait_for(need)
            for copy in copies[op]:
                copy.start()
                pending.append(copy)

    saves = []

    def keep(src, dst):
        copy = here(src, dst)
        copy.start()
        saves.append(copy)

    own_a = [here(w_self.at[i, :, lanes], wself.at[0, :, lane_of(i)]) for i in range(3)]
    own_a.append(here(prefix.at[:, :, lanes], pre.at[0]))
    own_b = [
        here(w_so.at[rows_c], wso_m.at[lane_of(0)]),
        here(w_so.at[rows_o], wso_o.at[lane_of(0)]),
        here(w_co.at[rows_c], wco_m.at[lane_of(0)]),
        here(w_co.at[rows_o], wco_o.at[lane_of(0)]),
        here(w_cq.at[:, lanes], wq_m.at[:, lane_of(0)]),
        here(w_cq.at[:, other_lanes], wq_o.at[:, lane_of(0)]),
        here(w_ckv.at[0, :, lanes], wkv.at[0, :, lane_of(0)]),
        here(w_ckv.at[1, :, lanes], wkv.at[0, :, lane_of(1)]),
    ]

    def bounds_of():
        seg_wait()
        mseg_wait()
        dec, men = seg_v[...], mseg_v[...]

        def below(values, d):
            return jnp.sum((values < d).astype(jnp.int32), axis=1, keepdims=True)

        def pick(counts):
            out = jnp.broadcast_to(counts[0], dec.shape)
            for d in range(1, 4):
                out = jnp.where(dec == d, counts[d], out)
            return out

        zero = jnp.zeros((1, 1), jnp.int32)
        full = jnp.full((1, 1), MLEN, jnp.int32)
        self_lo = pick([zero] + [below(dec, d) for d in range(1, 4)])
        mem_counts = [zero] + [below(men, d) for d in range(1, 4)] + [full]
        bounds[...] = jnp.concatenate(
            [self_lo, lax.broadcasted_iota(jnp.int32, dec.shape, 1), pick(mem_counts[:4]), pick(mem_counts[1:]) - 1]
            + [jnp.zeros_like(dec)] * 4,
            axis=0,
        )
        keep(bounds, o_bounds)

    def weight_needs(base, piece):
        found = [base + piece - 1, base + 2 + piece]
        return [op for op in found if op in copies]

    def project(dst, p, source, weight):
        def rows_of(t, _):
            rows = step(t * TILE, TILE, TILE)
            dst[p, rows, :] = nn(source[rows, :], weight[p]).astype(jnp.bfloat16)
            return 0

        lax.fori_loop(0, SEQ // TILE, rows_of, 0)

    def self_piece(p):
        project(qkv, p, tok, wself)
        vt[...] = qkv[p, :, 256:384].astype(jnp.float32).T.astype(jnp.bfloat16)
        kp = prefix_block(pre[p, 0])
        vpt = prefix_block(pre[p, 1]).astype(jnp.float32).T.astype(jnp.bfloat16)
        place = step(p * 128, 128, 128)
        for qi in range(SEQ // QB):
            width = (qi + 1) * QB
            rows = slice(qi * QB, (qi + 1) * QB)
            pos = lax.broadcasted_iota(jnp.int32, (width, QB), 0)
            mask = (pos >= bounds[0:1, rows]) & (pos <= bounds[1:2, rows])
            out, lse = attend_tile(qkv[p, rows, 0:128], qkv[p, 0:width, 128:256], vt[:, 0:width], mask, kp, vpt)
            sctx[rows, place] = out
            for h in range(2):
                slse[p, h : h + 1, rows] = lse[h]

    def cross_piece(p):
        project(kv, p, mem, wkv)
        vt[...] = kv[p, :, 128:256].astype(jnp.float32).T.astype(jnp.bfloat16)
        place = step(p * 128, 128, 128)

        def block(qi, _):
            rows = step(qi * QB, QB, QB)
            pos = lax.broadcasted_iota(jnp.int32, (MLEN, QB), 0)
            mask = (pos >= bounds[2:3, rows]) & (pos <= bounds[3:4, rows])
            out, lse = attend_tile(q_all[rows, place], kv[p, :, 0:128], vt[...], mask, None, None)
            cctx[rows, place] = out
            for h in range(2):
                clse[p, h : h + 1, rows] = lse[h]
            return 0

        lax.fori_loop(0, SEQ // QB, block, 0)

    def with_out(t, resid_before, ctx_m, ctx_o, w_m, w_o):
        rows = step(t * TILE, TILE, TILE)
        rows_all = step(c * half + t * TILE, TILE, TILE)
        return resid_before + nn(ctx_m[rows_all, :], w_m[...]) + nn(ctx_o[rows, :], w_o[...])

    def out_one(t, _):
        rows = step(t * TILE, TILE, TILE)
        rows_all = step(c * half + t * TILE, TILE, TILE)
        resid = with_out(t, tok[rows_all, :].astype(jnp.float32), sctx, sctx_o, wso_m, wso_o)
        resid1[rows, :] = resid
        normed = norm_forward(resid, gain[0:1, :], bias[0:1, :])
        hidden[rows, :] = normed
        low_one[rows, :] = normed.astype(jnp.bfloat16)
        return 0

    def out_two(t, _):
        rows = step(t * TILE, TILE, TILE)
        resid2[rows, :] = with_out(t, hidden[rows, :], cctx, cctx_o, wco_m, wco_o)
        return 0

    def q_rows(t, _):
        rows = step(t * TILE, TILE, TILE)
        rows_all = step(c * half + t * TILE, TILE, TILE)
        q_send[rows, :] = nn(low_one[rows, :], wq_o[...]).astype(jnp.bfloat16)
        q_all[rows_all, :] = nn(low_one[rows, :], wq_m[...]).astype(jnp.bfloat16)
        return 0

    def split_at(order, first, count):
        places = [order.index(first + k) for k in range(count)]
        starts = [0] + [place + 1 for place in places]
        return [order[a:b] for a, b in zip(starts, places)], order[places[-1] + 1 :]

    def pieces_loop(segments, ready, work, sends):
        def body(p, _):
            for k, segment in enumerate(segments):

                @pl.when(p == k)
                def _():
                    for op in segment:
                        launch(op)
                    ready(k)

            work(p)
            for k, copy in enumerate(sends):
                pl.when(p == k)(copy.start)
            return 0

        lax.fori_loop(0, len(segments), body, 0)
        pending.extend(sends)

    for copy in own_a[:3]:
        copy.start()
    own_a[3].start()
    seg_start()
    mseg_start()
    segments, rest = split_at(list(SCHEDULE), SELF_PIECE, 4)
    for op in segments[0]:
        launch(op)
    for copy in own_b:
        copy.start()
    bounds_of()
    for copy in own_a:
        copy.wait()
    segments[0] = []

    def self_ready(k):
        if k == 0:
            wait_for(TOK_C)
        else:
            for op in weight_needs(0, k):
                wait_for(op)

    pieces_loop(segments, self_ready, self_piece, sctx_out)
    for src, dst in ((qkv, o_qkv), (wself, o_wself), (sctx, o_sctx), (slse, o_slse), (pre, o_pre)):
        keep(src, dst)
    for copy in own_b:
        copy.wait()
    before, rest = split_at(rest, OUT_ONE, 1)
    for op in before[0]:
        launch(op)
    for copy in sctx_out:
        copy.wait_recv()
    wait_for(16 + 6)
    lax.fori_loop(0, half // TILE, out_one, 0)
    for src, dst in ((resid1, o_resid1), (wso_m, o_wso_m), (wso_o, o_wso_o)):
        keep(src, dst)
    before, rest = split_at(rest, CROSS_Q, 1)
    for op in before[0]:
        launch(op)
    wait_for(32 + 6)
    lax.fori_loop(0, half // TILE, q_rows, 0)
    q_out.start()
    pending.append(q_out)
    for src, dst in ((wq_m, o_wq_m), (wq_o, o_wq_o)):
        keep(src, dst)
    segments, rest = split_at(rest, CROSS_PIECE, 4)

    def cross_ready(k):
        if k == 0:
            wait_for(MEM_C)
            q_out.wait_recv()
        else:
            for op in weight_needs(48, k):
                wait_for(op)

    pieces_loop(segments, cross_ready, cross_piece, cctx_out)
    for src, dst in ((q_all, o_q), (kv, o_kv), (wkv, o_wkv), (cctx, o_cctx), (clse, o_clse)):
        keep(src, dst)
    before, rest = split_at(rest, OUT_TWO, 1)
    for op in before[0]:
        launch(op)
    for copy in cctx_out:
        copy.wait_recv()
    wait_for(64 + 6)
    lax.fori_loop(0, half // TILE, out_two, 0)
    for src, dst in ((resid2, o_resid2), (wco_m, o_wco_m), (wco_o, o_wco_o)):
        keep(src, dst)
    for op in rest:
        launch(op)
    for op in list(copies):
        wait_for(op)
    for copy in pending:
        copy.wait_send()
    for copy in saves:
        copy.wait()


class Held(typing.NamedTuple):
    wself: jax.Array
    qkv: jax.Array
    sctx: jax.Array
    slse: jax.Array
    pre: jax.Array
    wso_m: jax.Array
    wso_o: jax.Array
    wkv: jax.Array
    wq_m: jax.Array
    wq_o: jax.Array
    wco_m: jax.Array
    wco_o: jax.Array
    q: jax.Array
    kv: jax.Array
    cctx: jax.Array
    clse: jax.Array
    resid1: jax.Array
    resid2: jax.Array
    bounds: jax.Array
    fin: jax.Array
    fout: jax.Array
    fad: jax.Array


def forward_call(tokens, memory, seg, mseg, prefix, w_self, w_so, w_cq, w_ckv, w_co, fc_in, fc_out, ad, gain, bias):
    bf16, f32 = jnp.bfloat16, jnp.float32
    half, deep = tokens.shape
    shape = jax.ShapeDtypeStruct
    held = dict(
        wself=((4, deep, 384), bf16),
        qkv=((4, SEQ, 384), bf16),
        sctx=((SEQ, 512), bf16),
        slse=((4, 8, SEQ), f32),
        pre=((4, 2, 32, 128), bf16),
        wso_m=((512, deep), bf16),
        wso_o=((512, deep), bf16),
        wkv=((4, deep, 256), bf16),
        wq_m=((deep, 512), bf16),
        wq_o=((deep, 512), bf16),
        wco_m=((512, deep), bf16),
        wco_o=((512, deep), bf16),
        q=((SEQ, 512), bf16),
        kv=((4, MLEN, 256), bf16),
        cctx=((SEQ, 512), bf16),
        clse=((4, 8, SEQ), f32),
        resid1=((half, deep), f32),
        resid2=((half, deep), f32),
        bounds=((8, SEQ), jnp.int32),
    )
    outs = [shape(*value) for value in held.values()]
    outs += [shape((3,) + fc_in.shape, bf16), shape((3,) + fc_out.shape, bf16), shape((3,) + ad.shape, bf16)]
    scratch = [pltpu.VMEM(*value) for value in held.values()] + [
        pltpu.VMEM((SEQ, deep), bf16),
        pltpu.VMEM((MLEN, deep), bf16),
        pltpu.VMEM((half, 512), bf16),
        pltpu.VMEM((half, 512), bf16),
        pltpu.VMEM((half, 512), bf16),
        pltpu.VMEM((half, deep), f32),
        pltpu.VMEM((half, deep), bf16),
        pltpu.VMEM((128, SEQ), bf16),
        pltpu.VMEM((1, SEQ), jnp.int32),
        pltpu.VMEM((1, SEQ), jnp.int32),
        pltpu.SemaphoreType.DMA((SLOTS,)),
        pltpu.SemaphoreType.DMA((SLOTS,)),
        pltpu.SemaphoreType.DMA((LOCAL_SLOTS,)),
    ]
    anywhere = pl.BlockSpec(memory_space=pl.ANY)
    vmem = pl.BlockSpec(memory_space=pltpu.VMEM)
    results = pl.pallas_call(
        forward_kernel,
        out_shape=outs,
        in_specs=[anywhere] * 13 + [vmem] * 2,
        out_specs=[anywhere] * len(outs),
        scratch_shapes=scratch,
        compiler_params=pltpu.CompilerParams(
            collective_id=0, has_side_effects=True, vmem_limit_bytes=58 * 2**20
        ),
        name="layer_forward",
    )(tokens, memory, seg, mseg, prefix, w_self, w_so, w_cq, w_ckv, w_co, fc_in, fc_out, ad, gain, bias)
    return Held(*results)


def backward_kernel(has_prefix, first_bound, bounds_s, *refs):
    if has_prefix:
        qkv_ref, bounds, ctx_ref, dctx_ref, lse_ref, pre_ref, dqkv_ref, dpre_ref, kt_ref, dk_acc, dv_acc, dq_acc, dpre_acc = refs
        q_at = lambda rows: qkv_ref[0, rows, 0:128]
        k_at = lambda rows: qkv_ref[0, rows, 128:256]
        v_at = lambda rows: qkv_ref[0, rows, 256:384]
    else:
        q_ref, kv_ref, bounds, ctx_ref, dctx_ref, lse_ref, dq_ref, dkv_ref, kt_ref, dk_acc, dv_acc, dq_acc = refs
        q_at = lambda rows: q_ref[rows, :]
        k_at = lambda rows: kv_ref[0, rows, 0:128]
        v_at = lambda rows: kv_ref[0, rows, 128:256]
    scale = 0.125 * LOG2E
    kt_ref[...] = k_at(slice(None)).astype(jnp.float32).T.astype(jnp.bfloat16)
    dk_acc[...] = jnp.zeros_like(dk_acc)
    dv_acc[...] = jnp.zeros_like(dv_acc)
    if has_prefix:
        dpre_acc[...] = jnp.zeros_like(dpre_acc)
        kp = prefix_block(pre_ref[0, 0])
        vp = prefix_block(pre_ref[0, 1])
        kpt = kp.astype(jnp.float32).T.astype(jnp.bfloat16)

    def one(qi, _):
        q0 = pl.multiple_of(qi * QB, QB)
        span = pl.ds(q0, QB)
        q = q_at(span)
        dctx = dctx_ref[span, :]
        lo = bounds[first_bound : first_bound + 1, span]
        hi = bounds[first_bound + 1 : first_bound + 2, span]
        prod = (dctx.astype(jnp.float32) * ctx_ref[span, :].astype(jnp.float32)).T
        inner = [jnp.sum(prod[h * 64 : h * 64 + 64], axis=0, keepdims=True) for h in range(2)]
        lse = [lse_ref[0, h : h + 1, span] for h in range(2)]
        qh = [half_lanes(q, h) for h in range(2)]
        dh = [half_lanes(dctx, h) for h in range(2)]
        if has_prefix:
            sp = prefix_rows(nt(kp, q) * scale)
            rows = lambda pair: jnp.concatenate([jnp.broadcast_to(t, (64, QB)) for t in pair], axis=0)
            pp = jnp.exp2(sp - rows(lse))
            dpp = nt(vp, dctx)
            dsp = (pp * (dpp - rows(inner))).astype(jnp.bfloat16)
            dpre_acc[0] += nn(dsp, q)
            dpre_acc[1] += nn(pp.astype(jnp.bfloat16), dctx)
            dq_acc[...] = nn(kpt, dsp)
        else:
            dq_acc[...] = jnp.zeros_like(dq_acc)

        def chunk(ki, _):
            k0 = pl.multiple_of(ki * KB, KB)
            keys = pl.ds(k0, KB)
            k = k_at(keys)
            v = v_at(keys)
            pos = k0 + lax.broadcasted_iota(jnp.int32, (KB, QB), 0)
            mask = (pos >= lo) & (pos <= hi)
            ps, dss = [], []
            for h in range(2):
                s = nt(k, qh[h]) * scale
                p = jnp.exp2(jnp.where(mask, s, NEG) - lse[h])
                dp = nt(v, dh[h])
                ds = (p * (dp - inner[h])).astype(jnp.bfloat16)
                ps.append(p.astype(jnp.bfloat16))
                dss.append(ds)
                dq_acc[h * 64 : h * 64 + 64, :] += nn(kt_ref[h * 64 : h * 64 + 64, keys], ds)
            dv_acc[keys, :] += nn(ps[0], dh[0]) + nn(ps[1], dh[1])
            dk_acc[keys, :] += nn(dss[0], qh[0]) + nn(dss[1], qh[1])
            return 0

        lowest = lax.div(bounds_s[first_bound, q0], KB)
        highest = lax.div(bounds_s[first_bound + 1, q0 + QB - 1], KB) + 1
        lax.fori_loop(lowest, highest, chunk, 0)
        dq = (dq_acc[...].T * 0.125).astype(jnp.bfloat16)
        if has_prefix:
            dqkv_ref[0, span, 0:128] = dq
        else:
            dq_ref[span, :] = dq
        return 0

    lax.fori_loop(0, SEQ // QB, one, 0)
    dk = (dk_acc[...] * 0.125).astype(jnp.bfloat16)
    dv = dv_acc[...].astype(jnp.bfloat16)
    if has_prefix:
        dqkv_ref[0, :, 128:256] = dk
        dqkv_ref[0, :, 256:384] = dv
        lane = lax.broadcasted_iota(jnp.int32, (32, 128), 1)
        for i, factor in ((0, 0.125), (1, 1.0)):
            dpre_ref[0, i] = jnp.where(lane < 64, dpre_acc[i, 0:32], dpre_acc[i, 64:96]) * factor
    else:
        dkv_ref[0, :, 0:128] = dk
        dkv_ref[0, :, 128:256] = dv


def backward_call(has_prefix, arrays, bounds, ctx, dctx, lse, pre=None):
    col = pl.BlockSpec((SEQ, 128), lambda j, *_: (0, j))
    piece = lambda width: pl.BlockSpec((1, SEQ, width), lambda j, *_: (j, 0, 0))
    shape = jax.ShapeDtypeStruct
    bf16, f32 = jnp.bfloat16, jnp.float32
    if has_prefix:
        in_specs = [piece(384)]
        out_specs = [piece(384), pl.BlockSpec((1, 2, 32, 128), lambda j, *_: (j, 0, 0, 0))]
        out_shape = [shape((4, SEQ, 384), bf16), shape((4, 2, 32, 128), f32)]
    else:
        in_specs = [col, piece(256)]
        out_specs = [col, piece(256)]
        out_shape = [shape((SEQ, 512), bf16), shape((4, SEQ, 256), bf16)]
    in_specs += [
        pl.BlockSpec((8, SEQ), lambda j, *_: (0, 0)),
        col,
        col,
        pl.BlockSpec((1, 8, SEQ), lambda j, *_: (j, 0, 0)),
    ]
    args = list(arrays) + [bounds, ctx, dctx, lse]
    scratch = [
        pltpu.VMEM((128, SEQ), bf16),
        pltpu.VMEM((SEQ, 128), f32),
        pltpu.VMEM((SEQ, 128), f32),
        pltpu.VMEM((128, QB), f32),
    ]
    if has_prefix:
        in_specs.append(pl.BlockSpec((1, 2, 32, 128), lambda j, *_: (j, 0, 0, 0)))
        args.append(pre)
        scratch.append(pltpu.VMEM((2, 128, 128), f32))
    return pl.pallas_call(
        functools.partial(backward_kernel, has_prefix, 0 if has_prefix else 2),
        grid_spec=pltpu.PrefetchScalarGridSpec(
            num_scalar_prefetch=1, grid=(4,), in_specs=in_specs, out_specs=out_specs, scratch_shapes=scratch
        ),
        out_shape=out_shape,
        compiler_params=pltpu.CompilerParams(vmem_limit_bytes=40 * 2**20),
        cost_estimate=pl.CostEstimate(flops=10 * 8 * SEQ * SEQ * 64, bytes_accessed=10 * 2**20, transcendentals=8 * SEQ * SEQ),
        name="self_backward" if has_prefix else "cross_backward",
    )(bounds, *args)


HIDDEN = 512


def swap_halves(place, src, dst_there, dst_here, send, recv, local):
    moves = place.c != place.x
    away = pltpu.make_async_remote_copy(
        src_ref=src, dst_ref=dst_there, send_sem=send, recv_sem=recv, device_id=place.to_s, device_id_type=MESH
    )
    home = pltpu.make_async_copy(src, dst_here, local)

    def start():
        pl.when(moves)(away.start)
        pl.when(jnp.logical_not(moves))(home.start)

    def wait():
        pl.when(moves)(away.wait)
        pl.when(jnp.logical_not(moves))(home.wait)

    return start, wait


def feed_kernel(
    resid2, cotangent, gain, bias, wco_m, wco_o, fc_in, fin, fc_out, fout, ad, fad,
    out, grad_two, unit_sum, dctx,
    win, wout, down, up, slope, low, hidden, acc, gate, ada, branch_low, sem,
    cot, out_v, units, unit_send, unit_recv, near_send, near_recv, dctx_s, send, recv, local,
):
    place = Place()
    place.greet((place.to_x, place.to_y, place.to_d, place.to_c), True)
    c = place.c
    cot_start, cot_wait = swap_halves(place, cotangent, cot, cot, send.at[0], recv.at[0], local.at[0])
    out_start, out_wait = swap_halves(place, out_v, out, out, send.at[1], recv.at[1], local.at[1])
    cot_start()

    def there(slot, src, dst, device):
        return pltpu.make_async_remote_copy(
            src_ref=src, dst_ref=dst, send_sem=send.at[slot], recv_sem=recv.at[slot], device_id=device, device_id_type=MESH
        )

    half = resid2.shape[0]
    mine = pl.ds(pl.multiple_of(c * half, half), half)
    unit_core = there(2, unit_send, unit_recv, place.to_c)
    unit_near = [
        there(3 + i, near_send.at[i], near_recv.at[i], device) for i, device in enumerate((place.to_x, place.to_y, place.to_d))
    ]
    dctx_core = there(6, dctx_s, dctx.at[mine], place.to_c)
    bf16 = jnp.bfloat16
    per = fc_in.shape[1] // HIDDEN
    steps = 4 * per
    group = ad.shape[1]
    loads = []
    for j in range(steps):
        piece, part = divmod(j, per)
        cols = pl.ds(part * HIDDEN, HIDDEN)
        src = fc_in.at[:, cols] if piece == 0 else fin.at[piece - 1, :, cols]
        loads.append(pltpu.make_async_copy(src, win.at[j], sem.at[0, j]))
        src = fc_out.at[cols] if piece == 0 else fout.at[piece - 1, cols]
        loads.append(pltpu.make_async_copy(src, wout.at[j], sem.at[1, j]))
    ad_loads = []
    for piece in range(4):
        for i, dst in enumerate((down, up)):
            src = ad.at[i] if piece == 0 else fad.at[piece - 1, i]
            ad_loads.append(pltpu.make_async_copy(src, dst.at[pl.ds(group * piece, group)], sem.at[2, 2 * piece + i]))
    for copy in loads + ad_loads:
        copy.start()

    rows_all = resid2.shape[0]
    tiles = rows_all // TILE
    at = lambda t: pl.ds(pl.multiple_of(t * TILE, TILE), TILE)

    def begin(t, _):
        rows = at(t)
        normed = norm_forward(resid2[rows, :], gain[1:2, :], bias[1:2, :])
        hidden[rows, :] = normed
        low[rows, :] = normed.astype(bf16)
        return 0

    lax.fori_loop(0, tiles, begin, 0)
    for copy in ad_loads:
        copy.wait()
    pre = nt(low[...], down[...])
    sigma = jax.nn.sigmoid(pre)
    gate[...] = sigma * (1.0 + pre * (1.0 - sigma))
    ada[...] = (pre * sigma).astype(bf16)
    acc[...] = adapter_scale * nn(ada[...], up[...])

    def ahead(j, _):
        for i, buf in enumerate((win, wout)):
            pltpu.make_async_copy(buf.at[j], buf.at[j], sem.at[i, j]).wait()
        pre = nn(low[...], win[j])
        phi = 0.5 * (1.0 + lax.erf(pre * 0.7071067811865476))
        slope[j] = phi + pre * jnp.exp(-0.5 * pre * pre) * 0.3989422804014327
        acc[...] += nn((pre * phi).astype(bf16), wout[j])
        return 0

    lax.fori_loop(0, steps, ahead, 0)

    def middle(t, _):
        rows = at(t)
        resid = hidden[rows, :] + acc[rows, :]
        normed, inv = norm_parts(resid)
        out_v[rows, :] = (normed * gain[2:3, :] + bias[2:3, :]).astype(bf16)
        scaled = cot[rows, :].astype(jnp.float32) * gain[2:3, :]
        grad = inv * (
            scaled
            - jnp.mean(scaled, axis=-1, keepdims=True)
            - normed * jnp.mean(scaled * normed, axis=-1, keepdims=True)
        )
        acc[rows, :] = grad
        branch_low[rows, :] = grad.astype(bf16)
        return 0

    cot_wait()
    lax.fori_loop(0, tiles, middle, 0)
    out_start()
    grelu = (adapter_scale * nt(branch_low[...], up[...]) * gate[...]).astype(bf16)
    features = low.shape[1]
    some = group // 2
    for first, value in ((0, tn(grelu, low[...])), (features, adapter_scale * tn(ada[...], branch_low[...]))):
        for k in range(8):
            units[k // 2, k % 2, :, first : first + features] = value[some * k : some * (k + 1)]
    for i in range(4):
        unit_send[i] = units[i, 1 - c].astype(bf16)
    unit_core.start()
    acc[...] += nn(grelu, down[...])

    def behind(j, _):
        grad = (nt(branch_low[...], wout[j]) * slope[j]).astype(bf16)
        acc[...] += nt(grad, win[j])
        return 0

    lax.fori_loop(0, steps // 2, behind, 0)
    unit_core.wait()
    for i in range(3):
        near_send[i] = (units[i + 1, c] + unit_recv[i + 1].astype(jnp.float32)).astype(bf16)
    for copy in unit_near:
        copy.start()
    lax.fori_loop(steps // 2, steps, behind, 0)

    def finish(t, _):
        rows = at(t)
        grad = norm_backward(resid2[rows, :], gain[1:2, :], acc[rows, :])
        grad_two[rows, :] = grad
        small = grad.astype(bf16)
        low[rows, :] = small
        dctx_s[rows, :] = nt(small, wco_o[...]).astype(bf16)
        return 0

    lax.fori_loop(0, tiles, finish, 0)
    dctx_core.start()
    dctx[mine, :] = nt(low[...], wco_m[...]).astype(bf16)
    for copy in unit_near:
        copy.wait()
    total = units[0, c] + unit_recv[0].astype(jnp.float32)
    for i in range(3):
        total = total + near_recv[i].astype(jnp.float32)
    unit_sum[...] = total
    out_wait()
    dctx_core.wait()


def feed_call(resid2, cot, gain, bias, wco_m, wco_o, fc_in, fin, fc_out, fout, ad, fad):
    bf16, f32 = jnp.bfloat16, jnp.float32
    rows, deep = resid2.shape
    shape = jax.ShapeDtypeStruct
    anywhere = pl.BlockSpec(memory_space=pl.ANY)
    vmem = pl.BlockSpec(memory_space=pltpu.VMEM)
    steps = 4 * fc_in.shape[1] // HIDDEN
    units = 4 * ad.shape[1]
    some = ad.shape[1] // 2
    return pl.pallas_call(
        feed_kernel,
        out_shape=[
            shape((rows, deep), bf16),
            shape((rows, deep), f32),
            shape((some, 2 * deep), f32),
            shape((2 * rows, 512), bf16),
        ],
        in_specs=[vmem, anywhere] + [vmem] * 4 + [anywhere] * 6,
        out_specs=[anywhere] + [vmem] * 3,
        scratch_shapes=[
            pltpu.VMEM((steps, deep, HIDDEN), bf16),
            pltpu.VMEM((steps, HIDDEN, deep), bf16),
            pltpu.VMEM((units, deep), bf16),
            pltpu.VMEM((units, deep), bf16),
            pltpu.VMEM((steps, rows, HIDDEN), f32),
            pltpu.VMEM((rows, deep), bf16),
            pltpu.VMEM((rows, deep), f32),
            pltpu.VMEM((rows, deep), f32),
            pltpu.VMEM((rows, units), f32),
            pltpu.VMEM((rows, units), bf16),
            pltpu.VMEM((rows, deep), bf16),
            pltpu.SemaphoreType.DMA((3, 8)),
            pltpu.VMEM((rows, deep), bf16),
            pltpu.VMEM((rows, deep), bf16),
            pltpu.VMEM((4, 2, some, 2 * deep), f32),
            pltpu.VMEM((4, some, 2 * deep), bf16),
            pltpu.VMEM((4, some, 2 * deep), bf16),
            pltpu.VMEM((3, some, 2 * deep), bf16),
            pltpu.VMEM((3, some, 2 * deep), bf16),
            pltpu.VMEM((rows, 512), bf16),
            pltpu.SemaphoreType.DMA((7,)),
            pltpu.SemaphoreType.DMA((7,)),
            pltpu.SemaphoreType.DMA((2,)),
        ],
        compiler_params=pltpu.CompilerParams(
            collective_id=1, has_side_effects=True, vmem_limit_bytes=61 * 2**20
        ),
        name="feed_forward",
    )(resid2, cot, gain, bias, wco_m, wco_o, fc_in, fin, fc_out, fout, ad, fad)


def query_kernel(
    dq, dkv, wkv, wq_m, wq_o, grad_two, resid1, wso_m, wso_o, gain,
    grad_one, dctx, mem_sum,
    dq_o, mem_s, mem_r, dctx_s, low, send, recv,
):
    bf16 = jnp.bfloat16
    place = Place()
    place.greet((place.to_c,), False)
    c = place.c
    half = resid1.shape[0]
    mine = pl.ds(pl.multiple_of(c * half, half), half)
    others = pl.ds(pl.multiple_of((1 - c) * half, half), half)

    def there(slot, src, dst):
        return pltpu.make_async_remote_copy(
            src_ref=src, dst_ref=dst, send_sem=send.at[slot], recv_sem=recv.at[slot], device_id=place.to_c, device_id_type=MESH
        )

    dq_core = there(0, dq.at[others], dq_o)
    mem_core = there(1, mem_s, mem_r)
    dctx_core = there(2, dctx_s, dctx.at[mine])
    dq_core.start()
    tiles = half // TILE
    at = lambda t: pl.ds(pl.multiple_of(t * TILE, TILE), TILE)
    place_at = lambda first, t: pl.ds(pl.multiple_of(first * half + t * TILE, TILE), TILE)

    def memory_rows(rows):
        return sum(nt(dkv[p, rows, :], wkv[p]) for p in range(4))

    def far(t, _):
        mem_s[at(t), :] = memory_rows(place_at(1 - c, t)).astype(bf16)
        return 0

    lax.fori_loop(0, tiles, far, 0)
    mem_core.start()
    dq_core.wait()

    def one(t, _):
        rows = at(t)
        grad_in = grad_two[rows, :] + nt(dq[place_at(c, t), :], wq_m[...]) + nt(dq_o[rows, :], wq_o[...])
        grad = norm_backward(resid1[rows, :], gain[0:1, :], grad_in)
        grad_one[rows, :] = grad
        small = grad.astype(bf16)
        low[rows, :] = small
        dctx_s[rows, :] = nt(small, wso_o[...]).astype(bf16)
        return 0

    lax.fori_loop(0, tiles, one, 0)
    dctx_core.start()
    dctx[mine, :] = nt(low[...], wso_m[...]).astype(bf16)
    mem_core.wait()

    def near(t, _):
        mem_sum[at(t), :] = (memory_rows(place_at(c, t)) + mem_r[at(t), :].astype(jnp.float32)).astype(bf16)
        return 0

    lax.fori_loop(0, tiles, near, 0)
    dctx_core.wait()


def query_call(dq, dkv, wkv, wq_m, wq_o, grad_two, resid1, wso_m, wso_o, gain):
    bf16, f32 = jnp.bfloat16, jnp.float32
    half, deep = resid1.shape
    shape = jax.ShapeDtypeStruct
    vmem = pl.BlockSpec(memory_space=pltpu.VMEM)
    return pl.pallas_call(
        query_kernel,
        out_shape=[shape((half, deep), f32), shape((2 * half, 512), bf16), shape((half, deep), bf16)],
        in_specs=[vmem] * 10,
        out_specs=[vmem] * 3,
        scratch_shapes=[
            pltpu.VMEM((half, 512), bf16),
            pltpu.VMEM((half, deep), bf16),
            pltpu.VMEM((half, deep), bf16),
            pltpu.VMEM((half, 512), bf16),
            pltpu.VMEM((half, deep), bf16),
            pltpu.SemaphoreType.DMA((3,)),
            pltpu.SemaphoreType.DMA((3,)),
        ],
        compiler_params=pltpu.CompilerParams(collective_id=2, has_side_effects=True, vmem_limit_bytes=40 * 2**20),
        name="query_backward",
    )(dq, dkv, wkv, wq_m, wq_o, grad_two, resid1, wso_m, wso_o, gain)


def last_kernel(
    planes, dqkv, wself, grad_one, blocks, unit_sum,
    grad_input, prefix_grad, down_grad, up_grad,
    part_s, part_r, out_s, out_r, pre_near, pre_sum, pre_z, pre_c, unit_s, unit_z, unit_all, total, send, recv,
):
    bf16, f32 = jnp.bfloat16, jnp.float32
    place = Place()
    c, x, z = place.c, place.x, place.z
    steps = []
    step = 1
    while step < planes:
        other = z + step - 2 * step * lax.rem(lax.div(z, step), 2)
        steps.append((2 * other + c, place.head))
        step *= 2
    place.greet([place.to_x, place.to_y, place.to_d, place.to_c] + steps, True)
    moves = c != x
    half = grad_one.shape[0]
    slots = []

    def there(src, dst, device):
        slot = len(slots)
        slots.append(slot)
        return pltpu.make_async_remote_copy(
            src_ref=src, dst_ref=dst, send_sem=send.at[slot], recv_sem=recv.at[slot], device_id=device, device_id_type=MESH
        )

    tiles = half // TILE
    at = lambda t: pl.ds(t * TILE, TILE)
    place_at = lambda first, t: pl.ds(pl.multiple_of(first * half + t * TILE, TILE), TILE)
    pre_copies = [
        there(blocks.at[i + 1], pre_near.at[i], device) for i, device in enumerate((place.to_x, place.to_y, place.to_d))
    ]
    pre_steps = [there(pre_sum.at[i], pre_z.at[i], device) for i, device in enumerate(steps)]
    pre_core = there(pre_sum.at[len(steps)], pre_c, place.to_c)
    unit_steps = [there(unit_s.at[i], unit_z.at[i], device) for i, device in enumerate(steps)]
    unit_core = there(unit_s.at[len(steps)], unit_z.at[len(steps)], place.to_c)
    part_copies = [there(part_s.at[at(t)], part_r.at[at(t)], place.to_c) for t in range(tiles)]
    out_copies = [there(out_s.at[at(t)], out_r.at[at(t)], place.to_s) for t in range(tiles)]
    for copy in pre_copies:
        copy.start()
    unit_s[0] = unit_sum[...].astype(bf16)
    unit_steps[0].start()

    def input_rows(rows):
        return sum(nt(dqkv[p, rows, :], wself[p]) for p in range(4))

    part_s[at(0), :] = input_rows(place_at(1 - c, 0)).astype(bf16)
    part_copies[0].start()
    for copy in pre_copies:
        copy.wait()
    pre_sum[0] = blocks[0] + pre_near[0] + pre_near[1] + pre_near[2]
    pre_steps[0].start()
    for t in range(1, tiles):
        part_s[at(t), :] = input_rows(place_at(1 - c, t)).astype(bf16)
        part_copies[t].start()

    def advance(i):
        pre_steps[i].wait()
        pre_sum[i + 1] = pre_sum[i] + pre_z[i]
        if i + 1 < len(steps):
            pre_steps[i + 1].start()
        else:
            pre_core.start()
        unit_steps[i].wait()
        unit_s[i + 1] = (unit_s[i].astype(f32) + unit_z[i].astype(f32)).astype(bf16)
        if i + 1 < len(steps):
            unit_steps[i + 1].start()
        else:
            unit_core.start()

    for t in range(tiles):
        part_copies[t].wait()
        total[at(t), :] = input_rows(place_at(c, t)) + part_r[at(t), :].astype(f32) + grad_one[at(t), :]
        out_s[at(t), :] = total[at(t), :].astype(bf16)
        pl.when(moves)(out_copies[t].start)
        if t < len(steps):
            advance(t)
    for i in range(tiles, len(steps)):
        advance(i)
    pre_core.wait()
    unit_core.wait()
    my_lanes = pl.ds(pl.multiple_of(c * 128, 128), 128)
    other_lanes = pl.ds(pl.multiple_of((1 - c) * 128, 128), 128)
    prefix_grad[:, :, my_lanes] = pre_sum[len(steps)]
    prefix_grad[:, :, other_lanes] = pre_c[...]
    some = unit_sum.shape[0]
    unit_all[pl.ds(pl.multiple_of(c * some, some), some), :] = unit_s[len(steps)].astype(f32)
    unit_all[pl.ds(pl.multiple_of((1 - c) * some, some), some), :] = unit_z[len(steps)].astype(f32)
    features = grad_one.shape[1]
    down_grad[...] = unit_all[:, 0:features].T
    up_grad[...] = unit_all[:, features : 2 * features]

    @pl.when(moves)
    def _():
        for copy in out_copies:
            copy.wait()
        grad_input[...] = out_r[...].astype(f32)

    @pl.when(jnp.logical_not(moves))
    def _():
        grad_input[...] = total[...]


def last_call(planes, dqkv, wself, grad_one, blocks, unit_sum):
    bf16, f32 = jnp.bfloat16, jnp.float32
    half, deep = grad_one.shape
    some = unit_sum.shape[0]
    count = planes.bit_length() - 1
    shape = jax.ShapeDtypeStruct
    vmem = pl.BlockSpec(memory_space=pltpu.VMEM)
    return pl.pallas_call(
        functools.partial(last_kernel, planes),
        out_shape=[
            shape((half, deep), f32),
            shape((2, 32, 256), f32),
            shape((deep, 2 * some), f32),
            shape((2 * some, deep), f32),
        ],
        in_specs=[vmem] * 5,
        out_specs=[vmem] * 4,
        scratch_shapes=[
            pltpu.VMEM((half, deep), bf16),
            pltpu.VMEM((half, deep), bf16),
            pltpu.VMEM((half, deep), bf16),
            pltpu.VMEM((half, deep), bf16),
            pltpu.VMEM((3, 2, 32, 128), f32),
            pltpu.VMEM((count + 1, 2, 32, 128), f32),
            pltpu.VMEM((count, 2, 32, 128), f32),
            pltpu.VMEM((2, 32, 128), f32),
            pltpu.VMEM((count + 1, some, 2 * deep), bf16),
            pltpu.VMEM((count + 1, some, 2 * deep), bf16),
            pltpu.VMEM((2 * some, 2 * deep), f32),
            pltpu.VMEM((half, deep), f32),
            pltpu.SemaphoreType.DMA((3 + 2 * count + 2 + 2 * (half // TILE),)),
            pltpu.SemaphoreType.DMA((3 + 2 * count + 2 + 2 * (half // TILE),)),
        ],
        compiler_params=pltpu.CompilerParams(collective_id=3, has_side_effects=True, vmem_limit_bytes=40 * 2**20),
        name="last_sums",
    )(dqkv, wself, grad_one, blocks, unit_sum)


AXES = ("rows", "heads")


def fast_fits(mesh):
    rows, heads = mesh.shape["rows"], mesh.shape["heads"]
    return heads == 4 and rows % 4 == 0 and (rows & (rows - 1)) == 0


def pairs_of(rows, move):
    def number(z, c, y, x):
        return (z * 2 + c) * 4 + y * 2 + x

    found = []
    for z in range(rows // 2):
        for c in range(2):
            for y in range(2):
                for x in range(2):
                    found.append((number(z, c, y, x), number(*move(z, c, y, x))))
    return found


def swap_in(rows, value):
    def swapped(z, c, y, x):
        return (z, x, y, c)

    crossing = [pair for pair in pairs_of(rows, swapped) if pair[0] != pair[1]]
    stays = lax.axis_index("rows") % 2 == lax.axis_index("heads") % 2
    return jnp.where(stays, value, lax.ppermute(value, AXES, crossing))


def fast_body(
    rows,
    tokens,
    memory,
    cotangent,
    dec_seg,
    mem_seg,
    w_self,
    w_self_out,
    w_cross_q,
    w_cross_kv,
    w_cross_out,
    fc_in,
    fc_out,
    ad_down,
    ad_up,
    prefix,
    ln_gain,
    ln_bias,
):
    count = prefix.shape[1]
    ad = jnp.stack([ad_down.T, ad_up])
    held = forward_call(
        tokens,
        memory,
        dec_seg.reshape(2, 1, SEQ),
        mem_seg.reshape(2, 1, MLEN),
        jnp.pad(prefix, ((0, 0), (0, 32 - count), (0, 0))),
        w_self,
        w_self_out,
        w_cross_q,
        w_cross_kv,
        w_cross_out,
        fc_in,
        fc_out,
        ad,
        ln_gain,
        ln_bias,
    )
    output, grad_two, unit_sum, cross_dctx = feed_call(
        held.resid2, cotangent, ln_gain, ln_bias, held.wco_m, held.wco_o,
        fc_in, held.fin, fc_out, held.fout, ad, held.fad,
    )
    cross_dq, cross_dkv = backward_call(
        False, (held.q, held.kv), held.bounds, held.cctx, cross_dctx, held.clse
    )
    grad_one, self_dctx, memory_sum = query_call(
        cross_dq, cross_dkv, held.wkv, held.wq_m, held.wq_o, grad_two, held.resid1, held.wso_m, held.wso_o, ln_gain
    )
    grad_memory = swap_in(rows, memory_sum).astype(jnp.float32)
    self_dqkv, prefix_blocks = backward_call(
        True, (held.qkv,), held.bounds, held.sctx, self_dctx, held.slse, held.pre
    )
    grad_input, prefix_grad, down_grad, up_grad = last_call(
        rows // 2, self_dqkv, held.wself, grad_one, prefix_blocks, unit_sum
    )
    return (output, grad_input, grad_memory, prefix_grad[:, :count], down_grad, up_grad)


def solution(mesh):
    in_specs = (
        P(("rows", "heads"), None),
        P(("rows", "heads"), None),
        P(("rows", "heads"), None),
        P("rows"),
        P("rows"),
        P(None, None, "heads"),
        P("heads", None),
        P(None, "heads"),
        P(None, None, "heads"),
        P("heads", None),
        P(None, "heads"),
        P("heads", None),
        P(None, "heads"),
        P("heads", None),
        P(None, None, "heads"),
        P(),
        P(),
    )
    out_specs = (
        P(("rows", "heads"), None),
        P(("rows", "heads"), None),
        P(("rows", "heads"), None),
        P(None, None, "heads"),
        P(None, "heads"),
        P("heads", None),
    )
    chosen = functools.partial(fast_body, mesh.shape["rows"]) if fast_fits(mesh) else body
    return jax.shard_map(chosen, mesh=mesh, in_specs=in_specs, out_specs=out_specs, check_vma=False)
```

```python
import functools
import math
import typing

import jax
import jax.numpy as jnp
from jax import lax
from jax.experimental import pallas as pl
from jax.experimental.pallas import tpu as pltpu
from jax.sharding import PartitionSpec as P

HD = 64
SEQ = 1024
MLEN = 1024


epsilon = 1e-05
adapter_scale = 4.0
masked_score = -1e30


def dot_right(left, right):
    return lax.dot_general(
        left, right, (((1,), (1,)), ((), ())), preferred_element_type=jnp.float32
    )


def dot_left(left, right):
    return lax.dot_general(
        left, right, (((0,), (0,)), ((), ())), preferred_element_type=jnp.float32
    )


def norm_parts(resid):
    average = jnp.mean(resid, axis=-1, keepdims=True)
    centered = resid - average
    inv_scale = lax.rsqrt(jnp.mean(centered * centered, axis=-1, keepdims=True) + epsilon)
    return (centered * inv_scale, inv_scale)


def norm_forward(resid, gain, shift):
    normed, inv_scale = norm_parts(resid)
    return normed * gain + shift


def norm_backward(resid, gain, grad_out):
    normed, inv_scale = norm_parts(resid)
    scaled = grad_out * gain
    return inv_scale * (
        scaled
        - jnp.mean(scaled, axis=-1, keepdims=True)
        - normed * jnp.mean(scaled * normed, axis=-1, keepdims=True)
    )


def gelu_slope(pre_gelu):
    return (
        0.5 * (1.0 + lax.erf(pre_gelu * 0.7071067811865476))
        + pre_gelu * jnp.exp(-0.5 * pre_gelu * pre_gelu) * 0.3989422804014327
    )


def silu_slope(pre_relu):
    sigma = jax.nn.sigmoid(pre_relu)
    return sigma * (1.0 + pre_relu * (1.0 - sigma))


def to_heads(arrays, heads_here):
    return arrays.reshape(arrays.shape[0], arrays.shape[1], heads_here, HD).transpose(0, 2, 1, 3)


def from_heads(arrays):
    return arrays.transpose(0, 2, 1, 3).reshape(
        arrays.shape[0] * arrays.shape[2], arrays.shape[1] * arrays.shape[3]
    )


def join_blocks(stacked):
    moved = jnp.moveaxis(stacked, 0, 1)
    return moved.reshape((moved.shape[0], moved.shape[1] * moved.shape[2]) + moved.shape[3:])


def block_mask(row_segs, key_segs, offset, causal):
    allowed = row_segs[:, None] == key_segs[None, :]
    if causal:
        row_places = offset + lax.iota(jnp.int32, row_segs.shape[0])
        key_places = lax.iota(jnp.int32, key_segs.shape[0])
        allowed = allowed & (key_places[None, :] <= row_places[:, None])
    return allowed


def block_scores(queries, key_rows, allowed, prefix_keys):
    qk_scale = HD ** (-0.5)
    token_scores = (
        jnp.einsum("hqe,hke->hqk", queries, key_rows, preferred_element_type=jnp.float32) * qk_scale
    )
    token_scores = jnp.where(allowed[None], token_scores, masked_score)
    if prefix_keys is None:
        return (token_scores, None)
    prefix_scores = (
        jnp.einsum("hqe,hpe->hqp", queries, prefix_keys, preferred_element_type=jnp.float32)
        * qk_scale
    )
    return (token_scores, prefix_scores)


def attend_block(queries, key_rows, value_rows, allowed, prefix_keys, prefix_values):
    token_scores, prefix_scores = block_scores(queries, key_rows, allowed, prefix_keys)
    row_max = jnp.max(token_scores, axis=-1, keepdims=True)
    if prefix_scores is not None:
        row_max = jnp.maximum(row_max, jnp.max(prefix_scores, axis=-1, keepdims=True))
    token_weights = jnp.exp(token_scores - row_max)
    row_total = jnp.sum(token_weights, axis=-1, keepdims=True)
    if prefix_scores is not None:
        prefix_weights = jnp.exp(prefix_scores - row_max)
        row_total = row_total + jnp.sum(prefix_weights, axis=-1, keepdims=True)
    context = jnp.einsum(
        "hqk,hke->hqe",
        (token_weights / row_total).astype(jnp.bfloat16),
        value_rows,
        preferred_element_type=jnp.float32,
    )
    if prefix_scores is not None:
        context = context + jnp.einsum(
            "hqp,hpe->hqe",
            (prefix_weights / row_total).astype(jnp.bfloat16),
            prefix_values,
            preferred_element_type=jnp.float32,
        )
    return (context.astype(jnp.bfloat16), row_max + jnp.log(row_total))


def attend_back(
    queries, key_rows, value_rows, allowed, prefix_keys, prefix_values, log_total, context_grad
):
    qk_scale = HD ** (-0.5)
    token_scores, prefix_scores = block_scores(queries, key_rows, allowed, prefix_keys)
    token_probs = jnp.exp(token_scores - log_total)
    token_dprob = jnp.einsum(
        "hqe,hke->hqk", context_grad, value_rows, preferred_element_type=jnp.float32
    )
    inner = jnp.sum(token_probs * token_dprob, axis=-1, keepdims=True)
    if prefix_scores is not None:
        prefix_probs = jnp.exp(prefix_scores - log_total)
        prefix_dprob = jnp.einsum(
            "hqe,hpe->hqp", context_grad, prefix_values, preferred_element_type=jnp.float32
        )
        inner = inner + jnp.sum(prefix_probs * prefix_dprob, axis=-1, keepdims=True)
    token_dscore = (token_probs * (token_dprob - inner)).astype(jnp.bfloat16)
    query_grad = jnp.einsum(
        "hqk,hke->hqe", token_dscore, key_rows, preferred_element_type=jnp.float32
    )
    key_grad = (
        jnp.einsum("hqk,hqe->hke", token_dscore, queries, preferred_element_type=jnp.float32)
        * qk_scale
    )
    value_grad = jnp.einsum(
        "hqk,hqe->hke",
        token_probs.astype(jnp.bfloat16),
        context_grad,
        preferred_element_type=jnp.float32,
    )
    if prefix_scores is None:
        return (query_grad * qk_scale, (key_grad, value_grad))
    prefix_dscore = (prefix_probs * (prefix_dprob - inner)).astype(jnp.bfloat16)
    query_grad = query_grad + jnp.einsum(
        "hqp,hpe->hqe", prefix_dscore, prefix_keys, preferred_element_type=jnp.float32
    )
    prefix_key_grad = (
        jnp.einsum("hqp,hqe->hpe", prefix_dscore, queries, preferred_element_type=jnp.float32)
        * qk_scale
    )
    prefix_value_grad = jnp.einsum(
        "hqp,hqe->hpe",
        prefix_probs.astype(jnp.bfloat16),
        context_grad,
        preferred_element_type=jnp.float32,
    )
    return (query_grad * qk_scale, (key_grad, value_grad, prefix_key_grad, prefix_value_grad))


def sequence_forward(
    queries, key_rows, value_rows, row_segs, key_segs, prefix_keys, prefix_values, causal
):
    seq_width = queries.shape[1]
    block_rows = min(512, seq_width)

    def one_block(block_index):
        offset = block_index * block_rows
        allowed = block_mask(
            lax.dynamic_slice_in_dim(row_segs, offset, block_rows, 0), key_segs, offset, causal
        )
        query_part = lax.dynamic_slice_in_dim(queries, offset, block_rows, 1)
        return attend_block(query_part, key_rows, value_rows, allowed, prefix_keys, prefix_values)

    context, log_total = lax.map(one_block, jnp.arange(seq_width // block_rows, dtype=jnp.int32))
    return (join_blocks(context), join_blocks(log_total))


def sequence_backward(
    queries,
    key_rows,
    value_rows,
    row_segs,
    key_segs,
    prefix_keys,
    prefix_values,
    causal,
    log_total,
    context_grad,
):
    seq_width = queries.shape[1]
    block_rows = min(512, seq_width)
    key_zero = jnp.zeros(key_rows.shape, jnp.float32)
    initial = (key_zero, key_zero)
    if prefix_keys is not None:
        prefix_zero = jnp.zeros(prefix_keys.shape, jnp.float32)
        initial = initial + (prefix_zero, prefix_zero)

    def one_block(running, block_index):
        offset = block_index * block_rows
        allowed = block_mask(
            lax.dynamic_slice_in_dim(row_segs, offset, block_rows, 0), key_segs, offset, causal
        )
        query_part = lax.dynamic_slice_in_dim(queries, offset, block_rows, 1)
        total_part = lax.dynamic_slice_in_dim(log_total, offset, block_rows, 1)
        grad_part = lax.dynamic_slice_in_dim(context_grad, offset, block_rows, 1)
        query_grad, block_grads = attend_back(
            query_part,
            key_rows,
            value_rows,
            allowed,
            prefix_keys,
            prefix_values,
            total_part,
            grad_part,
        )
        return (tuple((summed + added for summed, added in zip(running, block_grads))), query_grad)

    running, query_grad = lax.scan(
        one_block, initial, jnp.arange(seq_width // block_rows, dtype=jnp.int32)
    )
    outputs = (
        join_blocks(query_grad).astype(jnp.bfloat16),
        running[0].astype(jnp.bfloat16),
        running[1].astype(jnp.bfloat16),
    )
    return outputs + running[2:]


def gather_rows(row_share):
    return lax.all_gather(row_share, "heads", axis=0, tiled=True)


def gather_grads(row_share):
    return lax.all_gather(row_share, "heads", axis=0, tiled=True)


def sum_rows(partial_value):
    return lax.psum_scatter(partial_value, "heads", scatter_dimension=0, tiled=True)


def sum_grads(partial_value):
    return lax.psum_scatter(partial_value, "heads", scatter_dimension=0, tiled=True)


def body(
    tokens,
    memory,
    cotangent,
    dec_seg,
    mem_seg,
    w_self,
    w_self_out,
    w_cross_q,
    w_cross_kv,
    w_cross_out,
    fc_in,
    fc_out,
    ad_down,
    ad_up,
    prefix,
    ln_gain,
    ln_bias,
):
    local_width = w_self.shape[2]
    heads_here = local_width // HD
    seg_dec = dec_seg.reshape(-1, SEQ)
    seg_mem = mem_seg.reshape(-1, MLEN)
    seq_count = seg_dec.shape[0]
    prefix_heads = to_heads(prefix, heads_here)
    prefix_keys = prefix_heads[0]
    prefix_values = prefix_heads[1]
    gathered_x = gather_rows(tokens)
    self_proj = jnp.einsum(
        "td,cdn->ctn", gathered_x, w_self, preferred_element_type=jnp.float32
    ).astype(jnp.bfloat16)
    self_proj = self_proj.reshape(3, seq_count, SEQ, local_width)
    self_queries = to_heads(self_proj[0], heads_here)
    self_keys = to_heads(self_proj[1], heads_here)
    self_values = to_heads(self_proj[2], heads_here)

    def self_forward(packed):
        return sequence_forward(
            packed[0], packed[1], packed[2], packed[3], packed[3], prefix_keys, prefix_values, True
        )

    self_context, self_total = lax.map(
        self_forward, (self_queries, self_keys, self_values, seg_dec)
    )
    attn_partial = jnp.dot(from_heads(self_context), w_self_out, preferred_element_type=jnp.float32)
    resid_one = tokens.astype(jnp.float32) + sum_rows(attn_partial)
    hidden_one = norm_forward(resid_one, ln_gain[0], ln_bias[0])
    gathered_one = gather_rows(hidden_one.astype(jnp.bfloat16))
    gathered_mem = lax.all_gather(memory, "heads", axis=0, tiled=True)
    cross_rows = jnp.dot(gathered_one, w_cross_q, preferred_element_type=jnp.float32).astype(
        jnp.bfloat16
    )
    cross_proj = jnp.einsum(
        "td,cdn->ctn", gathered_mem, w_cross_kv, preferred_element_type=jnp.float32
    ).astype(jnp.bfloat16)
    cross_queries = to_heads(cross_rows.reshape(seq_count, SEQ, local_width), heads_here)
    cross_proj = cross_proj.reshape(2, seq_count, MLEN, local_width)
    cross_keys = to_heads(cross_proj[0], heads_here)
    cross_values = to_heads(cross_proj[1], heads_here)

    def cross_forward(packed):
        return sequence_forward(
            packed[0], packed[1], packed[2], packed[3], packed[4], None, None, False
        )

    cross_context, cross_total = lax.map(
        cross_forward, (cross_queries, cross_keys, cross_values, seg_dec, seg_mem)
    )
    cross_partial = jnp.dot(
        from_heads(cross_context), w_cross_out, preferred_element_type=jnp.float32
    )
    resid_two = hidden_one + sum_rows(cross_partial)
    hidden_two = norm_forward(resid_two, ln_gain[1], ln_bias[1])
    hidden_low = hidden_two.astype(jnp.bfloat16)
    full_in, full_out, full_down, full_up = (fc_in, fc_out, ad_down, ad_up)
    ffn_rows = gather_rows(hidden_low)
    pre_gelu = jnp.dot(ffn_rows, full_in, preferred_element_type=jnp.float32)
    activated = jax.nn.gelu(pre_gelu, approximate=False).astype(jnp.bfloat16)
    pre_relu = jnp.dot(ffn_rows, full_down, preferred_element_type=jnp.float32)
    adapted = (pre_relu * jax.nn.sigmoid(pre_relu)).astype(jnp.bfloat16)
    branch = jnp.dot(
        activated, full_out, preferred_element_type=jnp.float32
    ) + adapter_scale * jnp.dot(adapted, full_up, preferred_element_type=jnp.float32)
    resid_three = hidden_two + sum_rows(branch)
    output = norm_forward(resid_three, ln_gain[2], ln_bias[2]).astype(jnp.bfloat16)
    grad_three = norm_backward(resid_three, ln_gain[2], cotangent.astype(jnp.float32))
    grad_branch = grad_three.astype(jnp.bfloat16)
    branch_rows = gather_grads(grad_branch)
    grad_gelu = (dot_right(branch_rows, full_out) * gelu_slope(pre_gelu)).astype(jnp.bfloat16)
    grad_relu = (adapter_scale * dot_right(branch_rows, full_up) * silu_slope(pre_relu)).astype(
        jnp.bfloat16
    )
    up_grad = adapter_scale * dot_left(adapted, branch_rows)
    down_grad = dot_left(ffn_rows, grad_relu)
    hidden_partial = dot_right(grad_gelu, full_in) + dot_right(grad_relu, full_down)
    grad_two_in = grad_three + sum_grads(hidden_partial)
    down_grad, up_grad = (
        lax.psum(down_grad.astype(jnp.bfloat16), "rows").astype(jnp.float32),
        lax.psum(up_grad.astype(jnp.bfloat16), "rows").astype(jnp.float32),
    )
    grad_two = norm_backward(resid_two, ln_gain[1], grad_two_in)
    cross_out_rows = gather_grads(grad_two.astype(jnp.bfloat16))
    cross_dctx = dot_right(cross_out_rows, w_cross_out).astype(jnp.bfloat16)
    cross_dctx = to_heads(cross_dctx.reshape(seq_count, SEQ, local_width), heads_here)

    def cross_back(packed):
        return sequence_backward(
            packed[0],
            packed[1],
            packed[2],
            packed[3],
            packed[4],
            None,
            None,
            False,
            packed[5],
            packed[6],
        )

    cross_qgrad, cross_kgrad, cross_vgrad = lax.map(
        cross_back,
        (cross_queries, cross_keys, cross_values, seg_dec, seg_mem, cross_total, cross_dctx),
    )
    memory_kv = jnp.stack([from_heads(cross_kgrad), from_heads(cross_vgrad)])
    one_partial = dot_right(from_heads(cross_qgrad), w_cross_q)
    grad_one_in = grad_two + sum_grads(one_partial)
    memory_partial = jnp.einsum(
        "ctn,cdn->td", memory_kv, w_cross_kv, preferred_element_type=jnp.float32
    )
    grad_memory = lax.psum_scatter(
        memory_partial.astype(jnp.bfloat16), "heads", scatter_dimension=0, tiled=True
    ).astype(jnp.float32)
    grad_one = norm_backward(resid_one, ln_gain[0], grad_one_in)
    attn_rows = gather_grads(grad_one.astype(jnp.bfloat16))
    self_dctx = dot_right(attn_rows, w_self_out).astype(jnp.bfloat16)
    self_dctx = to_heads(self_dctx.reshape(seq_count, SEQ, local_width), heads_here)

    def self_back(running, packed):
        query_grad, key_grad, value_grad, pkey_grad, pvalue_grad = sequence_backward(
            packed[0],
            packed[1],
            packed[2],
            packed[3],
            packed[3],
            prefix_keys,
            prefix_values,
            True,
            packed[4],
            packed[5],
        )
        return (
            (running[0] + pkey_grad, running[1] + pvalue_grad),
            (query_grad, key_grad, value_grad),
        )

    zero_grad = jnp.zeros(prefix_keys.shape, jnp.float32)
    prefix_sums, self_grads = lax.scan(
        self_back,
        (zero_grad, zero_grad),
        (self_queries, self_keys, self_values, seg_dec, self_total, self_dctx),
    )
    self_stack = jnp.stack(
        [from_heads(self_grads[0]), from_heads(self_grads[1]), from_heads(self_grads[2])]
    )
    input_partial = jnp.einsum(
        "ctn,cdn->td", self_stack, w_self, preferred_element_type=jnp.float32
    )
    grad_input = grad_one + sum_grads(input_partial)
    prefix_grad = (
        jnp.stack([prefix_sums[0], prefix_sums[1]])
        .transpose(0, 2, 1, 3)
        .reshape(2, prefix.shape[1], local_width)
    )
    prefix_grad = lax.psum(prefix_grad, "rows")
    return (output, grad_input, grad_memory, prefix_grad, down_grad, up_grad)


QB = 256
KB = 256
LOG2E = math.log2(math.e)
NEG = -1e30


def nt(a, b):
    return lax.dot_general(a, b, (((1,), (1,)), ((), ())), preferred_element_type=jnp.float32)


def nn(a, b):
    return lax.dot_general(a, b, (((1,), (0,)), ((), ())), preferred_element_type=jnp.float32)


def tn(a, b):
    return lax.dot_general(a, b, (((0,), (0,)), ((), ())), preferred_element_type=jnp.float32)


def half_lanes(v, h):
    lane = lax.broadcasted_iota(jnp.int32, v.shape, 1)
    keep = (lane < 64) if h == 0 else (lane >= 64)
    return jnp.where(keep, v, jnp.zeros_like(v))


def prefix_rows(scores):
    row = lax.broadcasted_iota(jnp.int32, scores.shape, 0)
    return jnp.where(lax.rem(row, 64) < 30, scores, NEG)


MESH = pl.DeviceIdType.MESH
TILE = 256

TOK, TOK_C, MEM, MEM_C = 112, 113, 114, 115
SELF_PIECE, OUT_ONE, CROSS_Q, CROSS_PIECE, OUT_TWO = 128, 132, 133, 134, 138
SLOTS, LOCAL_SLOTS = 128, 48
GROUPS = ((1, 0), (1, 0), (1, 0), (0, 1), (1, 1), (0, 0), (1, 0))
SCHEDULE = (16, 17, 65, 64, 20, 33, 32, 68, 97, 112, 35, 67, 36, 19, 114, 113, 18, 100, 49, 128, 0, 115, 21, 1, 22, 96, 3, 2, 4, 129, 48, 34, 98, 5, 130, 80, 37, 131, 81, 99, 38, 132, 133, 101, 134, 66, 50, 82, 135, 69, 102, 136, 70, 137, 86, 138)


class Place:
    def __init__(self):
        self.row, self.head = lax.axis_index("rows"), lax.axis_index("heads")
        self.c, self.z = lax.rem(self.row, 2), lax.div(self.row, 2)
        self.x, self.y = lax.rem(self.head, 2), lax.div(self.head, 2)
        self.odd = lax.rem(self.z, 2)
        c, x, y, z = self.c, self.x, self.y, self.z
        self.to_x = (self.row, 2 * y + 1 - x)
        self.to_y = (self.row, 2 * (1 - y) + x)
        self.to_d = (self.row, 2 * (1 - y) + 1 - x)
        self.to_z = (2 * (z + 1 - 2 * self.odd) + c, self.head)
        self.to_c = (2 * z + 1 - c, self.head)
        self.to_s = (2 * z + x, 2 * y + c)

    def greet(self, devices, swaps):
        barrier = pltpu.get_barrier_semaphore()
        for device in devices:
            pl.semaphore_signal(barrier, inc=1, device_id=device, device_id_type=MESH)
        count = len(devices)
        if swaps:
            moves = self.c != self.x

            @pl.when(moves)
            def _():
                pl.semaphore_signal(barrier, inc=1, device_id=self.to_s, device_id_type=MESH)

            count = count + moves.astype(jnp.int32)
        pl.semaphore_wait(barrier, count)


def prefix_block(rows):
    nothing = jnp.zeros_like(rows)
    return jnp.concatenate([half_lanes(rows, 0), nothing, half_lanes(rows, 1), nothing], axis=0)


def attend_tile(q, k, vt, mask, kp, vpt):
    scale = 0.125 * LOG2E
    rows = q.shape[0]
    if kp is not None:
        sp = prefix_rows(nt(kp, q) * scale)
    outs, tops, sums = [], [], []
    for h in range(2):
        s = jnp.where(mask, nt(k, half_lanes(q, h)) * scale, NEG)
        m = jnp.max(s, axis=0, keepdims=True)
        if kp is not None:
            m = jnp.maximum(m, jnp.max(sp[h * 64 : h * 64 + 32], axis=0, keepdims=True))
        e = jnp.exp2(s - m)
        outs.append(nn(vt[h * 64 : h * 64 + 64], e.astype(jnp.bfloat16)))
        sums.append(jnp.sum(e, axis=0, keepdims=True))
        tops.append(m)
    if kp is not None:
        mm = jnp.concatenate([jnp.broadcast_to(t, (64, rows)) for t in tops], axis=0)
        ep = jnp.exp2(sp - mm)
        sums = [sums[h] + jnp.sum(ep[h * 64 : h * 64 + 32], axis=0, keepdims=True) for h in range(2)]
        extra = nn(vpt, ep.astype(jnp.bfloat16))
        outs = [outs[h] + extra[h * 64 : h * 64 + 64] for h in range(2)]
    both = jnp.concatenate([outs[h] * (1.0 / sums[h]) for h in range(2)], axis=0)
    return both.T.astype(jnp.bfloat16), [tops[h] + jnp.log2(sums[h]) for h in range(2)]


def forward_kernel(
    tokens, memory, seg, mseg, prefix, w_self, w_so, w_cq, w_ckv, w_co, fc_in, fc_out, ad, gain, bias,
    o_wself, o_qkv, o_sctx, o_slse, o_pre, o_wso_m, o_wso_o, o_wkv, o_wq_m, o_wq_o, o_wco_m, o_wco_o,
    o_q, o_kv, o_cctx, o_clse, o_resid1, o_resid2, o_bounds, fin, fout, fad,
    wself, qkv, sctx, slse, pre, wso_m, wso_o, wkv, wq_m, wq_o, wco_m, wco_o,
    q_all, kv, cctx, clse, resid1, resid2, bounds, tok, mem, sctx_o, cctx_o, q_send, hidden, low_one, vt, seg_v, mseg_v,
    send, recv, local,
):
    place_of = Place()
    c, x, y, odd = place_of.c, place_of.x, place_of.y, place_of.odd
    to_x, to_y, to_z, to_c, to_s = place_of.to_x, place_of.to_y, place_of.to_z, place_of.to_c, place_of.to_s
    stays, moves = c == x, c != x
    place_of.greet((to_x, to_y, to_z, to_c), True)

    taken = []

    def there(src, dst, device):
        slot = len(taken)
        taken.append(slot)
        return pltpu.make_async_remote_copy(
            src_ref=src, dst_ref=dst, send_sem=send.at[slot], recv_sem=recv.at[slot], device_id=device, device_id_type=MESH
        )

    used = []

    def here(src, dst):
        slot = len(used)
        used.append(slot)
        return pltpu.make_async_copy(src, dst, local.at[slot])

    deep = w_self.shape[1]
    half = tok.shape[0] // 2
    step = lambda start, size, unit: pl.ds(pl.multiple_of(start, unit), size)
    mine = step(c * half, half, half)
    others = step((1 - c) * half, half, half)
    lanes = step(c * 128, 128, 128)
    other_lanes = step((1 - c) * 128, 128, 128)
    rows_c, rows_o = lanes, other_lanes
    foreign = pl.ds(128, 384)
    hid = fc_in.shape[1]
    units = ad.shape[1]
    pending = []

    def swap_of(src, target):
        away = there(src, target.at[step(x * half, half, half)], to_s)
        home = here(src, target.at[mine])
        back = there(target.at[mine], target.at[mine], to_c)

        def start():
            pl.when(moves)(away.start)
            pl.when(stays)(home.start)

        def wait():
            pl.when(moves)(away.wait)
            pl.when(stays)(home.wait)

        return start, wait, back

    def seg_of(src, dst):
        home = here(src.at[y], dst)
        away = there(src.at[y], dst, to_c)

        def start():
            pl.when(stays)(home.start)
            pl.when(stays)(away.start)

        def wait():
            pl.when(stays)(home.wait)
            pl.when(stays)(away.wait_send)
            pl.when(moves)(away.wait_recv)

        return start, wait

    def deep_rows(shared):
        return step(odd * (deep // 2), deep // 2, deep // 2) if shared else pl.ds(0, deep)

    def thin_rows(piece, shared):
        return step(128 * piece + odd * 64, 64, 64) if shared else pl.ds(128 * piece, 128)

    def thin_own(shared):
        return step(128 * c + odd * 64, 64, 64) if shared else rows_c

    def span(size, shared):
        return step(c * (size // 2) + odd * (size // 4), size // 4, size // 4) if shared else step(c * (size // 2), size // 2, size // 2)

    lane_of = lambda i: pl.ds(128 * i, 128)

    def group_a(shared):
        rows = deep_rows(shared)
        first = lambda piece: [(w_self.at[i, rows, lanes], wself.at[piece, rows, lane_of(i)]) for i in range(3)] + [
            (prefix.at[:, :, lanes], pre.at[piece])
        ]
        return first, lambda piece: [wself.at[piece, rows], pre.at[piece]], 1, []

    def group_thin(src, dst_m, dst_o, shared):
        first = lambda piece: [(src.at[thin_own(shared)], dst_m.at[thin_rows(piece, shared)])]
        return first, lambda piece: [dst_m.at[thin_rows(piece, shared)]], 1, [(dst_m.at[foreign], dst_o.at[foreign])]

    def group_q(shared):
        rows = deep_rows(shared)
        first = lambda piece: [(w_cq.at[rows, lanes], wq_m.at[rows, lane_of(piece)])]
        return first, lambda piece: [wq_m.at[rows, lane_of(piece)]], 1, [(wq_m.at[:, foreign], wq_o.at[:, foreign])]

    def group_v(shared):
        rows = deep_rows(shared)
        first = lambda piece: [(w_ckv.at[i, rows, lanes], wkv.at[piece, rows, lane_of(i)]) for i in range(2)]
        return first, lambda piece: [wkv.at[piece, rows]], 1, []

    def group_i(shared):
        cols = span(hid, shared)
        both = fin.at[:, :, span(hid, False)]
        first = lambda piece: [(fc_in.at[:, cols], fin.at[piece - 1, :, cols])]
        return first, lambda piece: [fin.at[piece - 1, :, cols]], 1, [(both, both)]

    def group_o(shared):
        rows, some = span(hid, shared), span(units, shared)
        both, both_units = fout.at[:, span(hid, False)], fad.at[:, :, span(units, False)]
        first = lambda piece: [(fc_out.at[rows], fout.at[piece - 1, rows]), (ad.at[:, some], fad.at[piece - 1, :, some])]
        hold = lambda piece: [fout.at[piece - 1, rows], fad.at[piece - 1, :, some]]
        return first, hold, 2, [(both, both), (both_units, both_units)]

    makers = [
        group_a,
        functools.partial(group_thin, w_so, wso_m, wso_o),
        group_q,
        group_v,
        functools.partial(group_thin, w_co, wco_m, wco_o),
        group_i,
        group_o,
    ]
    copies, needs = {}, {}
    for index, (make, (shared, through_x)) in enumerate(zip(makers, GROUPS)):
        first, hold, shared_count, cross = make(bool(shared))
        base = 16 * index
        copies[base] = [there(src, dst, to_x) for src, dst in first(1)]
        copies[base + 1] = [there(src, dst, to_y) for src, dst in first(2)]
        near, device = (2, to_x) if through_x else (1, to_y)
        copies[base + 2] = [there(src, dst, device) for src, dst in zip(hold(near), hold(3))]
        needs[base], needs[base + 1], needs[base + 2] = [], [], [base + near - 1]
        arrived = [base, base + 1, base + 2]
        if shared:
            for i in range(3):
                copies[base + 3 + i] = [there(ref, ref, to_z) for ref in hold(i + 1)[:shared_count]]
                needs[base + 3 + i] = [base + i]
                arrived.append(base + 3 + i)
        if cross:
            copies[base + 6] = [there(src, dst, to_c) for src, dst in cross]
            needs[base + 6] = arrived
    tok_start, tok_wait, tok_back = swap_of(tokens, tok)
    mem_start, mem_wait, mem_back = swap_of(memory, mem)
    copies[TOK_C], copies[MEM_C] = [tok_back], [mem_back]
    needs[TOK_C], needs[MEM_C] = [TOK], [MEM]
    seg_start, seg_wait = seg_of(seg, seg_v)
    mseg_start, mseg_wait = seg_of(mseg, mseg_v)
    sctx_out = [there(sctx.at[others, lane_of(i)], sctx_o.at[:, lane_of(i)], to_c) for i in range(4)]
    cctx_out = [there(cctx.at[others, lane_of(i)], cctx_o.at[:, lane_of(i)], to_c) for i in range(4)]
    q_out = there(q_send, q_all.at[mine], to_c)

    landed = set()

    def wait_for(op):
        if op in landed:
            return
        landed.add(op)
        if op == TOK:
            tok_wait()
        elif op == MEM:
            mem_wait()
        elif op in copies:
            for copy in copies[op]:
                copy.wait_recv()

    def launch(op):
        if op == TOK:
            tok_start()
        elif op == MEM:
            mem_start()
        else:
            for need in needs[op]:
                wait_for(need)
            for copy in copies[op]:
                copy.start()
                pending.append(copy)

    saves = []

    def keep(src, dst):
        copy = here(src, dst)
        copy.start()
        saves.append(copy)

    own_a = [here(w_self.at[i, :, lanes], wself.at[0, :, lane_of(i)]) for i in range(3)]
    own_a.append(here(prefix.at[:, :, lanes], pre.at[0]))
    own_b = [
        here(w_so.at[rows_c], wso_m.at[lane_of(0)]),
        here(w_so.at[rows_o], wso_o.at[lane_of(0)]),
        here(w_co.at[rows_c], wco_m.at[lane_of(0)]),
        here(w_co.at[rows_o], wco_o.at[lane_of(0)]),
        here(w_cq.at[:, lanes], wq_m.at[:, lane_of(0)]),
        here(w_cq.at[:, other_lanes], wq_o.at[:, lane_of(0)]),
        here(w_ckv.at[0, :, lanes], wkv.at[0, :, lane_of(0)]),
        here(w_ckv.at[1, :, lanes], wkv.at[0, :, lane_of(1)]),
    ]

    def bounds_of():
        seg_wait()
        mseg_wait()
        dec, men = seg_v[...], mseg_v[...]

        def below(values, d):
            return jnp.sum((values < d).astype(jnp.int32), axis=1, keepdims=True)

        def pick(counts):
            out = jnp.broadcast_to(counts[0], dec.shape)
            for d in range(1, 4):
                out = jnp.where(dec == d, counts[d], out)
            return out

        zero = jnp.zeros((1, 1), jnp.int32)
        full = jnp.full((1, 1), MLEN, jnp.int32)
        self_lo = pick([zero] + [below(dec, d) for d in range(1, 4)])
        mem_counts = [zero] + [below(men, d) for d in range(1, 4)] + [full]
        bounds[...] = jnp.concatenate(
            [self_lo, lax.broadcasted_iota(jnp.int32, dec.shape, 1), pick(mem_counts[:4]), pick(mem_counts[1:]) - 1]
            + [jnp.zeros_like(dec)] * 4,
            axis=0,
        )
        keep(bounds, o_bounds)

    def weight_needs(base, piece):
        found = [base + piece - 1, base + 2 + piece]
        return [op for op in found if op in copies]

    def project(dst, p, source, weight):
        def rows_of(t, _):
            rows = step(t * TILE, TILE, TILE)
            dst[p, rows, :] = nn(source[rows, :], weight[p]).astype(jnp.bfloat16)
            return 0

        lax.fori_loop(0, SEQ // TILE, rows_of, 0)

    def self_piece(p):
        project(qkv, p, tok, wself)
        vt[...] = qkv[p, :, 256:384].astype(jnp.float32).T.astype(jnp.bfloat16)
        kp = prefix_block(pre[p, 0])
        vpt = prefix_block(pre[p, 1]).astype(jnp.float32).T.astype(jnp.bfloat16)
        place = step(p * 128, 128, 128)
        for qi in range(SEQ // QB):
            width = (qi + 1) * QB
            rows = slice(qi * QB, (qi + 1) * QB)
            pos = lax.broadcasted_iota(jnp.int32, (width, QB), 0)
            mask = (pos >= bounds[0:1, rows]) & (pos <= bounds[1:2, rows])
            out, lse = attend_tile(qkv[p, rows, 0:128], qkv[p, 0:width, 128:256], vt[:, 0:width], mask, kp, vpt)
            sctx[rows, place] = out
            for h in range(2):
                slse[p, h : h + 1, rows] = lse[h]

    def cross_piece(p):
        project(kv, p, mem, wkv)
        vt[...] = kv[p, :, 128:256].astype(jnp.float32).T.astype(jnp.bfloat16)
        place = step(p * 128, 128, 128)

        def block(qi, _):
            rows = step(qi * QB, QB, QB)
            pos = lax.broadcasted_iota(jnp.int32, (MLEN, QB), 0)
            mask = (pos >= bounds[2:3, rows]) & (pos <= bounds[3:4, rows])
            out, lse = attend_tile(q_all[rows, place], kv[p, :, 0:128], vt[...], mask, None, None)
            cctx[rows, place] = out
            for h in range(2):
                clse[p, h : h + 1, rows] = lse[h]
            return 0

        lax.fori_loop(0, SEQ // QB, block, 0)

    def with_out(t, resid_before, ctx_m, ctx_o, w_m, w_o):
        rows = step(t * TILE, TILE, TILE)
        rows_all = step(c * half + t * TILE, TILE, TILE)
        return resid_before + nn(ctx_m[rows_all, :], w_m[...]) + nn(ctx_o[rows, :], w_o[...])

    def out_one(t, _):
        rows = step(t * TILE, TILE, TILE)
        rows_all = step(c * half + t * TILE, TILE, TILE)
        resid = with_out(t, tok[rows_all, :].astype(jnp.float32), sctx, sctx_o, wso_m, wso_o)
        resid1[rows, :] = resid
        normed = norm_forward(resid, gain[0:1, :], bias[0:1, :])
        hidden[rows, :] = normed
        low_one[rows, :] = normed.astype(jnp.bfloat16)
        return 0

    def out_two(t, _):
        rows = step(t * TILE, TILE, TILE)
        resid2[rows, :] = with_out(t, hidden[rows, :], cctx, cctx_o, wco_m, wco_o)
        return 0

    def q_rows(t, _):
        rows = step(t * TILE, TILE, TILE)
        rows_all = step(c * half + t * TILE, TILE, TILE)
        q_send[rows, :] = nn(low_one[rows, :], wq_o[...]).astype(jnp.bfloat16)
        q_all[rows_all, :] = nn(low_one[rows, :], wq_m[...]).astype(jnp.bfloat16)
        return 0

    def split_at(order, first, count):
        places = [order.index(first + k) for k in range(count)]
        starts = [0] + [place + 1 for place in places]
        return [order[a:b] for a, b in zip(starts, places)], order[places[-1] + 1 :]

    def pieces_loop(segments, ready, work, sends):
        def body(p, _):
            for k, segment in enumerate(segments):

                @pl.when(p == k)
                def _():
                    for op in segment:
                        launch(op)
                    ready(k)

            work(p)
            for k, copy in enumerate(sends):
                pl.when(p == k)(copy.start)
            return 0

        lax.fori_loop(0, len(segments), body, 0)
        pending.extend(sends)

    for copy in own_a[:3]:
        copy.start()
    own_a[3].start()
    seg_start()
    mseg_start()
    segments, rest = split_at(list(SCHEDULE), SELF_PIECE, 4)
    for op in segments[0]:
        launch(op)
    for copy in own_b:
        copy.start()
    bounds_of()
    for copy in own_a:
        copy.wait()
    segments[0] = []

    def self_ready(k):
        if k == 0:
            wait_for(TOK_C)
        else:
            for op in weight_needs(0, k):
                wait_for(op)

    pieces_loop(segments, self_ready, self_piece, sctx_out)
    for src, dst in ((qkv, o_qkv), (wself, o_wself), (sctx, o_sctx), (slse, o_slse), (pre, o_pre)):
        keep(src, dst)
    for copy in own_b:
        copy.wait()
    before, rest = split_at(rest, OUT_ONE, 1)
    for op in before[0]:
        launch(op)
    for copy in sctx_out:
        copy.wait_recv()
    wait_for(16 + 6)
    lax.fori_loop(0, half // TILE, out_one, 0)
    for src, dst in ((resid1, o_resid1), (wso_m, o_wso_m), (wso_o, o_wso_o)):
        keep(src, dst)
    before, rest = split_at(rest, CROSS_Q, 1)
    for op in before[0]:
        launch(op)
    wait_for(32 + 6)
    lax.fori_loop(0, half // TILE, q_rows, 0)
    q_out.start()
    pending.append(q_out)
    for src, dst in ((wq_m, o_wq_m), (wq_o, o_wq_o)):
        keep(src, dst)
    segments, rest = split_at(rest, CROSS_PIECE, 4)

    def cross_ready(k):
        if k == 0:
            wait_for(MEM_C)
            q_out.wait_recv()
        else:
            for op in weight_needs(48, k):
                wait_for(op)

    pieces_loop(segments, cross_ready, cross_piece, cctx_out)
    for src, dst in ((q_all, o_q), (kv, o_kv), (wkv, o_wkv), (cctx, o_cctx), (clse, o_clse)):
        keep(src, dst)
    before, rest = split_at(rest, OUT_TWO, 1)
    for op in before[0]:
        launch(op)
    for copy in cctx_out:
        copy.wait_recv()
    wait_for(64 + 6)
    lax.fori_loop(0, half // TILE, out_two, 0)
    for src, dst in ((resid2, o_resid2), (wco_m, o_wco_m), (wco_o, o_wco_o)):
        keep(src, dst)
    for op in rest:
        launch(op)
    for op in list(copies):
        wait_for(op)
    for copy in pending:
        copy.wait_send()
    for copy in saves:
        copy.wait()


class Held(typing.NamedTuple):
    wself: jax.Array
    qkv: jax.Array
    sctx: jax.Array
    slse: jax.Array
    pre: jax.Array
    wso_m: jax.Array
    wso_o: jax.Array
    wkv: jax.Array
    wq_m: jax.Array
    wq_o: jax.Array
    wco_m: jax.Array
    wco_o: jax.Array
    q: jax.Array
    kv: jax.Array
    cctx: jax.Array
    clse: jax.Array
    resid1: jax.Array
    resid2: jax.Array
    bounds: jax.Array
    fin: jax.Array
    fout: jax.Array
    fad: jax.Array


def forward_call(tokens, memory, seg, mseg, prefix, w_self, w_so, w_cq, w_ckv, w_co, fc_in, fc_out, ad, gain, bias):
    bf16, f32 = jnp.bfloat16, jnp.float32
    half, deep = tokens.shape
    shape = jax.ShapeDtypeStruct
    held = dict(
        wself=((4, deep, 384), bf16),
        qkv=((4, SEQ, 384), bf16),
        sctx=((SEQ, 512), bf16),
        slse=((4, 8, SEQ), f32),
        pre=((4, 2, 32, 128), bf16),
        wso_m=((512, deep), bf16),
        wso_o=((512, deep), bf16),
        wkv=((4, deep, 256), bf16),
        wq_m=((deep, 512), bf16),
        wq_o=((deep, 512), bf16),
        wco_m=((512, deep), bf16),
        wco_o=((512, deep), bf16),
        q=((SEQ, 512), bf16),
        kv=((4, MLEN, 256), bf16),
        cctx=((SEQ, 512), bf16),
        clse=((4, 8, SEQ), f32),
        resid1=((half, deep), f32),
        resid2=((half, deep), f32),
        bounds=((8, SEQ), jnp.int32),
    )
    outs = [shape(*value) for value in held.values()]
    outs += [shape((3,) + fc_in.shape, bf16), shape((3,) + fc_out.shape, bf16), shape((3,) + ad.shape, bf16)]
    scratch = [pltpu.VMEM(*value) for value in held.values()] + [
        pltpu.VMEM((SEQ, deep), bf16),
        pltpu.VMEM((MLEN, deep), bf16),
        pltpu.VMEM((half, 512), bf16),
        pltpu.VMEM((half, 512), bf16),
        pltpu.VMEM((half, 512), bf16),
        pltpu.VMEM((half, deep), f32),
        pltpu.VMEM((half, deep), bf16),
        pltpu.VMEM((128, SEQ), bf16),
        pltpu.VMEM((1, SEQ), jnp.int32),
        pltpu.VMEM((1, SEQ), jnp.int32),
        pltpu.SemaphoreType.DMA((SLOTS,)),
        pltpu.SemaphoreType.DMA((SLOTS,)),
        pltpu.SemaphoreType.DMA((LOCAL_SLOTS,)),
    ]
    anywhere = pl.BlockSpec(memory_space=pl.ANY)
    vmem = pl.BlockSpec(memory_space=pltpu.VMEM)
    results = pl.pallas_call(
        forward_kernel,
        out_shape=outs,
        in_specs=[anywhere] * 13 + [vmem] * 2,
        out_specs=[anywhere] * len(outs),
        scratch_shapes=scratch,
        compiler_params=pltpu.CompilerParams(
            collective_id=0, has_side_effects=True, vmem_limit_bytes=58 * 2**20
        ),
        name="layer_forward",
    )(tokens, memory, seg, mseg, prefix, w_self, w_so, w_cq, w_ckv, w_co, fc_in, fc_out, ad, gain, bias)
    return Held(*results)


TOGETHER = 4


def backward_kernel(has_prefix, first_bound, bounds_s, *refs):
    if has_prefix:
        qkv_ref, bounds, ctx_ref, dctx_ref, lse_ref, pre_ref, dqkv_ref, dpre_ref, dk_acc, dv_acc, dq_acc, dpre_acc = refs
        q_at = lambda g, rows: qkv_ref[g, rows, 0:128]
        k_at = lambda g, rows: qkv_ref[g, rows, 128:256]
        v_at = lambda g, rows: qkv_ref[g, rows, 256:384]
    else:
        q_ref, kv_ref, bounds, ctx_ref, dctx_ref, lse_ref, dq_ref, dkv_ref, dk_acc, dv_acc, dq_acc = refs
        q_at = lambda g, rows: q_ref[rows, 128 * g : 128 * g + 128]
        k_at = lambda g, rows: kv_ref[g, rows, 0:128]
        v_at = lambda g, rows: kv_ref[g, rows, 128:256]
    scale = 0.125 * LOG2E
    dk_acc[...] = jnp.zeros_like(dk_acc)
    dv_acc[...] = jnp.zeros_like(dv_acc)
    kps, vps = [], []
    for g in range(TOGETHER):
        if has_prefix:
            kps.append(prefix_block(pre_ref[g, 0]))
            vps.append(prefix_block(pre_ref[g, 1]))
    if has_prefix:
        dpre_acc[...] = jnp.zeros_like(dpre_acc)

    def one(qi, _):
        q0 = pl.multiple_of(qi * QB, QB)
        span = pl.ds(q0, QB)
        lo = bounds[first_bound : first_bound + 1, span]
        hi = bounds[first_bound + 1 : first_bound + 2, span]
        inner, lse, qh, dh = [], [], [], []
        for g in range(TOGETHER):
            q = q_at(g, span)
            dctx = dctx_ref[span, 128 * g : 128 * g + 128]
            ctx = ctx_ref[span, 128 * g : 128 * g + 128]
            prod = (dctx.astype(jnp.float32) * ctx.astype(jnp.float32)).T
            inner.append([jnp.sum(prod[h * 64 : h * 64 + 64], axis=0, keepdims=True) for h in range(2)])
            lse.append([lse_ref[g, h : h + 1, span] for h in range(2)])
            qh.append([half_lanes(q, h) for h in range(2)])
            dh.append([half_lanes(dctx, h) for h in range(2)])
            if has_prefix:
                sp = prefix_rows(nt(kps[g], q) * scale)
                rows = lambda pair: jnp.concatenate([jnp.broadcast_to(t, (64, QB)) for t in pair], axis=0)
                pp = jnp.exp2(sp - rows(lse[g]))
                dpp = nt(vps[g], dctx)
                dsp = (pp * (dpp - rows(inner[g]))).astype(jnp.bfloat16)
                dpre_acc[g, 0] += nn(dsp, q)
                dpre_acc[g, 1] += nn(pp.astype(jnp.bfloat16), dctx)
                dq_acc[g] = tn(dsp, kps[g])
            else:
                dq_acc[g] = jnp.zeros((QB, 128), jnp.float32)

        def chunk(ki, _):
            k0 = pl.multiple_of(ki * KB, KB)
            keys = pl.ds(k0, KB)
            pos = k0 + lax.broadcasted_iota(jnp.int32, (KB, QB), 0)
            mask = (pos >= lo) & (pos <= hi)
            for g in range(TOGETHER):
                k = k_at(g, keys)
                v = v_at(g, keys)
                ps, dss = [], []
                for h in range(2):
                    s = nt(k, qh[g][h]) * scale
                    p = jnp.exp2(jnp.where(mask, s, NEG) - lse[g][h])
                    dp = nt(v, dh[g][h])
                    ds = (p * (dp - inner[g][h])).astype(jnp.bfloat16)
                    ps.append(p.astype(jnp.bfloat16))
                    dss.append(ds)
                dv_acc[g, keys, :] += nn(jnp.concatenate(ps, axis=1), jnp.concatenate(dh[g], axis=0))
                dq_acc[g] += tn(jnp.concatenate(dss, axis=0), jnp.concatenate([half_lanes(k, 0), half_lanes(k, 1)], axis=0))
                dk_acc[g, keys, :] += nn(jnp.concatenate(dss, axis=1), jnp.concatenate(qh[g], axis=0))
            return 0

        lowest = lax.div(bounds_s[first_bound, q0], KB)
        highest = lax.div(bounds_s[first_bound + 1, q0 + QB - 1], KB) + 1
        lax.fori_loop(lowest, highest, chunk, 0)
        for g in range(TOGETHER):
            dq = (dq_acc[g] * 0.125).astype(jnp.bfloat16)
            if has_prefix:
                dqkv_ref[g, span, 0:128] = dq
            else:
                dq_ref[span, 128 * g : 128 * g + 128] = dq
        return 0

    lax.fori_loop(0, SEQ // QB, one, 0)
    for g in range(TOGETHER):
        dk = (dk_acc[g] * 0.125).astype(jnp.bfloat16)
        dv = dv_acc[g].astype(jnp.bfloat16)
        if has_prefix:
            dqkv_ref[g, :, 128:256] = dk
            dqkv_ref[g, :, 256:384] = dv
            lane = lax.broadcasted_iota(jnp.int32, (32, 128), 1)
            for i, factor in ((0, 0.125), (1, 1.0)):
                dpre_ref[g, i] = jnp.where(lane < 64, dpre_acc[g, i, 0:32], dpre_acc[g, i, 64:96]) * factor
        else:
            dkv_ref[g, :, 0:128] = dk
            dkv_ref[g, :, 128:256] = dv


def backward_call(has_prefix, arrays, bounds, ctx, dctx, lse, pre=None):
    col = pl.BlockSpec((SEQ, 128 * TOGETHER), lambda j, *_: (0, j))
    piece = lambda width: pl.BlockSpec((TOGETHER, SEQ, width), lambda j, *_: (j, 0, 0))
    shape = jax.ShapeDtypeStruct
    bf16, f32 = jnp.bfloat16, jnp.float32
    pre_spec = pl.BlockSpec((TOGETHER, 2, 32, 128), lambda j, *_: (j, 0, 0, 0))
    if has_prefix:
        in_specs = [piece(384)]
        out_specs = [piece(384), pre_spec]
        out_shape = [shape((4, SEQ, 384), bf16), shape((4, 2, 32, 128), f32)]
    else:
        in_specs = [col, piece(256)]
        out_specs = [col, piece(256)]
        out_shape = [shape((SEQ, 512), bf16), shape((4, SEQ, 256), bf16)]
    in_specs += [
        pl.BlockSpec((8, SEQ), lambda j, *_: (0, 0)),
        col,
        col,
        pl.BlockSpec((TOGETHER, 8, SEQ), lambda j, *_: (j, 0, 0)),
    ]
    args = list(arrays) + [bounds, ctx, dctx, lse]
    scratch = [
        pltpu.VMEM((TOGETHER, SEQ, 128), f32),
        pltpu.VMEM((TOGETHER, SEQ, 128), f32),
        pltpu.VMEM((TOGETHER, QB, 128), f32),
    ]
    if has_prefix:
        in_specs.append(pre_spec)
        args.append(pre)
        scratch.append(pltpu.VMEM((TOGETHER, 2, 128, 128), f32))
    return pl.pallas_call(
        functools.partial(backward_kernel, has_prefix, 0 if has_prefix else 2),
        grid_spec=pltpu.PrefetchScalarGridSpec(
            num_scalar_prefetch=1, grid=(4 // TOGETHER,), in_specs=in_specs, out_specs=out_specs, scratch_shapes=scratch
        ),
        out_shape=out_shape,
        compiler_params=pltpu.CompilerParams(vmem_limit_bytes=60 * 2**20),
        cost_estimate=pl.CostEstimate(flops=10 * 8 * SEQ * SEQ * 64, bytes_accessed=10 * 2**20, transcendentals=8 * SEQ * SEQ),
        name="self_backward" if has_prefix else "cross_backward",
    )(bounds, *args)


HIDDEN = 512


def swap_halves(place, src, dst_there, dst_here, send, recv, local):
    moves = place.c != place.x
    away = pltpu.make_async_remote_copy(
        src_ref=src, dst_ref=dst_there, send_sem=send, recv_sem=recv, device_id=place.to_s, device_id_type=MESH
    )
    home = pltpu.make_async_copy(src, dst_here, local)

    def start():
        pl.when(moves)(away.start)
        pl.when(jnp.logical_not(moves))(home.start)

    def wait():
        pl.when(moves)(away.wait)
        pl.when(jnp.logical_not(moves))(home.wait)

    return start, wait


def feed_kernel(
    resid2, cotangent, gain, bias, wco_m, wco_o, fc_in, fin, fc_out, fout, ad, fad,
    out, grad_two, unit_sum, dctx,
    win, wout, down, up, slope, low, hidden, acc, gate, ada, branch_low, sem,
    cot, out_v, units, unit_send, unit_recv, near_send, near_recv, dctx_s, send, recv, local,
):
    place = Place()
    place.greet((place.to_x, place.to_y, place.to_d, place.to_c), True)
    c = place.c
    cot_start, cot_wait = swap_halves(place, cotangent, cot, cot, send.at[0], recv.at[0], local.at[0])
    out_start, out_wait = swap_halves(place, out_v, out, out, send.at[1], recv.at[1], local.at[1])
    cot_start()

    def there(slot, src, dst, device):
        return pltpu.make_async_remote_copy(
            src_ref=src, dst_ref=dst, send_sem=send.at[slot], recv_sem=recv.at[slot], device_id=device, device_id_type=MESH
        )

    half = resid2.shape[0]
    mine = pl.ds(pl.multiple_of(c * half, half), half)
    unit_core = there(2, unit_send, unit_recv, place.to_c)
    unit_near = [
        there(3 + i, near_send.at[i], near_recv.at[i], device) for i, device in enumerate((place.to_x, place.to_y, place.to_d))
    ]
    dctx_core = there(6, dctx_s, dctx.at[mine], place.to_c)
    bf16 = jnp.bfloat16
    per = fc_in.shape[1] // HIDDEN
    steps = 4 * per
    group = ad.shape[1]
    loads = []
    for j in range(steps):
        piece, part = divmod(j, per)
        cols = pl.ds(part * HIDDEN, HIDDEN)
        src = fc_in.at[:, cols] if piece == 0 else fin.at[piece - 1, :, cols]
        loads.append(pltpu.make_async_copy(src, win.at[j], sem.at[0, j]))
        src = fc_out.at[cols] if piece == 0 else fout.at[piece - 1, cols]
        loads.append(pltpu.make_async_copy(src, wout.at[j], sem.at[1, j]))
    ad_loads = []
    for piece in range(4):
        for i, dst in enumerate((down, up)):
            src = ad.at[i] if piece == 0 else fad.at[piece - 1, i]
            ad_loads.append(pltpu.make_async_copy(src, dst.at[pl.ds(group * piece, group)], sem.at[2, 2 * piece + i]))
    for copy in loads + ad_loads:
        copy.start()

    rows_all = resid2.shape[0]
    tiles = rows_all // TILE
    at = lambda t: pl.ds(pl.multiple_of(t * TILE, TILE), TILE)

    def begin(t, _):
        rows = at(t)
        normed = norm_forward(resid2[rows, :], gain[1:2, :], bias[1:2, :])
        hidden[rows, :] = normed
        low[rows, :] = normed.astype(bf16)
        return 0

    lax.fori_loop(0, tiles, begin, 0)
    for copy in ad_loads:
        copy.wait()
    pre = nt(low[...], down[...])
    sigma = jax.nn.sigmoid(pre)
    gate[...] = sigma * (1.0 + pre * (1.0 - sigma))
    ada[...] = (pre * sigma).astype(bf16)
    acc[...] = adapter_scale * nn(ada[...], up[...])

    def ahead(j, _):
        for i, buf in enumerate((win, wout)):
            pltpu.make_async_copy(buf.at[j], buf.at[j], sem.at[i, j]).wait()
        pre = nn(low[...], win[j])
        phi = 0.5 * (1.0 + lax.erf(pre * 0.7071067811865476))
        slope[j] = phi + pre * jnp.exp(-0.5 * pre * pre) * 0.3989422804014327
        acc[...] += nn((pre * phi).astype(bf16), wout[j])
        return 0

    lax.fori_loop(0, steps, ahead, 0)

    def middle(t, _):
        rows = at(t)
        resid = hidden[rows, :] + acc[rows, :]
        normed, inv = norm_parts(resid)
        out_v[rows, :] = (normed * gain[2:3, :] + bias[2:3, :]).astype(bf16)
        scaled = cot[rows, :].astype(jnp.float32) * gain[2:3, :]
        grad = inv * (
            scaled
            - jnp.mean(scaled, axis=-1, keepdims=True)
            - normed * jnp.mean(scaled * normed, axis=-1, keepdims=True)
        )
        acc[rows, :] = grad
        branch_low[rows, :] = grad.astype(bf16)
        return 0

    cot_wait()
    lax.fori_loop(0, tiles, middle, 0)
    out_start()
    grelu = (adapter_scale * nt(branch_low[...], up[...]) * gate[...]).astype(bf16)
    features = low.shape[1]
    some = group // 2
    for first, value in ((0, tn(grelu, low[...])), (features, adapter_scale * tn(ada[...], branch_low[...]))):
        for k in range(8):
            units[k // 2, k % 2, :, first : first + features] = value[some * k : some * (k + 1)]
    for i in range(4):
        unit_send[i] = units[i, 1 - c].astype(bf16)
    unit_core.start()
    acc[...] += nn(grelu, down[...])

    def behind(j, _):
        grad = (nt(branch_low[...], wout[j]) * slope[j]).astype(bf16)
        acc[...] += nt(grad, win[j])
        return 0

    lax.fori_loop(0, steps // 2, behind, 0)
    unit_core.wait()
    for i in range(3):
        near_send[i] = (units[i + 1, c] + unit_recv[i + 1].astype(jnp.float32)).astype(bf16)
    for copy in unit_near:
        copy.start()
    lax.fori_loop(steps // 2, steps, behind, 0)

    def finish(t, _):
        rows = at(t)
        grad = norm_backward(resid2[rows, :], gain[1:2, :], acc[rows, :])
        grad_two[rows, :] = grad
        small = grad.astype(bf16)
        low[rows, :] = small
        dctx_s[rows, :] = nt(small, wco_o[...]).astype(bf16)
        return 0

    lax.fori_loop(0, tiles, finish, 0)
    dctx_core.start()
    dctx[mine, :] = nt(low[...], wco_m[...]).astype(bf16)
    for copy in unit_near:
        copy.wait()
    total = units[0, c] + unit_recv[0].astype(jnp.float32)
    for i in range(3):
        total = total + near_recv[i].astype(jnp.float32)
    unit_sum[...] = total
    out_wait()
    dctx_core.wait()


def feed_call(resid2, cot, gain, bias, wco_m, wco_o, fc_in, fin, fc_out, fout, ad, fad):
    bf16, f32 = jnp.bfloat16, jnp.float32
    rows, deep = resid2.shape
    shape = jax.ShapeDtypeStruct
    anywhere = pl.BlockSpec(memory_space=pl.ANY)
    vmem = pl.BlockSpec(memory_space=pltpu.VMEM)
    steps = 4 * fc_in.shape[1] // HIDDEN
    units = 4 * ad.shape[1]
    some = ad.shape[1] // 2
    return pl.pallas_call(
        feed_kernel,
        out_shape=[
            shape((rows, deep), bf16),
            shape((rows, deep), f32),
            shape((some, 2 * deep), f32),
            shape((2 * rows, 512), bf16),
        ],
        in_specs=[vmem, anywhere] + [vmem] * 4 + [anywhere] * 6,
        out_specs=[anywhere] + [vmem] * 3,
        scratch_shapes=[
            pltpu.VMEM((steps, deep, HIDDEN), bf16),
            pltpu.VMEM((steps, HIDDEN, deep), bf16),
            pltpu.VMEM((units, deep), bf16),
            pltpu.VMEM((units, deep), bf16),
            pltpu.VMEM((steps, rows, HIDDEN), f32),
            pltpu.VMEM((rows, deep), bf16),
            pltpu.VMEM((rows, deep), f32),
            pltpu.VMEM((rows, deep), f32),
            pltpu.VMEM((rows, units), f32),
            pltpu.VMEM((rows, units), bf16),
            pltpu.VMEM((rows, deep), bf16),
            pltpu.SemaphoreType.DMA((3, 8)),
            pltpu.VMEM((rows, deep), bf16),
            pltpu.VMEM((rows, deep), bf16),
            pltpu.VMEM((4, 2, some, 2 * deep), f32),
            pltpu.VMEM((4, some, 2 * deep), bf16),
            pltpu.VMEM((4, some, 2 * deep), bf16),
            pltpu.VMEM((3, some, 2 * deep), bf16),
            pltpu.VMEM((3, some, 2 * deep), bf16),
            pltpu.VMEM((rows, 512), bf16),
            pltpu.SemaphoreType.DMA((7,)),
            pltpu.SemaphoreType.DMA((7,)),
            pltpu.SemaphoreType.DMA((2,)),
        ],
        compiler_params=pltpu.CompilerParams(
            collective_id=1, has_side_effects=True, vmem_limit_bytes=61 * 2**20
        ),
        name="feed_forward",
    )(resid2, cot, gain, bias, wco_m, wco_o, fc_in, fin, fc_out, fout, ad, fad)


def query_kernel(
    dq, dkv, wkv, wq_m, wq_o, grad_two, resid1, wso_m, wso_o, gain,
    grad_one, dctx, mem_sum,
    dq_o, mem_s, mem_r, dctx_s, low, send, recv,
):
    bf16 = jnp.bfloat16
    place = Place()
    place.greet((place.to_c,), False)
    c = place.c
    half = resid1.shape[0]
    mine = pl.ds(pl.multiple_of(c * half, half), half)
    others = pl.ds(pl.multiple_of((1 - c) * half, half), half)

    def there(slot, src, dst):
        return pltpu.make_async_remote_copy(
            src_ref=src, dst_ref=dst, send_sem=send.at[slot], recv_sem=recv.at[slot], device_id=place.to_c, device_id_type=MESH
        )

    dq_core = there(0, dq.at[others], dq_o)
    mem_core = there(1, mem_s, mem_r)
    dctx_core = there(2, dctx_s, dctx.at[mine])
    dq_core.start()
    tiles = half // TILE
    at = lambda t: pl.ds(pl.multiple_of(t * TILE, TILE), TILE)
    place_at = lambda first, t: pl.ds(pl.multiple_of(first * half + t * TILE, TILE), TILE)

    def memory_rows(rows):
        return sum(nt(dkv[p, rows, :], wkv[p]) for p in range(4))

    def far(t, _):
        mem_s[at(t), :] = memory_rows(place_at(1 - c, t)).astype(bf16)
        return 0

    lax.fori_loop(0, tiles, far, 0)
    mem_core.start()
    dq_core.wait()

    def one(t, _):
        rows = at(t)
        grad_in = grad_two[rows, :] + nt(dq[place_at(c, t), :], wq_m[...]) + nt(dq_o[rows, :], wq_o[...])
        grad = norm_backward(resid1[rows, :], gain[0:1, :], grad_in)
        grad_one[rows, :] = grad
        small = grad.astype(bf16)
        low[rows, :] = small
        dctx_s[rows, :] = nt(small, wso_o[...]).astype(bf16)
        return 0

    lax.fori_loop(0, tiles, one, 0)
    dctx_core.start()
    dctx[mine, :] = nt(low[...], wso_m[...]).astype(bf16)
    mem_core.wait()

    def near(t, _):
        mem_sum[at(t), :] = (memory_rows(place_at(c, t)) + mem_r[at(t), :].astype(jnp.float32)).astype(bf16)
        return 0

    lax.fori_loop(0, tiles, near, 0)
    dctx_core.wait()


def query_call(dq, dkv, wkv, wq_m, wq_o, grad_two, resid1, wso_m, wso_o, gain):
    bf16, f32 = jnp.bfloat16, jnp.float32
    half, deep = resid1.shape
    shape = jax.ShapeDtypeStruct
    vmem = pl.BlockSpec(memory_space=pltpu.VMEM)
    return pl.pallas_call(
        query_kernel,
        out_shape=[shape((half, deep), f32), shape((2 * half, 512), bf16), shape((half, deep), bf16)],
        in_specs=[vmem] * 10,
        out_specs=[vmem] * 3,
        scratch_shapes=[
            pltpu.VMEM((half, 512), bf16),
            pltpu.VMEM((half, deep), bf16),
            pltpu.VMEM((half, deep), bf16),
            pltpu.VMEM((half, 512), bf16),
            pltpu.VMEM((half, deep), bf16),
            pltpu.SemaphoreType.DMA((3,)),
            pltpu.SemaphoreType.DMA((3,)),
        ],
        compiler_params=pltpu.CompilerParams(collective_id=2, has_side_effects=True, vmem_limit_bytes=40 * 2**20),
        name="query_backward",
    )(dq, dkv, wkv, wq_m, wq_o, grad_two, resid1, wso_m, wso_o, gain)


def last_kernel(
    planes, dqkv, wself, grad_one, blocks, unit_sum,
    grad_input, prefix_grad, down_grad, up_grad,
    part_s, part_r, out_s, out_r, pre_near, pre_sum, pre_z, pre_c, unit_s, unit_z, unit_all, total, send, recv,
):
    bf16, f32 = jnp.bfloat16, jnp.float32
    place = Place()
    c, x, z = place.c, place.x, place.z
    steps = []
    step = 1
    while step < planes:
        other = z + step - 2 * step * lax.rem(lax.div(z, step), 2)
        steps.append((2 * other + c, place.head))
        step *= 2
    place.greet([place.to_x, place.to_y, place.to_d, place.to_c] + steps, True)
    moves = c != x
    half = grad_one.shape[0]
    slots = []

    def there(src, dst, device):
        slot = len(slots)
        slots.append(slot)
        return pltpu.make_async_remote_copy(
            src_ref=src, dst_ref=dst, send_sem=send.at[slot], recv_sem=recv.at[slot], device_id=device, device_id_type=MESH
        )

    tiles = half // TILE
    at = lambda t: pl.ds(t * TILE, TILE)
    place_at = lambda first, t: pl.ds(pl.multiple_of(first * half + t * TILE, TILE), TILE)
    pre_copies = [
        there(blocks.at[i + 1], pre_near.at[i], device) for i, device in enumerate((place.to_x, place.to_y, place.to_d))
    ]
    pre_steps = [there(pre_sum.at[i], pre_z.at[i], device) for i, device in enumerate(steps)]
    pre_core = there(pre_sum.at[len(steps)], pre_c, place.to_c)
    unit_steps = [there(unit_s.at[i], unit_z.at[i], device) for i, device in enumerate(steps)]
    unit_core = there(unit_s.at[len(steps)], unit_z.at[len(steps)], place.to_c)
    part_copies = [there(part_s.at[at(t)], part_r.at[at(t)], place.to_c) for t in range(tiles)]
    out_copies = [there(out_s.at[at(t)], out_r.at[at(t)], place.to_s) for t in range(tiles)]
    for copy in pre_copies:
        copy.start()
    unit_s[0] = unit_sum[...].astype(bf16)
    unit_steps[0].start()

    def input_rows(rows):
        return sum(nt(dqkv[p, rows, :], wself[p]) for p in range(4))

    part_s[at(0), :] = input_rows(place_at(1 - c, 0)).astype(bf16)
    part_copies[0].start()
    for copy in pre_copies:
        copy.wait()
    pre_sum[0] = blocks[0] + pre_near[0] + pre_near[1] + pre_near[2]
    pre_steps[0].start()
    for t in range(1, tiles):
        part_s[at(t), :] = input_rows(place_at(1 - c, t)).astype(bf16)
        part_copies[t].start()

    def advance(i):
        pre_steps[i].wait()
        pre_sum[i + 1] = pre_sum[i] + pre_z[i]
        if i + 1 < len(steps):
            pre_steps[i + 1].start()
        else:
            pre_core.start()
        unit_steps[i].wait()
        unit_s[i + 1] = (unit_s[i].astype(f32) + unit_z[i].astype(f32)).astype(bf16)
        if i + 1 < len(steps):
            unit_steps[i + 1].start()
        else:
            unit_core.start()

    for t in range(tiles):
        part_copies[t].wait()
        total[at(t), :] = input_rows(place_at(c, t)) + part_r[at(t), :].astype(f32) + grad_one[at(t), :]
        out_s[at(t), :] = total[at(t), :].astype(bf16)
        pl.when(moves)(out_copies[t].start)
        if t < len(steps):
            advance(t)
    for i in range(tiles, len(steps)):
        advance(i)
    pre_core.wait()
    unit_core.wait()
    my_lanes = pl.ds(pl.multiple_of(c * 128, 128), 128)
    other_lanes = pl.ds(pl.multiple_of((1 - c) * 128, 128), 128)
    prefix_grad[:, :, my_lanes] = pre_sum[len(steps)]
    prefix_grad[:, :, other_lanes] = pre_c[...]
    some = unit_sum.shape[0]
    unit_all[pl.ds(pl.multiple_of(c * some, some), some), :] = unit_s[len(steps)].astype(f32)
    unit_all[pl.ds(pl.multiple_of((1 - c) * some, some), some), :] = unit_z[len(steps)].astype(f32)
    features = grad_one.shape[1]
    down_grad[...] = unit_all[:, 0:features].T
    up_grad[...] = unit_all[:, features : 2 * features]

    @pl.when(moves)
    def _():
        for copy in out_copies:
            copy.wait()
        grad_input[...] = out_r[...].astype(f32)

    @pl.when(jnp.logical_not(moves))
    def _():
        grad_input[...] = total[...]


def last_call(planes, dqkv, wself, grad_one, blocks, unit_sum):
    bf16, f32 = jnp.bfloat16, jnp.float32
    half, deep = grad_one.shape
    some = unit_sum.shape[0]
    count = planes.bit_length() - 1
    shape = jax.ShapeDtypeStruct
    vmem = pl.BlockSpec(memory_space=pltpu.VMEM)
    return pl.pallas_call(
        functools.partial(last_kernel, planes),
        out_shape=[
            shape((half, deep), f32),
            shape((2, 32, 256), f32),
            shape((deep, 2 * some), f32),
            shape((2 * some, deep), f32),
        ],
        in_specs=[vmem] * 5,
        out_specs=[vmem] * 4,
        scratch_shapes=[
            pltpu.VMEM((half, deep), bf16),
            pltpu.VMEM((half, deep), bf16),
            pltpu.VMEM((half, deep), bf16),
            pltpu.VMEM((half, deep), bf16),
            pltpu.VMEM((3, 2, 32, 128), f32),
            pltpu.VMEM((count + 1, 2, 32, 128), f32),
            pltpu.VMEM((count, 2, 32, 128), f32),
            pltpu.VMEM((2, 32, 128), f32),
            pltpu.VMEM((count + 1, some, 2 * deep), bf16),
            pltpu.VMEM((count + 1, some, 2 * deep), bf16),
            pltpu.VMEM((2 * some, 2 * deep), f32),
            pltpu.VMEM((half, deep), f32),
            pltpu.SemaphoreType.DMA((3 + 2 * count + 2 + 2 * (half // TILE),)),
            pltpu.SemaphoreType.DMA((3 + 2 * count + 2 + 2 * (half // TILE),)),
        ],
        compiler_params=pltpu.CompilerParams(collective_id=3, has_side_effects=True, vmem_limit_bytes=40 * 2**20),
        name="last_sums",
    )(dqkv, wself, grad_one, blocks, unit_sum)


AXES = ("rows", "heads")


def fast_fits(mesh):
    rows, heads = mesh.shape["rows"], mesh.shape["heads"]
    return heads == 4 and rows % 4 == 0 and (rows & (rows - 1)) == 0


def pairs_of(rows, move):
    def number(z, c, y, x):
        return (z * 2 + c) * 4 + y * 2 + x

    found = []
    for z in range(rows // 2):
        for c in range(2):
            for y in range(2):
                for x in range(2):
                    found.append((number(z, c, y, x), number(*move(z, c, y, x))))
    return found


def swap_in(rows, value):
    def swapped(z, c, y, x):
        return (z, x, y, c)

    crossing = [pair for pair in pairs_of(rows, swapped) if pair[0] != pair[1]]
    stays = lax.axis_index("rows") % 2 == lax.axis_index("heads") % 2
    return jnp.where(stays, value, lax.ppermute(value, AXES, crossing))


def fast_body(
    rows,
    tokens,
    memory,
    cotangent,
    dec_seg,
    mem_seg,
    w_self,
    w_self_out,
    w_cross_q,
    w_cross_kv,
    w_cross_out,
    fc_in,
    fc_out,
    ad_down,
    ad_up,
    prefix,
    ln_gain,
    ln_bias,
):
    count = prefix.shape[1]
    ad = jnp.stack([ad_down.T, ad_up])
    held = forward_call(
        tokens,
        memory,
        dec_seg.reshape(2, 1, SEQ),
        mem_seg.reshape(2, 1, MLEN),
        jnp.pad(prefix, ((0, 0), (0, 32 - count), (0, 0))),
        w_self,
        w_self_out,
        w_cross_q,
        w_cross_kv,
        w_cross_out,
        fc_in,
        fc_out,
        ad,
        ln_gain,
        ln_bias,
    )
    output, grad_two, unit_sum, cross_dctx = feed_call(
        held.resid2, cotangent, ln_gain, ln_bias, held.wco_m, held.wco_o,
        fc_in, held.fin, fc_out, held.fout, ad, held.fad,
    )
    cross_dq, cross_dkv = backward_call(
        False, (held.q, held.kv), held.bounds, held.cctx, cross_dctx, held.clse
    )
    grad_one, self_dctx, memory_sum = query_call(
        cross_dq, cross_dkv, held.wkv, held.wq_m, held.wq_o, grad_two, held.resid1, held.wso_m, held.wso_o, ln_gain
    )
    grad_memory = swap_in(rows, memory_sum).astype(jnp.float32)
    self_dqkv, prefix_blocks = backward_call(
        True, (held.qkv,), held.bounds, held.sctx, self_dctx, held.slse, held.pre
    )
    grad_input, prefix_grad, down_grad, up_grad = last_call(
        rows // 2, self_dqkv, held.wself, grad_one, prefix_blocks, unit_sum
    )
    return (output, grad_input, grad_memory, prefix_grad[:, :count], down_grad, up_grad)


def solution(mesh):
    in_specs = (
        P(("rows", "heads"), None),
        P(("rows", "heads"), None),
        P(("rows", "heads"), None),
        P("rows"),
        P("rows"),
        P(None, None, "heads"),
        P("heads", None),
        P(None, "heads"),
        P(None, None, "heads"),
        P("heads", None),
        P(None, "heads"),
        P("heads", None),
        P(None, "heads"),
        P("heads", None),
        P(None, None, "heads"),
        P(),
        P(),
    )
    out_specs = (
        P(("rows", "heads"), None),
        P(("rows", "heads"), None),
        P(("rows", "heads"), None),
        P(None, None, "heads"),
        P(None, "heads"),
        P("heads", None),
    )
    chosen = functools.partial(fast_body, mesh.shape["rows"]) if fast_fits(mesh) else body
    return jax.shard_map(chosen, mesh=mesh, in_specs=in_specs, out_specs=out_specs, check_vma=False)
```

```python
import functools
import math
import typing

import jax
import jax.numpy as jnp
from jax import lax
from jax.experimental import pallas as pl
from jax.experimental.pallas import tpu as pltpu
from jax.sharding import PartitionSpec as P

HD = 64
SEQ = 1024
MLEN = 1024


epsilon = 1e-05
adapter_scale = 4.0
masked_score = -1e30


def dot_right(left, right):
    return lax.dot_general(
        left, right, (((1,), (1,)), ((), ())), preferred_element_type=jnp.float32
    )


def dot_left(left, right):
    return lax.dot_general(
        left, right, (((0,), (0,)), ((), ())), preferred_element_type=jnp.float32
    )


def norm_parts(resid):
    average = jnp.mean(resid, axis=-1, keepdims=True)
    centered = resid - average
    inv_scale = lax.rsqrt(jnp.mean(centered * centered, axis=-1, keepdims=True) + epsilon)
    return (centered * inv_scale, inv_scale)


def norm_forward(resid, gain, shift):
    normed, inv_scale = norm_parts(resid)
    return normed * gain + shift


def norm_backward(resid, gain, grad_out):
    normed, inv_scale = norm_parts(resid)
    scaled = grad_out * gain
    return inv_scale * (
        scaled
        - jnp.mean(scaled, axis=-1, keepdims=True)
        - normed * jnp.mean(scaled * normed, axis=-1, keepdims=True)
    )


def gelu_slope(pre_gelu):
    return (
        0.5 * (1.0 + lax.erf(pre_gelu * 0.7071067811865476))
        + pre_gelu * jnp.exp(-0.5 * pre_gelu * pre_gelu) * 0.3989422804014327
    )


def silu_slope(pre_relu):
    sigma = jax.nn.sigmoid(pre_relu)
    return sigma * (1.0 + pre_relu * (1.0 - sigma))


def to_heads(arrays, heads_here):
    return arrays.reshape(arrays.shape[0], arrays.shape[1], heads_here, HD).transpose(0, 2, 1, 3)


def from_heads(arrays):
    return arrays.transpose(0, 2, 1, 3).reshape(
        arrays.shape[0] * arrays.shape[2], arrays.shape[1] * arrays.shape[3]
    )


def join_blocks(stacked):
    moved = jnp.moveaxis(stacked, 0, 1)
    return moved.reshape((moved.shape[0], moved.shape[1] * moved.shape[2]) + moved.shape[3:])


def block_mask(row_segs, key_segs, offset, causal):
    allowed = row_segs[:, None] == key_segs[None, :]
    if causal:
        row_places = offset + lax.iota(jnp.int32, row_segs.shape[0])
        key_places = lax.iota(jnp.int32, key_segs.shape[0])
        allowed = allowed & (key_places[None, :] <= row_places[:, None])
    return allowed


def block_scores(queries, key_rows, allowed, prefix_keys):
    qk_scale = HD ** (-0.5)
    token_scores = (
        jnp.einsum("hqe,hke->hqk", queries, key_rows, preferred_element_type=jnp.float32) * qk_scale
    )
    token_scores = jnp.where(allowed[None], token_scores, masked_score)
    if prefix_keys is None:
        return (token_scores, None)
    prefix_scores = (
        jnp.einsum("hqe,hpe->hqp", queries, prefix_keys, preferred_element_type=jnp.float32)
        * qk_scale
    )
    return (token_scores, prefix_scores)


def attend_block(queries, key_rows, value_rows, allowed, prefix_keys, prefix_values):
    token_scores, prefix_scores = block_scores(queries, key_rows, allowed, prefix_keys)
    row_max = jnp.max(token_scores, axis=-1, keepdims=True)
    if prefix_scores is not None:
        row_max = jnp.maximum(row_max, jnp.max(prefix_scores, axis=-1, keepdims=True))
    token_weights = jnp.exp(token_scores - row_max)
    row_total = jnp.sum(token_weights, axis=-1, keepdims=True)
    if prefix_scores is not None:
        prefix_weights = jnp.exp(prefix_scores - row_max)
        row_total = row_total + jnp.sum(prefix_weights, axis=-1, keepdims=True)
    context = jnp.einsum(
        "hqk,hke->hqe",
        (token_weights / row_total).astype(jnp.bfloat16),
        value_rows,
        preferred_element_type=jnp.float32,
    )
    if prefix_scores is not None:
        context = context + jnp.einsum(
            "hqp,hpe->hqe",
            (prefix_weights / row_total).astype(jnp.bfloat16),
            prefix_values,
            preferred_element_type=jnp.float32,
        )
    return (context.astype(jnp.bfloat16), row_max + jnp.log(row_total))


def attend_back(
    queries, key_rows, value_rows, allowed, prefix_keys, prefix_values, log_total, context_grad
):
    qk_scale = HD ** (-0.5)
    token_scores, prefix_scores = block_scores(queries, key_rows, allowed, prefix_keys)
    token_probs = jnp.exp(token_scores - log_total)
    token_dprob = jnp.einsum(
        "hqe,hke->hqk", context_grad, value_rows, preferred_element_type=jnp.float32
    )
    inner = jnp.sum(token_probs * token_dprob, axis=-1, keepdims=True)
    if prefix_scores is not None:
        prefix_probs = jnp.exp(prefix_scores - log_total)
        prefix_dprob = jnp.einsum(
            "hqe,hpe->hqp", context_grad, prefix_values, preferred_element_type=jnp.float32
        )
        inner = inner + jnp.sum(prefix_probs * prefix_dprob, axis=-1, keepdims=True)
    token_dscore = (token_probs * (token_dprob - inner)).astype(jnp.bfloat16)
    query_grad = jnp.einsum(
        "hqk,hke->hqe", token_dscore, key_rows, preferred_element_type=jnp.float32
    )
    key_grad = (
        jnp.einsum("hqk,hqe->hke", token_dscore, queries, preferred_element_type=jnp.float32)
        * qk_scale
    )
    value_grad = jnp.einsum(
        "hqk,hqe->hke",
        token_probs.astype(jnp.bfloat16),
        context_grad,
        preferred_element_type=jnp.float32,
    )
    if prefix_scores is None:
        return (query_grad * qk_scale, (key_grad, value_grad))
    prefix_dscore = (prefix_probs * (prefix_dprob - inner)).astype(jnp.bfloat16)
    query_grad = query_grad + jnp.einsum(
        "hqp,hpe->hqe", prefix_dscore, prefix_keys, preferred_element_type=jnp.float32
    )
    prefix_key_grad = (
        jnp.einsum("hqp,hqe->hpe", prefix_dscore, queries, preferred_element_type=jnp.float32)
        * qk_scale
    )
    prefix_value_grad = jnp.einsum(
        "hqp,hqe->hpe",
        prefix_probs.astype(jnp.bfloat16),
        context_grad,
        preferred_element_type=jnp.float32,
    )
    return (query_grad * qk_scale, (key_grad, value_grad, prefix_key_grad, prefix_value_grad))


def sequence_forward(
    queries, key_rows, value_rows, row_segs, key_segs, prefix_keys, prefix_values, causal
):
    seq_width = queries.shape[1]
    block_rows = min(512, seq_width)

    def one_block(block_index):
        offset = block_index * block_rows
        allowed = block_mask(
            lax.dynamic_slice_in_dim(row_segs, offset, block_rows, 0), key_segs, offset, causal
        )
        query_part = lax.dynamic_slice_in_dim(queries, offset, block_rows, 1)
        return attend_block(query_part, key_rows, value_rows, allowed, prefix_keys, prefix_values)

    context, log_total = lax.map(one_block, jnp.arange(seq_width // block_rows, dtype=jnp.int32))
    return (join_blocks(context), join_blocks(log_total))


def sequence_backward(
    queries,
    key_rows,
    value_rows,
    row_segs,
    key_segs,
    prefix_keys,
    prefix_values,
    causal,
    log_total,
    context_grad,
):
    seq_width = queries.shape[1]
    block_rows = min(512, seq_width)
    key_zero = jnp.zeros(key_rows.shape, jnp.float32)
    initial = (key_zero, key_zero)
    if prefix_keys is not None:
        prefix_zero = jnp.zeros(prefix_keys.shape, jnp.float32)
        initial = initial + (prefix_zero, prefix_zero)

    def one_block(running, block_index):
        offset = block_index * block_rows
        allowed = block_mask(
            lax.dynamic_slice_in_dim(row_segs, offset, block_rows, 0), key_segs, offset, causal
        )
        query_part = lax.dynamic_slice_in_dim(queries, offset, block_rows, 1)
        total_part = lax.dynamic_slice_in_dim(log_total, offset, block_rows, 1)
        grad_part = lax.dynamic_slice_in_dim(context_grad, offset, block_rows, 1)
        query_grad, block_grads = attend_back(
            query_part,
            key_rows,
            value_rows,
            allowed,
            prefix_keys,
            prefix_values,
            total_part,
            grad_part,
        )
        return (tuple((summed + added for summed, added in zip(running, block_grads))), query_grad)

    running, query_grad = lax.scan(
        one_block, initial, jnp.arange(seq_width // block_rows, dtype=jnp.int32)
    )
    outputs = (
        join_blocks(query_grad).astype(jnp.bfloat16),
        running[0].astype(jnp.bfloat16),
        running[1].astype(jnp.bfloat16),
    )
    return outputs + running[2:]


def gather_rows(row_share):
    return lax.all_gather(row_share, "heads", axis=0, tiled=True)


def gather_grads(row_share):
    return lax.all_gather(row_share, "heads", axis=0, tiled=True)


def sum_rows(partial_value):
    return lax.psum_scatter(partial_value, "heads", scatter_dimension=0, tiled=True)


def sum_grads(partial_value):
    return lax.psum_scatter(partial_value, "heads", scatter_dimension=0, tiled=True)


def body(
    tokens,
    memory,
    cotangent,
    dec_seg,
    mem_seg,
    w_self,
    w_self_out,
    w_cross_q,
    w_cross_kv,
    w_cross_out,
    fc_in,
    fc_out,
    ad_down,
    ad_up,
    prefix,
    ln_gain,
    ln_bias,
):
    local_width = w_self.shape[2]
    heads_here = local_width // HD
    seg_dec = dec_seg.reshape(-1, SEQ)
    seg_mem = mem_seg.reshape(-1, MLEN)
    seq_count = seg_dec.shape[0]
    prefix_heads = to_heads(prefix, heads_here)
    prefix_keys = prefix_heads[0]
    prefix_values = prefix_heads[1]
    gathered_x = gather_rows(tokens)
    self_proj = jnp.einsum(
        "td,cdn->ctn", gathered_x, w_self, preferred_element_type=jnp.float32
    ).astype(jnp.bfloat16)
    self_proj = self_proj.reshape(3, seq_count, SEQ, local_width)
    self_queries = to_heads(self_proj[0], heads_here)
    self_keys = to_heads(self_proj[1], heads_here)
    self_values = to_heads(self_proj[2], heads_here)

    def self_forward(packed):
        return sequence_forward(
            packed[0], packed[1], packed[2], packed[3], packed[3], prefix_keys, prefix_values, True
        )

    self_context, self_total = lax.map(
        self_forward, (self_queries, self_keys, self_values, seg_dec)
    )
    attn_partial = jnp.dot(from_heads(self_context), w_self_out, preferred_element_type=jnp.float32)
    resid_one = tokens.astype(jnp.float32) + sum_rows(attn_partial)
    hidden_one = norm_forward(resid_one, ln_gain[0], ln_bias[0])
    gathered_one = gather_rows(hidden_one.astype(jnp.bfloat16))
    gathered_mem = lax.all_gather(memory, "heads", axis=0, tiled=True)
    cross_rows = jnp.dot(gathered_one, w_cross_q, preferred_element_type=jnp.float32).astype(
        jnp.bfloat16
    )
    cross_proj = jnp.einsum(
        "td,cdn->ctn", gathered_mem, w_cross_kv, preferred_element_type=jnp.float32
    ).astype(jnp.bfloat16)
    cross_queries = to_heads(cross_rows.reshape(seq_count, SEQ, local_width), heads_here)
    cross_proj = cross_proj.reshape(2, seq_count, MLEN, local_width)
    cross_keys = to_heads(cross_proj[0], heads_here)
    cross_values = to_heads(cross_proj[1], heads_here)

    def cross_forward(packed):
        return sequence_forward(
            packed[0], packed[1], packed[2], packed[3], packed[4], None, None, False
        )

    cross_context, cross_total = lax.map(
        cross_forward, (cross_queries, cross_keys, cross_values, seg_dec, seg_mem)
    )
    cross_partial = jnp.dot(
        from_heads(cross_context), w_cross_out, preferred_element_type=jnp.float32
    )
    resid_two = hidden_one + sum_rows(cross_partial)
    hidden_two = norm_forward(resid_two, ln_gain[1], ln_bias[1])
    hidden_low = hidden_two.astype(jnp.bfloat16)
    full_in, full_out, full_down, full_up = (fc_in, fc_out, ad_down, ad_up)
    ffn_rows = gather_rows(hidden_low)
    pre_gelu = jnp.dot(ffn_rows, full_in, preferred_element_type=jnp.float32)
    activated = jax.nn.gelu(pre_gelu, approximate=False).astype(jnp.bfloat16)
    pre_relu = jnp.dot(ffn_rows, full_down, preferred_element_type=jnp.float32)
    adapted = (pre_relu * jax.nn.sigmoid(pre_relu)).astype(jnp.bfloat16)
    branch = jnp.dot(
        activated, full_out, preferred_element_type=jnp.float32
    ) + adapter_scale * jnp.dot(adapted, full_up, preferred_element_type=jnp.float32)
    resid_three = hidden_two + sum_rows(branch)
    output = norm_forward(resid_three, ln_gain[2], ln_bias[2]).astype(jnp.bfloat16)
    grad_three = norm_backward(resid_three, ln_gain[2], cotangent.astype(jnp.float32))
    grad_branch = grad_three.astype(jnp.bfloat16)
    branch_rows = gather_grads(grad_branch)
    grad_gelu = (dot_right(branch_rows, full_out) * gelu_slope(pre_gelu)).astype(jnp.bfloat16)
    grad_relu = (adapter_scale * dot_right(branch_rows, full_up) * silu_slope(pre_relu)).astype(
        jnp.bfloat16
    )
    up_grad = adapter_scale * dot_left(adapted, branch_rows)
    down_grad = dot_left(ffn_rows, grad_relu)
    hidden_partial = dot_right(grad_gelu, full_in) + dot_right(grad_relu, full_down)
    grad_two_in = grad_three + sum_grads(hidden_partial)
    down_grad, up_grad = (
        lax.psum(down_grad.astype(jnp.bfloat16), "rows").astype(jnp.float32),
        lax.psum(up_grad.astype(jnp.bfloat16), "rows").astype(jnp.float32),
    )
    grad_two = norm_backward(resid_two, ln_gain[1], grad_two_in)
    cross_out_rows = gather_grads(grad_two.astype(jnp.bfloat16))
    cross_dctx = dot_right(cross_out_rows, w_cross_out).astype(jnp.bfloat16)
    cross_dctx = to_heads(cross_dctx.reshape(seq_count, SEQ, local_width), heads_here)

    def cross_back(packed):
        return sequence_backward(
            packed[0],
            packed[1],
            packed[2],
            packed[3],
            packed[4],
            None,
            None,
            False,
            packed[5],
            packed[6],
        )

    cross_qgrad, cross_kgrad, cross_vgrad = lax.map(
        cross_back,
        (cross_queries, cross_keys, cross_values, seg_dec, seg_mem, cross_total, cross_dctx),
    )
    memory_kv = jnp.stack([from_heads(cross_kgrad), from_heads(cross_vgrad)])
    one_partial = dot_right(from_heads(cross_qgrad), w_cross_q)
    grad_one_in = grad_two + sum_grads(one_partial)
    memory_partial = jnp.einsum(
        "ctn,cdn->td", memory_kv, w_cross_kv, preferred_element_type=jnp.float32
    )
    grad_memory = lax.psum_scatter(
        memory_partial.astype(jnp.bfloat16), "heads", scatter_dimension=0, tiled=True
    ).astype(jnp.float32)
    grad_one = norm_backward(resid_one, ln_gain[0], grad_one_in)
    attn_rows = gather_grads(grad_one.astype(jnp.bfloat16))
    self_dctx = dot_right(attn_rows, w_self_out).astype(jnp.bfloat16)
    self_dctx = to_heads(self_dctx.reshape(seq_count, SEQ, local_width), heads_here)

    def self_back(running, packed):
        query_grad, key_grad, value_grad, pkey_grad, pvalue_grad = sequence_backward(
            packed[0],
            packed[1],
            packed[2],
            packed[3],
            packed[3],
            prefix_keys,
            prefix_values,
            True,
            packed[4],
            packed[5],
        )
        return (
            (running[0] + pkey_grad, running[1] + pvalue_grad),
            (query_grad, key_grad, value_grad),
        )

    zero_grad = jnp.zeros(prefix_keys.shape, jnp.float32)
    prefix_sums, self_grads = lax.scan(
        self_back,
        (zero_grad, zero_grad),
        (self_queries, self_keys, self_values, seg_dec, self_total, self_dctx),
    )
    self_stack = jnp.stack(
        [from_heads(self_grads[0]), from_heads(self_grads[1]), from_heads(self_grads[2])]
    )
    input_partial = jnp.einsum(
        "ctn,cdn->td", self_stack, w_self, preferred_element_type=jnp.float32
    )
    grad_input = grad_one + sum_grads(input_partial)
    prefix_grad = (
        jnp.stack([prefix_sums[0], prefix_sums[1]])
        .transpose(0, 2, 1, 3)
        .reshape(2, prefix.shape[1], local_width)
    )
    prefix_grad = lax.psum(prefix_grad, "rows")
    return (output, grad_input, grad_memory, prefix_grad, down_grad, up_grad)


QB = 256
KB = 256
LOG2E = math.log2(math.e)
NEG = -1e30


def nt(a, b):
    return lax.dot_general(a, b, (((1,), (1,)), ((), ())), preferred_element_type=jnp.float32)


def nn(a, b):
    return lax.dot_general(a, b, (((1,), (0,)), ((), ())), preferred_element_type=jnp.float32)


def tn(a, b):
    return lax.dot_general(a, b, (((0,), (0,)), ((), ())), preferred_element_type=jnp.float32)


def half_lanes(v, h):
    lane = lax.broadcasted_iota(jnp.int32, v.shape, 1)
    keep = (lane < 64) if h == 0 else (lane >= 64)
    return jnp.where(keep, v, jnp.zeros_like(v))


def prefix_rows(scores):
    row = lax.broadcasted_iota(jnp.int32, scores.shape, 0)
    return jnp.where(lax.rem(row, 64) < 30, scores, NEG)


MESH = pl.DeviceIdType.MESH
TILE = 256

TOK, TOK_C, MEM, MEM_C = 112, 113, 114, 115
SELF_PIECE, OUT_ONE, CROSS_Q, CROSS_PIECE, OUT_TWO = 128, 132, 133, 134, 138
SLOTS, LOCAL_SLOTS = 128, 48
GROUPS = ((1, 0), (1, 0), (1, 0), (0, 1), (1, 1), (0, 0), (1, 0))
SCHEDULE = (16, 17, 65, 64, 20, 33, 32, 68, 97, 112, 35, 67, 36, 19, 114, 113, 18, 100, 49, 128, 0, 115, 21, 1, 22, 96, 3, 2, 4, 129, 48, 34, 98, 5, 130, 80, 37, 131, 81, 99, 38, 132, 133, 101, 134, 66, 50, 82, 135, 69, 102, 136, 70, 137, 86, 138)


class Place:
    def __init__(self):
        self.row, self.head = lax.axis_index("rows"), lax.axis_index("heads")
        self.c, self.z = lax.rem(self.row, 2), lax.div(self.row, 2)
        self.x, self.y = lax.rem(self.head, 2), lax.div(self.head, 2)
        self.odd = lax.rem(self.z, 2)
        c, x, y, z = self.c, self.x, self.y, self.z
        self.to_x = (self.row, 2 * y + 1 - x)
        self.to_y = (self.row, 2 * (1 - y) + x)
        self.to_d = (self.row, 2 * (1 - y) + 1 - x)
        self.to_z = (2 * (z + 1 - 2 * self.odd) + c, self.head)
        self.to_c = (2 * z + 1 - c, self.head)
        self.to_s = (2 * z + x, 2 * y + c)

    def greet(self, devices, swaps):
        barrier = pltpu.get_barrier_semaphore()
        for device in devices:
            pl.semaphore_signal(barrier, inc=1, device_id=device, device_id_type=MESH)
        count = len(devices)
        if swaps:
            moves = self.c != self.x

            @pl.when(moves)
            def _():
                pl.semaphore_signal(barrier, inc=1, device_id=self.to_s, device_id_type=MESH)

            count = count + moves.astype(jnp.int32)
        pl.semaphore_wait(barrier, count)


def prefix_block(rows):
    nothing = jnp.zeros_like(rows)
    return jnp.concatenate([half_lanes(rows, 0), nothing, half_lanes(rows, 1), nothing], axis=0)


def attend_tile(q, k, vt, mask, kp, vpt):
    scale = 0.125 * LOG2E
    rows = q.shape[0]
    if kp is not None:
        sp = prefix_rows(nt(kp, q) * scale)
    outs, tops, sums = [], [], []
    for h in range(2):
        s = jnp.where(mask, nt(k, half_lanes(q, h)) * scale, NEG)
        m = jnp.max(s, axis=0, keepdims=True)
        if kp is not None:
            m = jnp.maximum(m, jnp.max(sp[h * 64 : h * 64 + 32], axis=0, keepdims=True))
        e = jnp.exp2(s - m)
        outs.append(nn(vt[h * 64 : h * 64 + 64], e.astype(jnp.bfloat16)))
        sums.append(jnp.sum(e, axis=0, keepdims=True))
        tops.append(m)
    if kp is not None:
        mm = jnp.concatenate([jnp.broadcast_to(t, (64, rows)) for t in tops], axis=0)
        ep = jnp.exp2(sp - mm)
        sums = [sums[h] + jnp.sum(ep[h * 64 : h * 64 + 32], axis=0, keepdims=True) for h in range(2)]
        extra = nn(vpt, ep.astype(jnp.bfloat16))
        outs = [outs[h] + extra[h * 64 : h * 64 + 64] for h in range(2)]
    both = jnp.concatenate([outs[h] * (1.0 / sums[h]) for h in range(2)], axis=0)
    return both.T.astype(jnp.bfloat16), [tops[h] + jnp.log2(sums[h]) for h in range(2)]


def forward_kernel(
    tokens, memory, seg, mseg, prefix, w_self, w_so, w_cq, w_ckv, w_co, fc_in, fc_out, ad_down, ad_up, gain, bias,
    o_wself, o_qkv, o_sctx, o_slse, o_pre, o_wso_m, o_wso_o, o_wkv, o_wq_m, o_wq_o, o_wco_m, o_wco_o,
    o_q, o_kv, o_cctx, o_clse, o_resid1, o_resid2, o_bounds, o_ad, fin, fout, fad,
    wself, qkv, sctx, slse, pre, wso_m, wso_o, wkv, wq_m, wq_o, wco_m, wco_o,
    q_all, kv, cctx, clse, resid1, resid2, bounds, ad, tok, mem, sctx_o, cctx_o, q_send, hidden, low_one, vt, seg_v, mseg_v,
    send, recv, local,
):
    place_of = Place()
    c, x, y, odd = place_of.c, place_of.x, place_of.y, place_of.odd
    to_x, to_y, to_z, to_c, to_s = place_of.to_x, place_of.to_y, place_of.to_z, place_of.to_c, place_of.to_s
    stays, moves = c == x, c != x
    place_of.greet((to_x, to_y, to_z, to_c), True)

    taken = []

    def there(src, dst, device):
        slot = len(taken)
        taken.append(slot)
        return pltpu.make_async_remote_copy(
            src_ref=src, dst_ref=dst, send_sem=send.at[slot], recv_sem=recv.at[slot], device_id=device, device_id_type=MESH
        )

    used = []

    def here(src, dst):
        slot = len(used)
        used.append(slot)
        return pltpu.make_async_copy(src, dst, local.at[slot])

    deep = w_self.shape[1]
    half = tok.shape[0] // 2
    step = lambda start, size, unit: pl.ds(pl.multiple_of(start, unit), size)
    mine = step(c * half, half, half)
    others = step((1 - c) * half, half, half)
    lanes = step(c * 128, 128, 128)
    other_lanes = step((1 - c) * 128, 128, 128)
    rows_c, rows_o = lanes, other_lanes
    foreign = pl.ds(128, 384)
    hid = fc_in.shape[1]
    units = ad.shape[1]
    pending = []

    def swap_of(src, target):
        away = there(src, target.at[step(x * half, half, half)], to_s)
        home = here(src, target.at[mine])
        back = there(target.at[mine], target.at[mine], to_c)

        def start():
            pl.when(moves)(away.start)
            pl.when(stays)(home.start)

        def wait():
            pl.when(moves)(away.wait)
            pl.when(stays)(home.wait)

        return start, wait, back

    def seg_of(src, dst):
        home = here(src.at[y], dst)
        away = there(src.at[y], dst, to_c)

        def start():
            pl.when(stays)(home.start)
            pl.when(stays)(away.start)

        def wait():
            pl.when(stays)(home.wait)
            pl.when(stays)(away.wait_send)
            pl.when(moves)(away.wait_recv)

        return start, wait

    def deep_rows(shared):
        return step(odd * (deep // 2), deep // 2, deep // 2) if shared else pl.ds(0, deep)

    def thin_rows(piece, shared):
        return step(128 * piece + odd * 64, 64, 64) if shared else pl.ds(128 * piece, 128)

    def thin_own(shared):
        return step(128 * c + odd * 64, 64, 64) if shared else rows_c

    def span(size, shared):
        return step(c * (size // 2) + odd * (size // 4), size // 4, size // 4) if shared else step(c * (size // 2), size // 2, size // 2)

    lane_of = lambda i: pl.ds(128 * i, 128)

    def group_a(shared):
        rows = deep_rows(shared)
        first = lambda piece: [(w_self.at[i, rows, lanes], wself.at[piece, rows, lane_of(i)]) for i in range(3)] + [
            (prefix.at[:, :, lanes], pre.at[piece])
        ]
        return first, lambda piece: [wself.at[piece, rows], pre.at[piece]], 1, []

    def group_thin(src, dst_m, dst_o, shared):
        first = lambda piece: [(src.at[thin_own(shared)], dst_m.at[thin_rows(piece, shared)])]
        return first, lambda piece: [dst_m.at[thin_rows(piece, shared)]], 1, [(dst_m.at[foreign], dst_o.at[foreign])]

    def group_q(shared):
        rows = deep_rows(shared)
        first = lambda piece: [(w_cq.at[rows, lanes], wq_m.at[rows, lane_of(piece)])]
        return first, lambda piece: [wq_m.at[rows, lane_of(piece)]], 1, [(wq_m.at[:, foreign], wq_o.at[:, foreign])]

    def group_v(shared):
        rows = deep_rows(shared)
        first = lambda piece: [(w_ckv.at[i, rows, lanes], wkv.at[piece, rows, lane_of(i)]) for i in range(2)]
        return first, lambda piece: [wkv.at[piece, rows]], 1, []

    def group_i(shared):
        cols = span(hid, shared)
        both = fin.at[:, :, span(hid, False)]
        first = lambda piece: [(fc_in.at[:, cols], fin.at[piece - 1, :, cols])]
        return first, lambda piece: [fin.at[piece - 1, :, cols]], 1, [(both, both)]

    def group_o(shared):
        rows, some = span(hid, shared), span(units, shared)
        both, both_units = fout.at[:, span(hid, False)], fad.at[:, :, span(units, False)]
        first = lambda piece: [(fc_out.at[rows], fout.at[piece - 1, rows]), (ad.at[:, some], fad.at[piece - 1, :, some])]
        hold = lambda piece: [fout.at[piece - 1, rows], fad.at[piece - 1, :, some]]
        return first, hold, 2, [(both, both), (both_units, both_units)]

    makers = [
        group_a,
        functools.partial(group_thin, w_so, wso_m, wso_o),
        group_q,
        group_v,
        functools.partial(group_thin, w_co, wco_m, wco_o),
        group_i,
        group_o,
    ]
    copies, needs = {}, {}
    for index, (make, (shared, through_x)) in enumerate(zip(makers, GROUPS)):
        first, hold, shared_count, cross = make(bool(shared))
        base = 16 * index
        copies[base] = [there(src, dst, to_x) for src, dst in first(1)]
        copies[base + 1] = [there(src, dst, to_y) for src, dst in first(2)]
        near, device = (2, to_x) if through_x else (1, to_y)
        copies[base + 2] = [there(src, dst, device) for src, dst in zip(hold(near), hold(3))]
        needs[base], needs[base + 1], needs[base + 2] = [], [], [base + near - 1]
        arrived = [base, base + 1, base + 2]
        if shared:
            for i in range(3):
                copies[base + 3 + i] = [there(ref, ref, to_z) for ref in hold(i + 1)[:shared_count]]
                needs[base + 3 + i] = [base + i]
                arrived.append(base + 3 + i)
        if cross:
            copies[base + 6] = [there(src, dst, to_c) for src, dst in cross]
            needs[base + 6] = arrived
    tok_start, tok_wait, tok_back = swap_of(tokens, tok)
    mem_start, mem_wait, mem_back = swap_of(memory, mem)
    copies[TOK_C], copies[MEM_C] = [tok_back], [mem_back]
    needs[TOK_C], needs[MEM_C] = [TOK], [MEM]
    seg_start, seg_wait = seg_of(seg, seg_v)
    mseg_start, mseg_wait = seg_of(mseg, mseg_v)
    sctx_out = [there(sctx.at[others, lane_of(i)], sctx_o.at[:, lane_of(i)], to_c) for i in range(4)]
    cctx_out = [there(cctx.at[others, lane_of(i)], cctx_o.at[:, lane_of(i)], to_c) for i in range(4)]
    q_out = there(q_send, q_all.at[mine], to_c)

    landed = set()

    def wait_for(op):
        if op in landed:
            return
        landed.add(op)
        if op == TOK:
            tok_wait()
        elif op == MEM:
            mem_wait()
        elif op in copies:
            for copy in copies[op]:
                copy.wait_recv()

    def launch(op):
        if op == TOK:
            tok_start()
        elif op == MEM:
            mem_start()
        else:
            for need in needs[op]:
                wait_for(need)
            for copy in copies[op]:
                copy.start()
                pending.append(copy)

    saves = []

    def keep(src, dst):
        copy = here(src, dst)
        copy.start()
        saves.append(copy)

    own_a = [here(w_self.at[i, :, lanes], wself.at[0, :, lane_of(i)]) for i in range(3)]
    own_a.append(here(prefix.at[:, :, lanes], pre.at[0]))
    own_b = [
        here(w_so.at[rows_c], wso_m.at[lane_of(0)]),
        here(w_so.at[rows_o], wso_o.at[lane_of(0)]),
        here(w_co.at[rows_c], wco_m.at[lane_of(0)]),
        here(w_co.at[rows_o], wco_o.at[lane_of(0)]),
        here(w_cq.at[:, lanes], wq_m.at[:, lane_of(0)]),
        here(w_cq.at[:, other_lanes], wq_o.at[:, lane_of(0)]),
        here(w_ckv.at[0, :, lanes], wkv.at[0, :, lane_of(0)]),
        here(w_ckv.at[1, :, lanes], wkv.at[0, :, lane_of(1)]),
    ]

    def bounds_of():
        seg_wait()
        mseg_wait()
        dec, men = seg_v[...], mseg_v[...]

        def below(values, d):
            return jnp.sum((values < d).astype(jnp.int32), axis=1, keepdims=True)

        def pick(counts):
            out = jnp.broadcast_to(counts[0], dec.shape)
            for d in range(1, 4):
                out = jnp.where(dec == d, counts[d], out)
            return out

        zero = jnp.zeros((1, 1), jnp.int32)
        full = jnp.full((1, 1), MLEN, jnp.int32)
        self_lo = pick([zero] + [below(dec, d) for d in range(1, 4)])
        mem_counts = [zero] + [below(men, d) for d in range(1, 4)] + [full]
        bounds[...] = jnp.concatenate(
            [self_lo, lax.broadcasted_iota(jnp.int32, dec.shape, 1), pick(mem_counts[:4]), pick(mem_counts[1:]) - 1]
            + [jnp.zeros_like(dec)] * 4,
            axis=0,
        )
        keep(bounds, o_bounds)

    def weight_needs(base, piece):
        found = [base + piece - 1, base + 2 + piece]
        return [op for op in found if op in copies]

    def project(dst, p, source, weight):
        def rows_of(t, _):
            rows = step(t * TILE, TILE, TILE)
            dst[p, rows, :] = nn(source[rows, :], weight[p]).astype(jnp.bfloat16)
            return 0

        lax.fori_loop(0, SEQ // TILE, rows_of, 0)

    def self_piece(p):
        project(qkv, p, tok, wself)
        vt[...] = qkv[p, :, 256:384].astype(jnp.float32).T.astype(jnp.bfloat16)
        kp = prefix_block(pre[p, 0])
        vpt = prefix_block(pre[p, 1]).astype(jnp.float32).T.astype(jnp.bfloat16)
        place = step(p * 128, 128, 128)
        for qi in range(SEQ // QB):
            width = (qi + 1) * QB
            rows = slice(qi * QB, (qi + 1) * QB)
            pos = lax.broadcasted_iota(jnp.int32, (width, QB), 0)
            mask = (pos >= bounds[0:1, rows]) & (pos <= bounds[1:2, rows])
            out, lse = attend_tile(qkv[p, rows, 0:128], qkv[p, 0:width, 128:256], vt[:, 0:width], mask, kp, vpt)
            sctx[rows, place] = out
            for h in range(2):
                slse[p, h : h + 1, rows] = lse[h]

    def cross_piece(p):
        project(kv, p, mem, wkv)
        vt[...] = kv[p, :, 128:256].astype(jnp.float32).T.astype(jnp.bfloat16)
        place = step(p * 128, 128, 128)

        def block(qi, _):
            rows = step(qi * QB, QB, QB)
            pos = lax.broadcasted_iota(jnp.int32, (MLEN, QB), 0)
            mask = (pos >= bounds[2:3, rows]) & (pos <= bounds[3:4, rows])
            out, lse = attend_tile(q_all[rows, place], kv[p, :, 0:128], vt[...], mask, None, None)
            cctx[rows, place] = out
            for h in range(2):
                clse[p, h : h + 1, rows] = lse[h]
            return 0

        lax.fori_loop(0, SEQ // QB, block, 0)

    def with_out(t, resid_before, ctx_m, ctx_o, w_m, w_o):
        rows = step(t * TILE, TILE, TILE)
        rows_all = step(c * half + t * TILE, TILE, TILE)
        return resid_before + nn(ctx_m[rows_all, :], w_m[...]) + nn(ctx_o[rows, :], w_o[...])

    def out_one(t, _):
        rows = step(t * TILE, TILE, TILE)
        rows_all = step(c * half + t * TILE, TILE, TILE)
        resid = with_out(t, tok[rows_all, :].astype(jnp.float32), sctx, sctx_o, wso_m, wso_o)
        resid1[rows, :] = resid
        normed = norm_forward(resid, gain[0:1, :], bias[0:1, :])
        hidden[rows, :] = normed
        low_one[rows, :] = normed.astype(jnp.bfloat16)
        return 0

    def out_two(t, _):
        rows = step(t * TILE, TILE, TILE)
        resid2[rows, :] = with_out(t, hidden[rows, :], cctx, cctx_o, wco_m, wco_o)
        return 0

    def q_rows(t, _):
        rows = step(t * TILE, TILE, TILE)
        rows_all = step(c * half + t * TILE, TILE, TILE)
        q_send[rows, :] = nn(low_one[rows, :], wq_o[...]).astype(jnp.bfloat16)
        q_all[rows_all, :] = nn(low_one[rows, :], wq_m[...]).astype(jnp.bfloat16)
        return 0

    def split_at(order, first, count):
        places = [order.index(first + k) for k in range(count)]
        starts = [0] + [place + 1 for place in places]
        return [order[a:b] for a, b in zip(starts, places)], order[places[-1] + 1 :]

    def pieces_loop(segments, ready, work, sends):
        def body(p, _):
            for k, segment in enumerate(segments):

                @pl.when(p == k)
                def _():
                    for op in segment:
                        launch(op)
                    ready(k)

            work(p)
            for k, copy in enumerate(sends):
                pl.when(p == k)(copy.start)
            return 0

        lax.fori_loop(0, len(segments), body, 0)
        pending.extend(sends)

    ad_copy = here(ad_up, ad.at[1])
    ad_copy.start()
    ad[0] = ad_down[...].astype(jnp.float32).T.astype(jnp.bfloat16)
    ad_copy.wait()
    keep(ad, o_ad)

    for copy in own_a[:3]:
        copy.start()
    own_a[3].start()
    seg_start()
    mseg_start()
    segments, rest = split_at(list(SCHEDULE), SELF_PIECE, 4)
    for op in segments[0]:
        launch(op)
    for copy in own_b:
        copy.start()
    bounds_of()
    for copy in own_a:
        copy.wait()
    segments[0] = []

    def self_ready(k):
        if k == 0:
            wait_for(TOK_C)
        else:
            for op in weight_needs(0, k):
                wait_for(op)

    pieces_loop(segments, self_ready, self_piece, sctx_out)
    for src, dst in ((qkv, o_qkv), (wself, o_wself), (sctx, o_sctx), (slse, o_slse), (pre, o_pre)):
        keep(src, dst)
    for copy in own_b:
        copy.wait()
    before, rest = split_at(rest, OUT_ONE, 1)
    for op in before[0]:
        launch(op)
    for copy in sctx_out:
        copy.wait_recv()
    wait_for(16 + 6)
    lax.fori_loop(0, half // TILE, out_one, 0)
    for src, dst in ((resid1, o_resid1), (wso_m, o_wso_m), (wso_o, o_wso_o)):
        keep(src, dst)
    before, rest = split_at(rest, CROSS_Q, 1)
    for op in before[0]:
        launch(op)
    wait_for(32 + 6)
    lax.fori_loop(0, half // TILE, q_rows, 0)
    q_out.start()
    pending.append(q_out)
    for src, dst in ((wq_m, o_wq_m), (wq_o, o_wq_o)):
        keep(src, dst)
    segments, rest = split_at(rest, CROSS_PIECE, 4)

    def cross_ready(k):
        if k == 0:
            wait_for(MEM_C)
            q_out.wait_recv()
        else:
            for op in weight_needs(48, k):
                wait_for(op)

    pieces_loop(segments, cross_ready, cross_piece, cctx_out)
    for src, dst in ((q_all, o_q), (kv, o_kv), (wkv, o_wkv), (cctx, o_cctx), (clse, o_clse)):
        keep(src, dst)
    before, rest = split_at(rest, OUT_TWO, 1)
    for op in before[0]:
        launch(op)
    for copy in cctx_out:
        copy.wait_recv()
    wait_for(64 + 6)
    lax.fori_loop(0, half // TILE, out_two, 0)
    for src, dst in ((resid2, o_resid2), (wco_m, o_wco_m), (wco_o, o_wco_o)):
        keep(src, dst)
    for op in rest:
        launch(op)
    for op in list(copies):
        wait_for(op)
    for copy in pending:
        copy.wait_send()
    for copy in saves:
        copy.wait()


class Held(typing.NamedTuple):
    wself: jax.Array
    qkv: jax.Array
    sctx: jax.Array
    slse: jax.Array
    pre: jax.Array
    wso_m: jax.Array
    wso_o: jax.Array
    wkv: jax.Array
    wq_m: jax.Array
    wq_o: jax.Array
    wco_m: jax.Array
    wco_o: jax.Array
    q: jax.Array
    kv: jax.Array
    cctx: jax.Array
    clse: jax.Array
    resid1: jax.Array
    resid2: jax.Array
    bounds: jax.Array
    ad: jax.Array
    fin: jax.Array
    fout: jax.Array
    fad: jax.Array


def forward_call(tokens, memory, seg, mseg, prefix, w_self, w_so, w_cq, w_ckv, w_co, fc_in, fc_out, ad_down, ad_up, gain, bias):
    bf16, f32 = jnp.bfloat16, jnp.float32
    half, deep = tokens.shape
    shape = jax.ShapeDtypeStruct
    held = dict(
        wself=((4, deep, 384), bf16),
        qkv=((4, SEQ, 384), bf16),
        sctx=((SEQ, 512), bf16),
        slse=((4, 8, SEQ), f32),
        pre=((4, 2, 32, 128), bf16),
        wso_m=((512, deep), bf16),
        wso_o=((512, deep), bf16),
        wkv=((4, deep, 256), bf16),
        wq_m=((deep, 512), bf16),
        wq_o=((deep, 512), bf16),
        wco_m=((512, deep), bf16),
        wco_o=((512, deep), bf16),
        q=((SEQ, 512), bf16),
        kv=((4, MLEN, 256), bf16),
        cctx=((SEQ, 512), bf16),
        clse=((4, 8, SEQ), f32),
        resid1=((half, deep), f32),
        resid2=((half, deep), f32),
        bounds=((8, SEQ), jnp.int32),
        ad=((2,) + ad_up.shape, bf16),
    )
    outs = [shape(*value) for value in held.values()]
    outs += [shape((3,) + fc_in.shape, bf16), shape((3,) + fc_out.shape, bf16), shape((3, 2) + ad_up.shape, bf16)]
    scratch = [pltpu.VMEM(*value) for value in held.values()] + [
        pltpu.VMEM((SEQ, deep), bf16),
        pltpu.VMEM((MLEN, deep), bf16),
        pltpu.VMEM((half, 512), bf16),
        pltpu.VMEM((half, 512), bf16),
        pltpu.VMEM((half, 512), bf16),
        pltpu.VMEM((half, deep), f32),
        pltpu.VMEM((half, deep), bf16),
        pltpu.VMEM((128, SEQ), bf16),
        pltpu.VMEM((1, SEQ), jnp.int32),
        pltpu.VMEM((1, SEQ), jnp.int32),
        pltpu.SemaphoreType.DMA((SLOTS,)),
        pltpu.SemaphoreType.DMA((SLOTS,)),
        pltpu.SemaphoreType.DMA((LOCAL_SLOTS,)),
    ]
    anywhere = pl.BlockSpec(memory_space=pl.ANY)
    vmem = pl.BlockSpec(memory_space=pltpu.VMEM)
    results = pl.pallas_call(
        forward_kernel,
        out_shape=outs,
        in_specs=[anywhere] * 12 + [vmem, anywhere] + [vmem] * 2,
        out_specs=[anywhere] * len(outs),
        scratch_shapes=scratch,
        compiler_params=pltpu.CompilerParams(
            collective_id=0, has_side_effects=True, vmem_limit_bytes=58 * 2**20
        ),
        name="layer_forward",
    )(tokens, memory, seg, mseg, prefix, w_self, w_so, w_cq, w_ckv, w_co, fc_in, fc_out, ad_down, ad_up, gain, bias)
    return Held(*results)


TOGETHER = 4


def backward_kernel(has_prefix, first_bound, bounds_s, *refs):
    if has_prefix:
        qkv_ref, bounds, ctx_ref, dctx_ref, lse_ref, pre_ref, dqkv_ref, dpre_ref, dk_acc, dv_acc, dq_acc, dpre_acc = refs
        q_at = lambda g, rows: qkv_ref[g, rows, 0:128]
        k_at = lambda g, rows: qkv_ref[g, rows, 128:256]
        v_at = lambda g, rows: qkv_ref[g, rows, 256:384]
    else:
        q_ref, kv_ref, bounds, ctx_ref, dctx_ref, lse_ref, dq_ref, dkv_ref, dk_acc, dv_acc, dq_acc = refs
        q_at = lambda g, rows: q_ref[rows, 128 * g : 128 * g + 128]
        k_at = lambda g, rows: kv_ref[g, rows, 0:128]
        v_at = lambda g, rows: kv_ref[g, rows, 128:256]
    scale = 0.125 * LOG2E
    dk_acc[...] = jnp.zeros_like(dk_acc)
    dv_acc[...] = jnp.zeros_like(dv_acc)
    kps, vps = [], []
    for g in range(TOGETHER):
        if has_prefix:
            kps.append(prefix_block(pre_ref[g, 0]))
            vps.append(prefix_block(pre_ref[g, 1]))
    if has_prefix:
        dpre_acc[...] = jnp.zeros_like(dpre_acc)

    def one(qi, _):
        q0 = pl.multiple_of(qi * QB, QB)
        span = pl.ds(q0, QB)
        lo = bounds[first_bound : first_bound + 1, span]
        hi = bounds[first_bound + 1 : first_bound + 2, span]
        inner, lse, qh, dh = [], [], [], []
        for g in range(TOGETHER):
            q = q_at(g, span)
            dctx = dctx_ref[span, 128 * g : 128 * g + 128]
            ctx = ctx_ref[span, 128 * g : 128 * g + 128]
            prod = (dctx.astype(jnp.float32) * ctx.astype(jnp.float32)).T
            inner.append([jnp.sum(prod[h * 64 : h * 64 + 64], axis=0, keepdims=True) for h in range(2)])
            lse.append([lse_ref[g, h : h + 1, span] for h in range(2)])
            qh.append([half_lanes(q, h) for h in range(2)])
            dh.append([half_lanes(dctx, h) for h in range(2)])
            if has_prefix:
                sp = prefix_rows(nt(kps[g], q) * scale)
                rows = lambda pair: jnp.concatenate([jnp.broadcast_to(t, (64, QB)) for t in pair], axis=0)
                pp = jnp.exp2(sp - rows(lse[g]))
                dpp = nt(vps[g], dctx)
                dsp = (pp * (dpp - rows(inner[g]))).astype(jnp.bfloat16)
                dpre_acc[g, 0] += nn(dsp, q)
                dpre_acc[g, 1] += nn(pp.astype(jnp.bfloat16), dctx)
                dq_acc[g] = tn(dsp, kps[g])
            else:
                dq_acc[g] = jnp.zeros((QB, 128), jnp.float32)

        def chunk(ki, _):
            k0 = pl.multiple_of(ki * KB, KB)
            keys = pl.ds(k0, KB)
            pos = k0 + lax.broadcasted_iota(jnp.int32, (KB, QB), 0)
            mask = (pos >= lo) & (pos <= hi)
            for g in range(TOGETHER):
                k = k_at(g, keys)
                v = v_at(g, keys)
                ps, dss = [], []
                for h in range(2):
                    s = nt(k, qh[g][h]) * scale
                    p = jnp.exp2(jnp.where(mask, s, NEG) - lse[g][h])
                    dp = nt(v, dh[g][h])
                    ds = (p * (dp - inner[g][h])).astype(jnp.bfloat16)
                    ps.append(p.astype(jnp.bfloat16))
                    dss.append(ds)
                dv_acc[g, keys, :] += nn(jnp.concatenate(ps, axis=1), jnp.concatenate(dh[g], axis=0))
                dq_acc[g] += tn(jnp.concatenate(dss, axis=0), jnp.concatenate([half_lanes(k, 0), half_lanes(k, 1)], axis=0))
                dk_acc[g, keys, :] += nn(jnp.concatenate(dss, axis=1), jnp.concatenate(qh[g], axis=0))
            return 0

        lowest = lax.div(bounds_s[first_bound, q0], KB)
        highest = lax.div(bounds_s[first_bound + 1, q0 + QB - 1], KB) + 1
        lax.fori_loop(lowest, highest, chunk, 0)
        for g in range(TOGETHER):
            dq = (dq_acc[g] * 0.125).astype(jnp.bfloat16)
            if has_prefix:
                dqkv_ref[g, span, 0:128] = dq
            else:
                dq_ref[span, 128 * g : 128 * g + 128] = dq
        return 0

    lax.fori_loop(0, SEQ // QB, one, 0)
    for g in range(TOGETHER):
        dk = (dk_acc[g] * 0.125).astype(jnp.bfloat16)
        dv = dv_acc[g].astype(jnp.bfloat16)
        if has_prefix:
            dqkv_ref[g, :, 128:256] = dk
            dqkv_ref[g, :, 256:384] = dv
            lane = lax.broadcasted_iota(jnp.int32, (32, 128), 1)
            for i, factor in ((0, 0.125), (1, 1.0)):
                dpre_ref[g, i] = jnp.where(lane < 64, dpre_acc[g, i, 0:32], dpre_acc[g, i, 64:96]) * factor
        else:
            dkv_ref[g, :, 0:128] = dk
            dkv_ref[g, :, 128:256] = dv


def backward_call(has_prefix, arrays, bounds, ctx, dctx, lse, pre=None):
    col = pl.BlockSpec((SEQ, 128 * TOGETHER), lambda j, *_: (0, j))
    piece = lambda width: pl.BlockSpec((TOGETHER, SEQ, width), lambda j, *_: (j, 0, 0))
    shape = jax.ShapeDtypeStruct
    bf16, f32 = jnp.bfloat16, jnp.float32
    pre_spec = pl.BlockSpec((TOGETHER, 2, 32, 128), lambda j, *_: (j, 0, 0, 0))
    if has_prefix:
        in_specs = [piece(384)]
        out_specs = [piece(384), pre_spec]
        out_shape = [shape((4, SEQ, 384), bf16), shape((4, 2, 32, 128), f32)]
    else:
        in_specs = [col, piece(256)]
        out_specs = [col, piece(256)]
        out_shape = [shape((SEQ, 512), bf16), shape((4, SEQ, 256), bf16)]
    in_specs += [
        pl.BlockSpec((8, SEQ), lambda j, *_: (0, 0)),
        col,
        col,
        pl.BlockSpec((TOGETHER, 8, SEQ), lambda j, *_: (j, 0, 0)),
    ]
    args = list(arrays) + [bounds, ctx, dctx, lse]
    scratch = [
        pltpu.VMEM((TOGETHER, SEQ, 128), f32),
        pltpu.VMEM((TOGETHER, SEQ, 128), f32),
        pltpu.VMEM((TOGETHER, QB, 128), f32),
    ]
    if has_prefix:
        in_specs.append(pre_spec)
        args.append(pre)
        scratch.append(pltpu.VMEM((TOGETHER, 2, 128, 128), f32))
    return pl.pallas_call(
        functools.partial(backward_kernel, has_prefix, 0 if has_prefix else 2),
        grid_spec=pltpu.PrefetchScalarGridSpec(
            num_scalar_prefetch=1, grid=(4 // TOGETHER,), in_specs=in_specs, out_specs=out_specs, scratch_shapes=scratch
        ),
        out_shape=out_shape,
        compiler_params=pltpu.CompilerParams(vmem_limit_bytes=60 * 2**20),
        cost_estimate=pl.CostEstimate(flops=10 * 8 * SEQ * SEQ * 64, bytes_accessed=10 * 2**20, transcendentals=8 * SEQ * SEQ),
        name="self_backward" if has_prefix else "cross_backward",
    )(bounds, *args)


HIDDEN = 512


def swap_halves(place, src, dst_there, dst_here, send, recv, local):
    moves = place.c != place.x
    away = pltpu.make_async_remote_copy(
        src_ref=src, dst_ref=dst_there, send_sem=send, recv_sem=recv, device_id=place.to_s, device_id_type=MESH
    )
    home = pltpu.make_async_copy(src, dst_here, local)

    def start():
        pl.when(moves)(away.start)
        pl.when(jnp.logical_not(moves))(home.start)

    def wait():
        pl.when(moves)(away.wait)
        pl.when(jnp.logical_not(moves))(home.wait)

    return start, wait


def feed_kernel(
    resid2, cotangent, gain, bias, wco_m_in, wco_o_in, fc_in, fin, fc_out, fout, ad, fad,
    out, grad_two, unit_sum, dctx,
    win, wout, down, up, slope, low, hidden, acc, gate, ada, branch_low, sem,
    cot, out_v, units, unit_send, unit_recv, near_send, near_recv, dctx_s, wco_m, wco_o, send, recv, local,
):
    place = Place()
    place.greet((place.to_x, place.to_y, place.to_d, place.to_c), True)
    c = place.c
    cot_start, cot_wait = swap_halves(place, cotangent, cot, cot, send.at[0], recv.at[0], local.at[0])
    out_copy = pltpu.make_async_copy(out_v, out, local.at[1])
    two_copy = pltpu.make_async_copy(acc, grad_two, local.at[2])
    co_copies = [
        pltpu.make_async_copy(wco_m_in, wco_m, local.at[3]),
        pltpu.make_async_copy(wco_o_in, wco_o, local.at[4]),
    ]
    cot_start()

    def there(slot, src, dst, device):
        return pltpu.make_async_remote_copy(
            src_ref=src, dst_ref=dst, send_sem=send.at[slot], recv_sem=recv.at[slot], device_id=device, device_id_type=MESH
        )

    half = resid2.shape[0]
    mine = pl.ds(pl.multiple_of(c * half, half), half)
    unit_core = there(2, unit_send, unit_recv, place.to_c)
    unit_near = [
        there(3 + i, near_send.at[i], near_recv.at[i], device) for i, device in enumerate((place.to_x, place.to_y, place.to_d))
    ]
    dctx_core = there(6, dctx_s, dctx.at[mine], place.to_c)
    bf16 = jnp.bfloat16
    per = fc_in.shape[1] // HIDDEN
    steps = 4 * per
    group = ad.shape[1]
    loads = []
    for j in range(steps):
        piece, part = divmod(j, per)
        cols = pl.ds(part * HIDDEN, HIDDEN)
        src = fc_in.at[:, cols] if piece == 0 else fin.at[piece - 1, :, cols]
        loads.append(pltpu.make_async_copy(src, win.at[j], sem.at[0, j]))
        src = fc_out.at[cols] if piece == 0 else fout.at[piece - 1, cols]
        loads.append(pltpu.make_async_copy(src, wout.at[j], sem.at[1, j]))
    ad_loads = []
    for piece in range(4):
        for i, dst in enumerate((down, up)):
            src = ad.at[i] if piece == 0 else fad.at[piece - 1, i]
            ad_loads.append(pltpu.make_async_copy(src, dst.at[pl.ds(group * piece, group)], sem.at[2, 2 * piece + i]))
    for copy in ad_loads + loads + co_copies:
        copy.start()

    rows_all = resid2.shape[0]
    tiles = rows_all // TILE
    at = lambda t: pl.ds(pl.multiple_of(t * TILE, TILE), TILE)

    def begin(t, _):
        rows = at(t)
        normed = norm_forward(resid2[rows, :], gain[1:2, :], bias[1:2, :])
        hidden[rows, :] = normed
        low[rows, :] = normed.astype(bf16)
        return 0

    lax.fori_loop(0, tiles, begin, 0)
    for copy in ad_loads:
        copy.wait()
    pre = nt(low[...], down[...])
    sigma = jax.nn.sigmoid(pre)
    gate[...] = sigma * (1.0 + pre * (1.0 - sigma))
    ada[...] = (pre * sigma).astype(bf16)
    acc[...] = adapter_scale * nn(ada[...], up[...])

    def ahead(j, _):
        for i, buf in enumerate((win, wout)):
            pltpu.make_async_copy(buf.at[j], buf.at[j], sem.at[i, j]).wait()
        pre = nn(low[...], win[j])
        phi = 0.5 * (1.0 + lax.erf(pre * 0.7071067811865476))
        slope[j] = phi + pre * jnp.exp(-0.5 * pre * pre) * 0.3989422804014327
        acc[...] += nn((pre * phi).astype(bf16), wout[j])
        return 0

    lax.fori_loop(0, steps, ahead, 0)

    def middle(t, _):
        rows = at(t)
        resid = hidden[rows, :] + acc[rows, :]
        normed, inv = norm_parts(resid)
        out_v[rows, :] = (normed * gain[2:3, :] + bias[2:3, :]).astype(bf16)
        scaled = cot[rows, :].astype(jnp.float32) * gain[2:3, :]
        grad = inv * (
            scaled
            - jnp.mean(scaled, axis=-1, keepdims=True)
            - normed * jnp.mean(scaled * normed, axis=-1, keepdims=True)
        )
        acc[rows, :] = grad
        branch_low[rows, :] = grad.astype(bf16)
        return 0

    cot_wait()
    lax.fori_loop(0, tiles, middle, 0)
    out_copy.start()
    grelu = (adapter_scale * nt(branch_low[...], up[...]) * gate[...]).astype(bf16)
    features = low.shape[1]
    some = group // 2
    for first, value in ((0, tn(grelu, low[...])), (features, adapter_scale * tn(ada[...], branch_low[...]))):
        for k in range(8):
            units[k // 2, k % 2, :, first : first + features] = value[some * k : some * (k + 1)]
    for i in range(4):
        unit_send[i] = units[i, 1 - c].astype(bf16)
    unit_core.start()
    acc[...] += nn(grelu, down[...])

    def behind(j, _):
        grad = (nt(branch_low[...], wout[j]) * slope[j]).astype(bf16)
        acc[...] += nt(grad, win[j])
        return 0

    lax.fori_loop(0, steps // 2, behind, 0)
    unit_core.wait()
    for i in range(3):
        near_send[i] = (units[i + 1, c] + unit_recv[i + 1].astype(jnp.float32)).astype(bf16)
    for copy in unit_near:
        copy.start()
    lax.fori_loop(steps // 2, steps, behind, 0)

    def finish(t, _):
        rows = at(t)
        grad = norm_backward(resid2[rows, :], gain[1:2, :], acc[rows, :])
        acc[rows, :] = grad
        small = grad.astype(bf16)
        low[rows, :] = small
        dctx_s[rows, :] = nt(small, wco_o[...]).astype(bf16)
        return 0

    for copy in co_copies:
        copy.wait()
    lax.fori_loop(0, tiles, finish, 0)
    dctx_core.start()
    two_copy.start()
    dctx[mine, :] = nt(low[...], wco_m[...]).astype(bf16)
    for copy in unit_near:
        copy.wait()
    total = units[0, c] + unit_recv[0].astype(jnp.float32)
    for i in range(3):
        total = total + near_recv[i].astype(jnp.float32)
    unit_sum[...] = total
    out_copy.wait()
    two_copy.wait()
    dctx_core.wait()


def feed_call(resid2, cot, gain, bias, wco_m, wco_o, fc_in, fin, fc_out, fout, ad, fad):
    bf16, f32 = jnp.bfloat16, jnp.float32
    rows, deep = resid2.shape
    shape = jax.ShapeDtypeStruct
    anywhere = pl.BlockSpec(memory_space=pl.ANY)
    vmem = pl.BlockSpec(memory_space=pltpu.VMEM)
    steps = 4 * fc_in.shape[1] // HIDDEN
    units = 4 * ad.shape[1]
    some = ad.shape[1] // 2
    return pl.pallas_call(
        feed_kernel,
        out_shape=[
            shape((rows, deep), bf16),
            shape((rows, deep), f32),
            shape((some, 2 * deep), f32),
            shape((2 * rows, 512), bf16),
        ],
        in_specs=[vmem, anywhere] + [vmem] * 2 + [anywhere] * 8,
        out_specs=[anywhere] * 2 + [vmem] * 2,
        scratch_shapes=[
            pltpu.VMEM((steps, deep, HIDDEN), bf16),
            pltpu.VMEM((steps, HIDDEN, deep), bf16),
            pltpu.VMEM((units, deep), bf16),
            pltpu.VMEM((units, deep), bf16),
            pltpu.VMEM((steps, rows, HIDDEN), f32),
            pltpu.VMEM((rows, deep), bf16),
            pltpu.VMEM((rows, deep), f32),
            pltpu.VMEM((rows, deep), f32),
            pltpu.VMEM((rows, units), f32),
            pltpu.VMEM((rows, units), bf16),
            pltpu.VMEM((rows, deep), bf16),
            pltpu.SemaphoreType.DMA((3, 8)),
            pltpu.VMEM((rows, deep), bf16),
            pltpu.VMEM((rows, deep), bf16),
            pltpu.VMEM((4, 2, some, 2 * deep), f32),
            pltpu.VMEM((4, some, 2 * deep), bf16),
            pltpu.VMEM((4, some, 2 * deep), bf16),
            pltpu.VMEM((3, some, 2 * deep), bf16),
            pltpu.VMEM((3, some, 2 * deep), bf16),
            pltpu.VMEM((rows, 512), bf16),
            pltpu.VMEM(wco_m.shape, bf16),
            pltpu.VMEM(wco_o.shape, bf16),
            pltpu.SemaphoreType.DMA((7,)),
            pltpu.SemaphoreType.DMA((7,)),
            pltpu.SemaphoreType.DMA((5,)),
        ],
        compiler_params=pltpu.CompilerParams(
            collective_id=1, has_side_effects=True, vmem_limit_bytes=61 * 2**20
        ),
        name="feed_forward",
    )(resid2, cot, gain, bias, wco_m, wco_o, fc_in, fin, fc_out, fout, ad, fad)


def query_kernel(
    dq_in, dkv_in, wkv_in, wq_m_in, wq_o_in, two_in, resid_in, wso_m_in, wso_o_in, gain,
    one_out, dctx, mem_out,
    dq, dkv, wkv, wq_m, wq_o, grad_two, resid1, wso_m, wso_o,
    grad_one, mem_sum, dq_o, mem_s, mem_r, dctx_s, dctx_m, low, send, recv, local,
):
    bf16 = jnp.bfloat16
    place = Place()
    c = place.c
    half = resid1.shape[0]
    mine = pl.ds(pl.multiple_of(c * half, half), half)
    others = pl.ds(pl.multiple_of((1 - c) * half, half), half)

    def there(slot, src, dst):
        return pltpu.make_async_remote_copy(
            src_ref=src, dst_ref=dst, send_sem=send.at[slot], recv_sem=recv.at[slot], device_id=place.to_c, device_id_type=MESH
        )

    def here(slot, src, dst):
        return pltpu.make_async_copy(src, dst, local.at[slot])

    wkv_copy, dkv_far, dkv_near = here(0, wkv_in, wkv), here(1, dkv_in.at[:, others], dkv.at[:, others]), here(2, dkv_in.at[:, mine], dkv.at[:, mine])
    pairs = (
        (dq_in.at[mine], dq), (wq_m_in, wq_m), (wq_o_in, wq_o), (two_in, grad_two), (resid_in, resid1), (wso_o_in, wso_o), (wso_m_in, wso_m)
    )
    rest = [here(3 + i, src, dst) for i, (src, dst) in enumerate(pairs)]
    for copy in [wkv_copy, dkv_far] + rest + [dkv_near]:
        copy.start()
    one_copy, mem_copy, dctx_copy = here(10, grad_one, one_out), here(11, mem_sum, mem_out), here(12, dctx_m, dctx.at[mine])
    place.greet((place.to_c,), False)
    dq_core = there(0, dq_in.at[others], dq_o)
    mem_core = there(1, mem_s, mem_r)
    dctx_core = there(2, dctx_s, dctx.at[mine])
    dq_core.start()
    tiles = half // TILE
    at = lambda t: pl.ds(pl.multiple_of(t * TILE, TILE), TILE)
    place_at = lambda first, t: pl.ds(pl.multiple_of(first * half + t * TILE, TILE), TILE)

    def memory_rows(rows):
        return sum(nt(dkv[p, rows, :], wkv[p]) for p in range(4))

    def far(t, _):
        mem_s[at(t), :] = memory_rows(place_at(1 - c, t)).astype(bf16)
        return 0

    wkv_copy.wait()
    dkv_far.wait()
    lax.fori_loop(0, tiles, far, 0)
    mem_core.start()
    for copy in rest:
        copy.wait()
    dq_core.wait()

    def one(t, _):
        rows = at(t)
        grad_in = grad_two[rows, :] + nt(dq[rows, :], wq_m[...]) + nt(dq_o[rows, :], wq_o[...])
        grad = norm_backward(resid1[rows, :], gain[0:1, :], grad_in)
        grad_one[rows, :] = grad
        small = grad.astype(bf16)
        low[rows, :] = small
        dctx_s[rows, :] = nt(small, wso_o[...]).astype(bf16)
        return 0

    lax.fori_loop(0, tiles, one, 0)
    dctx_core.start()
    one_copy.start()
    dctx_m[...] = nt(low[...], wso_m[...]).astype(bf16)
    dctx_copy.start()
    mem_core.wait()
    dkv_near.wait()

    def near(t, _):
        mem_sum[at(t), :] = (memory_rows(place_at(c, t)) + mem_r[at(t), :].astype(jnp.float32)).astype(bf16)
        return 0

    lax.fori_loop(0, tiles, near, 0)
    mem_copy.start()
    for copy in (dctx_core, one_copy, dctx_copy, mem_copy):
        copy.wait()


def query_call(dq, dkv, wkv, wq_m, wq_o, grad_two, resid1, wso_m, wso_o, gain):
    bf16, f32 = jnp.bfloat16, jnp.float32
    half, deep = resid1.shape
    shape = jax.ShapeDtypeStruct
    vmem = pl.BlockSpec(memory_space=pltpu.VMEM)
    anywhere = pl.BlockSpec(memory_space=pl.ANY)
    return pl.pallas_call(
        query_kernel,
        out_shape=[shape((half, deep), f32), shape((2 * half, 512), bf16), shape((half, deep), bf16)],
        in_specs=[anywhere] * 9 + [vmem],
        out_specs=[anywhere] * 3,
        scratch_shapes=[pltpu.VMEM((half, 512), bf16)]
        + [pltpu.VMEM(value.shape, value.dtype) for value in (dkv, wkv, wq_m, wq_o, grad_two, resid1, wso_m, wso_o)]
        + [
            pltpu.VMEM((half, deep), f32),
            pltpu.VMEM((half, deep), bf16),
            pltpu.VMEM((half, 512), bf16),
            pltpu.VMEM((half, deep), bf16),
            pltpu.VMEM((half, deep), bf16),
            pltpu.VMEM((half, 512), bf16),
            pltpu.VMEM((half, 512), bf16),
            pltpu.VMEM((half, deep), bf16),
            pltpu.SemaphoreType.DMA((3,)),
            pltpu.SemaphoreType.DMA((3,)),
            pltpu.SemaphoreType.DMA((13,)),
        ],
        compiler_params=pltpu.CompilerParams(collective_id=2, has_side_effects=True, vmem_limit_bytes=60 * 2**20),
        name="query_backward",
    )(dq, dkv, wkv, wq_m, wq_o, grad_two, resid1, wso_m, wso_o, gain)


def last_kernel(
    planes, dqkv_in, wself_in, one_in, blocks_in, unit_in,
    input_out, prefix_grad, down_grad, up_grad,
    dqkv, wself, grad_one, blocks, unit_sum, part_s, part_r, out_s, pre_near, pre_sum, pre_z, pre_c, unit_s, unit_z, unit_all, send, recv, local,
):
    bf16, f32 = jnp.bfloat16, jnp.float32
    place = Place()
    c, x, z = place.c, place.x, place.z
    steps = []
    step = 1
    while step < planes:
        other = z + step - 2 * step * lax.rem(lax.div(z, step), 2)
        steps.append((2 * other + c, place.head))
        step *= 2
    moves = c != x
    stays = c == x
    half = grad_one.shape[0]
    slots = []

    def there(src, dst, device):
        slot = len(slots)
        slots.append(slot)
        return pltpu.make_async_remote_copy(
            src_ref=src, dst_ref=dst, send_sem=send.at[slot], recv_sem=recv.at[slot], device_id=device, device_id_type=MESH
        )

    tiles = half // TILE
    at = lambda t: pl.ds(t * TILE, TILE)
    place_at = lambda first, t: pl.ds(pl.multiple_of(first * half + t * TILE, TILE), TILE)

    def here(slot, src, dst):
        return pltpu.make_async_copy(src, dst, local.at[slot])

    loads = [here(0, wself_in, wself), here(1, blocks_in, blocks), here(2, unit_in, unit_sum), here(3, one_in, grad_one)]
    far_loads = [here(4 + t, dqkv_in.at[:, place_at(1 - c, t)], dqkv.at[:, place_at(1 - c, t)]) for t in range(tiles)]
    near_loads = [
        here(4 + tiles + t, dqkv_in.at[:, place_at(c, t)], dqkv.at[:, place_at(c, t)]) for t in range(tiles)
    ]
    for copy in [loads[1], loads[2], far_loads[0], loads[0]] + far_loads[1:] + near_loads + [loads[3]]:
        copy.start()

    place.greet([place.to_x, place.to_y, place.to_d, place.to_c] + steps, True)
    pre_copies = [
        there(blocks.at[i + 1], pre_near.at[i], device) for i, device in enumerate((place.to_x, place.to_y, place.to_d))
    ]
    pre_steps = [there(pre_sum.at[i], pre_z.at[i], device) for i, device in enumerate(steps)]
    pre_core = there(pre_sum.at[len(steps)], pre_c, place.to_c)
    unit_steps = [there(unit_s.at[i], unit_z.at[i], device) for i, device in enumerate(steps)]
    unit_core = there(unit_s.at[len(steps)], unit_z.at[len(steps)], place.to_c)
    part_copies = [there(part_s.at[at(t)], part_r.at[at(t)], place.to_c) for t in range(tiles)]
    out_copies = [there(out_s.at[at(t)], input_out.at[at(t)], place.to_s) for t in range(tiles)]
    own_copies = [here(4 + 2 * tiles + t, out_s.at[at(t)], input_out.at[at(t)]) for t in range(tiles)]
    loads[1].wait()
    for copy in pre_copies:
        copy.start()
    loads[2].wait()
    unit_s[0] = unit_sum[...].astype(bf16)
    unit_steps[0].start()

    def input_rows(rows):
        return sum(nt(dqkv[p, rows, :], wself[p]) for p in range(4))

    loads[0].wait()
    far_loads[0].wait()
    part_s[at(0), :] = input_rows(place_at(1 - c, 0)).astype(bf16)
    part_copies[0].start()
    for copy in pre_copies:
        copy.wait()
    pre_sum[0] = blocks[0] + pre_near[0] + pre_near[1] + pre_near[2]
    pre_steps[0].start()
    for t in range(1, tiles):
        far_loads[t].wait()
        part_s[at(t), :] = input_rows(place_at(1 - c, t)).astype(bf16)
        part_copies[t].start()

    def advance(i):
        pre_steps[i].wait()
        pre_sum[i + 1] = pre_sum[i] + pre_z[i]
        if i + 1 < len(steps):
            pre_steps[i + 1].start()
        else:
            pre_core.start()
        unit_steps[i].wait()
        unit_s[i + 1] = (unit_s[i].astype(f32) + unit_z[i].astype(f32)).astype(bf16)
        if i + 1 < len(steps):
            unit_steps[i + 1].start()
        else:
            unit_core.start()

    loads[3].wait()
    for t in range(tiles):
        near_loads[t].wait()
        part_copies[t].wait()
        total = input_rows(place_at(c, t)) + part_r[at(t), :].astype(f32) + grad_one[at(t), :]
        out_s[at(t), :] = total.astype(bf16)
        pl.when(moves)(out_copies[t].start)
        pl.when(stays)(own_copies[t].start)
        if t < len(steps):
            advance(t)
    for i in range(tiles, len(steps)):
        advance(i)
    pre_core.wait()
    unit_core.wait()
    my_lanes = pl.ds(pl.multiple_of(c * 128, 128), 128)
    other_lanes = pl.ds(pl.multiple_of((1 - c) * 128, 128), 128)
    prefix_grad[:, :, my_lanes] = pre_sum[len(steps)]
    prefix_grad[:, :, other_lanes] = pre_c[...]
    some = unit_sum.shape[0]
    unit_all[pl.ds(pl.multiple_of(c * some, some), some), :] = unit_s[len(steps)].astype(f32)
    unit_all[pl.ds(pl.multiple_of((1 - c) * some, some), some), :] = unit_z[len(steps)].astype(f32)
    features = grad_one.shape[1]
    down_grad[...] = unit_all[:, 0:features].T
    up_grad[...] = unit_all[:, features : 2 * features]

    for t in range(tiles):
        pl.when(moves)(out_copies[t].wait)
        pl.when(stays)(own_copies[t].wait)


def last_call(planes, dqkv, wself, grad_one, blocks, unit_sum):
    bf16, f32 = jnp.bfloat16, jnp.float32
    half, deep = grad_one.shape
    some = unit_sum.shape[0]
    count = planes.bit_length() - 1
    shape = jax.ShapeDtypeStruct
    vmem = pl.BlockSpec(memory_space=pltpu.VMEM)
    anywhere = pl.BlockSpec(memory_space=pl.ANY)
    return pl.pallas_call(
        functools.partial(last_kernel, planes),
        out_shape=[
            shape((half, deep), bf16),
            shape((2, 32, 256), f32),
            shape((deep, 2 * some), f32),
            shape((2 * some, deep), f32),
        ],
        in_specs=[anywhere] * 5,
        out_specs=[anywhere] + [vmem] * 3,
        scratch_shapes=[pltpu.VMEM(value.shape, value.dtype) for value in (dqkv, wself, grad_one, blocks, unit_sum)]
        + [
            pltpu.VMEM((half, deep), bf16),
            pltpu.VMEM((half, deep), bf16),
            pltpu.VMEM((half, deep), bf16),
            pltpu.VMEM((3, 2, 32, 128), f32),
            pltpu.VMEM((count + 1, 2, 32, 128), f32),
            pltpu.VMEM((count, 2, 32, 128), f32),
            pltpu.VMEM((2, 32, 128), f32),
            pltpu.VMEM((count + 1, some, 2 * deep), bf16),
            pltpu.VMEM((count + 1, some, 2 * deep), bf16),
            pltpu.VMEM((2 * some, 2 * deep), f32),
            pltpu.SemaphoreType.DMA((3 + 2 * count + 2 + 2 * (half // TILE),)),
            pltpu.SemaphoreType.DMA((3 + 2 * count + 2 + 2 * (half // TILE),)),
            pltpu.SemaphoreType.DMA((4 + 3 * (half // TILE),)),
        ],
        compiler_params=pltpu.CompilerParams(collective_id=3, has_side_effects=True, vmem_limit_bytes=60 * 2**20),
        name="last_sums",
    )(dqkv, wself, grad_one, blocks, unit_sum)


AXES = ("rows", "heads")


def fast_fits(mesh):
    rows, heads = mesh.shape["rows"], mesh.shape["heads"]
    return heads == 4 and rows % 4 == 0 and (rows & (rows - 1)) == 0


def pairs_of(rows, move):
    def number(z, c, y, x):
        return (z * 2 + c) * 4 + y * 2 + x

    found = []
    for z in range(rows // 2):
        for c in range(2):
            for y in range(2):
                for x in range(2):
                    found.append((number(z, c, y, x), number(*move(z, c, y, x))))
    return found


def swapped_rows(rows, value):
    def swapped(z, c, y, x):
        return (z, x, y, c)

    crossing = [pair for pair in pairs_of(rows, swapped) if pair[0] != pair[1]]
    stays = lax.axis_index("rows") % 2 == lax.axis_index("heads") % 2
    return jnp.where(stays, value, lax.ppermute(value, AXES, crossing))


def fast_body(
    rows,
    tokens,
    memory,
    cotangent,
    dec_seg,
    mem_seg,
    w_self,
    w_self_out,
    w_cross_q,
    w_cross_kv,
    w_cross_out,
    fc_in,
    fc_out,
    ad_down,
    ad_up,
    prefix,
    ln_gain,
    ln_bias,
):
    count = prefix.shape[1]
    held = forward_call(
        tokens,
        memory,
        dec_seg.reshape(2, 1, SEQ),
        mem_seg.reshape(2, 1, MLEN),
        jnp.pad(prefix, ((0, 0), (0, 32 - count), (0, 0))),
        w_self,
        w_self_out,
        w_cross_q,
        w_cross_kv,
        w_cross_out,
        fc_in,
        fc_out,
        ad_down,
        ad_up,
        ln_gain,
        ln_bias,
    )
    out_own, grad_two, unit_sum, cross_dctx = feed_call(
        held.resid2, cotangent, ln_gain, ln_bias, held.wco_m, held.wco_o,
        fc_in, held.fin, fc_out, held.fout, held.ad, held.fad,
    )
    output = swapped_rows(rows, out_own)
    cross_dq, cross_dkv = backward_call(
        False, (held.q, held.kv), held.bounds, held.cctx, cross_dctx, held.clse
    )
    grad_one, self_dctx, memory_sum = query_call(
        cross_dq, cross_dkv, held.wkv, held.wq_m, held.wq_o, grad_two, held.resid1, held.wso_m, held.wso_o, ln_gain
    )
    grad_memory = swapped_rows(rows, memory_sum).astype(jnp.float32)
    self_dqkv, prefix_blocks = backward_call(
        True, (held.qkv,), held.bounds, held.sctx, self_dctx, held.slse, held.pre
    )
    grad_input, prefix_grad, down_grad, up_grad = last_call(
        rows // 2, self_dqkv, held.wself, grad_one, prefix_blocks, unit_sum
    )
    return (output, grad_input.astype(jnp.float32), grad_memory, prefix_grad[:, :count], down_grad, up_grad)


def solution(mesh):
    in_specs = (
        P(("rows", "heads"), None),
        P(("rows", "heads"), None),
        P(("rows", "heads"), None),
        P("rows"),
        P("rows"),
        P(None, None, "heads"),
        P("heads", None),
        P(None, "heads"),
        P(None, None, "heads"),
        P("heads", None),
        P(None, "heads"),
        P("heads", None),
        P(None, "heads"),
        P("heads", None),
        P(None, None, "heads"),
        P(),
        P(),
    )
    out_specs = (
        P(("rows", "heads"), None),
        P(("rows", "heads"), None),
        P(("rows", "heads"), None),
        P(None, None, "heads"),
        P(None, "heads"),
        P("heads", None),
    )
    chosen = functools.partial(fast_body, mesh.shape["rows"]) if fast_fits(mesh) else body
    return jax.shard_map(chosen, mesh=mesh, in_specs=in_specs, out_specs=out_specs, check_vma=False)
```

```python
import functools
import math
import typing

import jax
import jax.numpy as jnp
from jax import lax
from jax.experimental import pallas as pl
from jax.experimental.pallas import tpu as pltpu
from jax.sharding import PartitionSpec as P

HD = 64
SEQ = 1024
MLEN = 1024


epsilon = 1e-05
adapter_scale = 4.0
masked_score = -1e30


def dot_right(left, right):
    return lax.dot_general(
        left, right, (((1,), (1,)), ((), ())), preferred_element_type=jnp.float32
    )


def dot_left(left, right):
    return lax.dot_general(
        left, right, (((0,), (0,)), ((), ())), preferred_element_type=jnp.float32
    )


def norm_parts(resid):
    average = jnp.mean(resid, axis=-1, keepdims=True)
    centered = resid - average
    inv_scale = lax.rsqrt(jnp.mean(centered * centered, axis=-1, keepdims=True) + epsilon)
    return (centered * inv_scale, inv_scale)


def norm_forward(resid, gain, shift):
    normed, inv_scale = norm_parts(resid)
    return normed * gain + shift


def norm_backward(resid, gain, grad_out):
    normed, inv_scale = norm_parts(resid)
    scaled = grad_out * gain
    return inv_scale * (
        scaled
        - jnp.mean(scaled, axis=-1, keepdims=True)
        - normed * jnp.mean(scaled * normed, axis=-1, keepdims=True)
    )


def gelu_slope(pre_gelu):
    return (
        0.5 * (1.0 + lax.erf(pre_gelu * 0.7071067811865476))
        + pre_gelu * jnp.exp(-0.5 * pre_gelu * pre_gelu) * 0.3989422804014327
    )


def silu_slope(pre_relu):
    sigma = jax.nn.sigmoid(pre_relu)
    return sigma * (1.0 + pre_relu * (1.0 - sigma))


def to_heads(arrays, heads_here):
    return arrays.reshape(arrays.shape[0], arrays.shape[1], heads_here, HD).transpose(0, 2, 1, 3)


def from_heads(arrays):
    return arrays.transpose(0, 2, 1, 3).reshape(
        arrays.shape[0] * arrays.shape[2], arrays.shape[1] * arrays.shape[3]
    )


def join_blocks(stacked):
    moved = jnp.moveaxis(stacked, 0, 1)
    return moved.reshape((moved.shape[0], moved.shape[1] * moved.shape[2]) + moved.shape[3:])


def block_mask(row_segs, key_segs, offset, causal):
    allowed = row_segs[:, None] == key_segs[None, :]
    if causal:
        row_places = offset + lax.iota(jnp.int32, row_segs.shape[0])
        key_places = lax.iota(jnp.int32, key_segs.shape[0])
        allowed = allowed & (key_places[None, :] <= row_places[:, None])
    return allowed


def block_scores(queries, key_rows, allowed, prefix_keys):
    qk_scale = HD ** (-0.5)
    token_scores = (
        jnp.einsum("hqe,hke->hqk", queries, key_rows, preferred_element_type=jnp.float32) * qk_scale
    )
    token_scores = jnp.where(allowed[None], token_scores, masked_score)
    if prefix_keys is None:
        return (token_scores, None)
    prefix_scores = (
        jnp.einsum("hqe,hpe->hqp", queries, prefix_keys, preferred_element_type=jnp.float32)
        * qk_scale
    )
    return (token_scores, prefix_scores)


def attend_block(queries, key_rows, value_rows, allowed, prefix_keys, prefix_values):
    token_scores, prefix_scores = block_scores(queries, key_rows, allowed, prefix_keys)
    row_max = jnp.max(token_scores, axis=-1, keepdims=True)
    if prefix_scores is not None:
        row_max = jnp.maximum(row_max, jnp.max(prefix_scores, axis=-1, keepdims=True))
    token_weights = jnp.exp(token_scores - row_max)
    row_total = jnp.sum(token_weights, axis=-1, keepdims=True)
    if prefix_scores is not None:
        prefix_weights = jnp.exp(prefix_scores - row_max)
        row_total = row_total + jnp.sum(prefix_weights, axis=-1, keepdims=True)
    context = jnp.einsum(
        "hqk,hke->hqe",
        (token_weights / row_total).astype(jnp.bfloat16),
        value_rows,
        preferred_element_type=jnp.float32,
    )
    if prefix_scores is not None:
        context = context + jnp.einsum(
            "hqp,hpe->hqe",
            (prefix_weights / row_total).astype(jnp.bfloat16),
            prefix_values,
            preferred_element_type=jnp.float32,
        )
    return (context.astype(jnp.bfloat16), row_max + jnp.log(row_total))


def attend_back(
    queries, key_rows, value_rows, allowed, prefix_keys, prefix_values, log_total, context_grad
):
    qk_scale = HD ** (-0.5)
    token_scores, prefix_scores = block_scores(queries, key_rows, allowed, prefix_keys)
    token_probs = jnp.exp(token_scores - log_total)
    token_dprob = jnp.einsum(
        "hqe,hke->hqk", context_grad, value_rows, preferred_element_type=jnp.float32
    )
    inner = jnp.sum(token_probs * token_dprob, axis=-1, keepdims=True)
    if prefix_scores is not None:
        prefix_probs = jnp.exp(prefix_scores - log_total)
        prefix_dprob = jnp.einsum(
            "hqe,hpe->hqp", context_grad, prefix_values, preferred_element_type=jnp.float32
        )
        inner = inner + jnp.sum(prefix_probs * prefix_dprob, axis=-1, keepdims=True)
    token_dscore = (token_probs * (token_dprob - inner)).astype(jnp.bfloat16)
    query_grad = jnp.einsum(
        "hqk,hke->hqe", token_dscore, key_rows, preferred_element_type=jnp.float32
    )
    key_grad = (
        jnp.einsum("hqk,hqe->hke", token_dscore, queries, preferred_element_type=jnp.float32)
        * qk_scale
    )
    value_grad = jnp.einsum(
        "hqk,hqe->hke",
        token_probs.astype(jnp.bfloat16),
        context_grad,
        preferred_element_type=jnp.float32,
    )
    if prefix_scores is None:
        return (query_grad * qk_scale, (key_grad, value_grad))
    prefix_dscore = (prefix_probs * (prefix_dprob - inner)).astype(jnp.bfloat16)
    query_grad = query_grad + jnp.einsum(
        "hqp,hpe->hqe", prefix_dscore, prefix_keys, preferred_element_type=jnp.float32
    )
    prefix_key_grad = (
        jnp.einsum("hqp,hqe->hpe", prefix_dscore, queries, preferred_element_type=jnp.float32)
        * qk_scale
    )
    prefix_value_grad = jnp.einsum(
        "hqp,hqe->hpe",
        prefix_probs.astype(jnp.bfloat16),
        context_grad,
        preferred_element_type=jnp.float32,
    )
    return (query_grad * qk_scale, (key_grad, value_grad, prefix_key_grad, prefix_value_grad))


def sequence_forward(
    queries, key_rows, value_rows, row_segs, key_segs, prefix_keys, prefix_values, causal
):
    seq_width = queries.shape[1]
    block_rows = min(512, seq_width)

    def one_block(block_index):
        offset = block_index * block_rows
        allowed = block_mask(
            lax.dynamic_slice_in_dim(row_segs, offset, block_rows, 0), key_segs, offset, causal
        )
        query_part = lax.dynamic_slice_in_dim(queries, offset, block_rows, 1)
        return attend_block(query_part, key_rows, value_rows, allowed, prefix_keys, prefix_values)

    context, log_total = lax.map(one_block, jnp.arange(seq_width // block_rows, dtype=jnp.int32))
    return (join_blocks(context), join_blocks(log_total))


def sequence_backward(
    queries,
    key_rows,
    value_rows,
    row_segs,
    key_segs,
    prefix_keys,
    prefix_values,
    causal,
    log_total,
    context_grad,
):
    seq_width = queries.shape[1]
    block_rows = min(512, seq_width)
    key_zero = jnp.zeros(key_rows.shape, jnp.float32)
    initial = (key_zero, key_zero)
    if prefix_keys is not None:
        prefix_zero = jnp.zeros(prefix_keys.shape, jnp.float32)
        initial = initial + (prefix_zero, prefix_zero)

    def one_block(running, block_index):
        offset = block_index * block_rows
        allowed = block_mask(
            lax.dynamic_slice_in_dim(row_segs, offset, block_rows, 0), key_segs, offset, causal
        )
        query_part = lax.dynamic_slice_in_dim(queries, offset, block_rows, 1)
        total_part = lax.dynamic_slice_in_dim(log_total, offset, block_rows, 1)
        grad_part = lax.dynamic_slice_in_dim(context_grad, offset, block_rows, 1)
        query_grad, block_grads = attend_back(
            query_part,
            key_rows,
            value_rows,
            allowed,
            prefix_keys,
            prefix_values,
            total_part,
            grad_part,
        )
        return (tuple((summed + added for summed, added in zip(running, block_grads))), query_grad)

    running, query_grad = lax.scan(
        one_block, initial, jnp.arange(seq_width // block_rows, dtype=jnp.int32)
    )
    outputs = (
        join_blocks(query_grad).astype(jnp.bfloat16),
        running[0].astype(jnp.bfloat16),
        running[1].astype(jnp.bfloat16),
    )
    return outputs + running[2:]


def gather_rows(row_share):
    return lax.all_gather(row_share, "heads", axis=0, tiled=True)


def gather_grads(row_share):
    return lax.all_gather(row_share, "heads", axis=0, tiled=True)


def sum_rows(partial_value):
    return lax.psum_scatter(partial_value, "heads", scatter_dimension=0, tiled=True)


def sum_grads(partial_value):
    return lax.psum_scatter(partial_value, "heads", scatter_dimension=0, tiled=True)


def body(
    tokens,
    memory,
    cotangent,
    dec_seg,
    mem_seg,
    w_self,
    w_self_out,
    w_cross_q,
    w_cross_kv,
    w_cross_out,
    fc_in,
    fc_out,
    ad_down,
    ad_up,
    prefix,
    ln_gain,
    ln_bias,
):
    local_width = w_self.shape[2]
    heads_here = local_width // HD
    seg_dec = dec_seg.reshape(-1, SEQ)
    seg_mem = mem_seg.reshape(-1, MLEN)
    seq_count = seg_dec.shape[0]
    prefix_heads = to_heads(prefix, heads_here)
    prefix_keys = prefix_heads[0]
    prefix_values = prefix_heads[1]
    gathered_x = gather_rows(tokens)
    self_proj = jnp.einsum(
        "td,cdn->ctn", gathered_x, w_self, preferred_element_type=jnp.float32
    ).astype(jnp.bfloat16)
    self_proj = self_proj.reshape(3, seq_count, SEQ, local_width)
    self_queries = to_heads(self_proj[0], heads_here)
    self_keys = to_heads(self_proj[1], heads_here)
    self_values = to_heads(self_proj[2], heads_here)

    def self_forward(packed):
        return sequence_forward(
            packed[0], packed[1], packed[2], packed[3], packed[3], prefix_keys, prefix_values, True
        )

    self_context, self_total = lax.map(
        self_forward, (self_queries, self_keys, self_values, seg_dec)
    )
    attn_partial = jnp.dot(from_heads(self_context), w_self_out, preferred_element_type=jnp.float32)
    resid_one = tokens.astype(jnp.float32) + sum_rows(attn_partial)
    hidden_one = norm_forward(resid_one, ln_gain[0], ln_bias[0])
    gathered_one = gather_rows(hidden_one.astype(jnp.bfloat16))
    gathered_mem = lax.all_gather(memory, "heads", axis=0, tiled=True)
    cross_rows = jnp.dot(gathered_one, w_cross_q, preferred_element_type=jnp.float32).astype(
        jnp.bfloat16
    )
    cross_proj = jnp.einsum(
        "td,cdn->ctn", gathered_mem, w_cross_kv, preferred_element_type=jnp.float32
    ).astype(jnp.bfloat16)
    cross_queries = to_heads(cross_rows.reshape(seq_count, SEQ, local_width), heads_here)
    cross_proj = cross_proj.reshape(2, seq_count, MLEN, local_width)
    cross_keys = to_heads(cross_proj[0], heads_here)
    cross_values = to_heads(cross_proj[1], heads_here)

    def cross_forward(packed):
        return sequence_forward(
            packed[0], packed[1], packed[2], packed[3], packed[4], None, None, False
        )

    cross_context, cross_total = lax.map(
        cross_forward, (cross_queries, cross_keys, cross_values, seg_dec, seg_mem)
    )
    cross_partial = jnp.dot(
        from_heads(cross_context), w_cross_out, preferred_element_type=jnp.float32
    )
    resid_two = hidden_one + sum_rows(cross_partial)
    hidden_two = norm_forward(resid_two, ln_gain[1], ln_bias[1])
    hidden_low = hidden_two.astype(jnp.bfloat16)
    full_in, full_out, full_down, full_up = (fc_in, fc_out, ad_down, ad_up)
    ffn_rows = gather_rows(hidden_low)
    pre_gelu = jnp.dot(ffn_rows, full_in, preferred_element_type=jnp.float32)
    activated = jax.nn.gelu(pre_gelu, approximate=False).astype(jnp.bfloat16)
    pre_relu = jnp.dot(ffn_rows, full_down, preferred_element_type=jnp.float32)
    adapted = (pre_relu * jax.nn.sigmoid(pre_relu)).astype(jnp.bfloat16)
    branch = jnp.dot(
        activated, full_out, preferred_element_type=jnp.float32
    ) + adapter_scale * jnp.dot(adapted, full_up, preferred_element_type=jnp.float32)
    resid_three = hidden_two + sum_rows(branch)
    output = norm_forward(resid_three, ln_gain[2], ln_bias[2]).astype(jnp.bfloat16)
    grad_three = norm_backward(resid_three, ln_gain[2], cotangent.astype(jnp.float32))
    grad_branch = grad_three.astype(jnp.bfloat16)
    branch_rows = gather_grads(grad_branch)
    grad_gelu = (dot_right(branch_rows, full_out) * gelu_slope(pre_gelu)).astype(jnp.bfloat16)
    grad_relu = (adapter_scale * dot_right(branch_rows, full_up) * silu_slope(pre_relu)).astype(
        jnp.bfloat16
    )
    up_grad = adapter_scale * dot_left(adapted, branch_rows)
    down_grad = dot_left(ffn_rows, grad_relu)
    hidden_partial = dot_right(grad_gelu, full_in) + dot_right(grad_relu, full_down)
    grad_two_in = grad_three + sum_grads(hidden_partial)
    down_grad, up_grad = (
        lax.psum(down_grad.astype(jnp.bfloat16), "rows").astype(jnp.float32),
        lax.psum(up_grad.astype(jnp.bfloat16), "rows").astype(jnp.float32),
    )
    grad_two = norm_backward(resid_two, ln_gain[1], grad_two_in)
    cross_out_rows = gather_grads(grad_two.astype(jnp.bfloat16))
    cross_dctx = dot_right(cross_out_rows, w_cross_out).astype(jnp.bfloat16)
    cross_dctx = to_heads(cross_dctx.reshape(seq_count, SEQ, local_width), heads_here)

    def cross_back(packed):
        return sequence_backward(
            packed[0],
            packed[1],
            packed[2],
            packed[3],
            packed[4],
            None,
            None,
            False,
            packed[5],
            packed[6],
        )

    cross_qgrad, cross_kgrad, cross_vgrad = lax.map(
        cross_back,
        (cross_queries, cross_keys, cross_values, seg_dec, seg_mem, cross_total, cross_dctx),
    )
    memory_kv = jnp.stack([from_heads(cross_kgrad), from_heads(cross_vgrad)])
    one_partial = dot_right(from_heads(cross_qgrad), w_cross_q)
    grad_one_in = grad_two + sum_grads(one_partial)
    memory_partial = jnp.einsum(
        "ctn,cdn->td", memory_kv, w_cross_kv, preferred_element_type=jnp.float32
    )
    grad_memory = lax.psum_scatter(
        memory_partial.astype(jnp.bfloat16), "heads", scatter_dimension=0, tiled=True
    ).astype(jnp.float32)
    grad_one = norm_backward(resid_one, ln_gain[0], grad_one_in)
    attn_rows = gather_grads(grad_one.astype(jnp.bfloat16))
    self_dctx = dot_right(attn_rows, w_self_out).astype(jnp.bfloat16)
    self_dctx = to_heads(self_dctx.reshape(seq_count, SEQ, local_width), heads_here)

    def self_back(running, packed):
        query_grad, key_grad, value_grad, pkey_grad, pvalue_grad = sequence_backward(
            packed[0],
            packed[1],
            packed[2],
            packed[3],
            packed[3],
            prefix_keys,
            prefix_values,
            True,
            packed[4],
            packed[5],
        )
        return (
            (running[0] + pkey_grad, running[1] + pvalue_grad),
            (query_grad, key_grad, value_grad),
        )

    zero_grad = jnp.zeros(prefix_keys.shape, jnp.float32)
    prefix_sums, self_grads = lax.scan(
        self_back,
        (zero_grad, zero_grad),
        (self_queries, self_keys, self_values, seg_dec, self_total, self_dctx),
    )
    self_stack = jnp.stack(
        [from_heads(self_grads[0]), from_heads(self_grads[1]), from_heads(self_grads[2])]
    )
    input_partial = jnp.einsum(
        "ctn,cdn->td", self_stack, w_self, preferred_element_type=jnp.float32
    )
    grad_input = grad_one + sum_grads(input_partial)
    prefix_grad = (
        jnp.stack([prefix_sums[0], prefix_sums[1]])
        .transpose(0, 2, 1, 3)
        .reshape(2, prefix.shape[1], local_width)
    )
    prefix_grad = lax.psum(prefix_grad, "rows")
    return (output, grad_input, grad_memory, prefix_grad, down_grad, up_grad)


QB = 256
KB = 256
LOG2E = math.log2(math.e)
NEG = -1e30


def nt(a, b):
    return lax.dot_general(a, b, (((1,), (1,)), ((), ())), preferred_element_type=jnp.float32)


def nn(a, b):
    return lax.dot_general(a, b, (((1,), (0,)), ((), ())), preferred_element_type=jnp.float32)


def tn(a, b):
    return lax.dot_general(a, b, (((0,), (0,)), ((), ())), preferred_element_type=jnp.float32)


def half_lanes(v, h):
    lane = lax.broadcasted_iota(jnp.int32, v.shape, 1)
    keep = (lane < 64) if h == 0 else (lane >= 64)
    return jnp.where(keep, v, jnp.zeros_like(v))


def prefix_rows(scores):
    row = lax.broadcasted_iota(jnp.int32, scores.shape, 0)
    return jnp.where(lax.rem(row, 64) < 30, scores, NEG)


MESH = pl.DeviceIdType.MESH
TILE = 256

TOK, TOK_C, MEM, MEM_C = 112, 113, 114, 115
SELF_PIECE, OUT_ONE, CROSS_Q, CROSS_PIECE, OUT_TWO = 128, 132, 133, 134, 138
SLOTS, LOCAL_SLOTS = 128, 48
GROUPS = ((1, 0), (1, 0), (1, 1), (1, 0), (0, 0), (0, 1), (1, 0))
SCHEDULE = (33, 16, 17, 0, 36, 1, 19, 20, 34, 3, 2, 32, 114, 37, 65, 35, 5, 112, 38, 18, 115, 49, 21, 97, 52, 48, 22, 113, 4, 96, 128, 129, 50, 51, 130, 81, 80, 131, 100, 132, 133, 53, 134, 98, 99, 64, 135, 82, 136, 66, 101, 137, 70, 138)


class Place:
    def __init__(self):
        self.row, self.head = lax.axis_index("rows"), lax.axis_index("heads")
        self.c, self.z = lax.rem(self.row, 2), lax.div(self.row, 2)
        self.x, self.y = lax.rem(self.head, 2), lax.div(self.head, 2)
        self.odd = lax.rem(self.z, 2)
        c, x, y, z = self.c, self.x, self.y, self.z
        self.to_x = (self.row, 2 * y + 1 - x)
        self.to_y = (self.row, 2 * (1 - y) + x)
        self.to_d = (self.row, 2 * (1 - y) + 1 - x)
        self.to_z = (2 * (z + 1 - 2 * self.odd) + c, self.head)
        self.to_c = (2 * z + 1 - c, self.head)
        self.to_s = (2 * z + x, 2 * y + c)

    def greet(self, devices, swaps):
        barrier = pltpu.get_barrier_semaphore()
        for device in devices:
            pl.semaphore_signal(barrier, inc=1, device_id=device, device_id_type=MESH)
        count = len(devices)
        if swaps:
            moves = self.c != self.x

            @pl.when(moves)
            def _():
                pl.semaphore_signal(barrier, inc=1, device_id=self.to_s, device_id_type=MESH)

            count = count + moves.astype(jnp.int32)
        pl.semaphore_wait(barrier, count)


def prefix_block(rows):
    nothing = jnp.zeros_like(rows)
    return jnp.concatenate([half_lanes(rows, 0), nothing, half_lanes(rows, 1), nothing], axis=0)


def attend_tile(q, k, v, mask, kp, vp):
    scale = 0.125 * LOG2E
    if kp is not None:
        lane = lax.broadcasted_iota(jnp.int32, (q.shape[0], 128), 1)
        sp = jnp.where(lax.rem(lane, 64) < 30, nt(q, kp) * scale, NEG)
    tops, sums, es = [], [], []
    for h in range(2):
        s = jnp.where(mask, nt(half_lanes(q, h), k) * scale, NEG)
        m = jnp.max(s, axis=1, keepdims=True)
        if kp is not None:
            inside = (lane < 64) if h == 0 else (lane >= 64)
            m = jnp.maximum(m, jnp.max(jnp.where(inside, sp, NEG), axis=1, keepdims=True))
        e = jnp.exp2(s - m)
        sums.append(jnp.sum(e, axis=1, keepdims=True))
        es.append(e.astype(jnp.bfloat16))
        tops.append(m)
    out = nn(es[0], half_lanes(v, 0)) + nn(es[1], half_lanes(v, 1))
    side = lax.broadcasted_iota(jnp.int32, (q.shape[0], 128), 1) < 64
    if kp is not None:
        ep = jnp.exp2(sp - jnp.where(side, tops[0], tops[1]))
        sums = [sums[0] + jnp.sum(jnp.where(side, ep, 0.0), axis=1, keepdims=True), sums[1] + jnp.sum(jnp.where(side, 0.0, ep), axis=1, keepdims=True)]
        out = out + nn(ep.astype(jnp.bfloat16), vp)
    out = out * jnp.where(side, 1.0 / sums[0], 1.0 / sums[1])
    lse = jnp.where(side, tops[0] + jnp.log2(sums[0]), tops[1] + jnp.log2(sums[1])).T
    return out.astype(jnp.bfloat16), [lse[0:1], lse[64:65]]


def forward_kernel(
    tokens, memory, seg, mseg, prefix, w_self, w_so, w_cq, w_ckv, w_co, fc_in, fc_out, ad_down, ad_up, gain, bias,
    o_wself, o_qkv, o_sctx, o_slse, o_pre, o_wso_m, o_wso_o, o_wkv, o_wq_m, o_wq_o, o_wco_m, o_wco_o,
    o_q, o_kv, o_cctx, o_clse, o_resid1, o_resid2, o_bounds, o_ad, fin, fout, fad,
    wself, qkv, sctx, slse, pre, wso_m, wso_o, wkv, wq_m, wq_o, wco_m, wco_o,
    q_all, kv, cctx, clse, resid1, resid2, bounds, ad, tok, mem, sctx_o, cctx_o, q_send, hidden, low_one, columns, seg_v, mseg_v,
    send, recv, local,
):
    place_of = Place()
    c, x, y, odd = place_of.c, place_of.x, place_of.y, place_of.odd
    to_x, to_y, to_z, to_c, to_s = place_of.to_x, place_of.to_y, place_of.to_z, place_of.to_c, place_of.to_s
    stays, moves = c == x, c != x
    place_of.greet((to_x, to_y, to_z, to_c), True)

    taken = []

    def there(src, dst, device):
        slot = len(taken)
        taken.append(slot)
        return pltpu.make_async_remote_copy(
            src_ref=src, dst_ref=dst, send_sem=send.at[slot], recv_sem=recv.at[slot], device_id=device, device_id_type=MESH
        )

    used = []

    def here(src, dst):
        slot = len(used)
        used.append(slot)
        return pltpu.make_async_copy(src, dst, local.at[slot])

    deep = w_self.shape[1]
    half = tok.shape[0] // 2
    step = lambda start, size, unit: pl.ds(pl.multiple_of(start, unit), size)
    mine = step(c * half, half, half)
    others = step((1 - c) * half, half, half)
    lanes = step(c * 128, 128, 128)
    other_lanes = step((1 - c) * 128, 128, 128)
    rows_c, rows_o = lanes, other_lanes
    foreign = pl.ds(128, 384)
    hid = fc_in.shape[1]
    units = ad.shape[1]
    pending = []

    def swap_of(src, target):
        away = there(src, target.at[step(x * half, half, half)], to_s)
        home = here(src, target.at[mine])
        back = there(target.at[mine], target.at[mine], to_c)

        def start():
            pl.when(moves)(away.start)
            pl.when(stays)(home.start)

        def wait():
            pl.when(moves)(away.wait)
            pl.when(stays)(home.wait)

        return start, wait, back

    def seg_of(src, dst):
        home = here(src.at[y], dst)
        away = there(src.at[y], dst, to_c)

        def start():
            pl.when(stays)(home.start)
            pl.when(stays)(away.start)

        def wait():
            pl.when(stays)(home.wait)
            pl.when(stays)(away.wait_send)
            pl.when(moves)(away.wait_recv)

        return start, wait

    def deep_rows(shared):
        return step(odd * (deep // 2), deep // 2, deep // 2) if shared else pl.ds(0, deep)

    def thin_rows(piece, shared):
        return step(128 * piece + odd * 64, 64, 64) if shared else pl.ds(128 * piece, 128)

    def thin_own(shared):
        return step(128 * c + odd * 64, 64, 64) if shared else rows_c

    def span(size, shared):
        return step(c * (size // 2) + odd * (size // 4), size // 4, size // 4) if shared else step(c * (size // 2), size // 2, size // 2)

    lane_of = lambda i: pl.ds(128 * i, 128)

    def group_a(shared):
        rows = deep_rows(shared)
        first = lambda piece: [(w_self.at[i, rows, lanes], wself.at[piece, rows, lane_of(i)]) for i in range(3)] + [
            (prefix.at[:, :, lanes], pre.at[piece])
        ]
        return first, lambda piece: [wself.at[piece, rows], pre.at[piece]], 1, []

    def group_thin(src, dst_m, dst_o, shared):
        first = lambda piece: [(src.at[thin_own(shared)], dst_m.at[thin_rows(piece, shared)])]
        return first, lambda piece: [dst_m.at[thin_rows(piece, shared)]], 1, [(dst_m.at[foreign], dst_o.at[foreign])]

    def group_q(shared):
        rows = deep_rows(shared)
        first = lambda piece: [(w_cq.at[rows, lanes], wq_m.at[rows, lane_of(piece)])]
        return first, lambda piece: [wq_m.at[rows, lane_of(piece)]], 1, [(wq_m.at[:, foreign], wq_o.at[:, foreign])]

    def group_v(shared):
        rows = deep_rows(shared)
        first = lambda piece: [(w_ckv.at[i, rows, lanes], wkv.at[piece, rows, lane_of(i)]) for i in range(2)]
        return first, lambda piece: [wkv.at[piece, rows]], 1, []

    def group_i(shared):
        cols = span(hid, shared)
        first = lambda piece: [(fc_in.at[:, cols], fin.at[piece - 1, :, cols])]
        return first, lambda piece: [fin.at[piece - 1, :, cols]], 1, []

    def group_o(shared):
        rows, some = span(hid, shared), span(units, shared)
        first = lambda piece: [(fc_out.at[rows], fout.at[piece - 1, rows]), (ad.at[:, some], fad.at[piece - 1, :, some])]
        hold = lambda piece: [fout.at[piece - 1, rows], fad.at[piece - 1, :, some]]
        return first, hold, 2, []

    makers = [
        group_a,
        functools.partial(group_thin, w_so, wso_m, wso_o),
        group_q,
        group_v,
        functools.partial(group_thin, w_co, wco_m, wco_o),
        group_i,
        group_o,
    ]
    copies, needs = {}, {}
    for index, (make, (shared, through_x)) in enumerate(zip(makers, GROUPS)):
        first, hold, shared_count, cross = make(bool(shared))
        base = 16 * index
        copies[base] = [there(src, dst, to_x) for src, dst in first(1)]
        copies[base + 1] = [there(src, dst, to_y) for src, dst in first(2)]
        near, device = (2, to_x) if through_x else (1, to_y)
        copies[base + 2] = [there(src, dst, device) for src, dst in zip(hold(near), hold(3))]
        needs[base], needs[base + 1], needs[base + 2] = [], [], [base + near - 1]
        arrived = [base, base + 1, base + 2]
        if shared:
            for i in range(3):
                copies[base + 3 + i] = [there(ref, ref, to_z) for ref in hold(i + 1)[:shared_count]]
                needs[base + 3 + i] = [base + i]
                arrived.append(base + 3 + i)
        if cross:
            copies[base + 6] = [there(src, dst, to_c) for src, dst in cross]
            needs[base + 6] = arrived
    tok_start, tok_wait, tok_back = swap_of(tokens, tok)
    mem_start, mem_wait, mem_back = swap_of(memory, mem)
    copies[TOK_C], copies[MEM_C] = [tok_back], [mem_back]
    needs[TOK_C], needs[MEM_C] = [TOK], [MEM]
    seg_start, seg_wait = seg_of(seg, seg_v)
    mseg_start, mseg_wait = seg_of(mseg, mseg_v)
    sctx_out = [there(sctx.at[others, lane_of(i)], sctx_o.at[:, lane_of(i)], to_c) for i in range(4)]
    cctx_out = [there(cctx.at[others, lane_of(i)], cctx_o.at[:, lane_of(i)], to_c) for i in range(4)]
    q_out = there(q_send, q_all.at[mine], to_c)

    landed = set()

    def wait_for(op):
        if op in landed:
            return
        landed.add(op)
        if op == TOK:
            tok_wait()
        elif op == MEM:
            mem_wait()
        elif op in copies:
            for copy in copies[op]:
                copy.wait_recv()

    def launch(op):
        if op == TOK:
            tok_start()
        elif op == MEM:
            mem_start()
        else:
            for need in needs[op]:
                wait_for(need)
            for copy in copies[op]:
                copy.start()
                pending.append(copy)

    saves = []

    def keep(src, dst):
        copy = here(src, dst)
        copy.start()
        saves.append(copy)

    own_a = [here(w_self.at[i, :, lanes], wself.at[0, :, lane_of(i)]) for i in range(3)]
    own_a.append(here(prefix.at[:, :, lanes], pre.at[0]))
    own_b = [
        here(w_so.at[rows_c], wso_m.at[lane_of(0)]),
        here(w_so.at[rows_o], wso_o.at[lane_of(0)]),
        here(w_co.at[rows_c], wco_m.at[lane_of(0)]),
        here(w_co.at[rows_o], wco_o.at[lane_of(0)]),
        here(w_cq.at[:, lanes], wq_m.at[:, lane_of(0)]),
        here(w_cq.at[:, other_lanes], wq_o.at[:, lane_of(0)]),
        here(w_ckv.at[0, :, lanes], wkv.at[0, :, lane_of(0)]),
        here(w_ckv.at[1, :, lanes], wkv.at[0, :, lane_of(1)]),
    ]

    def bounds_of():
        seg_wait()
        mseg_wait()
        dec, men = seg_v[...], mseg_v[...]

        def below(values, d):
            return jnp.sum((values < d).astype(jnp.int32), axis=1, keepdims=True)

        def pick(counts):
            out = jnp.broadcast_to(counts[0], dec.shape)
            for d in range(1, 4):
                out = jnp.where(dec == d, counts[d], out)
            return out

        zero = jnp.zeros((1, 1), jnp.int32)
        full = jnp.full((1, 1), MLEN, jnp.int32)
        self_lo = pick([zero] + [below(dec, d) for d in range(1, 4)])
        mem_counts = [zero] + [below(men, d) for d in range(1, 4)] + [full]
        bounds[...] = jnp.concatenate(
            [self_lo, lax.broadcasted_iota(jnp.int32, dec.shape, 1), pick(mem_counts[:4]), pick(mem_counts[1:]) - 1]
            + [jnp.zeros_like(dec)] * 4,
            axis=0,
        )
        keep(bounds, o_bounds)
        wide = jnp.concatenate([bounds[...].astype(jnp.float32), jnp.zeros((120, SEQ), jnp.float32)], axis=0)
        columns[...] = wide.T.astype(jnp.int32)

    def weight_needs(base, piece):
        found = [base + piece - 1, base + 2 + piece]
        return [op for op in found if op in copies]

    def project(dst, p, source, weight):
        dst[p] = nn(source[...], weight[p]).astype(jnp.bfloat16)

    def self_piece(p):
        project(qkv, p, tok, wself)
        kp = prefix_block(pre[p, 0])
        vp = prefix_block(pre[p, 1])
        place = step(p * 128, 128, 128)
        for qi in range(SEQ // QB):
            width = (qi + 1) * QB
            rows = slice(qi * QB, (qi + 1) * QB)
            pos = lax.broadcasted_iota(jnp.int32, (QB, width), 1)
            limit = columns[rows, :]
            mask = (pos >= limit[:, 0:1]) & (pos <= limit[:, 1:2])
            out, lse = attend_tile(qkv[p, rows, 0:128], qkv[p, 0:width, 128:256], qkv[p, 0:width, 256:384], mask, kp, vp)
            sctx[rows, place] = out
            for h in range(2):
                slse[p, h : h + 1, rows] = lse[h]

    def cross_piece(p):
        project(kv, p, mem, wkv)
        place = step(p * 128, 128, 128)

        def block(qi, _):
            rows = step(qi * QB, QB, QB)
            pos = lax.broadcasted_iota(jnp.int32, (QB, MLEN), 1)
            limit = columns[rows, :]
            mask = (pos >= limit[:, 2:3]) & (pos <= limit[:, 3:4])
            out, lse = attend_tile(q_all[rows, place], kv[p, :, 0:128], kv[p, :, 128:256], mask, None, None)
            cctx[rows, place] = out
            for h in range(2):
                clse[p, h : h + 1, rows] = lse[h]
            return 0

        lax.fori_loop(0, SEQ // QB, block, 0)

    def with_out(t, resid_before, ctx_m, ctx_o, w_m, w_o):
        rows = step(t * TILE, TILE, TILE)
        rows_all = step(c * half + t * TILE, TILE, TILE)
        return resid_before + nn(ctx_m[rows_all, :], w_m[...]) + nn(ctx_o[rows, :], w_o[...])

    def out_one(t, _):
        rows = step(t * TILE, TILE, TILE)
        rows_all = step(c * half + t * TILE, TILE, TILE)
        resid = with_out(t, tok[rows_all, :].astype(jnp.float32), sctx, sctx_o, wso_m, wso_o)
        resid1[rows, :] = resid
        normed = norm_forward(resid, gain[0:1, :], bias[0:1, :])
        hidden[rows, :] = normed
        low_one[rows, :] = normed.astype(jnp.bfloat16)
        return 0

    def out_two(t, _):
        rows = step(t * TILE, TILE, TILE)
        resid2[rows, :] = with_out(t, hidden[rows, :], cctx, cctx_o, wco_m, wco_o)
        return 0

    def q_rows(t, _):
        rows = step(t * TILE, TILE, TILE)
        rows_all = step(c * half + t * TILE, TILE, TILE)
        q_send[rows, :] = nn(low_one[rows, :], wq_o[...]).astype(jnp.bfloat16)
        q_all[rows_all, :] = nn(low_one[rows, :], wq_m[...]).astype(jnp.bfloat16)
        return 0

    def split_at(order, first, count):
        places = [order.index(first + k) for k in range(count)]
        starts = [0] + [place + 1 for place in places]
        return [order[a:b] for a, b in zip(starts, places)], order[places[-1] + 1 :]

    def pieces_loop(segments, ready, work, sends):
        def body(p, _):
            for k, segment in enumerate(segments):

                @pl.when(p == k)
                def _():
                    for op in segment:
                        launch(op)
                    ready(k)

            work(p)
            for k, copy in enumerate(sends):
                pl.when(p == k)(copy.start)
            return 0

        lax.fori_loop(0, len(segments), body, 0)
        pending.extend(sends)

    ad_copy = here(ad_up, ad.at[1])
    ad_copy.start()
    ad[0] = ad_down[...].astype(jnp.float32).T.astype(jnp.bfloat16)
    ad_copy.wait()
    keep(ad, o_ad)

    for copy in own_a[:3]:
        copy.start()
    own_a[3].start()
    seg_start()
    mseg_start()
    segments, rest = split_at(list(SCHEDULE), SELF_PIECE, 4)
    for op in segments[0]:
        launch(op)
    for copy in own_b:
        copy.start()
    bounds_of()
    for copy in own_a:
        copy.wait()
    segments[0] = []

    def self_ready(k):
        if k == 0:
            wait_for(TOK_C)
        else:
            for op in weight_needs(0, k):
                wait_for(op)

    pieces_loop(segments, self_ready, self_piece, sctx_out)
    for src, dst in ((qkv, o_qkv), (wself, o_wself), (sctx, o_sctx), (slse, o_slse), (pre, o_pre)):
        keep(src, dst)
    for copy in own_b:
        copy.wait()
    before, rest = split_at(rest, OUT_ONE, 1)
    for op in before[0]:
        launch(op)
    for copy in sctx_out:
        copy.wait_recv()
    wait_for(16 + 6)
    lax.fori_loop(0, half // TILE, out_one, 0)
    for src, dst in ((resid1, o_resid1), (wso_m, o_wso_m), (wso_o, o_wso_o)):
        keep(src, dst)
    before, rest = split_at(rest, CROSS_Q, 1)
    for op in before[0]:
        launch(op)
    wait_for(32 + 6)
    lax.fori_loop(0, half // TILE, q_rows, 0)
    q_out.start()
    pending.append(q_out)
    for src, dst in ((wq_m, o_wq_m), (wq_o, o_wq_o)):
        keep(src, dst)
    segments, rest = split_at(rest, CROSS_PIECE, 4)

    def cross_ready(k):
        if k == 0:
            wait_for(MEM_C)
            q_out.wait_recv()
        else:
            for op in weight_needs(48, k):
                wait_for(op)

    pieces_loop(segments, cross_ready, cross_piece, cctx_out)
    for src, dst in ((q_all, o_q), (kv, o_kv), (wkv, o_wkv), (cctx, o_cctx), (clse, o_clse)):
        keep(src, dst)
    before, rest = split_at(rest, OUT_TWO, 1)
    for op in before[0]:
        launch(op)
    for copy in cctx_out:
        copy.wait_recv()
    wait_for(64 + 6)
    lax.fori_loop(0, half // TILE, out_two, 0)
    for src, dst in ((resid2, o_resid2), (wco_m, o_wco_m), (wco_o, o_wco_o)):
        keep(src, dst)
    for op in rest:
        launch(op)
    for op in list(copies):
        wait_for(op)
    for copy in pending:
        copy.wait_send()
    for copy in saves:
        copy.wait()


class Held(typing.NamedTuple):
    wself: jax.Array
    qkv: jax.Array
    sctx: jax.Array
    slse: jax.Array
    pre: jax.Array
    wso_m: jax.Array
    wso_o: jax.Array
    wkv: jax.Array
    wq_m: jax.Array
    wq_o: jax.Array
    wco_m: jax.Array
    wco_o: jax.Array
    q: jax.Array
    kv: jax.Array
    cctx: jax.Array
    clse: jax.Array
    resid1: jax.Array
    resid2: jax.Array
    bounds: jax.Array
    ad: jax.Array
    fin: jax.Array
    fout: jax.Array
    fad: jax.Array


def forward_call(tokens, memory, seg, mseg, prefix, w_self, w_so, w_cq, w_ckv, w_co, fc_in, fc_out, ad_down, ad_up, gain, bias):
    bf16, f32 = jnp.bfloat16, jnp.float32
    half, deep = tokens.shape
    shape = jax.ShapeDtypeStruct
    held = dict(
        wself=((4, deep, 384), bf16),
        qkv=((4, SEQ, 384), bf16),
        sctx=((SEQ, 512), bf16),
        slse=((4, 8, SEQ), f32),
        pre=((4, 2, 32, 128), bf16),
        wso_m=((512, deep), bf16),
        wso_o=((512, deep), bf16),
        wkv=((4, deep, 256), bf16),
        wq_m=((deep, 512), bf16),
        wq_o=((deep, 512), bf16),
        wco_m=((512, deep), bf16),
        wco_o=((512, deep), bf16),
        q=((SEQ, 512), bf16),
        kv=((4, MLEN, 256), bf16),
        cctx=((SEQ, 512), bf16),
        clse=((4, 8, SEQ), f32),
        resid1=((half, deep), f32),
        resid2=((half, deep), f32),
        bounds=((8, SEQ), jnp.int32),
        ad=((2,) + ad_up.shape, bf16),
    )
    outs = [shape(*value) for value in held.values()]
    outs += [shape((3,) + fc_in.shape, bf16), shape((3,) + fc_out.shape, bf16), shape((3, 2) + ad_up.shape, bf16)]
    scratch = [pltpu.VMEM(*value) for value in held.values()] + [
        pltpu.VMEM((SEQ, deep), bf16),
        pltpu.VMEM((MLEN, deep), bf16),
        pltpu.VMEM((half, 512), bf16),
        pltpu.VMEM((half, 512), bf16),
        pltpu.VMEM((half, 512), bf16),
        pltpu.VMEM((half, deep), f32),
        pltpu.VMEM((half, deep), bf16),
        pltpu.VMEM((SEQ, 128), jnp.int32),
        pltpu.VMEM((1, SEQ), jnp.int32),
        pltpu.VMEM((1, SEQ), jnp.int32),
        pltpu.SemaphoreType.DMA((SLOTS,)),
        pltpu.SemaphoreType.DMA((SLOTS,)),
        pltpu.SemaphoreType.DMA((LOCAL_SLOTS,)),
    ]
    anywhere = pl.BlockSpec(memory_space=pl.ANY)
    vmem = pl.BlockSpec(memory_space=pltpu.VMEM)
    results = pl.pallas_call(
        forward_kernel,
        out_shape=outs,
        in_specs=[anywhere] * 12 + [vmem, anywhere] + [vmem] * 2,
        out_specs=[anywhere] * len(outs),
        scratch_shapes=scratch,
        compiler_params=pltpu.CompilerParams(
            collective_id=0, has_side_effects=True, vmem_limit_bytes=58 * 2**20
        ),
        name="layer_forward",
    )(tokens, memory, seg, mseg, prefix, w_self, w_so, w_cq, w_ckv, w_co, fc_in, fc_out, ad_down, ad_up, gain, bias)
    return Held(*results)


TOGETHER = 4


def backward_kernel(has_prefix, first_bound, bounds_s, *refs):
    if has_prefix:
        qkv_ref, bounds, ctx_ref, dctx_ref, lse_ref, pre_ref, dqkv_ref, dpre_ref, dk_acc, dv_acc, dq_acc, dpre_acc = refs
        q_at = lambda g, rows: qkv_ref[g, rows, 0:128]
        k_at = lambda g, rows: qkv_ref[g, rows, 128:256]
        v_at = lambda g, rows: qkv_ref[g, rows, 256:384]
    else:
        q_ref, kv_ref, bounds, ctx_ref, dctx_ref, lse_ref, dq_ref, dkv_ref, dk_acc, dv_acc, dq_acc = refs
        q_at = lambda g, rows: q_ref[rows, 128 * g : 128 * g + 128]
        k_at = lambda g, rows: kv_ref[g, rows, 0:128]
        v_at = lambda g, rows: kv_ref[g, rows, 128:256]
    scale = 0.125 * LOG2E
    dk_acc[...] = jnp.zeros_like(dk_acc)
    dv_acc[...] = jnp.zeros_like(dv_acc)
    kps, vps = [], []
    for g in range(TOGETHER):
        if has_prefix:
            kps.append(prefix_block(pre_ref[g, 0]))
            vps.append(prefix_block(pre_ref[g, 1]))
    if has_prefix:
        dpre_acc[...] = jnp.zeros_like(dpre_acc)

    def one(qi, _):
        q0 = pl.multiple_of(qi * QB, QB)
        span = pl.ds(q0, QB)
        lo = bounds[first_bound : first_bound + 1, span]
        hi = bounds[first_bound + 1 : first_bound + 2, span]
        inner, lse, qh, dh = [], [], [], []
        for g in range(TOGETHER):
            q = q_at(g, span)
            dctx = dctx_ref[span, 128 * g : 128 * g + 128]
            ctx = ctx_ref[span, 128 * g : 128 * g + 128]
            prod = (dctx.astype(jnp.float32) * ctx.astype(jnp.float32)).T
            inner.append([jnp.sum(prod[h * 64 : h * 64 + 64], axis=0, keepdims=True) for h in range(2)])
            lse.append([lse_ref[g, h : h + 1, span] for h in range(2)])
            qh.append([half_lanes(q, h) for h in range(2)])
            dh.append([half_lanes(dctx, h) for h in range(2)])
            if has_prefix:
                sp = prefix_rows(nt(kps[g], q) * scale)
                rows = lambda pair: jnp.concatenate([jnp.broadcast_to(t, (64, QB)) for t in pair], axis=0)
                pp = jnp.exp2(sp - rows(lse[g]))
                dpp = nt(vps[g], dctx)
                dsp = (pp * (dpp - rows(inner[g]))).astype(jnp.bfloat16)
                dpre_acc[g, 0] += nn(dsp, q)
                dpre_acc[g, 1] += nn(pp.astype(jnp.bfloat16), dctx)
                dq_acc[g] = tn(dsp, kps[g])
            else:
                dq_acc[g] = jnp.zeros((QB, 128), jnp.float32)

        def chunk(ki, _):
            k0 = pl.multiple_of(ki * KB, KB)
            keys = pl.ds(k0, KB)
            pos = k0 + lax.broadcasted_iota(jnp.int32, (KB, QB), 0)
            mask = (pos >= lo) & (pos <= hi)
            for g in range(TOGETHER):
                k = k_at(g, keys)
                v = v_at(g, keys)
                ps, dss = [], []
                for h in range(2):
                    s = nt(k, qh[g][h]) * scale
                    p = jnp.exp2(jnp.where(mask, s, NEG) - lse[g][h])
                    dp = nt(v, dh[g][h])
                    ds = (p * (dp - inner[g][h])).astype(jnp.bfloat16)
                    ps.append(p.astype(jnp.bfloat16))
                    dss.append(ds)
                dv_acc[g, keys, :] += nn(jnp.concatenate(ps, axis=1), jnp.concatenate(dh[g], axis=0))
                dq_acc[g] += tn(jnp.concatenate(dss, axis=0), jnp.concatenate([half_lanes(k, 0), half_lanes(k, 1)], axis=0))
                dk_acc[g, keys, :] += nn(jnp.concatenate(dss, axis=1), jnp.concatenate(qh[g], axis=0))
            return 0

        lowest = lax.div(bounds_s[first_bound, q0], KB)
        highest = lax.div(bounds_s[first_bound + 1, q0 + QB - 1], KB) + 1
        lax.fori_loop(lowest, highest, chunk, 0)
        for g in range(TOGETHER):
            dq = (dq_acc[g] * 0.125).astype(jnp.bfloat16)
            if has_prefix:
                dqkv_ref[g, span, 0:128] = dq
            else:
                dq_ref[span, 128 * g : 128 * g + 128] = dq
        return 0

    lax.fori_loop(0, SEQ // QB, one, 0)
    for g in range(TOGETHER):
        dk = (dk_acc[g] * 0.125).astype(jnp.bfloat16)
        dv = dv_acc[g].astype(jnp.bfloat16)
        if has_prefix:
            dqkv_ref[g, :, 128:256] = dk
            dqkv_ref[g, :, 256:384] = dv
            lane = lax.broadcasted_iota(jnp.int32, (32, 128), 1)
            for i, factor in ((0, 0.125), (1, 1.0)):
                dpre_ref[g, i] = jnp.where(lane < 64, dpre_acc[g, i, 0:32], dpre_acc[g, i, 64:96]) * factor
        else:
            dkv_ref[g, :, 0:128] = dk
            dkv_ref[g, :, 128:256] = dv


def backward_call(has_prefix, arrays, bounds, ctx, dctx, lse, pre=None):
    col = pl.BlockSpec((SEQ, 128 * TOGETHER), lambda j, *_: (0, j))
    piece = lambda width: pl.BlockSpec((TOGETHER, SEQ, width), lambda j, *_: (j, 0, 0))
    shape = jax.ShapeDtypeStruct
    bf16, f32 = jnp.bfloat16, jnp.float32
    pre_spec = pl.BlockSpec((TOGETHER, 2, 32, 128), lambda j, *_: (j, 0, 0, 0))
    if has_prefix:
        in_specs = [piece(384)]
        out_specs = [piece(384), pre_spec]
        out_shape = [shape((4, SEQ, 384), bf16), shape((4, 2, 32, 128), f32)]
    else:
        in_specs = [col, piece(256)]
        out_specs = [col, piece(256)]
        out_shape = [shape((SEQ, 512), bf16), shape((4, SEQ, 256), bf16)]
    in_specs += [
        pl.BlockSpec((8, SEQ), lambda j, *_: (0, 0)),
        col,
        col,
        pl.BlockSpec((TOGETHER, 8, SEQ), lambda j, *_: (j, 0, 0)),
    ]
    args = list(arrays) + [bounds, ctx, dctx, lse]
    scratch = [
        pltpu.VMEM((TOGETHER, SEQ, 128), f32),
        pltpu.VMEM((TOGETHER, SEQ, 128), f32),
        pltpu.VMEM((TOGETHER, QB, 128), f32),
    ]
    if has_prefix:
        in_specs.append(pre_spec)
        args.append(pre)
        scratch.append(pltpu.VMEM((TOGETHER, 2, 128, 128), f32))
    return pl.pallas_call(
        functools.partial(backward_kernel, has_prefix, 0 if has_prefix else 2),
        grid_spec=pltpu.PrefetchScalarGridSpec(
            num_scalar_prefetch=1, grid=(4 // TOGETHER,), in_specs=in_specs, out_specs=out_specs, scratch_shapes=scratch
        ),
        out_shape=out_shape,
        compiler_params=pltpu.CompilerParams(vmem_limit_bytes=60 * 2**20),
        cost_estimate=pl.CostEstimate(flops=10 * 8 * SEQ * SEQ * 64, bytes_accessed=10 * 2**20, transcendentals=8 * SEQ * SEQ),
        name="self_backward" if has_prefix else "cross_backward",
    )(bounds, *args)


HIDDEN = 512


def swap_halves(place, src, dst_there, dst_here, send, recv, local):
    moves = place.c != place.x
    away = pltpu.make_async_remote_copy(
        src_ref=src, dst_ref=dst_there, send_sem=send, recv_sem=recv, device_id=place.to_s, device_id_type=MESH
    )
    home = pltpu.make_async_copy(src, dst_here, local)

    def start():
        pl.when(moves)(away.start)
        pl.when(jnp.logical_not(moves))(home.start)

    def wait():
        pl.when(moves)(away.wait)
        pl.when(jnp.logical_not(moves))(home.wait)

    return start, wait


def feed_kernel(
    resid2, cotangent, gain, bias, wco_m_in, wco_o_in, fc_in, fin, fc_out, fout, ad, fad,
    out, grad_two, unit_sum, dctx,
    win, wout, adw, slope, low, hidden, acc, gate, ada, branch_low, sem,
    cot, out_v, units, unit_send, unit_recv, near_send, near_recv, dctx_s, wco_m, wco_o, send, recv, local,
):
    place = Place()
    place.greet((place.to_x, place.to_y, place.to_d, place.to_c), True)
    c = place.c
    cot_start, cot_wait = swap_halves(place, cotangent, cot, cot, send.at[0], recv.at[0], local.at[0])
    out_copy = pltpu.make_async_copy(out_v, out, local.at[1])
    two_copy = pltpu.make_async_copy(acc, grad_two, local.at[2])
    co_copies = [
        pltpu.make_async_copy(wco_m_in, wco_m, local.at[3]),
        pltpu.make_async_copy(wco_o_in, wco_o, local.at[4]),
    ]
    cot_start()

    def there(slot, src, dst, device):
        return pltpu.make_async_remote_copy(
            src_ref=src, dst_ref=dst, send_sem=send.at[slot], recv_sem=recv.at[slot], device_id=device, device_id_type=MESH
        )

    half = resid2.shape[0]
    mine = pl.ds(pl.multiple_of(c * half, half), half)
    unit_core = there(2, unit_send, unit_recv, place.to_c)
    unit_near = [
        there(3 + i, near_send.at[i], near_recv.at[i], device) for i, device in enumerate((place.to_x, place.to_y, place.to_d))
    ]
    dctx_core = there(6, dctx_s, dctx.at[mine], place.to_c)
    bf16 = jnp.bfloat16
    per = fc_in.shape[1] // HIDDEN
    steps = 4 * per
    down, up = adw.at[0], adw.at[1]
    group = ad.shape[1]
    some = group // 2
    hidden_c = pl.ds(pl.multiple_of(c * HIDDEN, HIDDEN), HIDDEN)
    units_c = pl.ds(pl.multiple_of(c * some, some), some)
    loads, ad_loads, crossing = [], [], []
    for piece in range(4):
        ad_rows = pl.ds(pl.multiple_of(group * piece + c * some, some), some)
        own_in = win.at[2 * piece + c]
        own_out = wout.at[2 * piece + c]
        if piece == 0:
            loads.append(pltpu.make_async_copy(fc_in.at[:, hidden_c], own_in, sem.at[0, 0]))
            loads.append(pltpu.make_async_copy(fc_out.at[hidden_c], own_out, sem.at[1, 0]))
            hidden_o = pl.ds(pl.multiple_of((1 - c) * HIDDEN, HIDDEN), HIDDEN)
            loads.append(pltpu.make_async_copy(fc_in.at[:, hidden_o], win.at[1 - c], sem.at[0, 1]))
            loads.append(pltpu.make_async_copy(fc_out.at[hidden_o], wout.at[1 - c], sem.at[1, 1]))
            ad_loads.append(pltpu.make_async_copy(ad, adw.at[:, pl.ds(0, group)], sem.at[2, 0]))
        else:
            src_in, src_out, src_ad = fin.at[piece - 1, :, hidden_c], fout.at[piece - 1, hidden_c], fad.at[piece - 1, :, units_c]
            loads.append(pltpu.make_async_copy(src_in, own_in, sem.at[0, 2 * piece]))
            loads.append(pltpu.make_async_copy(src_out, own_out, sem.at[1, 2 * piece]))
            ad_loads.append(pltpu.make_async_copy(src_ad, adw.at[:, ad_rows], sem.at[2, piece]))
            crossing.append(there(4 + 3 * piece, src_in, own_in, place.to_c))
            crossing.append(there(5 + 3 * piece, src_out, own_out, place.to_c))
            crossing.append(there(6 + 3 * piece, src_ad, adw.at[:, ad_rows], place.to_c))
    for copy in crossing + loads + ad_loads + co_copies:
        copy.start()

    rows_all = resid2.shape[0]
    tiles = rows_all // TILE
    at = lambda t: pl.ds(pl.multiple_of(t * TILE, TILE), TILE)

    def begin(t, _):
        rows = at(t)
        normed = norm_forward(resid2[rows, :], gain[1:2, :], bias[1:2, :])
        hidden[rows, :] = normed
        low[rows, :] = normed.astype(bf16)
        return 0

    lax.fori_loop(0, tiles, begin, 0)
    acc[...] = jnp.zeros_like(acc)

    def ahead(s, _):
        piece, late = lax.div(s, 2), lax.rem(s, 2)
        j = 2 * piece + c + late * (1 - 2 * c)
        for k in range(1, 4):

            @pl.when(s == 2 * k + 1)
            def _():
                crossing[3 * k - 3].wait_recv()
                crossing[3 * k - 2].wait_recv()

        @pl.when((late == 0) | (s == 1))
        def _():
            for i, buf in enumerate((win, wout)):
                pltpu.make_async_copy(buf.at[j], buf.at[j], sem.at[i, s]).wait()

        pre = nn(low[...], win[j])
        phi = 0.5 * (1.0 + lax.erf(pre * 0.7071067811865476))
        slope[j] = phi + pre * jnp.exp(-0.5 * pre * pre) * 0.3989422804014327
        acc[...] += nn((pre * phi).astype(bf16), wout[j])
        return 0

    lax.fori_loop(0, steps, ahead, 0)
    for copy in ad_loads + crossing[2::3]:
        copy.wait()
    pre = nt(low[...], down[...])
    sigma = jax.nn.sigmoid(pre)
    gate[...] = sigma * (1.0 + pre * (1.0 - sigma))
    ada[...] = (pre * sigma).astype(bf16)
    acc[...] += adapter_scale * nn(ada[...], up[...])

    def middle(t, _):
        rows = at(t)
        resid = hidden[rows, :] + acc[rows, :]
        normed, inv = norm_parts(resid)
        out_v[rows, :] = (normed * gain[2:3, :] + bias[2:3, :]).astype(bf16)
        scaled = cot[rows, :].astype(jnp.float32) * gain[2:3, :]
        grad = inv * (
            scaled
            - jnp.mean(scaled, axis=-1, keepdims=True)
            - normed * jnp.mean(scaled * normed, axis=-1, keepdims=True)
        )
        acc[rows, :] = grad
        branch_low[rows, :] = grad.astype(bf16)
        return 0

    cot_wait()
    lax.fori_loop(0, tiles, middle, 0)
    out_copy.start()
    grelu = (adapter_scale * nt(branch_low[...], up[...]) * gate[...]).astype(bf16)
    features = low.shape[1]
    for first, value in ((0, tn(grelu, low[...])), (features, adapter_scale * tn(ada[...], branch_low[...]))):
        for k in range(8):
            units[k // 2, k % 2, :, first : first + features] = value[some * k : some * (k + 1)]
    for i in range(4):
        unit_send[i] = units[i, 1 - c].astype(bf16)
    unit_core.start()
    acc[...] += nn(grelu, down[...])

    def behind(j, _):
        grad = (nt(branch_low[...], wout[j]) * slope[j]).astype(bf16)
        acc[...] += nt(grad, win[j])
        return 0

    lax.fori_loop(0, steps // 2, behind, 0)
    unit_core.wait()
    for i in range(3):
        near_send[i] = (units[i + 1, c] + unit_recv[i + 1].astype(jnp.float32)).astype(bf16)
    for copy in unit_near:
        copy.start()
    lax.fori_loop(steps // 2, steps, behind, 0)

    def finish(t, _):
        rows = at(t)
        grad = norm_backward(resid2[rows, :], gain[1:2, :], acc[rows, :])
        acc[rows, :] = grad
        small = grad.astype(bf16)
        low[rows, :] = small
        dctx_s[rows, :] = nt(small, wco_o[...]).astype(bf16)
        return 0

    for copy in co_copies:
        copy.wait()
    lax.fori_loop(0, tiles, finish, 0)
    dctx_core.start()
    two_copy.start()
    dctx[mine, :] = nt(low[...], wco_m[...]).astype(bf16)
    for copy in unit_near:
        copy.wait()
    total = units[0, c] + unit_recv[0].astype(jnp.float32)
    for i in range(3):
        total = total + near_recv[i].astype(jnp.float32)
    unit_sum[...] = total
    out_copy.wait()
    two_copy.wait()
    for k in range(3):
        crossing[3 * k].wait_send()
        crossing[3 * k + 1].wait_send()
    dctx_core.wait()


def feed_call(resid2, cot, gain, bias, wco_m, wco_o, fc_in, fin, fc_out, fout, ad, fad):
    bf16, f32 = jnp.bfloat16, jnp.float32
    rows, deep = resid2.shape
    shape = jax.ShapeDtypeStruct
    anywhere = pl.BlockSpec(memory_space=pl.ANY)
    vmem = pl.BlockSpec(memory_space=pltpu.VMEM)
    steps = 4 * fc_in.shape[1] // HIDDEN
    units = 4 * ad.shape[1]
    some = ad.shape[1] // 2
    return pl.pallas_call(
        feed_kernel,
        out_shape=[
            shape((rows, deep), bf16),
            shape((rows, deep), f32),
            shape((some, 2 * deep), f32),
            shape((2 * rows, 512), bf16),
        ],
        in_specs=[vmem, anywhere] + [vmem] * 2 + [anywhere] * 8,
        out_specs=[anywhere] * 2 + [vmem] * 2,
        scratch_shapes=[
            pltpu.VMEM((steps, deep, HIDDEN), bf16),
            pltpu.VMEM((steps, HIDDEN, deep), bf16),
            pltpu.VMEM((2, units, deep), bf16),
            pltpu.VMEM((steps, rows, HIDDEN), f32),
            pltpu.VMEM((rows, deep), bf16),
            pltpu.VMEM((rows, deep), f32),
            pltpu.VMEM((rows, deep), f32),
            pltpu.VMEM((rows, units), f32),
            pltpu.VMEM((rows, units), bf16),
            pltpu.VMEM((rows, deep), bf16),
            pltpu.SemaphoreType.DMA((3, 8)),
            pltpu.VMEM((rows, deep), bf16),
            pltpu.VMEM((rows, deep), bf16),
            pltpu.VMEM((4, 2, some, 2 * deep), f32),
            pltpu.VMEM((4, some, 2 * deep), bf16),
            pltpu.VMEM((4, some, 2 * deep), bf16),
            pltpu.VMEM((3, some, 2 * deep), bf16),
            pltpu.VMEM((3, some, 2 * deep), bf16),
            pltpu.VMEM((rows, 512), bf16),
            pltpu.VMEM(wco_m.shape, bf16),
            pltpu.VMEM(wco_o.shape, bf16),
            pltpu.SemaphoreType.DMA((16,)),
            pltpu.SemaphoreType.DMA((16,)),
            pltpu.SemaphoreType.DMA((5,)),
        ],
        compiler_params=pltpu.CompilerParams(
            collective_id=1, has_side_effects=True, vmem_limit_bytes=61 * 2**20
        ),
        name="feed_forward",
    )(resid2, cot, gain, bias, wco_m, wco_o, fc_in, fin, fc_out, fout, ad, fad)


def query_kernel(
    dq_in, dkv_in, wkv_in, wq_m_in, wq_o_in, two_in, resid_in, wso_m_in, wso_o_in, gain,
    one_out, dctx, mem_out,
    dq, dkv, wkv, wq_m, wq_o, grad_two, resid1, wso_m, wso_o,
    grad_one, mem_sum, dq_o, mem_s, mem_r, dctx_s, dctx_m, low, send, recv, local,
):
    bf16 = jnp.bfloat16
    place = Place()
    c = place.c
    half = resid1.shape[0]
    mine = pl.ds(pl.multiple_of(c * half, half), half)
    others = pl.ds(pl.multiple_of((1 - c) * half, half), half)

    def there(slot, src, dst):
        return pltpu.make_async_remote_copy(
            src_ref=src, dst_ref=dst, send_sem=send.at[slot], recv_sem=recv.at[slot], device_id=place.to_c, device_id_type=MESH
        )

    def here(slot, src, dst):
        return pltpu.make_async_copy(src, dst, local.at[slot])

    wkv_copy, dkv_far, dkv_near = here(0, wkv_in, wkv), here(1, dkv_in.at[:, others], dkv.at[:, others]), here(2, dkv_in.at[:, mine], dkv.at[:, mine])
    pairs = (
        (dq_in.at[mine], dq), (wq_m_in, wq_m), (wq_o_in, wq_o), (two_in, grad_two), (resid_in, resid1), (wso_o_in, wso_o), (wso_m_in, wso_m)
    )
    rest = [here(3 + i, src, dst) for i, (src, dst) in enumerate(pairs)]
    for copy in [wkv_copy, dkv_far] + rest + [dkv_near]:
        copy.start()
    one_copy, mem_copy, dctx_copy = here(10, grad_one, one_out), here(11, mem_sum, mem_out), here(12, dctx_m, dctx.at[mine])
    place.greet((place.to_c,), False)
    dq_core = there(0, dq_in.at[others], dq_o)
    mem_core = there(1, mem_s, mem_r)
    dctx_core = there(2, dctx_s, dctx.at[mine])
    dq_core.start()
    tiles = half // TILE
    at = lambda t: pl.ds(pl.multiple_of(t * TILE, TILE), TILE)
    place_at = lambda first, t: pl.ds(pl.multiple_of(first * half + t * TILE, TILE), TILE)

    def memory_rows(rows):
        return sum(nt(dkv[p, rows, :], wkv[p]) for p in range(4))

    def far(t, _):
        mem_s[at(t), :] = memory_rows(place_at(1 - c, t)).astype(bf16)
        return 0

    wkv_copy.wait()
    dkv_far.wait()
    lax.fori_loop(0, tiles, far, 0)
    mem_core.start()
    for copy in rest:
        copy.wait()
    dq_core.wait()

    def one(t, _):
        rows = at(t)
        grad_in = grad_two[rows, :] + nt(dq[rows, :], wq_m[...]) + nt(dq_o[rows, :], wq_o[...])
        grad = norm_backward(resid1[rows, :], gain[0:1, :], grad_in)
        grad_one[rows, :] = grad
        small = grad.astype(bf16)
        low[rows, :] = small
        dctx_s[rows, :] = nt(small, wso_o[...]).astype(bf16)
        return 0

    lax.fori_loop(0, tiles, one, 0)
    dctx_core.start()
    one_copy.start()
    dctx_m[...] = nt(low[...], wso_m[...]).astype(bf16)
    dctx_copy.start()
    mem_core.wait()
    dkv_near.wait()

    def near(t, _):
        mem_sum[at(t), :] = (memory_rows(place_at(c, t)) + mem_r[at(t), :].astype(jnp.float32)).astype(bf16)
        return 0

    lax.fori_loop(0, tiles, near, 0)
    mem_copy.start()
    for copy in (dctx_core, one_copy, dctx_copy, mem_copy):
        copy.wait()


def query_call(dq, dkv, wkv, wq_m, wq_o, grad_two, resid1, wso_m, wso_o, gain):
    bf16, f32 = jnp.bfloat16, jnp.float32
    half, deep = resid1.shape
    shape = jax.ShapeDtypeStruct
    vmem = pl.BlockSpec(memory_space=pltpu.VMEM)
    anywhere = pl.BlockSpec(memory_space=pl.ANY)
    return pl.pallas_call(
        query_kernel,
        out_shape=[shape((half, deep), f32), shape((2 * half, 512), bf16), shape((half, deep), bf16)],
        in_specs=[anywhere] * 9 + [vmem],
        out_specs=[anywhere] * 3,
        scratch_shapes=[pltpu.VMEM((half, 512), bf16)]
        + [pltpu.VMEM(value.shape, value.dtype) for value in (dkv, wkv, wq_m, wq_o, grad_two, resid1, wso_m, wso_o)]
        + [
            pltpu.VMEM((half, deep), f32),
            pltpu.VMEM((half, deep), bf16),
            pltpu.VMEM((half, 512), bf16),
            pltpu.VMEM((half, deep), bf16),
            pltpu.VMEM((half, deep), bf16),
            pltpu.VMEM((half, 512), bf16),
            pltpu.VMEM((half, 512), bf16),
            pltpu.VMEM((half, deep), bf16),
            pltpu.SemaphoreType.DMA((3,)),
            pltpu.SemaphoreType.DMA((3,)),
            pltpu.SemaphoreType.DMA((13,)),
        ],
        compiler_params=pltpu.CompilerParams(collective_id=2, has_side_effects=True, vmem_limit_bytes=60 * 2**20),
        name="query_backward",
    )(dq, dkv, wkv, wq_m, wq_o, grad_two, resid1, wso_m, wso_o, gain)


def last_kernel(
    planes, dqkv_in, wself_in, one_in, blocks_in, unit_in,
    input_out, prefix_grad, down_grad, up_grad,
    dqkv, wself, grad_one, blocks, unit_sum, part_s, part_r, out_s, pre_near, pre_sum, pre_z, pre_c, unit_s, unit_z, unit_all, send, recv, local,
):
    bf16, f32 = jnp.bfloat16, jnp.float32
    place = Place()
    c, x, z = place.c, place.x, place.z
    steps = []
    step = 1
    while step < planes:
        other = z + step - 2 * step * lax.rem(lax.div(z, step), 2)
        steps.append((2 * other + c, place.head))
        step *= 2
    moves = c != x
    stays = c == x
    half = grad_one.shape[0]
    slots = []

    def there(src, dst, device):
        slot = len(slots)
        slots.append(slot)
        return pltpu.make_async_remote_copy(
            src_ref=src, dst_ref=dst, send_sem=send.at[slot], recv_sem=recv.at[slot], device_id=device, device_id_type=MESH
        )

    tiles = half // TILE
    at = lambda t: pl.ds(t * TILE, TILE)
    place_at = lambda first, t: pl.ds(pl.multiple_of(first * half + t * TILE, TILE), TILE)

    def here(slot, src, dst):
        return pltpu.make_async_copy(src, dst, local.at[slot])

    loads = [here(0, wself_in, wself), here(1, blocks_in, blocks), here(2, unit_in, unit_sum), here(3, one_in, grad_one)]
    far_loads = [here(4 + t, dqkv_in.at[:, place_at(1 - c, t)], dqkv.at[:, place_at(1 - c, t)]) for t in range(tiles)]
    near_loads = [
        here(4 + tiles + t, dqkv_in.at[:, place_at(c, t)], dqkv.at[:, place_at(c, t)]) for t in range(tiles)
    ]
    for copy in [loads[1], loads[2], far_loads[0], loads[0]] + far_loads[1:] + near_loads + [loads[3]]:
        copy.start()

    place.greet([place.to_x, place.to_y, place.to_d, place.to_c] + steps, True)
    pre_copies = [
        there(blocks.at[i + 1], pre_near.at[i], device) for i, device in enumerate((place.to_x, place.to_y, place.to_d))
    ]
    pre_steps = [there(pre_sum.at[i], pre_z.at[i], device) for i, device in enumerate(steps)]
    pre_core = there(pre_sum.at[len(steps)], pre_c, place.to_c)
    unit_steps = [there(unit_s.at[i], unit_z.at[i], device) for i, device in enumerate(steps)]
    unit_core = there(unit_s.at[len(steps)], unit_z.at[len(steps)], place.to_c)
    part_copies = [there(part_s.at[at(t)], part_r.at[at(t)], place.to_c) for t in range(tiles)]
    out_copies = [there(out_s.at[at(t)], input_out.at[at(t)], place.to_s) for t in range(tiles)]
    own_copies = [here(4 + 2 * tiles + t, out_s.at[at(t)], input_out.at[at(t)]) for t in range(tiles)]
    loads[1].wait()
    for copy in pre_copies:
        copy.start()
    loads[2].wait()
    unit_s[0] = unit_sum[...].astype(bf16)
    unit_steps[0].start()

    def input_rows(rows):
        return sum(nt(dqkv[p, rows, :], wself[p]) for p in range(4))

    loads[0].wait()
    far_loads[0].wait()
    part_s[at(0), :] = input_rows(place_at(1 - c, 0)).astype(bf16)
    part_copies[0].start()
    for copy in pre_copies:
        copy.wait()
    pre_sum[0] = blocks[0] + pre_near[0] + pre_near[1] + pre_near[2]
    pre_steps[0].start()
    for t in range(1, tiles):
        far_loads[t].wait()
        part_s[at(t), :] = input_rows(place_at(1 - c, t)).astype(bf16)
        part_copies[t].start()

    def advance(i):
        pre_steps[i].wait()
        pre_sum[i + 1] = pre_sum[i] + pre_z[i]
        if i + 1 < len(steps):
            pre_steps[i + 1].start()
        else:
            pre_core.start()
        unit_steps[i].wait()
        unit_s[i + 1] = (unit_s[i].astype(f32) + unit_z[i].astype(f32)).astype(bf16)
        if i + 1 < len(steps):
            unit_steps[i + 1].start()
        else:
            unit_core.start()

    loads[3].wait()
    for t in range(tiles):
        near_loads[t].wait()
        part_copies[t].wait()
        total = input_rows(place_at(c, t)) + part_r[at(t), :].astype(f32) + grad_one[at(t), :]
        out_s[at(t), :] = total.astype(bf16)
        pl.when(moves)(out_copies[t].start)
        pl.when(stays)(own_copies[t].start)
        if t < len(steps):
            advance(t)
    for i in range(tiles, len(steps)):
        advance(i)
    pre_core.wait()
    unit_core.wait()
    my_lanes = pl.ds(pl.multiple_of(c * 128, 128), 128)
    other_lanes = pl.ds(pl.multiple_of((1 - c) * 128, 128), 128)
    prefix_grad[:, :, my_lanes] = pre_sum[len(steps)]
    prefix_grad[:, :, other_lanes] = pre_c[...]
    some = unit_sum.shape[0]
    unit_all[pl.ds(pl.multiple_of(c * some, some), some), :] = unit_s[len(steps)].astype(f32)
    unit_all[pl.ds(pl.multiple_of((1 - c) * some, some), some), :] = unit_z[len(steps)].astype(f32)
    features = grad_one.shape[1]
    down_grad[...] = unit_all[:, 0:features].T
    up_grad[...] = unit_all[:, features : 2 * features]

    for t in range(tiles):
        pl.when(moves)(out_copies[t].wait)
        pl.when(stays)(own_copies[t].wait)


def last_call(planes, dqkv, wself, grad_one, blocks, unit_sum):
    bf16, f32 = jnp.bfloat16, jnp.float32
    half, deep = grad_one.shape
    some = unit_sum.shape[0]
    count = planes.bit_length() - 1
    shape = jax.ShapeDtypeStruct
    vmem = pl.BlockSpec(memory_space=pltpu.VMEM)
    anywhere = pl.BlockSpec(memory_space=pl.ANY)
    return pl.pallas_call(
        functools.partial(last_kernel, planes),
        out_shape=[
            shape((half, deep), bf16),
            shape((2, 32, 256), f32),
            shape((deep, 2 * some), f32),
            shape((2 * some, deep), f32),
        ],
        in_specs=[anywhere] * 5,
        out_specs=[anywhere] + [vmem] * 3,
        scratch_shapes=[pltpu.VMEM(value.shape, value.dtype) for value in (dqkv, wself, grad_one, blocks, unit_sum)]
        + [
            pltpu.VMEM((half, deep), bf16),
            pltpu.VMEM((half, deep), bf16),
            pltpu.VMEM((half, deep), bf16),
            pltpu.VMEM((3, 2, 32, 128), f32),
            pltpu.VMEM((count + 1, 2, 32, 128), f32),
            pltpu.VMEM((count, 2, 32, 128), f32),
            pltpu.VMEM((2, 32, 128), f32),
            pltpu.VMEM((count + 1, some, 2 * deep), bf16),
            pltpu.VMEM((count + 1, some, 2 * deep), bf16),
            pltpu.VMEM((2 * some, 2 * deep), f32),
            pltpu.SemaphoreType.DMA((3 + 2 * count + 2 + 2 * (half // TILE),)),
            pltpu.SemaphoreType.DMA((3 + 2 * count + 2 + 2 * (half // TILE),)),
            pltpu.SemaphoreType.DMA((4 + 3 * (half // TILE),)),
        ],
        compiler_params=pltpu.CompilerParams(collective_id=3, has_side_effects=True, vmem_limit_bytes=60 * 2**20),
        name="last_sums",
    )(dqkv, wself, grad_one, blocks, unit_sum)


AXES = ("rows", "heads")


def fast_fits(mesh):
    rows, heads = mesh.shape["rows"], mesh.shape["heads"]
    return heads == 4 and rows % 4 == 0 and (rows & (rows - 1)) == 0


def pairs_of(rows, move):
    def number(z, c, y, x):
        return (z * 2 + c) * 4 + y * 2 + x

    found = []
    for z in range(rows // 2):
        for c in range(2):
            for y in range(2):
                for x in range(2):
                    found.append((number(z, c, y, x), number(*move(z, c, y, x))))
    return found


def swapped_rows(rows, value):
    def swapped(z, c, y, x):
        return (z, x, y, c)

    crossing = [pair for pair in pairs_of(rows, swapped) if pair[0] != pair[1]]
    stays = lax.axis_index("rows") % 2 == lax.axis_index("heads") % 2
    return jnp.where(stays, value, lax.ppermute(value, AXES, crossing))


def fast_body(
    rows,
    tokens,
    memory,
    cotangent,
    dec_seg,
    mem_seg,
    w_self,
    w_self_out,
    w_cross_q,
    w_cross_kv,
    w_cross_out,
    fc_in,
    fc_out,
    ad_down,
    ad_up,
    prefix,
    ln_gain,
    ln_bias,
):
    count = prefix.shape[1]
    held = forward_call(
        tokens,
        memory,
        dec_seg.reshape(2, 1, SEQ),
        mem_seg.reshape(2, 1, MLEN),
        jnp.pad(prefix, ((0, 0), (0, 32 - count), (0, 0))),
        w_self,
        w_self_out,
        w_cross_q,
        w_cross_kv,
        w_cross_out,
        fc_in,
        fc_out,
        ad_down,
        ad_up,
        ln_gain,
        ln_bias,
    )
    out_own, grad_two, unit_sum, cross_dctx = feed_call(
        held.resid2, cotangent, ln_gain, ln_bias, held.wco_m, held.wco_o,
        fc_in, held.fin, fc_out, held.fout, held.ad, held.fad,
    )
    output = swapped_rows(rows, out_own)
    cross_dq, cross_dkv = backward_call(
        False, (held.q, held.kv), held.bounds, held.cctx, cross_dctx, held.clse
    )
    grad_one, self_dctx, memory_sum = query_call(
        cross_dq, cross_dkv, held.wkv, held.wq_m, held.wq_o, grad_two, held.resid1, held.wso_m, held.wso_o, ln_gain
    )
    grad_memory = swapped_rows(rows, memory_sum).astype(jnp.float32)
    self_dqkv, prefix_blocks = backward_call(
        True, (held.qkv,), held.bounds, held.sctx, self_dctx, held.slse, held.pre
    )
    grad_input, prefix_grad, down_grad, up_grad = last_call(
        rows // 2, self_dqkv, held.wself, grad_one, prefix_blocks, unit_sum
    )
    return (output, grad_input.astype(jnp.float32), grad_memory, prefix_grad[:, :count], down_grad, up_grad)


def solution(mesh):
    in_specs = (
        P(("rows", "heads"), None),
        P(("rows", "heads"), None),
        P(("rows", "heads"), None),
        P("rows"),
        P("rows"),
        P(None, None, "heads"),
        P("heads", None),
        P(None, "heads"),
        P(None, None, "heads"),
        P("heads", None),
        P(None, "heads"),
        P("heads", None),
        P(None, "heads"),
        P("heads", None),
        P(None, None, "heads"),
        P(),
        P(),
    )
    out_specs = (
        P(("rows", "heads"), None),
        P(("rows", "heads"), None),
        P(("rows", "heads"), None),
        P(None, None, "heads"),
        P(None, "heads"),
        P("heads", None),
    )
    chosen = functools.partial(fast_body, mesh.shape["rows"]) if fast_fits(mesh) else body
    return jax.shard_map(chosen, mesh=mesh, in_specs=in_specs, out_specs=out_specs, check_vma=False)
```

```python
import functools
import math
import typing

import jax
import jax.numpy as jnp
from jax import lax
from jax.experimental import pallas as pl
from jax.experimental.pallas import tpu as pltpu
from jax.sharding import PartitionSpec as P

HD = 64
SEQ = 1024
MLEN = 1024


epsilon = 1e-05
adapter_scale = 4.0
masked_score = -1e30


def dot_right(left, right):
    return lax.dot_general(
        left, right, (((1,), (1,)), ((), ())), preferred_element_type=jnp.float32
    )


def dot_left(left, right):
    return lax.dot_general(
        left, right, (((0,), (0,)), ((), ())), preferred_element_type=jnp.float32
    )


def norm_parts(resid):
    average = jnp.mean(resid, axis=-1, keepdims=True)
    centered = resid - average
    inv_scale = lax.rsqrt(jnp.mean(centered * centered, axis=-1, keepdims=True) + epsilon)
    return (centered * inv_scale, inv_scale)


def norm_forward(resid, gain, shift):
    normed, inv_scale = norm_parts(resid)
    return normed * gain + shift


def norm_backward(resid, gain, grad_out):
    normed, inv_scale = norm_parts(resid)
    scaled = grad_out * gain
    return inv_scale * (
        scaled
        - jnp.mean(scaled, axis=-1, keepdims=True)
        - normed * jnp.mean(scaled * normed, axis=-1, keepdims=True)
    )


def gelu_slope(pre_gelu):
    return (
        0.5 * (1.0 + lax.erf(pre_gelu * 0.7071067811865476))
        + pre_gelu * jnp.exp(-0.5 * pre_gelu * pre_gelu) * 0.3989422804014327
    )


def silu_slope(pre_relu):
    sigma = jax.nn.sigmoid(pre_relu)
    return sigma * (1.0 + pre_relu * (1.0 - sigma))


def to_heads(arrays, heads_here):
    return arrays.reshape(arrays.shape[0], arrays.shape[1], heads_here, HD).transpose(0, 2, 1, 3)


def from_heads(arrays):
    return arrays.transpose(0, 2, 1, 3).reshape(
        arrays.shape[0] * arrays.shape[2], arrays.shape[1] * arrays.shape[3]
    )


def join_blocks(stacked):
    moved = jnp.moveaxis(stacked, 0, 1)
    return moved.reshape((moved.shape[0], moved.shape[1] * moved.shape[2]) + moved.shape[3:])


def block_mask(row_segs, key_segs, offset, causal):
    allowed = row_segs[:, None] == key_segs[None, :]
    if causal:
        row_places = offset + lax.iota(jnp.int32, row_segs.shape[0])
        key_places = lax.iota(jnp.int32, key_segs.shape[0])
        allowed = allowed & (key_places[None, :] <= row_places[:, None])
    return allowed


def block_scores(queries, key_rows, allowed, prefix_keys):
    qk_scale = HD ** (-0.5)
    token_scores = (
        jnp.einsum("hqe,hke->hqk", queries, key_rows, preferred_element_type=jnp.float32) * qk_scale
    )
    token_scores = jnp.where(allowed[None], token_scores, masked_score)
    if prefix_keys is None:
        return (token_scores, None)
    prefix_scores = (
        jnp.einsum("hqe,hpe->hqp", queries, prefix_keys, preferred_element_type=jnp.float32)
        * qk_scale
    )
    return (token_scores, prefix_scores)


def attend_block(queries, key_rows, value_rows, allowed, prefix_keys, prefix_values):
    token_scores, prefix_scores = block_scores(queries, key_rows, allowed, prefix_keys)
    row_max = jnp.max(token_scores, axis=-1, keepdims=True)
    if prefix_scores is not None:
        row_max = jnp.maximum(row_max, jnp.max(prefix_scores, axis=-1, keepdims=True))
    token_weights = jnp.exp(token_scores - row_max)
    row_total = jnp.sum(token_weights, axis=-1, keepdims=True)
    if prefix_scores is not None:
        prefix_weights = jnp.exp(prefix_scores - row_max)
        row_total = row_total + jnp.sum(prefix_weights, axis=-1, keepdims=True)
    context = jnp.einsum(
        "hqk,hke->hqe",
        (token_weights / row_total).astype(jnp.bfloat16),
        value_rows,
        preferred_element_type=jnp.float32,
    )
    if prefix_scores is not None:
        context = context + jnp.einsum(
            "hqp,hpe->hqe",
            (prefix_weights / row_total).astype(jnp.bfloat16),
            prefix_values,
            preferred_element_type=jnp.float32,
        )
    return (context.astype(jnp.bfloat16), row_max + jnp.log(row_total))


def attend_back(
    queries, key_rows, value_rows, allowed, prefix_keys, prefix_values, log_total, context_grad
):
    qk_scale = HD ** (-0.5)
    token_scores, prefix_scores = block_scores(queries, key_rows, allowed, prefix_keys)
    token_probs = jnp.exp(token_scores - log_total)
    token_dprob = jnp.einsum(
        "hqe,hke->hqk", context_grad, value_rows, preferred_element_type=jnp.float32
    )
    inner = jnp.sum(token_probs * token_dprob, axis=-1, keepdims=True)
    if prefix_scores is not None:
        prefix_probs = jnp.exp(prefix_scores - log_total)
        prefix_dprob = jnp.einsum(
            "hqe,hpe->hqp", context_grad, prefix_values, preferred_element_type=jnp.float32
        )
        inner = inner + jnp.sum(prefix_probs * prefix_dprob, axis=-1, keepdims=True)
    token_dscore = (token_probs * (token_dprob - inner)).astype(jnp.bfloat16)
    query_grad = jnp.einsum(
        "hqk,hke->hqe", token_dscore, key_rows, preferred_element_type=jnp.float32
    )
    key_grad = (
        jnp.einsum("hqk,hqe->hke", token_dscore, queries, preferred_element_type=jnp.float32)
        * qk_scale
    )
    value_grad = jnp.einsum(
        "hqk,hqe->hke",
        token_probs.astype(jnp.bfloat16),
        context_grad,
        preferred_element_type=jnp.float32,
    )
    if prefix_scores is None:
        return (query_grad * qk_scale, (key_grad, value_grad))
    prefix_dscore = (prefix_probs * (prefix_dprob - inner)).astype(jnp.bfloat16)
    query_grad = query_grad + jnp.einsum(
        "hqp,hpe->hqe", prefix_dscore, prefix_keys, preferred_element_type=jnp.float32
    )
    prefix_key_grad = (
        jnp.einsum("hqp,hqe->hpe", prefix_dscore, queries, preferred_element_type=jnp.float32)
        * qk_scale
    )
    prefix_value_grad = jnp.einsum(
        "hqp,hqe->hpe",
        prefix_probs.astype(jnp.bfloat16),
        context_grad,
        preferred_element_type=jnp.float32,
    )
    return (query_grad * qk_scale, (key_grad, value_grad, prefix_key_grad, prefix_value_grad))


def sequence_forward(
    queries, key_rows, value_rows, row_segs, key_segs, prefix_keys, prefix_values, causal
):
    seq_width = queries.shape[1]
    block_rows = min(512, seq_width)

    def one_block(block_index):
        offset = block_index * block_rows
        allowed = block_mask(
            lax.dynamic_slice_in_dim(row_segs, offset, block_rows, 0), key_segs, offset, causal
        )
        query_part = lax.dynamic_slice_in_dim(queries, offset, block_rows, 1)
        return attend_block(query_part, key_rows, value_rows, allowed, prefix_keys, prefix_values)

    context, log_total = lax.map(one_block, jnp.arange(seq_width // block_rows, dtype=jnp.int32))
    return (join_blocks(context), join_blocks(log_total))


def sequence_backward(
    queries,
    key_rows,
    value_rows,
    row_segs,
    key_segs,
    prefix_keys,
    prefix_values,
    causal,
    log_total,
    context_grad,
):
    seq_width = queries.shape[1]
    block_rows = min(512, seq_width)
    key_zero = jnp.zeros(key_rows.shape, jnp.float32)
    initial = (key_zero, key_zero)
    if prefix_keys is not None:
        prefix_zero = jnp.zeros(prefix_keys.shape, jnp.float32)
        initial = initial + (prefix_zero, prefix_zero)

    def one_block(running, block_index):
        offset = block_index * block_rows
        allowed = block_mask(
            lax.dynamic_slice_in_dim(row_segs, offset, block_rows, 0), key_segs, offset, causal
        )
        query_part = lax.dynamic_slice_in_dim(queries, offset, block_rows, 1)
        total_part = lax.dynamic_slice_in_dim(log_total, offset, block_rows, 1)
        grad_part = lax.dynamic_slice_in_dim(context_grad, offset, block_rows, 1)
        query_grad, block_grads = attend_back(
            query_part,
            key_rows,
            value_rows,
            allowed,
            prefix_keys,
            prefix_values,
            total_part,
            grad_part,
        )
        return (tuple((summed + added for summed, added in zip(running, block_grads))), query_grad)

    running, query_grad = lax.scan(
        one_block, initial, jnp.arange(seq_width // block_rows, dtype=jnp.int32)
    )
    outputs = (
        join_blocks(query_grad).astype(jnp.bfloat16),
        running[0].astype(jnp.bfloat16),
        running[1].astype(jnp.bfloat16),
    )
    return outputs + running[2:]


def gather_rows(row_share):
    return lax.all_gather(row_share, "heads", axis=0, tiled=True)


def gather_grads(row_share):
    return lax.all_gather(row_share, "heads", axis=0, tiled=True)


def sum_rows(partial_value):
    return lax.psum_scatter(partial_value, "heads", scatter_dimension=0, tiled=True)


def sum_grads(partial_value):
    return lax.psum_scatter(partial_value, "heads", scatter_dimension=0, tiled=True)


def body(
    tokens,
    memory,
    cotangent,
    dec_seg,
    mem_seg,
    w_self,
    w_self_out,
    w_cross_q,
    w_cross_kv,
    w_cross_out,
    fc_in,
    fc_out,
    ad_down,
    ad_up,
    prefix,
    ln_gain,
    ln_bias,
):
    local_width = w_self.shape[2]
    heads_here = local_width // HD
    seg_dec = dec_seg.reshape(-1, SEQ)
    seg_mem = mem_seg.reshape(-1, MLEN)
    seq_count = seg_dec.shape[0]
    prefix_heads = to_heads(prefix, heads_here)
    prefix_keys = prefix_heads[0]
    prefix_values = prefix_heads[1]
    gathered_x = gather_rows(tokens)
    self_proj = jnp.einsum(
        "td,cdn->ctn", gathered_x, w_self, preferred_element_type=jnp.float32
    ).astype(jnp.bfloat16)
    self_proj = self_proj.reshape(3, seq_count, SEQ, local_width)
    self_queries = to_heads(self_proj[0], heads_here)
    self_keys = to_heads(self_proj[1], heads_here)
    self_values = to_heads(self_proj[2], heads_here)

    def self_forward(packed):
        return sequence_forward(
            packed[0], packed[1], packed[2], packed[3], packed[3], prefix_keys, prefix_values, True
        )

    self_context, self_total = lax.map(
        self_forward, (self_queries, self_keys, self_values, seg_dec)
    )
    attn_partial = jnp.dot(from_heads(self_context), w_self_out, preferred_element_type=jnp.float32)
    resid_one = tokens.astype(jnp.float32) + sum_rows(attn_partial)
    hidden_one = norm_forward(resid_one, ln_gain[0], ln_bias[0])
    gathered_one = gather_rows(hidden_one.astype(jnp.bfloat16))
    gathered_mem = lax.all_gather(memory, "heads", axis=0, tiled=True)
    cross_rows = jnp.dot(gathered_one, w_cross_q, preferred_element_type=jnp.float32).astype(
        jnp.bfloat16
    )
    cross_proj = jnp.einsum(
        "td,cdn->ctn", gathered_mem, w_cross_kv, preferred_element_type=jnp.float32
    ).astype(jnp.bfloat16)
    cross_queries = to_heads(cross_rows.reshape(seq_count, SEQ, local_width), heads_here)
    cross_proj = cross_proj.reshape(2, seq_count, MLEN, local_width)
    cross_keys = to_heads(cross_proj[0], heads_here)
    cross_values = to_heads(cross_proj[1], heads_here)

    def cross_forward(packed):
        return sequence_forward(
            packed[0], packed[1], packed[2], packed[3], packed[4], None, None, False
        )

    cross_context, cross_total = lax.map(
        cross_forward, (cross_queries, cross_keys, cross_values, seg_dec, seg_mem)
    )
    cross_partial = jnp.dot(
        from_heads(cross_context), w_cross_out, preferred_element_type=jnp.float32
    )
    resid_two = hidden_one + sum_rows(cross_partial)
    hidden_two = norm_forward(resid_two, ln_gain[1], ln_bias[1])
    hidden_low = hidden_two.astype(jnp.bfloat16)
    full_in, full_out, full_down, full_up = (fc_in, fc_out, ad_down, ad_up)
    ffn_rows = gather_rows(hidden_low)
    pre_gelu = jnp.dot(ffn_rows, full_in, preferred_element_type=jnp.float32)
    activated = jax.nn.gelu(pre_gelu, approximate=False).astype(jnp.bfloat16)
    pre_relu = jnp.dot(ffn_rows, full_down, preferred_element_type=jnp.float32)
    adapted = (pre_relu * jax.nn.sigmoid(pre_relu)).astype(jnp.bfloat16)
    branch = jnp.dot(
        activated, full_out, preferred_element_type=jnp.float32
    ) + adapter_scale * jnp.dot(adapted, full_up, preferred_element_type=jnp.float32)
    resid_three = hidden_two + sum_rows(branch)
    output = norm_forward(resid_three, ln_gain[2], ln_bias[2]).astype(jnp.bfloat16)
    grad_three = norm_backward(resid_three, ln_gain[2], cotangent.astype(jnp.float32))
    grad_branch = grad_three.astype(jnp.bfloat16)
    branch_rows = gather_grads(grad_branch)
    grad_gelu = (dot_right(branch_rows, full_out) * gelu_slope(pre_gelu)).astype(jnp.bfloat16)
    grad_relu = (adapter_scale * dot_right(branch_rows, full_up) * silu_slope(pre_relu)).astype(
        jnp.bfloat16
    )
    up_grad = adapter_scale * dot_left(adapted, branch_rows)
    down_grad = dot_left(ffn_rows, grad_relu)
    hidden_partial = dot_right(grad_gelu, full_in) + dot_right(grad_relu, full_down)
    grad_two_in = grad_three + sum_grads(hidden_partial)
    down_grad, up_grad = (
        lax.psum(down_grad.astype(jnp.bfloat16), "rows").astype(jnp.float32),
        lax.psum(up_grad.astype(jnp.bfloat16), "rows").astype(jnp.float32),
    )
    grad_two = norm_backward(resid_two, ln_gain[1], grad_two_in)
    cross_out_rows = gather_grads(grad_two.astype(jnp.bfloat16))
    cross_dctx = dot_right(cross_out_rows, w_cross_out).astype(jnp.bfloat16)
    cross_dctx = to_heads(cross_dctx.reshape(seq_count, SEQ, local_width), heads_here)

    def cross_back(packed):
        return sequence_backward(
            packed[0],
            packed[1],
            packed[2],
            packed[3],
            packed[4],
            None,
            None,
            False,
            packed[5],
            packed[6],
        )

    cross_qgrad, cross_kgrad, cross_vgrad = lax.map(
        cross_back,
        (cross_queries, cross_keys, cross_values, seg_dec, seg_mem, cross_total, cross_dctx),
    )
    memory_kv = jnp.stack([from_heads(cross_kgrad), from_heads(cross_vgrad)])
    one_partial = dot_right(from_heads(cross_qgrad), w_cross_q)
    grad_one_in = grad_two + sum_grads(one_partial)
    memory_partial = jnp.einsum(
        "ctn,cdn->td", memory_kv, w_cross_kv, preferred_element_type=jnp.float32
    )
    grad_memory = lax.psum_scatter(
        memory_partial.astype(jnp.bfloat16), "heads", scatter_dimension=0, tiled=True
    ).astype(jnp.float32)
    grad_one = norm_backward(resid_one, ln_gain[0], grad_one_in)
    attn_rows = gather_grads(grad_one.astype(jnp.bfloat16))
    self_dctx = dot_right(attn_rows, w_self_out).astype(jnp.bfloat16)
    self_dctx = to_heads(self_dctx.reshape(seq_count, SEQ, local_width), heads_here)

    def self_back(running, packed):
        query_grad, key_grad, value_grad, pkey_grad, pvalue_grad = sequence_backward(
            packed[0],
            packed[1],
            packed[2],
            packed[3],
            packed[3],
            prefix_keys,
            prefix_values,
            True,
            packed[4],
            packed[5],
        )
        return (
            (running[0] + pkey_grad, running[1] + pvalue_grad),
            (query_grad, key_grad, value_grad),
        )

    zero_grad = jnp.zeros(prefix_keys.shape, jnp.float32)
    prefix_sums, self_grads = lax.scan(
        self_back,
        (zero_grad, zero_grad),
        (self_queries, self_keys, self_values, seg_dec, self_total, self_dctx),
    )
    self_stack = jnp.stack(
        [from_heads(self_grads[0]), from_heads(self_grads[1]), from_heads(self_grads[2])]
    )
    input_partial = jnp.einsum(
        "ctn,cdn->td", self_stack, w_self, preferred_element_type=jnp.float32
    )
    grad_input = grad_one + sum_grads(input_partial)
    prefix_grad = (
        jnp.stack([prefix_sums[0], prefix_sums[1]])
        .transpose(0, 2, 1, 3)
        .reshape(2, prefix.shape[1], local_width)
    )
    prefix_grad = lax.psum(prefix_grad, "rows")
    return (output, grad_input, grad_memory, prefix_grad, down_grad, up_grad)


QB = 256
KB = 256
LOG2E = math.log2(math.e)
NEG = -1e30


def nt(a, b):
    return lax.dot_general(a, b, (((1,), (1,)), ((), ())), preferred_element_type=jnp.float32)


def nn(a, b):
    return lax.dot_general(a, b, (((1,), (0,)), ((), ())), preferred_element_type=jnp.float32)


def tn(a, b):
    return lax.dot_general(a, b, (((0,), (0,)), ((), ())), preferred_element_type=jnp.float32)


def half_lanes(v, h):
    lane = lax.broadcasted_iota(jnp.int32, v.shape, 1)
    keep = (lane < 64) if h == 0 else (lane >= 64)
    return jnp.where(keep, v, jnp.zeros_like(v))


def prefix_rows(scores):
    row = lax.broadcasted_iota(jnp.int32, scores.shape, 0)
    return jnp.where(lax.rem(row, 64) < 30, scores, NEG)


MESH = pl.DeviceIdType.MESH
TILE = 256

TOK, TOK_C, MEM, MEM_C = 112, 113, 114, 115
SELF_PIECE, OUT_ONE, CROSS_Q, CROSS_PIECE, OUT_TWO = 128, 132, 133, 134, 138
SLOTS, LOCAL_SLOTS = 128, 48
GROUPS = ((1, 0), (1, 0), (1, 1), (1, 0), (0, 0), (0, 1), (1, 0))
SCHEDULE = (33, 16, 17, 0, 36, 1, 19, 20, 34, 3, 2, 32, 114, 37, 65, 35, 5, 112, 38, 18, 115, 49, 21, 97, 52, 48, 22, 113, 4, 96, 128, 129, 50, 51, 130, 81, 80, 131, 100, 132, 133, 53, 134, 98, 99, 64, 135, 82, 136, 66, 101, 137, 70, 138)


class Place:
    def __init__(self):
        self.row, self.head = lax.axis_index("rows"), lax.axis_index("heads")
        self.c, self.z = lax.rem(self.row, 2), lax.div(self.row, 2)
        self.x, self.y = lax.rem(self.head, 2), lax.div(self.head, 2)
        self.odd = lax.rem(self.z, 2)
        c, x, y, z = self.c, self.x, self.y, self.z
        self.to_x = (self.row, 2 * y + 1 - x)
        self.to_y = (self.row, 2 * (1 - y) + x)
        self.to_d = (self.row, 2 * (1 - y) + 1 - x)
        self.to_z = (2 * (z + 1 - 2 * self.odd) + c, self.head)
        self.to_c = (2 * z + 1 - c, self.head)
        self.to_s = (2 * z + x, 2 * y + c)

    def greet(self, devices, swaps):
        barrier = pltpu.get_barrier_semaphore()
        for device in devices:
            pl.semaphore_signal(barrier, inc=1, device_id=device, device_id_type=MESH)
        count = len(devices)
        if swaps:
            moves = self.c != self.x

            @pl.when(moves)
            def _():
                pl.semaphore_signal(barrier, inc=1, device_id=self.to_s, device_id_type=MESH)

            count = count + moves.astype(jnp.int32)
        pl.semaphore_wait(barrier, count)


def prefix_block(rows):
    nothing = jnp.zeros_like(rows)
    return jnp.concatenate([half_lanes(rows, 0), nothing, half_lanes(rows, 1), nothing], axis=0)


def attend_tile(q, k, v, mask, kp, vp):
    scale = 0.125 * LOG2E
    if kp is not None:
        lane = lax.broadcasted_iota(jnp.int32, (q.shape[0], 128), 1)
        sp = jnp.where(lax.rem(lane, 64) < 30, nt(q, kp) * scale, NEG)
    tops, sums, es = [], [], []
    for h in range(2):
        s = jnp.where(mask, nt(half_lanes(q, h), k) * scale, NEG)
        m = jnp.max(s, axis=1, keepdims=True)
        if kp is not None:
            inside = (lane < 64) if h == 0 else (lane >= 64)
            m = jnp.maximum(m, jnp.max(jnp.where(inside, sp, NEG), axis=1, keepdims=True))
        e = jnp.exp2(s - m)
        sums.append(jnp.sum(e, axis=1, keepdims=True))
        es.append(e.astype(jnp.bfloat16))
        tops.append(m)
    out = nn(es[0], half_lanes(v, 0)) + nn(es[1], half_lanes(v, 1))
    side = lax.broadcasted_iota(jnp.int32, (q.shape[0], 128), 1) < 64
    if kp is not None:
        ep = jnp.exp2(sp - jnp.where(side, tops[0], tops[1]))
        sums = [sums[0] + jnp.sum(jnp.where(side, ep, 0.0), axis=1, keepdims=True), sums[1] + jnp.sum(jnp.where(side, 0.0, ep), axis=1, keepdims=True)]
        out = out + nn(ep.astype(jnp.bfloat16), vp)
    out = out * jnp.where(side, 1.0 / sums[0], 1.0 / sums[1])
    lse = jnp.where(side, tops[0] + jnp.log2(sums[0]), tops[1] + jnp.log2(sums[1])).T
    return out.astype(jnp.bfloat16), [lse[0:1], lse[64:65]]


def forward_kernel(
    tokens, memory, seg, mseg, prefix, w_self, w_so, w_cq, w_ckv, w_co, fc_in, fc_out, ad_down, ad_up, gain, bias,
    o_wself, o_qkv, o_sctx, o_slse, o_pre, o_wso_m, o_wso_o, o_wkv, o_wq_m, o_wq_o, o_wco_m, o_wco_o,
    o_q, o_kv, o_cctx, o_clse, o_resid1, o_resid2, o_bounds, o_ad, fin, fout, fad,
    wself, qkv, sctx, slse, pre, wso_m, wso_o, wkv, wq_m, wq_o, wco_m, wco_o,
    q_all, kv, cctx, clse, resid1, resid2, bounds, ad, tok, mem, sctx_o, cctx_o, q_send, hidden, low_one, columns, seg_v, mseg_v,
    send, recv, local,
):
    place_of = Place()
    c, x, y, odd = place_of.c, place_of.x, place_of.y, place_of.odd
    to_x, to_y, to_z, to_c, to_s = place_of.to_x, place_of.to_y, place_of.to_z, place_of.to_c, place_of.to_s
    stays, moves = c == x, c != x
    place_of.greet((to_x, to_y, to_z, to_c), True)

    taken = []

    def there(src, dst, device):
        slot = len(taken)
        taken.append(slot)
        return pltpu.make_async_remote_copy(
            src_ref=src, dst_ref=dst, send_sem=send.at[slot], recv_sem=recv.at[slot], device_id=device, device_id_type=MESH
        )

    used = []

    def here(src, dst):
        slot = len(used)
        used.append(slot)
        return pltpu.make_async_copy(src, dst, local.at[slot])

    deep = w_self.shape[1]
    half = tok.shape[0] // 2
    step = lambda start, size, unit: pl.ds(pl.multiple_of(start, unit), size)
    mine = step(c * half, half, half)
    others = step((1 - c) * half, half, half)
    lanes = step(c * 128, 128, 128)
    other_lanes = step((1 - c) * 128, 128, 128)
    rows_c, rows_o = lanes, other_lanes
    foreign = pl.ds(128, 384)
    hid = fc_in.shape[1]
    units = ad.shape[1]
    pending = []

    def swap_of(src, target):
        away = there(src, target.at[step(x * half, half, half)], to_s)
        home = here(src, target.at[mine])
        back = there(target.at[mine], target.at[mine], to_c)

        def start():
            pl.when(moves)(away.start)
            pl.when(stays)(home.start)

        def wait():
            pl.when(moves)(away.wait)
            pl.when(stays)(home.wait)

        return start, wait, back

    def seg_of(src, dst):
        home = here(src.at[y], dst)
        away = there(src.at[y], dst, to_c)

        def start():
            pl.when(stays)(home.start)
            pl.when(stays)(away.start)

        def wait():
            pl.when(stays)(home.wait)
            pl.when(stays)(away.wait_send)
            pl.when(moves)(away.wait_recv)

        return start, wait

    def deep_rows(shared):
        return step(odd * (deep // 2), deep // 2, deep // 2) if shared else pl.ds(0, deep)

    def thin_rows(piece, shared):
        return step(128 * piece + odd * 64, 64, 64) if shared else pl.ds(128 * piece, 128)

    def thin_own(shared):
        return step(128 * c + odd * 64, 64, 64) if shared else rows_c

    def span(size, shared):
        return step(c * (size // 2) + odd * (size // 4), size // 4, size // 4) if shared else step(c * (size // 2), size // 2, size // 2)

    lane_of = lambda i: pl.ds(128 * i, 128)

    def group_a(shared):
        rows = deep_rows(shared)
        first = lambda piece: [(w_self.at[i, rows, lanes], wself.at[piece, rows, lane_of(i)]) for i in range(3)] + [
            (prefix.at[:, :, lanes], pre.at[piece])
        ]
        return first, lambda piece: [wself.at[piece, rows], pre.at[piece]], 1, []

    def group_thin(src, dst_m, dst_o, shared):
        first = lambda piece: [(src.at[thin_own(shared)], dst_m.at[thin_rows(piece, shared)])]
        return first, lambda piece: [dst_m.at[thin_rows(piece, shared)]], 1, [(dst_m.at[foreign], dst_o.at[foreign])]

    def group_q(shared):
        rows = deep_rows(shared)
        first = lambda piece: [(w_cq.at[rows, lanes], wq_m.at[rows, lane_of(piece)])]
        return first, lambda piece: [wq_m.at[rows, lane_of(piece)]], 1, [(wq_m.at[:, foreign], wq_o.at[:, foreign])]

    def group_v(shared):
        rows = deep_rows(shared)
        first = lambda piece: [(w_ckv.at[i, rows, lanes], wkv.at[piece, rows, lane_of(i)]) for i in range(2)]
        return first, lambda piece: [wkv.at[piece, rows]], 1, []

    def group_i(shared):
        cols = span(hid, shared)
        first = lambda piece: [(fc_in.at[:, cols], fin.at[piece - 1, :, cols])]
        return first, lambda piece: [fin.at[piece - 1, :, cols]], 1, []

    def group_o(shared):
        rows, some = span(hid, shared), span(units, shared)
        first = lambda piece: [(fc_out.at[rows], fout.at[piece - 1, rows]), (ad.at[:, some], fad.at[piece - 1, :, some])]
        hold = lambda piece: [fout.at[piece - 1, rows], fad.at[piece - 1, :, some]]
        return first, hold, 2, []

    makers = [
        group_a,
        functools.partial(group_thin, w_so, wso_m, wso_o),
        group_q,
        group_v,
        functools.partial(group_thin, w_co, wco_m, wco_o),
        group_i,
        group_o,
    ]
    copies, needs = {}, {}
    for index, (make, (shared, through_x)) in enumerate(zip(makers, GROUPS)):
        first, hold, shared_count, cross = make(bool(shared))
        base = 16 * index
        copies[base] = [there(src, dst, to_x) for src, dst in first(1)]
        copies[base + 1] = [there(src, dst, to_y) for src, dst in first(2)]
        near, device = (2, to_x) if through_x else (1, to_y)
        copies[base + 2] = [there(src, dst, device) for src, dst in zip(hold(near), hold(3))]
        needs[base], needs[base + 1], needs[base + 2] = [], [], [base + near - 1]
        arrived = [base, base + 1, base + 2]
        if shared:
            for i in range(3):
                copies[base + 3 + i] = [there(ref, ref, to_z) for ref in hold(i + 1)[:shared_count]]
                needs[base + 3 + i] = [base + i]
                arrived.append(base + 3 + i)
        if cross:
            copies[base + 6] = [there(src, dst, to_c) for src, dst in cross]
            needs[base + 6] = arrived
    tok_start, tok_wait, tok_back = swap_of(tokens, tok)
    mem_start, mem_wait, mem_back = swap_of(memory, mem)
    copies[TOK_C], copies[MEM_C] = [tok_back], [mem_back]
    needs[TOK_C], needs[MEM_C] = [TOK], [MEM]
    seg_start, seg_wait = seg_of(seg, seg_v)
    mseg_start, mseg_wait = seg_of(mseg, mseg_v)
    sctx_out = [there(sctx.at[others, lane_of(i)], sctx_o.at[:, lane_of(i)], to_c) for i in range(4)]
    cctx_out = [there(cctx.at[others, lane_of(i)], cctx_o.at[:, lane_of(i)], to_c) for i in range(4)]
    q_out = there(q_send, q_all.at[mine], to_c)

    landed = set()

    def wait_for(op):
        if op in landed:
            return
        landed.add(op)
        if op == TOK:
            tok_wait()
        elif op == MEM:
            mem_wait()
        elif op in copies:
            for copy in copies[op]:
                copy.wait_recv()

    def launch(op):
        if op == TOK:
            tok_start()
        elif op == MEM:
            mem_start()
        else:
            for need in needs[op]:
                wait_for(need)
            for copy in copies[op]:
                copy.start()
                pending.append(copy)

    saves = []

    def keep(src, dst):
        copy = here(src, dst)
        copy.start()
        saves.append(copy)

    own_a = [here(w_self.at[i, :, lanes], wself.at[0, :, lane_of(i)]) for i in range(3)]
    own_a.append(here(prefix.at[:, :, lanes], pre.at[0]))
    own_b = [
        here(w_so.at[rows_c], wso_m.at[lane_of(0)]),
        here(w_so.at[rows_o], wso_o.at[lane_of(0)]),
        here(w_co.at[rows_c], wco_m.at[lane_of(0)]),
        here(w_co.at[rows_o], wco_o.at[lane_of(0)]),
        here(w_cq.at[:, lanes], wq_m.at[:, lane_of(0)]),
        here(w_cq.at[:, other_lanes], wq_o.at[:, lane_of(0)]),
        here(w_ckv.at[0, :, lanes], wkv.at[0, :, lane_of(0)]),
        here(w_ckv.at[1, :, lanes], wkv.at[0, :, lane_of(1)]),
    ]

    def bounds_of():
        seg_wait()
        mseg_wait()
        dec, men = seg_v[...], mseg_v[...]

        def below(values, d):
            return jnp.sum((values < d).astype(jnp.int32), axis=1, keepdims=True)

        def pick(counts):
            out = jnp.broadcast_to(counts[0], dec.shape)
            for d in range(1, 4):
                out = jnp.where(dec == d, counts[d], out)
            return out

        zero = jnp.zeros((1, 1), jnp.int32)
        full = jnp.full((1, 1), MLEN, jnp.int32)
        self_lo = pick([zero] + [below(dec, d) for d in range(1, 4)])
        mem_counts = [zero] + [below(men, d) for d in range(1, 4)] + [full]
        bounds[...] = jnp.concatenate(
            [self_lo, lax.broadcasted_iota(jnp.int32, dec.shape, 1), pick(mem_counts[:4]), pick(mem_counts[1:]) - 1]
            + [jnp.zeros_like(dec)] * 4,
            axis=0,
        )
        keep(bounds, o_bounds)
        wide = jnp.concatenate([bounds[...].astype(jnp.float32), jnp.zeros((120, SEQ), jnp.float32)], axis=0)
        columns[...] = wide.T.astype(jnp.int32)

    def weight_needs(base, piece):
        found = [base + piece - 1, base + 2 + piece]
        return [op for op in found if op in copies]

    def project(dst, p, source, weight):
        dst[p] = nn(source[...], weight[p]).astype(jnp.bfloat16)

    def self_piece(p):
        project(qkv, p, tok, wself)
        kp = prefix_block(pre[p, 0])
        vp = prefix_block(pre[p, 1])
        place = step(p * 128, 128, 128)
        for qi in range(SEQ // QB):
            width = (qi + 1) * QB
            rows = slice(qi * QB, (qi + 1) * QB)
            pos = lax.broadcasted_iota(jnp.int32, (QB, width), 1)
            limit = columns[rows, :]
            mask = (pos >= limit[:, 0:1]) & (pos <= limit[:, 1:2])
            out, lse = attend_tile(qkv[p, rows, 0:128], qkv[p, 0:width, 128:256], qkv[p, 0:width, 256:384], mask, kp, vp)
            sctx[rows, place] = out
            for h in range(2):
                slse[p, h : h + 1, rows] = lse[h]

    def cross_piece(p):
        project(kv, p, mem, wkv)
        place = step(p * 128, 128, 128)

        def block(qi, _):
            rows = step(qi * QB, QB, QB)
            pos = lax.broadcasted_iota(jnp.int32, (QB, MLEN), 1)
            limit = columns[rows, :]
            mask = (pos >= limit[:, 2:3]) & (pos <= limit[:, 3:4])
            out, lse = attend_tile(q_all[rows, place], kv[p, :, 0:128], kv[p, :, 128:256], mask, None, None)
            cctx[rows, place] = out
            for h in range(2):
                clse[p, h : h + 1, rows] = lse[h]
            return 0

        lax.fori_loop(0, SEQ // QB, block, 0)

    def with_out(t, resid_before, ctx_m, ctx_o, w_m, w_o):
        rows = step(t * TILE, TILE, TILE)
        rows_all = step(c * half + t * TILE, TILE, TILE)
        return resid_before + nn(ctx_m[rows_all, :], w_m[...]) + nn(ctx_o[rows, :], w_o[...])

    def out_one(t, _):
        rows = step(t * TILE, TILE, TILE)
        rows_all = step(c * half + t * TILE, TILE, TILE)
        resid = with_out(t, tok[rows_all, :].astype(jnp.float32), sctx, sctx_o, wso_m, wso_o)
        resid1[rows, :] = resid
        normed = norm_forward(resid, gain[0:1, :], bias[0:1, :])
        hidden[rows, :] = normed
        low_one[rows, :] = normed.astype(jnp.bfloat16)
        return 0

    def out_two(t, _):
        rows = step(t * TILE, TILE, TILE)
        resid2[rows, :] = with_out(t, hidden[rows, :], cctx, cctx_o, wco_m, wco_o)
        return 0

    def q_rows(t, _):
        rows = step(t * TILE, TILE, TILE)
        rows_all = step(c * half + t * TILE, TILE, TILE)
        q_send[rows, :] = nn(low_one[rows, :], wq_o[...]).astype(jnp.bfloat16)
        q_all[rows_all, :] = nn(low_one[rows, :], wq_m[...]).astype(jnp.bfloat16)
        return 0

    def split_at(order, first, count):
        places = [order.index(first + k) for k in range(count)]
        starts = [0] + [place + 1 for place in places]
        return [order[a:b] for a, b in zip(starts, places)], order[places[-1] + 1 :]

    def pieces_loop(segments, ready, work, sends):
        def body(p, _):
            for k, segment in enumerate(segments):

                @pl.when(p == k)
                def _():
                    for op in segment:
                        launch(op)
                    ready(k)

            work(p)
            for k, copy in enumerate(sends):
                pl.when(p == k)(copy.start)
            return 0

        lax.fori_loop(0, len(segments), body, 0)
        pending.extend(sends)

    ad_copy = here(ad_up, ad.at[1])
    ad_copy.start()
    ad[0] = ad_down[...].astype(jnp.float32).T.astype(jnp.bfloat16)
    ad_copy.wait()
    keep(ad, o_ad)

    for copy in own_a[:3]:
        copy.start()
    own_a[3].start()
    seg_start()
    mseg_start()
    segments, rest = split_at(list(SCHEDULE), SELF_PIECE, 4)
    for op in segments[0]:
        launch(op)
    for copy in own_b:
        copy.start()
    bounds_of()
    for copy in own_a:
        copy.wait()
    segments[0] = []

    def self_ready(k):
        if k == 0:
            wait_for(TOK_C)
        else:
            for op in weight_needs(0, k):
                wait_for(op)

    pieces_loop(segments, self_ready, self_piece, sctx_out)
    for src, dst in ((qkv, o_qkv), (wself, o_wself), (sctx, o_sctx), (slse, o_slse), (pre, o_pre)):
        keep(src, dst)
    for copy in own_b:
        copy.wait()
    before, rest = split_at(rest, OUT_ONE, 1)
    for op in before[0]:
        launch(op)
    for copy in sctx_out:
        copy.wait_recv()
    wait_for(16 + 6)
    lax.fori_loop(0, half // TILE, out_one, 0)
    for src, dst in ((resid1, o_resid1), (wso_m, o_wso_m), (wso_o, o_wso_o)):
        keep(src, dst)
    before, rest = split_at(rest, CROSS_Q, 1)
    for op in before[0]:
        launch(op)
    wait_for(32 + 6)
    lax.fori_loop(0, half // TILE, q_rows, 0)
    q_out.start()
    pending.append(q_out)
    for src, dst in ((wq_m, o_wq_m), (wq_o, o_wq_o)):
        keep(src, dst)
    segments, rest = split_at(rest, CROSS_PIECE, 4)

    def cross_ready(k):
        if k == 0:
            wait_for(MEM_C)
            q_out.wait_recv()
        else:
            for op in weight_needs(48, k):
                wait_for(op)

    pieces_loop(segments, cross_ready, cross_piece, cctx_out)
    for src, dst in ((q_all, o_q), (kv, o_kv), (wkv, o_wkv), (cctx, o_cctx), (clse, o_clse)):
        keep(src, dst)
    before, rest = split_at(rest, OUT_TWO, 1)
    for op in before[0]:
        launch(op)
    for copy in cctx_out:
        copy.wait_recv()
    wait_for(64 + 6)
    lax.fori_loop(0, half // TILE, out_two, 0)
    for src, dst in ((resid2, o_resid2), (wco_m, o_wco_m), (wco_o, o_wco_o)):
        keep(src, dst)
    for op in rest:
        launch(op)
    for op in list(copies):
        wait_for(op)
    for copy in pending:
        copy.wait_send()
    for copy in saves:
        copy.wait()


class Held(typing.NamedTuple):
    wself: jax.Array
    qkv: jax.Array
    sctx: jax.Array
    slse: jax.Array
    pre: jax.Array
    wso_m: jax.Array
    wso_o: jax.Array
    wkv: jax.Array
    wq_m: jax.Array
    wq_o: jax.Array
    wco_m: jax.Array
    wco_o: jax.Array
    q: jax.Array
    kv: jax.Array
    cctx: jax.Array
    clse: jax.Array
    resid1: jax.Array
    resid2: jax.Array
    bounds: jax.Array
    ad: jax.Array
    fin: jax.Array
    fout: jax.Array
    fad: jax.Array


def forward_call(tokens, memory, seg, mseg, prefix, w_self, w_so, w_cq, w_ckv, w_co, fc_in, fc_out, ad_down, ad_up, gain, bias):
    bf16, f32 = jnp.bfloat16, jnp.float32
    half, deep = tokens.shape
    shape = jax.ShapeDtypeStruct
    held = dict(
        wself=((4, deep, 384), bf16),
        qkv=((4, SEQ, 384), bf16),
        sctx=((SEQ, 512), bf16),
        slse=((4, 8, SEQ), f32),
        pre=((4, 2, 32, 128), bf16),
        wso_m=((512, deep), bf16),
        wso_o=((512, deep), bf16),
        wkv=((4, deep, 256), bf16),
        wq_m=((deep, 512), bf16),
        wq_o=((deep, 512), bf16),
        wco_m=((512, deep), bf16),
        wco_o=((512, deep), bf16),
        q=((SEQ, 512), bf16),
        kv=((4, MLEN, 256), bf16),
        cctx=((SEQ, 512), bf16),
        clse=((4, 8, SEQ), f32),
        resid1=((half, deep), f32),
        resid2=((half, deep), f32),
        bounds=((8, SEQ), jnp.int32),
        ad=((2,) + ad_up.shape, bf16),
    )
    outs = [shape(*value) for value in held.values()]
    outs += [shape((3,) + fc_in.shape, bf16), shape((3,) + fc_out.shape, bf16), shape((3, 2) + ad_up.shape, bf16)]
    scratch = [pltpu.VMEM(*value) for value in held.values()] + [
        pltpu.VMEM((SEQ, deep), bf16),
        pltpu.VMEM((MLEN, deep), bf16),
        pltpu.VMEM((half, 512), bf16),
        pltpu.VMEM((half, 512), bf16),
        pltpu.VMEM((half, 512), bf16),
        pltpu.VMEM((half, deep), f32),
        pltpu.VMEM((half, deep), bf16),
        pltpu.VMEM((SEQ, 128), jnp.int32),
        pltpu.VMEM((1, SEQ), jnp.int32),
        pltpu.VMEM((1, SEQ), jnp.int32),
        pltpu.SemaphoreType.DMA((SLOTS,)),
        pltpu.SemaphoreType.DMA((SLOTS,)),
        pltpu.SemaphoreType.DMA((LOCAL_SLOTS,)),
    ]
    anywhere = pl.BlockSpec(memory_space=pl.ANY)
    vmem = pl.BlockSpec(memory_space=pltpu.VMEM)
    results = pl.pallas_call(
        forward_kernel,
        out_shape=outs,
        in_specs=[anywhere] * 12 + [vmem, anywhere] + [vmem] * 2,
        out_specs=[anywhere] * len(outs),
        scratch_shapes=scratch,
        compiler_params=pltpu.CompilerParams(
            collective_id=0, has_side_effects=True, vmem_limit_bytes=58 * 2**20
        ),
        name="layer_forward",
    )(tokens, memory, seg, mseg, prefix, w_self, w_so, w_cq, w_ckv, w_co, fc_in, fc_out, ad_down, ad_up, gain, bias)
    return Held(*results)


TOGETHER = 4


def backward_kernel(has_prefix, first_bound, bounds_s, *refs):
    if has_prefix:
        qkv_ref, bounds, ctx_ref, dctx_ref, lse_ref, pre_ref, dqkv_ref, dpre_ref, dk_acc, dv_acc, dq_acc, dpre_acc = refs
        q_at = lambda g, rows: qkv_ref[g, rows, 0:128]
        k_at = lambda g, rows: qkv_ref[g, rows, 128:256]
        v_at = lambda g, rows: qkv_ref[g, rows, 256:384]
    else:
        q_ref, kv_ref, bounds, ctx_ref, dctx_ref, lse_ref, dq_ref, dkv_ref, dk_acc, dv_acc, dq_acc = refs
        q_at = lambda g, rows: q_ref[rows, 128 * g : 128 * g + 128]
        k_at = lambda g, rows: kv_ref[g, rows, 0:128]
        v_at = lambda g, rows: kv_ref[g, rows, 128:256]
    scale = 0.125 * LOG2E
    dk_acc[...] = jnp.zeros_like(dk_acc)
    dv_acc[...] = jnp.zeros_like(dv_acc)
    kps, vps = [], []
    for g in range(TOGETHER):
        if has_prefix:
            kps.append(prefix_block(pre_ref[g, 0]))
            vps.append(prefix_block(pre_ref[g, 1]))
    if has_prefix:
        dpre_acc[...] = jnp.zeros_like(dpre_acc)

    def one(qi, _):
        q0 = pl.multiple_of(qi * QB, QB)
        span = pl.ds(q0, QB)
        lo = bounds[first_bound : first_bound + 1, span]
        hi = bounds[first_bound + 1 : first_bound + 2, span]
        inner, lse, qh, dh = [], [], [], []
        for g in range(TOGETHER):
            q = q_at(g, span)
            dctx = dctx_ref[span, 128 * g : 128 * g + 128]
            ctx = ctx_ref[span, 128 * g : 128 * g + 128]
            prod = (dctx.astype(jnp.float32) * ctx.astype(jnp.float32)).T
            inner.append([jnp.sum(prod[h * 64 : h * 64 + 64], axis=0, keepdims=True) for h in range(2)])
            lse.append([lse_ref[g, h : h + 1, span] for h in range(2)])
            qh.append([half_lanes(q, h) for h in range(2)])
            dh.append([half_lanes(dctx, h) for h in range(2)])
            if has_prefix:
                sp = prefix_rows(nt(kps[g], q) * scale)
                rows = lambda pair: jnp.concatenate([jnp.broadcast_to(t, (64, QB)) for t in pair], axis=0)
                pp = jnp.exp2(sp - rows(lse[g]))
                dpp = nt(vps[g], dctx)
                dsp = (pp * (dpp - rows(inner[g]))).astype(jnp.bfloat16)
                dpre_acc[g, 0] += nn(dsp, q)
                dpre_acc[g, 1] += nn(pp.astype(jnp.bfloat16), dctx)
                dq_acc[g] = tn(dsp, kps[g])
            else:
                dq_acc[g] = jnp.zeros((QB, 128), jnp.float32)

        def chunk(ki, _):
            k0 = pl.multiple_of(ki * KB, KB)
            keys = pl.ds(k0, KB)
            pos = k0 + lax.broadcasted_iota(jnp.int32, (KB, QB), 0)
            mask = (pos >= lo) & (pos <= hi)
            for g in range(TOGETHER):
                k = k_at(g, keys)
                v = v_at(g, keys)
                ps, dss = [], []
                for h in range(2):
                    s = nt(k, qh[g][h]) * scale
                    p = jnp.exp2(jnp.where(mask, s, NEG) - lse[g][h])
                    dp = nt(v, dh[g][h])
                    ds = (p * (dp - inner[g][h])).astype(jnp.bfloat16)
                    ps.append(p.astype(jnp.bfloat16))
                    dss.append(ds)
                dv_acc[g, keys, :] += nn(jnp.concatenate(ps, axis=1), jnp.concatenate(dh[g], axis=0))
                dq_acc[g] += tn(jnp.concatenate(dss, axis=0), jnp.concatenate([half_lanes(k, 0), half_lanes(k, 1)], axis=0))
                dk_acc[g, keys, :] += nn(jnp.concatenate(dss, axis=1), jnp.concatenate(qh[g], axis=0))
            return 0

        lowest = lax.div(bounds_s[first_bound, q0], KB)
        highest = lax.div(bounds_s[first_bound + 1, q0 + QB - 1], KB) + 1
        lax.fori_loop(lowest, highest, chunk, 0)
        for g in range(TOGETHER):
            dq = (dq_acc[g] * 0.125).astype(jnp.bfloat16)
            if has_prefix:
                dqkv_ref[g, span, 0:128] = dq
            else:
                dq_ref[span, 128 * g : 128 * g + 128] = dq
        return 0

    lax.fori_loop(0, SEQ // QB, one, 0)
    for g in range(TOGETHER):
        dk = (dk_acc[g] * 0.125).astype(jnp.bfloat16)
        dv = dv_acc[g].astype(jnp.bfloat16)
        if has_prefix:
            dqkv_ref[g, :, 128:256] = dk
            dqkv_ref[g, :, 256:384] = dv
            lane = lax.broadcasted_iota(jnp.int32, (32, 128), 1)
            for i, factor in ((0, 0.125), (1, 1.0)):
                dpre_ref[g, i] = jnp.where(lane < 64, dpre_acc[g, i, 0:32], dpre_acc[g, i, 64:96]) * factor
        else:
            dkv_ref[g, :, 0:128] = dk
            dkv_ref[g, :, 128:256] = dv


def backward_call(has_prefix, arrays, bounds, ctx, dctx, lse, pre=None):
    col = pl.BlockSpec((SEQ, 128 * TOGETHER), lambda j, *_: (0, j))
    piece = lambda width: pl.BlockSpec((TOGETHER, SEQ, width), lambda j, *_: (j, 0, 0))
    shape = jax.ShapeDtypeStruct
    bf16, f32 = jnp.bfloat16, jnp.float32
    pre_spec = pl.BlockSpec((TOGETHER, 2, 32, 128), lambda j, *_: (j, 0, 0, 0))
    if has_prefix:
        in_specs = [piece(384)]
        out_specs = [piece(384), pre_spec]
        out_shape = [shape((4, SEQ, 384), bf16), shape((4, 2, 32, 128), f32)]
    else:
        in_specs = [col, piece(256)]
        out_specs = [col, piece(256)]
        out_shape = [shape((SEQ, 512), bf16), shape((4, SEQ, 256), bf16)]
    in_specs += [
        pl.BlockSpec((8, SEQ), lambda j, *_: (0, 0)),
        col,
        col,
        pl.BlockSpec((TOGETHER, 8, SEQ), lambda j, *_: (j, 0, 0)),
    ]
    args = list(arrays) + [bounds, ctx, dctx, lse]
    scratch = [
        pltpu.VMEM((TOGETHER, SEQ, 128), f32),
        pltpu.VMEM((TOGETHER, SEQ, 128), f32),
        pltpu.VMEM((TOGETHER, QB, 128), f32),
    ]
    if has_prefix:
        in_specs.append(pre_spec)
        args.append(pre)
        scratch.append(pltpu.VMEM((TOGETHER, 2, 128, 128), f32))
    return pl.pallas_call(
        functools.partial(backward_kernel, has_prefix, 0 if has_prefix else 2),
        grid_spec=pltpu.PrefetchScalarGridSpec(
            num_scalar_prefetch=1, grid=(4 // TOGETHER,), in_specs=in_specs, out_specs=out_specs, scratch_shapes=scratch
        ),
        out_shape=out_shape,
        compiler_params=pltpu.CompilerParams(vmem_limit_bytes=60 * 2**20),
        cost_estimate=pl.CostEstimate(flops=10 * 8 * SEQ * SEQ * 64, bytes_accessed=10 * 2**20, transcendentals=8 * SEQ * SEQ),
        name="self_backward" if has_prefix else "cross_backward",
    )(bounds, *args)


HIDDEN = 512


def swap_halves(place, src, dst_there, dst_here, send, recv, local):
    moves = place.c != place.x
    away = pltpu.make_async_remote_copy(
        src_ref=src, dst_ref=dst_there, send_sem=send, recv_sem=recv, device_id=place.to_s, device_id_type=MESH
    )
    home = pltpu.make_async_copy(src, dst_here, local)

    def start():
        pl.when(moves)(away.start)
        pl.when(jnp.logical_not(moves))(home.start)

    def wait():
        pl.when(moves)(away.wait)
        pl.when(jnp.logical_not(moves))(home.wait)

    return start, wait


def feed_kernel(
    resid2, cotangent, gain, bias, wco_m_in, wco_o_in, fc_in, fin, fc_out, fout, ad, fad,
    out, grad_two, unit_sum, dctx,
    win, wout, adw, slope, low, hidden, acc, gate, ada, branch_low, sem,
    cot, out_v, units, unit_send, unit_recv, near_send, near_recv, dctx_s, wco_m, wco_o, send, recv, local,
):
    place = Place()
    place.greet((place.to_x, place.to_y, place.to_d, place.to_c), True)
    c = place.c
    cot_start, cot_wait = swap_halves(place, cotangent, cot, cot, send.at[0], recv.at[0], local.at[0])
    out_copy = pltpu.make_async_copy(out_v, out, local.at[1])
    two_copy = pltpu.make_async_copy(acc, grad_two, local.at[2])
    co_copies = [
        pltpu.make_async_copy(wco_m_in, wco_m, local.at[3]),
        pltpu.make_async_copy(wco_o_in, wco_o, local.at[4]),
    ]
    cot_start()

    def there(slot, src, dst, device):
        return pltpu.make_async_remote_copy(
            src_ref=src, dst_ref=dst, send_sem=send.at[slot], recv_sem=recv.at[slot], device_id=device, device_id_type=MESH
        )

    half = resid2.shape[0]
    mine = pl.ds(pl.multiple_of(c * half, half), half)
    unit_core = there(2, unit_send, unit_recv, place.to_c)
    unit_near = [
        there(3 + i, near_send.at[i], near_recv.at[i], device) for i, device in enumerate((place.to_x, place.to_y, place.to_d))
    ]
    dctx_core = there(6, dctx_s, dctx.at[mine], place.to_c)
    bf16 = jnp.bfloat16
    per = fc_in.shape[1] // HIDDEN
    steps = 4 * per
    down, up = adw.at[0], adw.at[1]
    group = ad.shape[1]
    some = group // 2
    hidden_c = pl.ds(pl.multiple_of(c * HIDDEN, HIDDEN), HIDDEN)
    units_c = pl.ds(pl.multiple_of(c * some, some), some)
    loads, ad_loads, crossing = [], [], []
    for piece in range(4):
        ad_rows = pl.ds(pl.multiple_of(group * piece + c * some, some), some)
        own_in = win.at[2 * piece + c]
        own_out = wout.at[2 * piece + c]
        if piece == 0:
            loads.append(pltpu.make_async_copy(fc_in.at[:, hidden_c], own_in, sem.at[0, 0]))
            loads.append(pltpu.make_async_copy(fc_out.at[hidden_c], own_out, sem.at[1, 0]))
            hidden_o = pl.ds(pl.multiple_of((1 - c) * HIDDEN, HIDDEN), HIDDEN)
            loads.append(pltpu.make_async_copy(fc_in.at[:, hidden_o], win.at[1 - c], sem.at[0, 1]))
            loads.append(pltpu.make_async_copy(fc_out.at[hidden_o], wout.at[1 - c], sem.at[1, 1]))
            ad_loads.append(pltpu.make_async_copy(ad, adw.at[:, pl.ds(0, group)], sem.at[2, 0]))
        else:
            src_in, src_out, src_ad = fin.at[piece - 1, :, hidden_c], fout.at[piece - 1, hidden_c], fad.at[piece - 1, :, units_c]
            loads.append(pltpu.make_async_copy(src_in, own_in, sem.at[0, 2 * piece]))
            loads.append(pltpu.make_async_copy(src_out, own_out, sem.at[1, 2 * piece]))
            ad_loads.append(pltpu.make_async_copy(src_ad, adw.at[:, ad_rows], sem.at[2, piece]))
            crossing.append(there(4 + 3 * piece, src_in, own_in, place.to_c))
            crossing.append(there(5 + 3 * piece, src_out, own_out, place.to_c))
            crossing.append(there(6 + 3 * piece, src_ad, adw.at[:, ad_rows], place.to_c))
    for copy in crossing + loads + ad_loads + co_copies:
        copy.start()

    rows_all = resid2.shape[0]
    tiles = rows_all // TILE
    at = lambda t: pl.ds(pl.multiple_of(t * TILE, TILE), TILE)

    def begin(t, _):
        rows = at(t)
        normed = norm_forward(resid2[rows, :], gain[1:2, :], bias[1:2, :])
        hidden[rows, :] = normed
        low[rows, :] = normed.astype(bf16)
        return 0

    lax.fori_loop(0, tiles, begin, 0)
    acc[...] = jnp.zeros_like(acc)

    def ahead(s, _):
        piece, late = lax.div(s, 2), lax.rem(s, 2)
        j = 2 * piece + c + late * (1 - 2 * c)
        for k in range(1, 4):

            @pl.when(s == 2 * k + 1)
            def _():
                crossing[3 * k - 3].wait_recv()
                crossing[3 * k - 2].wait_recv()

        @pl.when((late == 0) | (s == 1))
        def _():
            for i, buf in enumerate((win, wout)):
                pltpu.make_async_copy(buf.at[j], buf.at[j], sem.at[i, s]).wait()

        pre = nn(low[...], win[j])
        phi = 0.5 * (1.0 + lax.erf(pre * 0.7071067811865476))
        slope[j] = phi + pre * jnp.exp(-0.5 * pre * pre) * 0.3989422804014327
        acc[...] += nn((pre * phi).astype(bf16), wout[j])
        return 0

    lax.fori_loop(0, steps, ahead, 0)
    for copy in ad_loads + crossing[2::3]:
        copy.wait()
    pre = nt(low[...], down[...])
    sigma = jax.nn.sigmoid(pre)
    gate[...] = sigma * (1.0 + pre * (1.0 - sigma))
    ada[...] = (pre * sigma).astype(bf16)
    acc[...] += adapter_scale * nn(ada[...], up[...])

    def middle(t, _):
        rows = at(t)
        resid = hidden[rows, :] + acc[rows, :]
        normed, inv = norm_parts(resid)
        out_v[rows, :] = (normed * gain[2:3, :] + bias[2:3, :]).astype(bf16)
        scaled = cot[rows, :].astype(jnp.float32) * gain[2:3, :]
        grad = inv * (
            scaled
            - jnp.mean(scaled, axis=-1, keepdims=True)
            - normed * jnp.mean(scaled * normed, axis=-1, keepdims=True)
        )
        acc[rows, :] = grad
        branch_low[rows, :] = grad.astype(bf16)
        return 0

    cot_wait()
    lax.fori_loop(0, tiles, middle, 0)
    out_copy.start()
    grelu = (adapter_scale * nt(branch_low[...], up[...]) * gate[...]).astype(bf16)
    features = low.shape[1]
    for first, value in ((0, tn(grelu, low[...])), (features, adapter_scale * tn(ada[...], branch_low[...]))):
        for k in range(8):
            units[k // 2, k % 2, :, first : first + features] = value[some * k : some * (k + 1)]
    for i in range(4):
        unit_send[i] = units[i, 1 - c].astype(bf16)
    unit_core.start()
    acc[...] += nn(grelu, down[...])

    def behind(j, _):
        grad = (nt(branch_low[...], wout[j]) * slope[j]).astype(bf16)
        acc[...] += nt(grad, win[j])
        return 0

    lax.fori_loop(0, 2, behind, 0)
    unit_core.wait()
    for i in range(3):
        near_send[i] = (units[i + 1, c] + unit_recv[i + 1].astype(jnp.float32)).astype(bf16)
    for copy in unit_near:
        copy.start()
    lax.fori_loop(2, steps, behind, 0)

    def finish(t, _):
        rows = at(t)
        grad = norm_backward(resid2[rows, :], gain[1:2, :], acc[rows, :])
        acc[rows, :] = grad
        small = grad.astype(bf16)
        low[rows, :] = small
        dctx_s[rows, :] = nt(small, wco_o[...]).astype(bf16)
        return 0

    for copy in co_copies:
        copy.wait()
    lax.fori_loop(0, tiles, finish, 0)
    dctx_core.start()
    two_copy.start()
    dctx[mine, :] = nt(low[...], wco_m[...]).astype(bf16)
    for copy in unit_near:
        copy.wait()
    total = units[0, c] + unit_recv[0].astype(jnp.float32)
    for i in range(3):
        total = total + near_recv[i].astype(jnp.float32)
    unit_sum[...] = total
    out_copy.wait()
    two_copy.wait()
    for k in range(3):
        crossing[3 * k].wait_send()
        crossing[3 * k + 1].wait_send()
    dctx_core.wait()


def feed_call(resid2, cot, gain, bias, wco_m, wco_o, fc_in, fin, fc_out, fout, ad, fad):
    bf16, f32 = jnp.bfloat16, jnp.float32
    rows, deep = resid2.shape
    shape = jax.ShapeDtypeStruct
    anywhere = pl.BlockSpec(memory_space=pl.ANY)
    vmem = pl.BlockSpec(memory_space=pltpu.VMEM)
    steps = 4 * fc_in.shape[1] // HIDDEN
    units = 4 * ad.shape[1]
    some = ad.shape[1] // 2
    return pl.pallas_call(
        feed_kernel,
        out_shape=[
            shape((rows, deep), bf16),
            shape((rows, deep), f32),
            shape((some, 2 * deep), f32),
            shape((2 * rows, 512), bf16),
        ],
        in_specs=[vmem, anywhere] + [vmem] * 2 + [anywhere] * 8,
        out_specs=[anywhere] * 2 + [vmem] * 2,
        scratch_shapes=[
            pltpu.VMEM((steps, deep, HIDDEN), bf16),
            pltpu.VMEM((steps, HIDDEN, deep), bf16),
            pltpu.VMEM((2, units, deep), bf16),
            pltpu.VMEM((steps, rows, HIDDEN), f32),
            pltpu.VMEM((rows, deep), bf16),
            pltpu.VMEM((rows, deep), f32),
            pltpu.VMEM((rows, deep), f32),
            pltpu.VMEM((rows, units), f32),
            pltpu.VMEM((rows, units), bf16),
            pltpu.VMEM((rows, deep), bf16),
            pltpu.SemaphoreType.DMA((3, 8)),
            pltpu.VMEM((rows, deep), bf16),
            pltpu.VMEM((rows, deep), bf16),
            pltpu.VMEM((4, 2, some, 2 * deep), f32),
            pltpu.VMEM((4, some, 2 * deep), bf16),
            pltpu.VMEM((4, some, 2 * deep), bf16),
            pltpu.VMEM((3, some, 2 * deep), bf16),
            pltpu.VMEM((3, some, 2 * deep), bf16),
            pltpu.VMEM((rows, 512), bf16),
            pltpu.VMEM(wco_m.shape, bf16),
            pltpu.VMEM(wco_o.shape, bf16),
            pltpu.SemaphoreType.DMA((16,)),
            pltpu.SemaphoreType.DMA((16,)),
            pltpu.SemaphoreType.DMA((5,)),
        ],
        compiler_params=pltpu.CompilerParams(
            collective_id=1, has_side_effects=True, vmem_limit_bytes=61 * 2**20
        ),
        name="feed_forward",
    )(resid2, cot, gain, bias, wco_m, wco_o, fc_in, fin, fc_out, fout, ad, fad)


def query_kernel(
    dq_in, dkv_in, wkv_in, wq_m_in, wq_o_in, two_in, resid_in, wso_m_in, wso_o_in, gain,
    one_out, dctx, mem_out,
    dq, dkv, wkv, wq_m, wq_o, grad_two, resid1, wso_m, wso_o,
    grad_one, mem_sum, dq_o, mem_s, mem_r, dctx_s, dctx_m, low, send, recv, local,
):
    bf16 = jnp.bfloat16
    place = Place()
    c = place.c
    half = resid1.shape[0]
    mine = pl.ds(pl.multiple_of(c * half, half), half)
    others = pl.ds(pl.multiple_of((1 - c) * half, half), half)

    def there(slot, src, dst):
        return pltpu.make_async_remote_copy(
            src_ref=src, dst_ref=dst, send_sem=send.at[slot], recv_sem=recv.at[slot], device_id=place.to_c, device_id_type=MESH
        )

    def here(slot, src, dst):
        return pltpu.make_async_copy(src, dst, local.at[slot])

    wkv_copy, dkv_far, dkv_near = here(0, wkv_in, wkv), here(1, dkv_in.at[:, others], dkv.at[:, others]), here(2, dkv_in.at[:, mine], dkv.at[:, mine])
    pairs = (
        (dq_in.at[mine], dq), (wq_m_in, wq_m), (wq_o_in, wq_o), (two_in, grad_two), (resid_in, resid1), (wso_o_in, wso_o), (wso_m_in, wso_m)
    )
    rest = [here(3 + i, src, dst) for i, (src, dst) in enumerate(pairs)]
    for copy in [wkv_copy, dkv_far] + rest + [dkv_near]:
        copy.start()
    one_copy, mem_copy, dctx_copy = here(10, grad_one, one_out), here(11, mem_sum, mem_out), here(12, dctx_m, dctx.at[mine])
    place.greet((place.to_c,), False)
    dq_core = there(0, dq_in.at[others], dq_o)
    mem_core = there(1, mem_s, mem_r)
    dctx_core = there(2, dctx_s, dctx.at[mine])
    dq_core.start()
    tiles = half // TILE
    at = lambda t: pl.ds(pl.multiple_of(t * TILE, TILE), TILE)
    place_at = lambda first, t: pl.ds(pl.multiple_of(first * half + t * TILE, TILE), TILE)

    def memory_rows(rows):
        return sum(nt(dkv[p, rows, :], wkv[p]) for p in range(4))

    def far(t, _):
        mem_s[at(t), :] = memory_rows(place_at(1 - c, t)).astype(bf16)
        return 0

    wkv_copy.wait()
    dkv_far.wait()
    lax.fori_loop(0, tiles, far, 0)
    mem_core.start()
    for copy in rest:
        copy.wait()
    dq_core.wait()

    def one(t, _):
        rows = at(t)
        grad_in = grad_two[rows, :] + nt(dq[rows, :], wq_m[...]) + nt(dq_o[rows, :], wq_o[...])
        grad = norm_backward(resid1[rows, :], gain[0:1, :], grad_in)
        grad_one[rows, :] = grad
        small = grad.astype(bf16)
        low[rows, :] = small
        dctx_s[rows, :] = nt(small, wso_o[...]).astype(bf16)
        return 0

    lax.fori_loop(0, tiles, one, 0)
    dctx_core.start()
    one_copy.start()
    dctx_m[...] = nt(low[...], wso_m[...]).astype(bf16)
    dctx_copy.start()
    mem_core.wait()
    dkv_near.wait()

    def near(t, _):
        mem_sum[at(t), :] = (memory_rows(place_at(c, t)) + mem_r[at(t), :].astype(jnp.float32)).astype(bf16)
        return 0

    lax.fori_loop(0, tiles, near, 0)
    mem_copy.start()
    for copy in (dctx_core, one_copy, dctx_copy, mem_copy):
        copy.wait()


def query_call(dq, dkv, wkv, wq_m, wq_o, grad_two, resid1, wso_m, wso_o, gain):
    bf16, f32 = jnp.bfloat16, jnp.float32
    half, deep = resid1.shape
    shape = jax.ShapeDtypeStruct
    vmem = pl.BlockSpec(memory_space=pltpu.VMEM)
    anywhere = pl.BlockSpec(memory_space=pl.ANY)
    return pl.pallas_call(
        query_kernel,
        out_shape=[shape((half, deep), f32), shape((2 * half, 512), bf16), shape((half, deep), bf16)],
        in_specs=[anywhere] * 9 + [vmem],
        out_specs=[anywhere] * 3,
        scratch_shapes=[pltpu.VMEM((half, 512), bf16)]
        + [pltpu.VMEM(value.shape, value.dtype) for value in (dkv, wkv, wq_m, wq_o, grad_two, resid1, wso_m, wso_o)]
        + [
            pltpu.VMEM((half, deep), f32),
            pltpu.VMEM((half, deep), bf16),
            pltpu.VMEM((half, 512), bf16),
            pltpu.VMEM((half, deep), bf16),
            pltpu.VMEM((half, deep), bf16),
            pltpu.VMEM((half, 512), bf16),
            pltpu.VMEM((half, 512), bf16),
            pltpu.VMEM((half, deep), bf16),
            pltpu.SemaphoreType.DMA((3,)),
            pltpu.SemaphoreType.DMA((3,)),
            pltpu.SemaphoreType.DMA((13,)),
        ],
        compiler_params=pltpu.CompilerParams(collective_id=2, has_side_effects=True, vmem_limit_bytes=60 * 2**20),
        name="query_backward",
    )(dq, dkv, wkv, wq_m, wq_o, grad_two, resid1, wso_m, wso_o, gain)


def last_kernel(
    planes, dqkv_in, wself_in, one_in, blocks_in, unit_in,
    input_out, prefix_grad, down_grad, up_grad,
    dqkv, wself, grad_one, blocks, unit_sum, part_s, part_r, out_s, pre_near, pre_sum, pre_z, pre_c, unit_s, unit_z, unit_a, unit_o, unit_all, send, recv, local,
):
    bf16, f32 = jnp.bfloat16, jnp.float32
    place = Place()
    c, x, z = place.c, place.x, place.z
    steps = []
    step = 1
    while step < planes:
        other = z + step - 2 * step * lax.rem(lax.div(z, step), 2)
        steps.append((2 * other + c, place.head))
        step *= 2
    moves = c != x
    stays = c == x
    half = grad_one.shape[0]
    slots = []

    def there(src, dst, device):
        slot = len(slots)
        slots.append(slot)
        return pltpu.make_async_remote_copy(
            src_ref=src, dst_ref=dst, send_sem=send.at[slot], recv_sem=recv.at[slot], device_id=device, device_id_type=MESH
        )

    tiles = half // TILE
    at = lambda t: pl.ds(t * TILE, TILE)
    place_at = lambda first, t: pl.ds(pl.multiple_of(first * half + t * TILE, TILE), TILE)

    def here(slot, src, dst):
        return pltpu.make_async_copy(src, dst, local.at[slot])

    loads = [here(0, wself_in, wself), here(1, blocks_in, blocks), here(2, unit_in, unit_sum), here(3, one_in, grad_one)]
    far_loads = [here(4 + t, dqkv_in.at[:, place_at(1 - c, t)], dqkv.at[:, place_at(1 - c, t)]) for t in range(tiles)]
    near_loads = [
        here(4 + tiles + t, dqkv_in.at[:, place_at(c, t)], dqkv.at[:, place_at(c, t)]) for t in range(tiles)
    ]
    for copy in [loads[1], loads[2], far_loads[0], loads[0], near_loads[0], loads[3]] + far_loads[1:] + near_loads[1:]:
        copy.start()

    place.greet([place.to_x, place.to_y, place.to_d, place.to_c] + steps, True)
    pre_copies = [
        there(blocks.at[i + 1], pre_near.at[i], device) for i, device in enumerate((place.to_x, place.to_y, place.to_d))
    ]
    pre_steps = [there(pre_sum.at[i], pre_z.at[i], device) for i, device in enumerate(steps)]
    pre_core = there(pre_sum.at[len(steps)], pre_c, place.to_c)
    start, size = 0, unit_sum.shape[0]
    unit_down, unit_up, kept = [], [], []
    for i, device in enumerate(steps):
        bit = lax.rem(lax.div(z, 2**i), 2)
        size = size // 2
        away = pl.ds(pl.multiple_of(start + (1 - bit) * size, size), size)
        start = start + bit * size
        kept.append(pl.ds(pl.multiple_of(start, size), size))
        unit_down.append(there(unit_s.at[away], unit_z.at[i, away], device))
        unit_up.append(there(unit_a.at[kept[-1]], unit_a.at[kept[-1]], device))
    unit_core = there(unit_a, unit_o, place.to_c)
    part_copies = [there(part_s.at[at(t)], part_r.at[at(t)], place.to_c) for t in range(tiles)]
    out_copies = [there(out_s.at[at(t)], input_out.at[at(t)], place.to_s) for t in range(tiles)]
    own_copies = [here(4 + 2 * tiles + t, out_s.at[at(t)], input_out.at[at(t)]) for t in range(tiles)]
    loads[1].wait()
    for copy in pre_copies:
        copy.start()
    loads[2].wait()
    unit_s[...] = unit_sum[...].astype(bf16)
    unit_down[0].start()

    def input_rows(rows):
        return sum(nt(dqkv[p, rows, :], wself[p]) for p in range(4))

    def advance(i):
        pre_steps[i].wait()
        pre_sum[i + 1] = pre_sum[i] + pre_z[i]
        if i + 1 < len(steps):
            pre_steps[i + 1].start()
        else:
            pre_core.start()

    def reduce_units(i):
        unit_down[i].wait()
        total = unit_sum[kept[i], :] + unit_z[i, kept[i], :].astype(f32)
        if i + 1 < len(steps):
            unit_sum[kept[i], :] = total
            unit_s[kept[i], :] = total.astype(bf16)
            unit_down[i + 1].start()
        else:
            unit_a[kept[i], :] = total.astype(bf16)
            unit_up[i].start()

    loads[0].wait()
    for t in range(tiles):
        far_loads[t].wait()
        part_s[at(t), :] = input_rows(place_at(1 - c, t)).astype(bf16)
        part_copies[t].start()
        near_loads[t].wait()
        near = input_rows(place_at(c, t))
        if t == 0:
            loads[3].wait()
        part_copies[t].wait()
        out_s[at(t), :] = (near + part_r[at(t), :].astype(f32) + grad_one[at(t), :]).astype(bf16)
        pl.when(moves)(out_copies[t].start)
        pl.when(stays)(own_copies[t].start)
        if t == 0:
            for copy in pre_copies:
                copy.wait()
            pre_sum[0] = blocks[0] + pre_near[0] + pre_near[1] + pre_near[2]
            pre_steps[0].start()
        if t < len(steps):
            reduce_units(t)
    for i in range(tiles, len(steps)):
        reduce_units(i)
    for i in range(len(steps)):
        advance(i)
        unit_up[len(steps) - 1 - i].wait()
        if i + 1 < len(steps):
            unit_up[len(steps) - 2 - i].start()
        else:
            unit_core.start()
    pre_core.wait()
    unit_core.wait()
    my_lanes = pl.ds(pl.multiple_of(c * 128, 128), 128)
    other_lanes = pl.ds(pl.multiple_of((1 - c) * 128, 128), 128)
    prefix_grad[:, :, my_lanes] = pre_sum[len(steps)]
    prefix_grad[:, :, other_lanes] = pre_c[...]
    some = unit_sum.shape[0]
    unit_all[pl.ds(pl.multiple_of(c * some, some), some), :] = unit_a[...].astype(f32)
    unit_all[pl.ds(pl.multiple_of((1 - c) * some, some), some), :] = unit_o[...].astype(f32)
    features = grad_one.shape[1]
    down_grad[...] = unit_all[:, 0:features].T
    up_grad[...] = unit_all[:, features : 2 * features]

    for t in range(tiles):
        pl.when(moves)(out_copies[t].wait)
        pl.when(stays)(own_copies[t].wait)


def last_call(planes, dqkv, wself, grad_one, blocks, unit_sum):
    bf16, f32 = jnp.bfloat16, jnp.float32
    half, deep = grad_one.shape
    some = unit_sum.shape[0]
    count = planes.bit_length() - 1
    shape = jax.ShapeDtypeStruct
    vmem = pl.BlockSpec(memory_space=pltpu.VMEM)
    anywhere = pl.BlockSpec(memory_space=pl.ANY)
    return pl.pallas_call(
        functools.partial(last_kernel, planes),
        out_shape=[
            shape((half, deep), bf16),
            shape((2, 32, 256), f32),
            shape((deep, 2 * some), f32),
            shape((2 * some, deep), f32),
        ],
        in_specs=[anywhere] * 5,
        out_specs=[vmem] * 4,
        scratch_shapes=[pltpu.VMEM(value.shape, value.dtype) for value in (dqkv, wself, grad_one, blocks, unit_sum)]
        + [
            pltpu.VMEM((half, deep), bf16),
            pltpu.VMEM((half, deep), bf16),
            pltpu.VMEM((half, deep), bf16),
            pltpu.VMEM((3, 2, 32, 128), f32),
            pltpu.VMEM((count + 1, 2, 32, 128), f32),
            pltpu.VMEM((count, 2, 32, 128), f32),
            pltpu.VMEM((2, 32, 128), f32),
            pltpu.VMEM((some, 2 * deep), bf16),
            pltpu.VMEM((count, some, 2 * deep), bf16),
            pltpu.VMEM((some, 2 * deep), bf16),
            pltpu.VMEM((some, 2 * deep), bf16),
            pltpu.VMEM((2 * some, 2 * deep), f32),
            pltpu.SemaphoreType.DMA((3 + 3 * count + 2 + 2 * (half // TILE),)),
            pltpu.SemaphoreType.DMA((3 + 3 * count + 2 + 2 * (half // TILE),)),
            pltpu.SemaphoreType.DMA((4 + 3 * (half // TILE),)),
        ],
        compiler_params=pltpu.CompilerParams(collective_id=3, has_side_effects=True, vmem_limit_bytes=60 * 2**20),
        name="last_sums",
    )(dqkv, wself, grad_one, blocks, unit_sum)


AXES = ("rows", "heads")


def fast_fits(mesh):
    rows, heads = mesh.shape["rows"], mesh.shape["heads"]
    return heads == 4 and rows in (4, 8)


def pairs_of(rows, move):
    def number(z, c, y, x):
        return (z * 2 + c) * 4 + y * 2 + x

    found = []
    for z in range(rows // 2):
        for c in range(2):
            for y in range(2):
                for x in range(2):
                    found.append((number(z, c, y, x), number(*move(z, c, y, x))))
    return found


def swapped_rows(rows, value):
    def swapped(z, c, y, x):
        return (z, x, y, c)

    crossing = [pair for pair in pairs_of(rows, swapped) if pair[0] != pair[1]]
    stays = lax.axis_index("rows") % 2 == lax.axis_index("heads") % 2
    return jnp.where(stays, value, lax.ppermute(value, AXES, crossing))


def fast_body(
    rows,
    tokens,
    memory,
    cotangent,
    dec_seg,
    mem_seg,
    w_self,
    w_self_out,
    w_cross_q,
    w_cross_kv,
    w_cross_out,
    fc_in,
    fc_out,
    ad_down,
    ad_up,
    prefix,
    ln_gain,
    ln_bias,
):
    count = prefix.shape[1]
    held = forward_call(
        tokens,
        memory,
        dec_seg.reshape(2, 1, SEQ),
        mem_seg.reshape(2, 1, MLEN),
        jnp.pad(prefix, ((0, 0), (0, 32 - count), (0, 0))),
        w_self,
        w_self_out,
        w_cross_q,
        w_cross_kv,
        w_cross_out,
        fc_in,
        fc_out,
        ad_down,
        ad_up,
        ln_gain,
        ln_bias,
    )
    out_own, grad_two, unit_sum, cross_dctx = feed_call(
        held.resid2, cotangent, ln_gain, ln_bias, held.wco_m, held.wco_o,
        fc_in, held.fin, fc_out, held.fout, held.ad, held.fad,
    )
    output = swapped_rows(rows, out_own)
    cross_dq, cross_dkv = backward_call(
        False, (held.q, held.kv), held.bounds, held.cctx, cross_dctx, held.clse
    )
    grad_one, self_dctx, memory_sum = query_call(
        cross_dq, cross_dkv, held.wkv, held.wq_m, held.wq_o, grad_two, held.resid1, held.wso_m, held.wso_o, ln_gain
    )
    grad_memory = swapped_rows(rows, memory_sum).astype(jnp.float32)
    self_dqkv, prefix_blocks = backward_call(
        True, (held.qkv,), held.bounds, held.sctx, self_dctx, held.slse, held.pre
    )
    grad_input, prefix_grad, down_grad, up_grad = last_call(
        rows // 2, self_dqkv, held.wself, grad_one, prefix_blocks, unit_sum
    )
    return (output, grad_input.astype(jnp.float32), grad_memory, prefix_grad[:, :count], down_grad, up_grad)


def solution(mesh):
    in_specs = (
        P(("rows", "heads"), None),
        P(("rows", "heads"), None),
        P(("rows", "heads"), None),
        P("rows"),
        P("rows"),
        P(None, None, "heads"),
        P("heads", None),
        P(None, "heads"),
        P(None, None, "heads"),
        P("heads", None),
        P(None, "heads"),
        P("heads", None),
        P(None, "heads"),
        P("heads", None),
        P(None, None, "heads"),
        P(),
        P(),
    )
    out_specs = (
        P(("rows", "heads"), None),
        P(("rows", "heads"), None),
        P(("rows", "heads"), None),
        P(None, None, "heads"),
        P(None, "heads"),
        P("heads", None),
    )
    chosen = functools.partial(fast_body, mesh.shape["rows"]) if fast_fits(mesh) else body
    return jax.shard_map(chosen, mesh=mesh, in_specs=in_specs, out_specs=out_specs, check_vma=False)
```

```python
import functools
import math
import typing

import jax
import jax.numpy as jnp
from jax import lax
from jax.experimental import pallas as pl
from jax.experimental.pallas import tpu as pltpu
from jax.sharding import PartitionSpec as P

HD = 64
SEQ = 1024
MLEN = 1024


epsilon = 1e-05
adapter_scale = 4.0
masked_score = -1e30


def dot_right(left, right):
    return lax.dot_general(
        left, right, (((1,), (1,)), ((), ())), preferred_element_type=jnp.float32
    )


def dot_left(left, right):
    return lax.dot_general(
        left, right, (((0,), (0,)), ((), ())), preferred_element_type=jnp.float32
    )


def norm_parts(resid):
    average = jnp.mean(resid, axis=-1, keepdims=True)
    centered = resid - average
    inv_scale = lax.rsqrt(jnp.mean(centered * centered, axis=-1, keepdims=True) + epsilon)
    return (centered * inv_scale, inv_scale)


def norm_forward(resid, gain, shift):
    normed, inv_scale = norm_parts(resid)
    return normed * gain + shift


def norm_backward(resid, gain, grad_out):
    normed, inv_scale = norm_parts(resid)
    scaled = grad_out * gain
    return inv_scale * (
        scaled
        - jnp.mean(scaled, axis=-1, keepdims=True)
        - normed * jnp.mean(scaled * normed, axis=-1, keepdims=True)
    )


def gelu_slope(pre_gelu):
    return (
        0.5 * (1.0 + lax.erf(pre_gelu * 0.7071067811865476))
        + pre_gelu * jnp.exp(-0.5 * pre_gelu * pre_gelu) * 0.3989422804014327
    )


def silu_slope(pre_relu):
    sigma = jax.nn.sigmoid(pre_relu)
    return sigma * (1.0 + pre_relu * (1.0 - sigma))


def to_heads(arrays, heads_here):
    return arrays.reshape(arrays.shape[0], arrays.shape[1], heads_here, HD).transpose(0, 2, 1, 3)


def from_heads(arrays):
    return arrays.transpose(0, 2, 1, 3).reshape(
        arrays.shape[0] * arrays.shape[2], arrays.shape[1] * arrays.shape[3]
    )


def join_blocks(stacked):
    moved = jnp.moveaxis(stacked, 0, 1)
    return moved.reshape((moved.shape[0], moved.shape[1] * moved.shape[2]) + moved.shape[3:])


def block_mask(row_segs, key_segs, offset, causal):
    allowed = row_segs[:, None] == key_segs[None, :]
    if causal:
        row_places = offset + lax.iota(jnp.int32, row_segs.shape[0])
        key_places = lax.iota(jnp.int32, key_segs.shape[0])
        allowed = allowed & (key_places[None, :] <= row_places[:, None])
    return allowed


def block_scores(queries, key_rows, allowed, prefix_keys):
    qk_scale = HD ** (-0.5)
    token_scores = (
        jnp.einsum("hqe,hke->hqk", queries, key_rows, preferred_element_type=jnp.float32) * qk_scale
    )
    token_scores = jnp.where(allowed[None], token_scores, masked_score)
    if prefix_keys is None:
        return (token_scores, None)
    prefix_scores = (
        jnp.einsum("hqe,hpe->hqp", queries, prefix_keys, preferred_element_type=jnp.float32)
        * qk_scale
    )
    return (token_scores, prefix_scores)


def attend_block(queries, key_rows, value_rows, allowed, prefix_keys, prefix_values):
    token_scores, prefix_scores = block_scores(queries, key_rows, allowed, prefix_keys)
    row_max = jnp.max(token_scores, axis=-1, keepdims=True)
    if prefix_scores is not None:
        row_max = jnp.maximum(row_max, jnp.max(prefix_scores, axis=-1, keepdims=True))
    token_weights = jnp.exp(token_scores - row_max)
    row_total = jnp.sum(token_weights, axis=-1, keepdims=True)
    if prefix_scores is not None:
        prefix_weights = jnp.exp(prefix_scores - row_max)
        row_total = row_total + jnp.sum(prefix_weights, axis=-1, keepdims=True)
    context = jnp.einsum(
        "hqk,hke->hqe",
        (token_weights / row_total).astype(jnp.bfloat16),
        value_rows,
        preferred_element_type=jnp.float32,
    )
    if prefix_scores is not None:
        context = context + jnp.einsum(
            "hqp,hpe->hqe",
            (prefix_weights / row_total).astype(jnp.bfloat16),
            prefix_values,
            preferred_element_type=jnp.float32,
        )
    return (context.astype(jnp.bfloat16), row_max + jnp.log(row_total))


def attend_back(
    queries, key_rows, value_rows, allowed, prefix_keys, prefix_values, log_total, context_grad
):
    qk_scale = HD ** (-0.5)
    token_scores, prefix_scores = block_scores(queries, key_rows, allowed, prefix_keys)
    token_probs = jnp.exp(token_scores - log_total)
    token_dprob = jnp.einsum(
        "hqe,hke->hqk", context_grad, value_rows, preferred_element_type=jnp.float32
    )
    inner = jnp.sum(token_probs * token_dprob, axis=-1, keepdims=True)
    if prefix_scores is not None:
        prefix_probs = jnp.exp(prefix_scores - log_total)
        prefix_dprob = jnp.einsum(
            "hqe,hpe->hqp", context_grad, prefix_values, preferred_element_type=jnp.float32
        )
        inner = inner + jnp.sum(prefix_probs * prefix_dprob, axis=-1, keepdims=True)
    token_dscore = (token_probs * (token_dprob - inner)).astype(jnp.bfloat16)
    query_grad = jnp.einsum(
        "hqk,hke->hqe", token_dscore, key_rows, preferred_element_type=jnp.float32
    )
    key_grad = (
        jnp.einsum("hqk,hqe->hke", token_dscore, queries, preferred_element_type=jnp.float32)
        * qk_scale
    )
    value_grad = jnp.einsum(
        "hqk,hqe->hke",
        token_probs.astype(jnp.bfloat16),
        context_grad,
        preferred_element_type=jnp.float32,
    )
    if prefix_scores is None:
        return (query_grad * qk_scale, (key_grad, value_grad))
    prefix_dscore = (prefix_probs * (prefix_dprob - inner)).astype(jnp.bfloat16)
    query_grad = query_grad + jnp.einsum(
        "hqp,hpe->hqe", prefix_dscore, prefix_keys, preferred_element_type=jnp.float32
    )
    prefix_key_grad = (
        jnp.einsum("hqp,hqe->hpe", prefix_dscore, queries, preferred_element_type=jnp.float32)
        * qk_scale
    )
    prefix_value_grad = jnp.einsum(
        "hqp,hqe->hpe",
        prefix_probs.astype(jnp.bfloat16),
        context_grad,
        preferred_element_type=jnp.float32,
    )
    return (query_grad * qk_scale, (key_grad, value_grad, prefix_key_grad, prefix_value_grad))


def sequence_forward(
    queries, key_rows, value_rows, row_segs, key_segs, prefix_keys, prefix_values, causal
):
    seq_width = queries.shape[1]
    block_rows = min(512, seq_width)

    def one_block(block_index):
        offset = block_index * block_rows
        allowed = block_mask(
            lax.dynamic_slice_in_dim(row_segs, offset, block_rows, 0), key_segs, offset, causal
        )
        query_part = lax.dynamic_slice_in_dim(queries, offset, block_rows, 1)
        return attend_block(query_part, key_rows, value_rows, allowed, prefix_keys, prefix_values)

    context, log_total = lax.map(one_block, jnp.arange(seq_width // block_rows, dtype=jnp.int32))
    return (join_blocks(context), join_blocks(log_total))


def sequence_backward(
    queries,
    key_rows,
    value_rows,
    row_segs,
    key_segs,
    prefix_keys,
    prefix_values,
    causal,
    log_total,
    context_grad,
):
    seq_width = queries.shape[1]
    block_rows = min(512, seq_width)
    key_zero = jnp.zeros(key_rows.shape, jnp.float32)
    initial = (key_zero, key_zero)
    if prefix_keys is not None:
        prefix_zero = jnp.zeros(prefix_keys.shape, jnp.float32)
        initial = initial + (prefix_zero, prefix_zero)

    def one_block(running, block_index):
        offset = block_index * block_rows
        allowed = block_mask(
            lax.dynamic_slice_in_dim(row_segs, offset, block_rows, 0), key_segs, offset, causal
        )
        query_part = lax.dynamic_slice_in_dim(queries, offset, block_rows, 1)
        total_part = lax.dynamic_slice_in_dim(log_total, offset, block_rows, 1)
        grad_part = lax.dynamic_slice_in_dim(context_grad, offset, block_rows, 1)
        query_grad, block_grads = attend_back(
            query_part,
            key_rows,
            value_rows,
            allowed,
            prefix_keys,
            prefix_values,
            total_part,
            grad_part,
        )
        return (tuple((summed + added for summed, added in zip(running, block_grads))), query_grad)

    running, query_grad = lax.scan(
        one_block, initial, jnp.arange(seq_width // block_rows, dtype=jnp.int32)
    )
    outputs = (
        join_blocks(query_grad).astype(jnp.bfloat16),
        running[0].astype(jnp.bfloat16),
        running[1].astype(jnp.bfloat16),
    )
    return outputs + running[2:]


def gather_rows(row_share):
    return lax.all_gather(row_share, "heads", axis=0, tiled=True)


def gather_grads(row_share):
    return lax.all_gather(row_share, "heads", axis=0, tiled=True)


def sum_rows(partial_value):
    return lax.psum_scatter(partial_value, "heads", scatter_dimension=0, tiled=True)


def sum_grads(partial_value):
    return lax.psum_scatter(partial_value, "heads", scatter_dimension=0, tiled=True)


def body(
    tokens,
    memory,
    cotangent,
    dec_seg,
    mem_seg,
    w_self,
    w_self_out,
    w_cross_q,
    w_cross_kv,
    w_cross_out,
    fc_in,
    fc_out,
    ad_down,
    ad_up,
    prefix,
    ln_gain,
    ln_bias,
):
    local_width = w_self.shape[2]
    heads_here = local_width // HD
    seg_dec = dec_seg.reshape(-1, SEQ)
    seg_mem = mem_seg.reshape(-1, MLEN)
    seq_count = seg_dec.shape[0]
    prefix_heads = to_heads(prefix, heads_here)
    prefix_keys = prefix_heads[0]
    prefix_values = prefix_heads[1]
    gathered_x = gather_rows(tokens)
    self_proj = jnp.einsum(
        "td,cdn->ctn", gathered_x, w_self, preferred_element_type=jnp.float32
    ).astype(jnp.bfloat16)
    self_proj = self_proj.reshape(3, seq_count, SEQ, local_width)
    self_queries = to_heads(self_proj[0], heads_here)
    self_keys = to_heads(self_proj[1], heads_here)
    self_values = to_heads(self_proj[2], heads_here)

    def self_forward(packed):
        return sequence_forward(
            packed[0], packed[1], packed[2], packed[3], packed[3], prefix_keys, prefix_values, True
        )

    self_context, self_total = lax.map(
        self_forward, (self_queries, self_keys, self_values, seg_dec)
    )
    attn_partial = jnp.dot(from_heads(self_context), w_self_out, preferred_element_type=jnp.float32)
    resid_one = tokens.astype(jnp.float32) + sum_rows(attn_partial)
    hidden_one = norm_forward(resid_one, ln_gain[0], ln_bias[0])
    gathered_one = gather_rows(hidden_one.astype(jnp.bfloat16))
    gathered_mem = lax.all_gather(memory, "heads", axis=0, tiled=True)
    cross_rows = jnp.dot(gathered_one, w_cross_q, preferred_element_type=jnp.float32).astype(
        jnp.bfloat16
    )
    cross_proj = jnp.einsum(
        "td,cdn->ctn", gathered_mem, w_cross_kv, preferred_element_type=jnp.float32
    ).astype(jnp.bfloat16)
    cross_queries = to_heads(cross_rows.reshape(seq_count, SEQ, local_width), heads_here)
    cross_proj = cross_proj.reshape(2, seq_count, MLEN, local_width)
    cross_keys = to_heads(cross_proj[0], heads_here)
    cross_values = to_heads(cross_proj[1], heads_here)

    def cross_forward(packed):
        return sequence_forward(
            packed[0], packed[1], packed[2], packed[3], packed[4], None, None, False
        )

    cross_context, cross_total = lax.map(
        cross_forward, (cross_queries, cross_keys, cross_values, seg_dec, seg_mem)
    )
    cross_partial = jnp.dot(
        from_heads(cross_context), w_cross_out, preferred_element_type=jnp.float32
    )
    resid_two = hidden_one + sum_rows(cross_partial)
    hidden_two = norm_forward(resid_two, ln_gain[1], ln_bias[1])
    hidden_low = hidden_two.astype(jnp.bfloat16)
    full_in, full_out, full_down, full_up = (fc_in, fc_out, ad_down, ad_up)
    ffn_rows = gather_rows(hidden_low)
    pre_gelu = jnp.dot(ffn_rows, full_in, preferred_element_type=jnp.float32)
    activated = jax.nn.gelu(pre_gelu, approximate=False).astype(jnp.bfloat16)
    pre_relu = jnp.dot(ffn_rows, full_down, preferred_element_type=jnp.float32)
    adapted = (pre_relu * jax.nn.sigmoid(pre_relu)).astype(jnp.bfloat16)
    branch = jnp.dot(
        activated, full_out, preferred_element_type=jnp.float32
    ) + adapter_scale * jnp.dot(adapted, full_up, preferred_element_type=jnp.float32)
    resid_three = hidden_two + sum_rows(branch)
    output = norm_forward(resid_three, ln_gain[2], ln_bias[2]).astype(jnp.bfloat16)
    grad_three = norm_backward(resid_three, ln_gain[2], cotangent.astype(jnp.float32))
    grad_branch = grad_three.astype(jnp.bfloat16)
    branch_rows = gather_grads(grad_branch)
    grad_gelu = (dot_right(branch_rows, full_out) * gelu_slope(pre_gelu)).astype(jnp.bfloat16)
    grad_relu = (adapter_scale * dot_right(branch_rows, full_up) * silu_slope(pre_relu)).astype(
        jnp.bfloat16
    )
    up_grad = adapter_scale * dot_left(adapted, branch_rows)
    down_grad = dot_left(ffn_rows, grad_relu)
    hidden_partial = dot_right(grad_gelu, full_in) + dot_right(grad_relu, full_down)
    grad_two_in = grad_three + sum_grads(hidden_partial)
    down_grad, up_grad = (
        lax.psum(down_grad.astype(jnp.bfloat16), "rows").astype(jnp.float32),
        lax.psum(up_grad.astype(jnp.bfloat16), "rows").astype(jnp.float32),
    )
    grad_two = norm_backward(resid_two, ln_gain[1], grad_two_in)
    cross_out_rows = gather_grads(grad_two.astype(jnp.bfloat16))
    cross_dctx = dot_right(cross_out_rows, w_cross_out).astype(jnp.bfloat16)
    cross_dctx = to_heads(cross_dctx.reshape(seq_count, SEQ, local_width), heads_here)

    def cross_back(packed):
        return sequence_backward(
            packed[0],
            packed[1],
            packed[2],
            packed[3],
            packed[4],
            None,
            None,
            False,
            packed[5],
            packed[6],
        )

    cross_qgrad, cross_kgrad, cross_vgrad = lax.map(
        cross_back,
        (cross_queries, cross_keys, cross_values, seg_dec, seg_mem, cross_total, cross_dctx),
    )
    memory_kv = jnp.stack([from_heads(cross_kgrad), from_heads(cross_vgrad)])
    one_partial = dot_right(from_heads(cross_qgrad), w_cross_q)
    grad_one_in = grad_two + sum_grads(one_partial)
    memory_partial = jnp.einsum(
        "ctn,cdn->td", memory_kv, w_cross_kv, preferred_element_type=jnp.float32
    )
    grad_memory = lax.psum_scatter(
        memory_partial.astype(jnp.bfloat16), "heads", scatter_dimension=0, tiled=True
    ).astype(jnp.float32)
    grad_one = norm_backward(resid_one, ln_gain[0], grad_one_in)
    attn_rows = gather_grads(grad_one.astype(jnp.bfloat16))
    self_dctx = dot_right(attn_rows, w_self_out).astype(jnp.bfloat16)
    self_dctx = to_heads(self_dctx.reshape(seq_count, SEQ, local_width), heads_here)

    def self_back(running, packed):
        query_grad, key_grad, value_grad, pkey_grad, pvalue_grad = sequence_backward(
            packed[0],
            packed[1],
            packed[2],
            packed[3],
            packed[3],
            prefix_keys,
            prefix_values,
            True,
            packed[4],
            packed[5],
        )
        return (
            (running[0] + pkey_grad, running[1] + pvalue_grad),
            (query_grad, key_grad, value_grad),
        )

    zero_grad = jnp.zeros(prefix_keys.shape, jnp.float32)
    prefix_sums, self_grads = lax.scan(
        self_back,
        (zero_grad, zero_grad),
        (self_queries, self_keys, self_values, seg_dec, self_total, self_dctx),
    )
    self_stack = jnp.stack(
        [from_heads(self_grads[0]), from_heads(self_grads[1]), from_heads(self_grads[2])]
    )
    input_partial = jnp.einsum(
        "ctn,cdn->td", self_stack, w_self, preferred_element_type=jnp.float32
    )
    grad_input = grad_one + sum_grads(input_partial)
    prefix_grad = (
        jnp.stack([prefix_sums[0], prefix_sums[1]])
        .transpose(0, 2, 1, 3)
        .reshape(2, prefix.shape[1], local_width)
    )
    prefix_grad = lax.psum(prefix_grad, "rows")
    return (output, grad_input, grad_memory, prefix_grad, down_grad, up_grad)


QB = 256
KB = 256
LOG2E = math.log2(math.e)
NEG = -1e30


def nt(a, b):
    return lax.dot_general(a, b, (((1,), (1,)), ((), ())), preferred_element_type=jnp.float32)


def nn(a, b):
    return lax.dot_general(a, b, (((1,), (0,)), ((), ())), preferred_element_type=jnp.float32)


def tn(a, b):
    return lax.dot_general(a, b, (((0,), (0,)), ((), ())), preferred_element_type=jnp.float32)


def half_lanes(v, h):
    lane = lax.broadcasted_iota(jnp.int32, v.shape, 1)
    keep = (lane < 64) if h == 0 else (lane >= 64)
    return jnp.where(keep, v, jnp.zeros_like(v))


def prefix_rows(scores):
    row = lax.broadcasted_iota(jnp.int32, scores.shape, 0)
    return jnp.where(lax.rem(row, 64) < 30, scores, NEG)


MESH = pl.DeviceIdType.MESH
TILE = 256

TOK, TOK_C, MEM, MEM_C = 112, 113, 114, 115
SELF_PIECE, OUT_ONE, CROSS_Q, CROSS_PIECE, OUT_TWO = 128, 132, 133, 134, 138
SLOTS, LOCAL_SLOTS = 128, 48
GROUPS = ((1, 0), (1, 0), (1, 1), (1, 0), (0, 0), (0, 1), (1, 0))
SCHEDULE = (33, 16, 17, 0, 36, 1, 19, 20, 34, 3, 2, 32, 114, 37, 65, 35, 5, 112, 38, 18, 115, 49, 21, 97, 52, 48, 22, 113, 4, 96, 128, 129, 50, 51, 130, 81, 80, 131, 100, 132, 133, 53, 134, 98, 99, 64, 135, 82, 136, 66, 101, 137, 70, 138)


class Place:
    def __init__(self):
        self.row, self.head = lax.axis_index("rows"), lax.axis_index("heads")
        self.c, self.z = lax.rem(self.row, 2), lax.div(self.row, 2)
        self.x, self.y = lax.rem(self.head, 2), lax.div(self.head, 2)
        self.odd = lax.rem(self.z, 2)
        c, x, y, z = self.c, self.x, self.y, self.z
        self.to_x = (self.row, 2 * y + 1 - x)
        self.to_y = (self.row, 2 * (1 - y) + x)
        self.to_d = (self.row, 2 * (1 - y) + 1 - x)
        self.to_z = (2 * (z + 1 - 2 * self.odd) + c, self.head)
        self.to_c = (2 * z + 1 - c, self.head)
        self.to_s = (2 * z + x, 2 * y + c)

    def greet(self, devices, swaps):
        barrier = pltpu.get_barrier_semaphore()
        for device in devices:
            pl.semaphore_signal(barrier, inc=1, device_id=device, device_id_type=MESH)
        count = len(devices)
        if swaps:
            moves = self.c != self.x

            @pl.when(moves)
            def _():
                pl.semaphore_signal(barrier, inc=1, device_id=self.to_s, device_id_type=MESH)

            count = count + moves.astype(jnp.int32)
        pl.semaphore_wait(barrier, count)


def prefix_block(rows):
    nothing = jnp.zeros_like(rows)
    return jnp.concatenate([half_lanes(rows, 0), nothing, half_lanes(rows, 1), nothing], axis=0)


def attend_tile(q, k, v, mask, kp, vp):
    scale = 0.125 * LOG2E
    if kp is not None:
        lane = lax.broadcasted_iota(jnp.int32, (q.shape[0], 128), 1)
        sp = jnp.where(lax.rem(lane, 64) < 30, nt(q, kp) * scale, NEG)
    tops, sums, es = [], [], []
    for h in range(2):
        s = jnp.where(mask, nt(half_lanes(q, h), k) * scale, NEG)
        m = jnp.max(s, axis=1, keepdims=True)
        if kp is not None:
            inside = (lane < 64) if h == 0 else (lane >= 64)
            m = jnp.maximum(m, jnp.max(jnp.where(inside, sp, NEG), axis=1, keepdims=True))
        e = jnp.exp2(s - m)
        sums.append(jnp.sum(e, axis=1, keepdims=True))
        es.append(e.astype(jnp.bfloat16))
        tops.append(m)
    out = nn(es[0], half_lanes(v, 0)) + nn(es[1], half_lanes(v, 1))
    side = lax.broadcasted_iota(jnp.int32, (q.shape[0], 128), 1) < 64
    if kp is not None:
        ep = jnp.exp2(sp - jnp.where(side, tops[0], tops[1]))
        sums = [sums[0] + jnp.sum(jnp.where(side, ep, 0.0), axis=1, keepdims=True), sums[1] + jnp.sum(jnp.where(side, 0.0, ep), axis=1, keepdims=True)]
        out = out + nn(ep.astype(jnp.bfloat16), vp)
    out = out * jnp.where(side, 1.0 / sums[0], 1.0 / sums[1])
    lse = jnp.where(side, tops[0] + jnp.log2(sums[0]), tops[1] + jnp.log2(sums[1])).T
    return out.astype(jnp.bfloat16), [lse[0:1], lse[64:65]]


def forward_kernel(
    tokens, memory, seg, mseg, prefix, w_self, w_so, w_cq, w_ckv, w_co, fc_in, fc_out, ad_down, ad_up, gain, bias,
    o_wself, o_qkv, o_sctx, o_slse, o_pre, o_wso_m, o_wso_o, o_wkv, o_wq_m, o_wq_o, o_wco_m, o_wco_o,
    o_q, o_kv, o_cctx, o_clse, o_resid1, o_resid2, o_bounds, o_ad, fin, fout, fad,
    wself, qkv, sctx, slse, pre, wso_m, wso_o, wkv, wq_m, wq_o, wco_m, wco_o,
    q_all, kv, cctx, clse, resid1, resid2, bounds, ad, tok, mem, sctx_o, cctx_o, q_send, hidden, low_one, columns, seg_v, mseg_v,
    send, recv, local,
):
    place_of = Place()
    c, x, y, odd = place_of.c, place_of.x, place_of.y, place_of.odd
    to_x, to_y, to_z, to_c, to_s = place_of.to_x, place_of.to_y, place_of.to_z, place_of.to_c, place_of.to_s
    stays, moves = c == x, c != x
    place_of.greet((to_x, to_y, to_z, to_c), True)

    taken = []

    def there(src, dst, device):
        slot = len(taken)
        taken.append(slot)
        return pltpu.make_async_remote_copy(
            src_ref=src, dst_ref=dst, send_sem=send.at[slot], recv_sem=recv.at[slot], device_id=device, device_id_type=MESH
        )

    used = []

    def here(src, dst):
        slot = len(used)
        used.append(slot)
        return pltpu.make_async_copy(src, dst, local.at[slot])

    deep = w_self.shape[1]
    half = tok.shape[0] // 2
    step = lambda start, size, unit: pl.ds(pl.multiple_of(start, unit), size)
    mine = step(c * half, half, half)
    others = step((1 - c) * half, half, half)
    lanes = step(c * 128, 128, 128)
    other_lanes = step((1 - c) * 128, 128, 128)
    rows_c, rows_o = lanes, other_lanes
    foreign = pl.ds(128, 384)
    hid = fc_in.shape[1]
    units = ad.shape[1]
    pending = []

    def swap_of(src, target):
        away = there(src, target.at[step(x * half, half, half)], to_s)
        home = here(src, target.at[mine])
        back = there(target.at[mine], target.at[mine], to_c)

        def start():
            pl.when(moves)(away.start)
            pl.when(stays)(home.start)

        def wait():
            pl.when(moves)(away.wait)
            pl.when(stays)(home.wait)

        return start, wait, back

    def seg_of(src, dst):
        home = here(src.at[y], dst)
        away = there(src.at[y], dst, to_c)

        def start():
            pl.when(stays)(home.start)
            pl.when(stays)(away.start)

        def wait():
            pl.when(stays)(home.wait)
            pl.when(stays)(away.wait_send)
            pl.when(moves)(away.wait_recv)

        return start, wait

    def deep_rows(shared):
        return step(odd * (deep // 2), deep // 2, deep // 2) if shared else pl.ds(0, deep)

    def thin_rows(piece, shared):
        return step(128 * piece + odd * 64, 64, 64) if shared else pl.ds(128 * piece, 128)

    def thin_own(shared):
        return step(128 * c + odd * 64, 64, 64) if shared else rows_c

    def span(size, shared):
        return step(c * (size // 2) + odd * (size // 4), size // 4, size // 4) if shared else step(c * (size // 2), size // 2, size // 2)

    lane_of = lambda i: pl.ds(128 * i, 128)

    def group_a(shared):
        rows = deep_rows(shared)
        first = lambda piece: [(w_self.at[i, rows, lanes], wself.at[piece, rows, lane_of(i)]) for i in range(3)] + [
            (prefix.at[:, :, lanes], pre.at[piece])
        ]
        return first, lambda piece: [wself.at[piece, rows], pre.at[piece]], 1, []

    def group_thin(src, dst_m, dst_o, shared):
        first = lambda piece: [(src.at[thin_own(shared)], dst_m.at[thin_rows(piece, shared)])]
        return first, lambda piece: [dst_m.at[thin_rows(piece, shared)]], 1, [(dst_m.at[foreign], dst_o.at[foreign])]

    def group_q(shared):
        rows = deep_rows(shared)
        first = lambda piece: [(w_cq.at[rows, lanes], wq_m.at[rows, lane_of(piece)])]
        return first, lambda piece: [wq_m.at[rows, lane_of(piece)]], 1, [(wq_m.at[:, foreign], wq_o.at[:, foreign])]

    def group_v(shared):
        rows = deep_rows(shared)
        first = lambda piece: [(w_ckv.at[i, rows, lanes], wkv.at[piece, rows, lane_of(i)]) for i in range(2)]
        return first, lambda piece: [wkv.at[piece, rows]], 1, []

    def group_i(shared):
        cols = span(hid, shared)
        first = lambda piece: [(fc_in.at[:, cols], fin.at[piece - 1, :, cols])]
        return first, lambda piece: [fin.at[piece - 1, :, cols]], 1, []

    def group_o(shared):
        rows, some = span(hid, shared), span(units, shared)
        first = lambda piece: [(fc_out.at[rows], fout.at[piece - 1, rows]), (ad.at[:, some], fad.at[piece - 1, :, some])]
        hold = lambda piece: [fout.at[piece - 1, rows], fad.at[piece - 1, :, some]]
        return first, hold, 2, []

    makers = [
        group_a,
        functools.partial(group_thin, w_so, wso_m, wso_o),
        group_q,
        group_v,
        functools.partial(group_thin, w_co, wco_m, wco_o),
        group_i,
        group_o,
    ]
    copies, needs = {}, {}
    for index, (make, (shared, through_x)) in enumerate(zip(makers, GROUPS)):
        first, hold, shared_count, cross = make(bool(shared))
        base = 16 * index
        copies[base] = [there(src, dst, to_x) for src, dst in first(1)]
        copies[base + 1] = [there(src, dst, to_y) for src, dst in first(2)]
        near, device = (2, to_x) if through_x else (1, to_y)
        copies[base + 2] = [there(src, dst, device) for src, dst in zip(hold(near), hold(3))]
        needs[base], needs[base + 1], needs[base + 2] = [], [], [base + near - 1]
        arrived = [base, base + 1, base + 2]
        if shared:
            for i in range(3):
                copies[base + 3 + i] = [there(ref, ref, to_z) for ref in hold(i + 1)[:shared_count]]
                needs[base + 3 + i] = [base + i]
                arrived.append(base + 3 + i)
        if cross:
            copies[base + 6] = [there(src, dst, to_c) for src, dst in cross]
            needs[base + 6] = arrived
    tok_start, tok_wait, tok_back = swap_of(tokens, tok)
    mem_start, mem_wait, mem_back = swap_of(memory, mem)
    copies[TOK_C], copies[MEM_C] = [tok_back], [mem_back]
    needs[TOK_C], needs[MEM_C] = [TOK], [MEM]
    seg_start, seg_wait = seg_of(seg, seg_v)
    mseg_start, mseg_wait = seg_of(mseg, mseg_v)
    sctx_out = [there(sctx.at[others, lane_of(i)], sctx_o.at[:, lane_of(i)], to_c) for i in range(4)]
    cctx_out = [there(cctx.at[others, lane_of(i)], cctx_o.at[:, lane_of(i)], to_c) for i in range(4)]
    q_out = there(q_send, q_all.at[mine], to_c)

    landed = set()

    def wait_for(op):
        if op in landed:
            return
        landed.add(op)
        if op == TOK:
            tok_wait()
        elif op == MEM:
            mem_wait()
        elif op in copies:
            for copy in copies[op]:
                copy.wait_recv()

    def launch(op):
        if op == TOK:
            tok_start()
        elif op == MEM:
            mem_start()
        else:
            for need in needs[op]:
                wait_for(need)
            for copy in copies[op]:
                copy.start()
                pending.append(copy)

    saves = []

    def keep(src, dst):
        copy = here(src, dst)
        copy.start()
        saves.append(copy)

    own_a = [here(w_self.at[i, :, lanes], wself.at[0, :, lane_of(i)]) for i in range(3)]
    own_a.append(here(prefix.at[:, :, lanes], pre.at[0]))
    own_b = [
        here(w_so.at[rows_c], wso_m.at[lane_of(0)]),
        here(w_so.at[rows_o], wso_o.at[lane_of(0)]),
        here(w_co.at[rows_c], wco_m.at[lane_of(0)]),
        here(w_co.at[rows_o], wco_o.at[lane_of(0)]),
        here(w_cq.at[:, lanes], wq_m.at[:, lane_of(0)]),
        here(w_cq.at[:, other_lanes], wq_o.at[:, lane_of(0)]),
        here(w_ckv.at[0, :, lanes], wkv.at[0, :, lane_of(0)]),
        here(w_ckv.at[1, :, lanes], wkv.at[0, :, lane_of(1)]),
    ]

    def bounds_of():
        seg_wait()
        mseg_wait()
        dec, men = seg_v[...], mseg_v[...]

        def below(values, d):
            return jnp.sum((values < d).astype(jnp.int32), axis=1, keepdims=True)

        def pick(counts):
            out = jnp.broadcast_to(counts[0], dec.shape)
            for d in range(1, 4):
                out = jnp.where(dec == d, counts[d], out)
            return out

        zero = jnp.zeros((1, 1), jnp.int32)
        full = jnp.full((1, 1), MLEN, jnp.int32)
        self_lo = pick([zero] + [below(dec, d) for d in range(1, 4)])
        mem_counts = [zero] + [below(men, d) for d in range(1, 4)] + [full]
        bounds[...] = jnp.concatenate(
            [self_lo, lax.broadcasted_iota(jnp.int32, dec.shape, 1), pick(mem_counts[:4]), pick(mem_counts[1:]) - 1]
            + [jnp.zeros_like(dec)] * 4,
            axis=0,
        )
        keep(bounds, o_bounds)
        wide = jnp.concatenate([bounds[...].astype(jnp.float32), jnp.zeros((120, SEQ), jnp.float32)], axis=0)
        columns[...] = wide.T.astype(jnp.int32)

    def weight_needs(base, piece):
        found = [base + piece - 1, base + 2 + piece]
        return [op for op in found if op in copies]

    def project(dst, p, source, weight):
        dst[p] = nn(source[...], weight[p]).astype(jnp.bfloat16)

    def self_piece(p):
        project(qkv, p, tok, wself)
        kp = prefix_block(pre[p, 0])
        vp = prefix_block(pre[p, 1])
        place = step(p * 128, 128, 128)
        for qi in range(SEQ // QB):
            width = (qi + 1) * QB
            rows = slice(qi * QB, (qi + 1) * QB)
            pos = lax.broadcasted_iota(jnp.int32, (QB, width), 1)
            limit = columns[rows, :]
            mask = (pos >= limit[:, 0:1]) & (pos <= limit[:, 1:2])
            out, lse = attend_tile(qkv[p, rows, 0:128], qkv[p, 0:width, 128:256], qkv[p, 0:width, 256:384], mask, kp, vp)
            sctx[rows, place] = out
            for h in range(2):
                slse[p, h : h + 1, rows] = lse[h]

    def cross_piece(p):
        project(kv, p, mem, wkv)
        place = step(p * 128, 128, 128)

        def block(qi, _):
            rows = step(qi * QB, QB, QB)
            pos = lax.broadcasted_iota(jnp.int32, (QB, MLEN), 1)
            limit = columns[rows, :]
            mask = (pos >= limit[:, 2:3]) & (pos <= limit[:, 3:4])
            out, lse = attend_tile(q_all[rows, place], kv[p, :, 0:128], kv[p, :, 128:256], mask, None, None)
            cctx[rows, place] = out
            for h in range(2):
                clse[p, h : h + 1, rows] = lse[h]
            return 0

        lax.fori_loop(0, SEQ // QB, block, 0)

    def with_out(t, resid_before, ctx_m, ctx_o, w_m, w_o):
        rows = step(t * TILE, TILE, TILE)
        rows_all = step(c * half + t * TILE, TILE, TILE)
        return resid_before + nn(ctx_m[rows_all, :], w_m[...]) + nn(ctx_o[rows, :], w_o[...])

    def out_one(t, _):
        rows = step(t * TILE, TILE, TILE)
        rows_all = step(c * half + t * TILE, TILE, TILE)
        resid = with_out(t, tok[rows_all, :].astype(jnp.float32), sctx, sctx_o, wso_m, wso_o)
        resid1[rows, :] = resid
        normed = norm_forward(resid, gain[0:1, :], bias[0:1, :])
        hidden[rows, :] = normed
        low_one[rows, :] = normed.astype(jnp.bfloat16)
        return 0

    def out_two(t, _):
        rows = step(t * TILE, TILE, TILE)
        resid2[rows, :] = with_out(t, hidden[rows, :], cctx, cctx_o, wco_m, wco_o)
        return 0

    def q_rows(t, _):
        rows = step(t * TILE, TILE, TILE)
        rows_all = step(c * half + t * TILE, TILE, TILE)
        q_send[rows, :] = nn(low_one[rows, :], wq_o[...]).astype(jnp.bfloat16)
        q_all[rows_all, :] = nn(low_one[rows, :], wq_m[...]).astype(jnp.bfloat16)
        return 0

    def split_at(order, first, count):
        places = [order.index(first + k) for k in range(count)]
        starts = [0] + [place + 1 for place in places]
        return [order[a:b] for a, b in zip(starts, places)], order[places[-1] + 1 :]

    def pieces_loop(segments, ready, work, sends):
        def body(p, _):
            for k, segment in enumerate(segments):

                @pl.when(p == k)
                def _():
                    for op in segment:
                        launch(op)
                    ready(k)

            work(p)
            for k, copy in enumerate(sends):
                pl.when(p == k)(copy.start)
            return 0

        lax.fori_loop(0, len(segments), body, 0)
        pending.extend(sends)

    ad_copy = here(ad_up, ad.at[1])
    ad_copy.start()
    ad[0] = ad_down[...].astype(jnp.float32).T.astype(jnp.bfloat16)
    ad_copy.wait()
    keep(ad, o_ad)

    for copy in own_a[:3]:
        copy.start()
    own_a[3].start()
    seg_start()
    mseg_start()
    segments, rest = split_at(list(SCHEDULE), SELF_PIECE, 4)
    for op in segments[0]:
        launch(op)
    for copy in own_b:
        copy.start()
    bounds_of()
    for copy in own_a:
        copy.wait()
    segments[0] = []

    def self_ready(k):
        if k == 0:
            wait_for(TOK_C)
        else:
            for op in weight_needs(0, k):
                wait_for(op)

    pieces_loop(segments, self_ready, self_piece, sctx_out)
    for src, dst in ((qkv, o_qkv), (wself, o_wself), (sctx, o_sctx), (slse, o_slse), (pre, o_pre)):
        keep(src, dst)
    for copy in own_b:
        copy.wait()
    before, rest = split_at(rest, OUT_ONE, 1)
    for op in before[0]:
        launch(op)
    for copy in sctx_out:
        copy.wait_recv()
    wait_for(16 + 6)
    lax.fori_loop(0, half // TILE, out_one, 0)
    for src, dst in ((resid1, o_resid1), (wso_m, o_wso_m), (wso_o, o_wso_o)):
        keep(src, dst)
    before, rest = split_at(rest, CROSS_Q, 1)
    for op in before[0]:
        launch(op)
    wait_for(32 + 6)
    lax.fori_loop(0, half // TILE, q_rows, 0)
    q_out.start()
    pending.append(q_out)
    for src, dst in ((wq_m, o_wq_m), (wq_o, o_wq_o)):
        keep(src, dst)
    segments, rest = split_at(rest, CROSS_PIECE, 4)

    def cross_ready(k):
        if k == 0:
            wait_for(MEM_C)
            q_out.wait_recv()
        else:
            for op in weight_needs(48, k):
                wait_for(op)

    pieces_loop(segments, cross_ready, cross_piece, cctx_out)
    for src, dst in ((q_all, o_q), (kv, o_kv), (wkv, o_wkv), (cctx, o_cctx), (clse, o_clse)):
        keep(src, dst)
    before, rest = split_at(rest, OUT_TWO, 1)
    for op in before[0]:
        launch(op)
    for copy in cctx_out:
        copy.wait_recv()
    wait_for(64 + 6)
    lax.fori_loop(0, half // TILE, out_two, 0)
    for src, dst in ((resid2, o_resid2), (wco_m, o_wco_m), (wco_o, o_wco_o)):
        keep(src, dst)
    for op in rest:
        launch(op)
    for op in list(copies):
        wait_for(op)
    for copy in pending:
        copy.wait_send()
    for copy in saves:
        copy.wait()


class Held(typing.NamedTuple):
    wself: jax.Array
    qkv: jax.Array
    sctx: jax.Array
    slse: jax.Array
    pre: jax.Array
    wso_m: jax.Array
    wso_o: jax.Array
    wkv: jax.Array
    wq_m: jax.Array
    wq_o: jax.Array
    wco_m: jax.Array
    wco_o: jax.Array
    q: jax.Array
    kv: jax.Array
    cctx: jax.Array
    clse: jax.Array
    resid1: jax.Array
    resid2: jax.Array
    bounds: jax.Array
    ad: jax.Array
    fin: jax.Array
    fout: jax.Array
    fad: jax.Array


def forward_call(tokens, memory, seg, mseg, prefix, w_self, w_so, w_cq, w_ckv, w_co, fc_in, fc_out, ad_down, ad_up, gain, bias):
    bf16, f32 = jnp.bfloat16, jnp.float32
    half, deep = tokens.shape
    shape = jax.ShapeDtypeStruct
    held = dict(
        wself=((4, deep, 384), bf16),
        qkv=((4, SEQ, 384), bf16),
        sctx=((SEQ, 512), bf16),
        slse=((4, 8, SEQ), f32),
        pre=((4, 2, 32, 128), bf16),
        wso_m=((512, deep), bf16),
        wso_o=((512, deep), bf16),
        wkv=((4, deep, 256), bf16),
        wq_m=((deep, 512), bf16),
        wq_o=((deep, 512), bf16),
        wco_m=((512, deep), bf16),
        wco_o=((512, deep), bf16),
        q=((SEQ, 512), bf16),
        kv=((4, MLEN, 256), bf16),
        cctx=((SEQ, 512), bf16),
        clse=((4, 8, SEQ), f32),
        resid1=((half, deep), f32),
        resid2=((half, deep), f32),
        bounds=((8, SEQ), jnp.int32),
        ad=((2,) + ad_up.shape, bf16),
    )
    outs = [shape(*value) for value in held.values()]
    outs += [shape((3,) + fc_in.shape, bf16), shape((3,) + fc_out.shape, bf16), shape((3, 2) + ad_up.shape, bf16)]
    scratch = [pltpu.VMEM(*value) for value in held.values()] + [
        pltpu.VMEM((SEQ, deep), bf16),
        pltpu.VMEM((MLEN, deep), bf16),
        pltpu.VMEM((half, 512), bf16),
        pltpu.VMEM((half, 512), bf16),
        pltpu.VMEM((half, 512), bf16),
        pltpu.VMEM((half, deep), f32),
        pltpu.VMEM((half, deep), bf16),
        pltpu.VMEM((SEQ, 128), jnp.int32),
        pltpu.VMEM((1, SEQ), jnp.int32),
        pltpu.VMEM((1, SEQ), jnp.int32),
        pltpu.SemaphoreType.DMA((SLOTS,)),
        pltpu.SemaphoreType.DMA((SLOTS,)),
        pltpu.SemaphoreType.DMA((LOCAL_SLOTS,)),
    ]
    anywhere = pl.BlockSpec(memory_space=pl.ANY)
    vmem = pl.BlockSpec(memory_space=pltpu.VMEM)
    results = pl.pallas_call(
        forward_kernel,
        out_shape=outs,
        in_specs=[anywhere] * 12 + [vmem, anywhere] + [vmem] * 2,
        out_specs=[anywhere] * len(outs),
        scratch_shapes=scratch,
        compiler_params=pltpu.CompilerParams(
            collective_id=0, has_side_effects=True, vmem_limit_bytes=58 * 2**20
        ),
        name="layer_forward",
    )(tokens, memory, seg, mseg, prefix, w_self, w_so, w_cq, w_ckv, w_co, fc_in, fc_out, ad_down, ad_up, gain, bias)
    return Held(*results)


TOGETHER = 4


def backward_kernel(has_prefix, first_bound, bounds_s, *refs):
    if has_prefix:
        qkv_ref, bounds, ctx_ref, dctx_ref, lse_ref, pre_ref, dqkv_ref, dpre_ref, dk_acc, dv_acc, dq_acc, dpre_acc = refs
        q_at = lambda g, rows: qkv_ref[g, rows, 0:128]
        k_at = lambda g, rows: qkv_ref[g, rows, 128:256]
        v_at = lambda g, rows: qkv_ref[g, rows, 256:384]
    else:
        q_ref, kv_ref, bounds, ctx_ref, dctx_ref, lse_ref, dq_ref, dkv_ref, dk_acc, dv_acc, dq_acc = refs
        q_at = lambda g, rows: q_ref[rows, 128 * g : 128 * g + 128]
        k_at = lambda g, rows: kv_ref[g, rows, 0:128]
        v_at = lambda g, rows: kv_ref[g, rows, 128:256]
    scale = 0.125 * LOG2E
    dk_acc[...] = jnp.zeros_like(dk_acc)
    dv_acc[...] = jnp.zeros_like(dv_acc)
    kps, vps = [], []
    for g in range(TOGETHER):
        if has_prefix:
            kps.append(prefix_block(pre_ref[g, 0]))
            vps.append(prefix_block(pre_ref[g, 1]))
    if has_prefix:
        dpre_acc[...] = jnp.zeros_like(dpre_acc)

    def one(qi, _):
        q0 = pl.multiple_of(qi * QB, QB)
        span = pl.ds(q0, QB)
        lo = bounds[first_bound : first_bound + 1, span]
        hi = bounds[first_bound + 1 : first_bound + 2, span]
        inner, lse, qh, dh = [], [], [], []
        for g in range(TOGETHER):
            q = q_at(g, span)
            dctx = dctx_ref[span, 128 * g : 128 * g + 128]
            ctx = ctx_ref[span, 128 * g : 128 * g + 128]
            prod = (dctx.astype(jnp.float32) * ctx.astype(jnp.float32)).T
            inner.append([jnp.sum(prod[h * 64 : h * 64 + 64], axis=0, keepdims=True) for h in range(2)])
            lse.append([lse_ref[g, h : h + 1, span] for h in range(2)])
            qh.append([half_lanes(q, h) for h in range(2)])
            dh.append([half_lanes(dctx, h) for h in range(2)])
            if has_prefix:
                sp = prefix_rows(nt(kps[g], q) * scale)
                rows = lambda pair: jnp.concatenate([jnp.broadcast_to(t, (64, QB)) for t in pair], axis=0)
                pp = jnp.exp2(sp - rows(lse[g]))
                dpp = nt(vps[g], dctx)
                dsp = (pp * (dpp - rows(inner[g]))).astype(jnp.bfloat16)
                dpre_acc[g, 0] += nn(dsp, q)
                dpre_acc[g, 1] += nn(pp.astype(jnp.bfloat16), dctx)
                dq_acc[g] = tn(dsp, kps[g])
            else:
                dq_acc[g] = jnp.zeros((QB, 128), jnp.float32)

        first_key = lax.div(bounds_s[first_bound, q0], 16) * 16
        parts = lax.div(bounds_s[first_bound + 1, q0 + QB - 1] - first_key + KB // 2, KB // 2)
        chunks, tail = lax.div(parts, 2), lax.rem(parts, 2)
        first_key = jnp.minimum(first_key, SEQ - parts * (KB // 2))

        def chunk(ki, size):
            k0 = pl.multiple_of(first_key + ki * KB, 16)
            keys = pl.ds(k0, size)
            pos = k0 + lax.broadcasted_iota(jnp.int32, (size, QB), 0)
            mask = (pos >= lo) & (pos <= hi)
            for g in range(TOGETHER):
                k = k_at(g, keys)
                v = v_at(g, keys)
                ps, dss = [], []
                for h in range(2):
                    s = nt(k, qh[g][h]) * scale
                    p = jnp.exp2(jnp.where(mask, s, NEG) - lse[g][h])
                    dp = nt(v, dh[g][h])
                    ds = (p * (dp - inner[g][h])).astype(jnp.bfloat16)
                    ps.append(p.astype(jnp.bfloat16))
                    dss.append(ds)
                dv_acc[g, keys, :] += nn(jnp.concatenate(ps, axis=1), jnp.concatenate(dh[g], axis=0))
                dq_acc[g] += tn(jnp.concatenate(dss, axis=0), jnp.concatenate([half_lanes(k, 0), half_lanes(k, 1)], axis=0))
                dk_acc[g, keys, :] += nn(jnp.concatenate(dss, axis=1), jnp.concatenate(qh[g], axis=0))

        def whole_chunk(ki, _):
            chunk(ki, KB)
            return 0

        lax.fori_loop(0, chunks, whole_chunk, 0)
        pl.when(tail == 1)(lambda: chunk(chunks, KB // 2))
        for g in range(TOGETHER):
            dq = (dq_acc[g] * 0.125).astype(jnp.bfloat16)
            if has_prefix:
                dqkv_ref[g, span, 0:128] = dq
            else:
                dq_ref[span, 128 * g : 128 * g + 128] = dq
        return 0

    lax.fori_loop(0, SEQ // QB, one, 0)
    for g in range(TOGETHER):
        dk = (dk_acc[g] * 0.125).astype(jnp.bfloat16)
        dv = dv_acc[g].astype(jnp.bfloat16)
        if has_prefix:
            dqkv_ref[g, :, 128:256] = dk
            dqkv_ref[g, :, 256:384] = dv
            lane = lax.broadcasted_iota(jnp.int32, (32, 128), 1)
            for i, factor in ((0, 0.125), (1, 1.0)):
                dpre_ref[g, i] = jnp.where(lane < 64, dpre_acc[g, i, 0:32], dpre_acc[g, i, 64:96]) * factor
        else:
            dkv_ref[g, :, 0:128] = dk
            dkv_ref[g, :, 128:256] = dv


def backward_call(has_prefix, arrays, bounds, ctx, dctx, lse, pre=None):
    col = pl.BlockSpec((SEQ, 128 * TOGETHER), lambda j, *_: (0, j))
    piece = lambda width: pl.BlockSpec((TOGETHER, SEQ, width), lambda j, *_: (j, 0, 0))
    shape = jax.ShapeDtypeStruct
    bf16, f32 = jnp.bfloat16, jnp.float32
    pre_spec = pl.BlockSpec((TOGETHER, 2, 32, 128), lambda j, *_: (j, 0, 0, 0))
    if has_prefix:
        in_specs = [piece(384)]
        out_specs = [piece(384), pre_spec]
        out_shape = [shape((4, SEQ, 384), bf16), shape((4, 2, 32, 128), f32)]
    else:
        in_specs = [col, piece(256)]
        out_specs = [col, piece(256)]
        out_shape = [shape((SEQ, 512), bf16), shape((4, SEQ, 256), bf16)]
    in_specs += [
        pl.BlockSpec((8, SEQ), lambda j, *_: (0, 0)),
        col,
        col,
        pl.BlockSpec((TOGETHER, 8, SEQ), lambda j, *_: (j, 0, 0)),
    ]
    args = list(arrays) + [bounds, ctx, dctx, lse]
    scratch = [
        pltpu.VMEM((TOGETHER, SEQ, 128), f32),
        pltpu.VMEM((TOGETHER, SEQ, 128), f32),
        pltpu.VMEM((TOGETHER, QB, 128), f32),
    ]
    if has_prefix:
        in_specs.append(pre_spec)
        args.append(pre)
        scratch.append(pltpu.VMEM((TOGETHER, 2, 128, 128), f32))
    return pl.pallas_call(
        functools.partial(backward_kernel, has_prefix, 0 if has_prefix else 2),
        grid_spec=pltpu.PrefetchScalarGridSpec(
            num_scalar_prefetch=1, grid=(4 // TOGETHER,), in_specs=in_specs, out_specs=out_specs, scratch_shapes=scratch
        ),
        out_shape=out_shape,
        compiler_params=pltpu.CompilerParams(vmem_limit_bytes=60 * 2**20),
        cost_estimate=pl.CostEstimate(flops=10 * 8 * SEQ * SEQ * 64, bytes_accessed=10 * 2**20, transcendentals=8 * SEQ * SEQ),
        name="self_backward" if has_prefix else "cross_backward",
    )(bounds, *args)


HIDDEN = 512


def swap_halves(place, src, dst_there, dst_here, send, recv, local):
    moves = place.c != place.x
    away = pltpu.make_async_remote_copy(
        src_ref=src, dst_ref=dst_there, send_sem=send, recv_sem=recv, device_id=place.to_s, device_id_type=MESH
    )
    home = pltpu.make_async_copy(src, dst_here, local)

    def start():
        pl.when(moves)(away.start)
        pl.when(jnp.logical_not(moves))(home.start)

    def wait():
        pl.when(moves)(away.wait)
        pl.when(jnp.logical_not(moves))(home.wait)

    return start, wait


def feed_kernel(
    resid2, cotangent, gain, bias, wco_m_in, wco_o_in, fc_in, fin, fc_out, fout, ad, fad,
    out, grad_two, unit_sum, dctx,
    win, wout, adw, slope, low, hidden, acc, gate, ada, branch_low, sem,
    cot, out_v, units, unit_send, unit_recv, near_send, near_recv, dctx_s, wco_m, wco_o, send, recv, local,
):
    place = Place()
    place.greet((place.to_x, place.to_y, place.to_d, place.to_c), True)
    c = place.c
    cot_start, cot_wait = swap_halves(place, cotangent, cot, cot, send.at[0], recv.at[0], local.at[0])
    out_copy = pltpu.make_async_copy(out_v, out, local.at[1])
    two_copy = pltpu.make_async_copy(acc, grad_two, local.at[2])
    co_copies = [
        pltpu.make_async_copy(wco_m_in, wco_m, local.at[3]),
        pltpu.make_async_copy(wco_o_in, wco_o, local.at[4]),
    ]
    cot_start()

    def there(slot, src, dst, device):
        return pltpu.make_async_remote_copy(
            src_ref=src, dst_ref=dst, send_sem=send.at[slot], recv_sem=recv.at[slot], device_id=device, device_id_type=MESH
        )

    half = resid2.shape[0]
    mine = pl.ds(pl.multiple_of(c * half, half), half)
    unit_core = there(2, unit_send, unit_recv, place.to_c)
    unit_near = [
        there(3 + i, near_send.at[i], near_recv.at[i], device) for i, device in enumerate((place.to_x, place.to_y, place.to_d))
    ]
    dctx_core = there(6, dctx_s, dctx.at[mine], place.to_c)
    bf16 = jnp.bfloat16
    per = fc_in.shape[1] // HIDDEN
    steps = 4 * per
    down, up = adw.at[0], adw.at[1]
    group = ad.shape[1]
    some = group // 2
    hidden_c = pl.ds(pl.multiple_of(c * HIDDEN, HIDDEN), HIDDEN)
    units_c = pl.ds(pl.multiple_of(c * some, some), some)
    loads, ad_loads, crossing = [], [], []
    for piece in range(4):
        ad_rows = pl.ds(pl.multiple_of(group * piece + c * some, some), some)
        own_in = win.at[2 * piece + c]
        own_out = wout.at[2 * piece + c]
        if piece == 0:
            loads.append(pltpu.make_async_copy(fc_in.at[:, hidden_c], own_in, sem.at[0, 0]))
            loads.append(pltpu.make_async_copy(fc_out.at[hidden_c], own_out, sem.at[1, 0]))
            hidden_o = pl.ds(pl.multiple_of((1 - c) * HIDDEN, HIDDEN), HIDDEN)
            loads.append(pltpu.make_async_copy(fc_in.at[:, hidden_o], win.at[1 - c], sem.at[0, 1]))
            loads.append(pltpu.make_async_copy(fc_out.at[hidden_o], wout.at[1 - c], sem.at[1, 1]))
            ad_loads.append(pltpu.make_async_copy(ad, adw.at[:, pl.ds(0, group)], sem.at[2, 0]))
        else:
            src_in, src_out, src_ad = fin.at[piece - 1, :, hidden_c], fout.at[piece - 1, hidden_c], fad.at[piece - 1, :, units_c]
            loads.append(pltpu.make_async_copy(src_in, own_in, sem.at[0, 2 * piece]))
            loads.append(pltpu.make_async_copy(src_out, own_out, sem.at[1, 2 * piece]))
            ad_loads.append(pltpu.make_async_copy(src_ad, adw.at[:, ad_rows], sem.at[2, piece]))
            crossing.append(there(4 + 3 * piece, src_in, own_in, place.to_c))
            crossing.append(there(5 + 3 * piece, src_out, own_out, place.to_c))
            crossing.append(there(6 + 3 * piece, src_ad, adw.at[:, ad_rows], place.to_c))
    for copy in crossing + loads + ad_loads + co_copies:
        copy.start()

    rows_all = resid2.shape[0]
    tiles = rows_all // TILE
    at = lambda t: pl.ds(pl.multiple_of(t * TILE, TILE), TILE)

    def begin(t, _):
        rows = at(t)
        normed = norm_forward(resid2[rows, :], gain[1:2, :], bias[1:2, :])
        hidden[rows, :] = normed
        low[rows, :] = normed.astype(bf16)
        return 0

    lax.fori_loop(0, tiles, begin, 0)
    acc[...] = jnp.zeros_like(acc)

    def ahead(s, _):
        piece, late = lax.div(s, 2), lax.rem(s, 2)
        j = 2 * piece + c + late * (1 - 2 * c)
        for k in range(1, 4):

            @pl.when(s == 2 * k + 1)
            def _():
                crossing[3 * k - 3].wait_recv()
                crossing[3 * k - 2].wait_recv()

        @pl.when((late == 0) | (s == 1))
        def _():
            for i, buf in enumerate((win, wout)):
                pltpu.make_async_copy(buf.at[j], buf.at[j], sem.at[i, s]).wait()

        pre = nn(low[...], win[j])
        phi = 0.5 * (1.0 + lax.erf(pre * 0.7071067811865476))
        slope[j] = phi + pre * jnp.exp(-0.5 * pre * pre) * 0.3989422804014327
        acc[...] += nn((pre * phi).astype(bf16), wout[j])
        return 0

    lax.fori_loop(0, steps, ahead, 0)
    for copy in ad_loads + crossing[2::3]:
        copy.wait()
    pre = nt(low[...], down[...])
    sigma = jax.nn.sigmoid(pre)
    gate[...] = sigma * (1.0 + pre * (1.0 - sigma))
    ada[...] = (pre * sigma).astype(bf16)
    acc[...] += adapter_scale * nn(ada[...], up[...])

    def middle(t, _):
        rows = at(t)
        resid = hidden[rows, :] + acc[rows, :]
        normed, inv = norm_parts(resid)
        out_v[rows, :] = (normed * gain[2:3, :] + bias[2:3, :]).astype(bf16)
        scaled = cot[rows, :].astype(jnp.float32) * gain[2:3, :]
        grad = inv * (
            scaled
            - jnp.mean(scaled, axis=-1, keepdims=True)
            - normed * jnp.mean(scaled * normed, axis=-1, keepdims=True)
        )
        acc[rows, :] = grad
        branch_low[rows, :] = grad.astype(bf16)
        return 0

    cot_wait()
    lax.fori_loop(0, tiles, middle, 0)
    out_copy.start()
    grelu = (adapter_scale * nt(branch_low[...], up[...]) * gate[...]).astype(bf16)
    features = low.shape[1]
    for first, value in ((0, tn(grelu, low[...])), (features, adapter_scale * tn(ada[...], branch_low[...]))):
        for k in range(8):
            units[k // 2, k % 2, :, first : first + features] = value[some * k : some * (k + 1)]
    for i in range(4):
        unit_send[i] = units[i, 1 - c].astype(bf16)
    unit_core.start()
    acc[...] += nn(grelu, down[...])

    def behind(j, _):
        grad = (nt(branch_low[...], wout[j]) * slope[j]).astype(bf16)
        acc[...] += nt(grad, win[j])
        return 0

    lax.fori_loop(0, 2, behind, 0)
    unit_core.wait()
    for i in range(3):
        near_send[i] = (units[i + 1, c] + unit_recv[i + 1].astype(jnp.float32)).astype(bf16)
    for copy in unit_near:
        copy.start()
    lax.fori_loop(2, steps, behind, 0)

    def finish(t, _):
        rows = at(t)
        grad = norm_backward(resid2[rows, :], gain[1:2, :], acc[rows, :])
        acc[rows, :] = grad
        small = grad.astype(bf16)
        low[rows, :] = small
        dctx_s[rows, :] = nt(small, wco_o[...]).astype(bf16)
        return 0

    for copy in co_copies:
        copy.wait()
    lax.fori_loop(0, tiles, finish, 0)
    dctx_core.start()
    two_copy.start()
    dctx[mine, :] = nt(low[...], wco_m[...]).astype(bf16)
    for copy in unit_near:
        copy.wait()
    total = units[0, c] + unit_recv[0].astype(jnp.float32)
    for i in range(3):
        total = total + near_recv[i].astype(jnp.float32)
    unit_sum[...] = total
    out_copy.wait()
    two_copy.wait()
    for k in range(3):
        crossing[3 * k].wait_send()
        crossing[3 * k + 1].wait_send()
    dctx_core.wait()


def feed_call(resid2, cot, gain, bias, wco_m, wco_o, fc_in, fin, fc_out, fout, ad, fad):
    bf16, f32 = jnp.bfloat16, jnp.float32
    rows, deep = resid2.shape
    shape = jax.ShapeDtypeStruct
    anywhere = pl.BlockSpec(memory_space=pl.ANY)
    vmem = pl.BlockSpec(memory_space=pltpu.VMEM)
    steps = 4 * fc_in.shape[1] // HIDDEN
    units = 4 * ad.shape[1]
    some = ad.shape[1] // 2
    return pl.pallas_call(
        feed_kernel,
        out_shape=[
            shape((rows, deep), bf16),
            shape((rows, deep), f32),
            shape((some, 2 * deep), f32),
            shape((2 * rows, 512), bf16),
        ],
        in_specs=[vmem, anywhere] + [vmem] * 2 + [anywhere] * 8,
        out_specs=[anywhere] * 2 + [vmem] * 2,
        scratch_shapes=[
            pltpu.VMEM((steps, deep, HIDDEN), bf16),
            pltpu.VMEM((steps, HIDDEN, deep), bf16),
            pltpu.VMEM((2, units, deep), bf16),
            pltpu.VMEM((steps, rows, HIDDEN), f32),
            pltpu.VMEM((rows, deep), bf16),
            pltpu.VMEM((rows, deep), f32),
            pltpu.VMEM((rows, deep), f32),
            pltpu.VMEM((rows, units), f32),
            pltpu.VMEM((rows, units), bf16),
            pltpu.VMEM((rows, deep), bf16),
            pltpu.SemaphoreType.DMA((3, 8)),
            pltpu.VMEM((rows, deep), bf16),
            pltpu.VMEM((rows, deep), bf16),
            pltpu.VMEM((4, 2, some, 2 * deep), f32),
            pltpu.VMEM((4, some, 2 * deep), bf16),
            pltpu.VMEM((4, some, 2 * deep), bf16),
            pltpu.VMEM((3, some, 2 * deep), bf16),
            pltpu.VMEM((3, some, 2 * deep), bf16),
            pltpu.VMEM((rows, 512), bf16),
            pltpu.VMEM(wco_m.shape, bf16),
            pltpu.VMEM(wco_o.shape, bf16),
            pltpu.SemaphoreType.DMA((16,)),
            pltpu.SemaphoreType.DMA((16,)),
            pltpu.SemaphoreType.DMA((5,)),
        ],
        compiler_params=pltpu.CompilerParams(
            collective_id=1, has_side_effects=True, vmem_limit_bytes=61 * 2**20
        ),
        name="feed_forward",
    )(resid2, cot, gain, bias, wco_m, wco_o, fc_in, fin, fc_out, fout, ad, fad)


def query_kernel(
    dq_in, dkv_in, wkv_in, wq_m_in, wq_o_in, two_in, resid_in, wso_m_in, wso_o_in, gain,
    one_out, dctx, mem_out,
    dq, dkv, wkv, wq_m, wq_o, grad_two, resid1, wso_m, wso_o,
    grad_one, mem_sum, dq_o, mem_s, mem_r, dctx_s, dctx_m, low, send, recv, local,
):
    bf16 = jnp.bfloat16
    place = Place()
    c = place.c
    half = resid1.shape[0]
    mine = pl.ds(pl.multiple_of(c * half, half), half)
    others = pl.ds(pl.multiple_of((1 - c) * half, half), half)

    def there(slot, src, dst):
        return pltpu.make_async_remote_copy(
            src_ref=src, dst_ref=dst, send_sem=send.at[slot], recv_sem=recv.at[slot], device_id=place.to_c, device_id_type=MESH
        )

    def here(slot, src, dst):
        return pltpu.make_async_copy(src, dst, local.at[slot])

    wkv_copy, dkv_far, dkv_near = here(0, wkv_in, wkv), here(1, dkv_in.at[:, others], dkv.at[:, others]), here(2, dkv_in.at[:, mine], dkv.at[:, mine])
    pairs = (
        (dq_in.at[mine], dq), (wq_m_in, wq_m), (wq_o_in, wq_o), (two_in, grad_two), (resid_in, resid1), (wso_o_in, wso_o), (wso_m_in, wso_m)
    )
    rest = [here(3 + i, src, dst) for i, (src, dst) in enumerate(pairs)]
    for copy in [wkv_copy, dkv_far] + rest + [dkv_near]:
        copy.start()
    one_copy, mem_copy, dctx_copy = here(10, grad_one, one_out), here(11, mem_sum, mem_out), here(12, dctx_m, dctx.at[mine])
    place.greet((place.to_c,), False)
    dq_core = there(0, dq_in.at[others], dq_o)
    mem_core = there(1, mem_s, mem_r)
    dctx_core = there(2, dctx_s, dctx.at[mine])
    dq_core.start()
    tiles = half // TILE
    at = lambda t: pl.ds(pl.multiple_of(t * TILE, TILE), TILE)
    place_at = lambda first, t: pl.ds(pl.multiple_of(first * half + t * TILE, TILE), TILE)

    def memory_rows(rows):
        return sum(nt(dkv[p, rows, :], wkv[p]) for p in range(4))

    def far(t, _):
        mem_s[at(t), :] = memory_rows(place_at(1 - c, t)).astype(bf16)
        return 0

    wkv_copy.wait()
    dkv_far.wait()
    lax.fori_loop(0, tiles, far, 0)
    mem_core.start()
    for copy in rest:
        copy.wait()
    dq_core.wait()

    def one(t, _):
        rows = at(t)
        grad_in = grad_two[rows, :] + nt(dq[rows, :], wq_m[...]) + nt(dq_o[rows, :], wq_o[...])
        grad = norm_backward(resid1[rows, :], gain[0:1, :], grad_in)
        grad_one[rows, :] = grad
        small = grad.astype(bf16)
        low[rows, :] = small
        dctx_s[rows, :] = nt(small, wso_o[...]).astype(bf16)
        return 0

    lax.fori_loop(0, tiles, one, 0)
    dctx_core.start()
    one_copy.start()
    dctx_m[...] = nt(low[...], wso_m[...]).astype(bf16)
    dctx_copy.start()
    mem_core.wait()
    dkv_near.wait()

    def near(t, _):
        mem_sum[at(t), :] = (memory_rows(place_at(c, t)) + mem_r[at(t), :].astype(jnp.float32)).astype(bf16)
        return 0

    lax.fori_loop(0, tiles, near, 0)
    mem_copy.start()
    for copy in (dctx_core, one_copy, dctx_copy, mem_copy):
        copy.wait()


def query_call(dq, dkv, wkv, wq_m, wq_o, grad_two, resid1, wso_m, wso_o, gain):
    bf16, f32 = jnp.bfloat16, jnp.float32
    half, deep = resid1.shape
    shape = jax.ShapeDtypeStruct
    vmem = pl.BlockSpec(memory_space=pltpu.VMEM)
    anywhere = pl.BlockSpec(memory_space=pl.ANY)
    return pl.pallas_call(
        query_kernel,
        out_shape=[shape((half, deep), f32), shape((2 * half, 512), bf16), shape((half, deep), bf16)],
        in_specs=[anywhere] * 9 + [vmem],
        out_specs=[anywhere] * 3,
        scratch_shapes=[pltpu.VMEM((half, 512), bf16)]
        + [pltpu.VMEM(value.shape, value.dtype) for value in (dkv, wkv, wq_m, wq_o, grad_two, resid1, wso_m, wso_o)]
        + [
            pltpu.VMEM((half, deep), f32),
            pltpu.VMEM((half, deep), bf16),
            pltpu.VMEM((half, 512), bf16),
            pltpu.VMEM((half, deep), bf16),
            pltpu.VMEM((half, deep), bf16),
            pltpu.VMEM((half, 512), bf16),
            pltpu.VMEM((half, 512), bf16),
            pltpu.VMEM((half, deep), bf16),
            pltpu.SemaphoreType.DMA((3,)),
            pltpu.SemaphoreType.DMA((3,)),
            pltpu.SemaphoreType.DMA((13,)),
        ],
        compiler_params=pltpu.CompilerParams(collective_id=2, has_side_effects=True, vmem_limit_bytes=60 * 2**20),
        name="query_backward",
    )(dq, dkv, wkv, wq_m, wq_o, grad_two, resid1, wso_m, wso_o, gain)


def last_kernel(
    planes, dqkv_in, wself_in, one_in, blocks_in, unit_in,
    input_out, prefix_grad, down_grad, up_grad,
    dqkv, wself, grad_one, blocks, unit_sum, part_s, part_r, out_s, pre_near, pre_sum, pre_z, pre_c, unit_s, unit_z, unit_a, unit_o, unit_all, send, recv, local,
):
    bf16, f32 = jnp.bfloat16, jnp.float32
    place = Place()
    c, x, z = place.c, place.x, place.z
    steps = []
    step = 1
    while step < planes:
        other = z + step - 2 * step * lax.rem(lax.div(z, step), 2)
        steps.append((2 * other + c, place.head))
        step *= 2
    moves = c != x
    stays = c == x
    half = grad_one.shape[0]
    slots = []

    def there(src, dst, device):
        slot = len(slots)
        slots.append(slot)
        return pltpu.make_async_remote_copy(
            src_ref=src, dst_ref=dst, send_sem=send.at[slot], recv_sem=recv.at[slot], device_id=device, device_id_type=MESH
        )

    tiles = half // TILE
    at = lambda t: pl.ds(t * TILE, TILE)
    place_at = lambda first, t: pl.ds(pl.multiple_of(first * half + t * TILE, TILE), TILE)

    def here(slot, src, dst):
        return pltpu.make_async_copy(src, dst, local.at[slot])

    loads = [here(0, wself_in, wself), here(1, blocks_in, blocks), here(2, unit_in, unit_sum), here(3, one_in, grad_one)]
    far_loads = [here(4 + t, dqkv_in.at[:, place_at(1 - c, t)], dqkv.at[:, place_at(1 - c, t)]) for t in range(tiles)]
    near_loads = [
        here(4 + tiles + t, dqkv_in.at[:, place_at(c, t)], dqkv.at[:, place_at(c, t)]) for t in range(tiles)
    ]
    for copy in [loads[1], loads[2], far_loads[0], loads[0], near_loads[0], loads[3]] + far_loads[1:] + near_loads[1:]:
        copy.start()

    place.greet([place.to_x, place.to_y, place.to_d, place.to_c] + steps, True)
    pre_copies = [
        there(blocks.at[i + 1], pre_near.at[i], device) for i, device in enumerate((place.to_x, place.to_y, place.to_d))
    ]
    pre_steps = [there(pre_sum.at[i], pre_z.at[i], device) for i, device in enumerate(steps)]
    pre_core = there(pre_sum.at[len(steps)], pre_c, place.to_c)
    start, size = 0, unit_sum.shape[0]
    unit_down, unit_up, kept = [], [], []
    for i, device in enumerate(steps):
        bit = lax.rem(lax.div(z, 2**i), 2)
        size = size // 2
        away = pl.ds(pl.multiple_of(start + (1 - bit) * size, size), size)
        start = start + bit * size
        kept.append(pl.ds(pl.multiple_of(start, size), size))
        unit_down.append(there(unit_s.at[away], unit_z.at[i, away], device))
        unit_up.append(there(unit_a.at[kept[-1]], unit_a.at[kept[-1]], device))
    unit_core = there(unit_a, unit_o, place.to_c)
    part_copies = [there(part_s.at[at(t)], part_r.at[at(t)], place.to_c) for t in range(tiles)]
    out_copies = [there(out_s.at[at(t)], input_out.at[at(t)], place.to_s) for t in range(tiles)]
    own_copies = [here(4 + 2 * tiles + t, out_s.at[at(t)], input_out.at[at(t)]) for t in range(tiles)]
    loads[1].wait()
    for copy in pre_copies:
        copy.start()
    loads[2].wait()
    unit_s[...] = unit_sum[...].astype(bf16)
    unit_down[0].start()

    def input_rows(rows):
        return sum(nt(dqkv[p, rows, :], wself[p]) for p in range(4))

    def advance(i):
        pre_steps[i].wait()
        pre_sum[i + 1] = pre_sum[i] + pre_z[i]
        if i + 1 < len(steps):
            pre_steps[i + 1].start()
        else:
            pre_core.start()

    def reduce_units(i):
        unit_down[i].wait()
        total = unit_sum[kept[i], :] + unit_z[i, kept[i], :].astype(f32)
        if i + 1 < len(steps):
            unit_sum[kept[i], :] = total
            unit_s[kept[i], :] = total.astype(bf16)
            unit_down[i + 1].start()
        else:
            unit_a[kept[i], :] = total.astype(bf16)
            unit_up[i].start()

    loads[0].wait()
    for t in range(tiles):
        far_loads[t].wait()
        part_s[at(t), :] = input_rows(place_at(1 - c, t)).astype(bf16)
        part_copies[t].start()
        near_loads[t].wait()
        near = input_rows(place_at(c, t))
        if t == 0:
            loads[3].wait()
        part_copies[t].wait()
        out_s[at(t), :] = (near + part_r[at(t), :].astype(f32) + grad_one[at(t), :]).astype(bf16)
        pl.when(moves)(out_copies[t].start)
        pl.when(stays)(own_copies[t].start)
        if t == 0:
            for copy in pre_copies:
                copy.wait()
            pre_sum[0] = blocks[0] + pre_near[0] + pre_near[1] + pre_near[2]
            pre_steps[0].start()
        if t < len(steps):
            reduce_units(t)
    for i in range(tiles, len(steps)):
        reduce_units(i)
    for i in range(len(steps)):
        advance(i)
        unit_up[len(steps) - 1 - i].wait()
        if i + 1 < len(steps):
            unit_up[len(steps) - 2 - i].start()
        else:
            unit_core.start()
    pre_core.wait()
    unit_core.wait()
    my_lanes = pl.ds(pl.multiple_of(c * 128, 128), 128)
    other_lanes = pl.ds(pl.multiple_of((1 - c) * 128, 128), 128)
    prefix_grad[:, :, my_lanes] = pre_sum[len(steps)]
    prefix_grad[:, :, other_lanes] = pre_c[...]
    some = unit_sum.shape[0]
    unit_all[pl.ds(pl.multiple_of(c * some, some), some), :] = unit_a[...].astype(f32)
    unit_all[pl.ds(pl.multiple_of((1 - c) * some, some), some), :] = unit_o[...].astype(f32)
    features = grad_one.shape[1]
    down_grad[...] = unit_all[:, 0:features].T
    up_grad[...] = unit_all[:, features : 2 * features]

    for t in range(tiles):
        pl.when(moves)(out_copies[t].wait)
        pl.when(stays)(own_copies[t].wait)


def last_call(planes, dqkv, wself, grad_one, blocks, unit_sum):
    bf16, f32 = jnp.bfloat16, jnp.float32
    half, deep = grad_one.shape
    some = unit_sum.shape[0]
    count = planes.bit_length() - 1
    shape = jax.ShapeDtypeStruct
    vmem = pl.BlockSpec(memory_space=pltpu.VMEM)
    anywhere = pl.BlockSpec(memory_space=pl.ANY)
    return pl.pallas_call(
        functools.partial(last_kernel, planes),
        out_shape=[
            shape((half, deep), bf16),
            shape((2, 32, 256), f32),
            shape((deep, 2 * some), f32),
            shape((2 * some, deep), f32),
        ],
        in_specs=[anywhere] * 5,
        out_specs=[vmem] * 4,
        scratch_shapes=[pltpu.VMEM(value.shape, value.dtype) for value in (dqkv, wself, grad_one, blocks, unit_sum)]
        + [
            pltpu.VMEM((half, deep), bf16),
            pltpu.VMEM((half, deep), bf16),
            pltpu.VMEM((half, deep), bf16),
            pltpu.VMEM((3, 2, 32, 128), f32),
            pltpu.VMEM((count + 1, 2, 32, 128), f32),
            pltpu.VMEM((count, 2, 32, 128), f32),
            pltpu.VMEM((2, 32, 128), f32),
            pltpu.VMEM((some, 2 * deep), bf16),
            pltpu.VMEM((count, some, 2 * deep), bf16),
            pltpu.VMEM((some, 2 * deep), bf16),
            pltpu.VMEM((some, 2 * deep), bf16),
            pltpu.VMEM((2 * some, 2 * deep), f32),
            pltpu.SemaphoreType.DMA((3 + 3 * count + 2 + 2 * (half // TILE),)),
            pltpu.SemaphoreType.DMA((3 + 3 * count + 2 + 2 * (half // TILE),)),
            pltpu.SemaphoreType.DMA((4 + 3 * (half // TILE),)),
        ],
        compiler_params=pltpu.CompilerParams(collective_id=3, has_side_effects=True, vmem_limit_bytes=60 * 2**20),
        name="last_sums",
    )(dqkv, wself, grad_one, blocks, unit_sum)


AXES = ("rows", "heads")


def fast_fits(mesh):
    rows, heads = mesh.shape["rows"], mesh.shape["heads"]
    return heads == 4 and rows in (4, 8)


def pairs_of(rows, move):
    def number(z, c, y, x):
        return (z * 2 + c) * 4 + y * 2 + x

    found = []
    for z in range(rows // 2):
        for c in range(2):
            for y in range(2):
                for x in range(2):
                    found.append((number(z, c, y, x), number(*move(z, c, y, x))))
    return found


def swapped_rows(rows, value):
    def swapped(z, c, y, x):
        return (z, x, y, c)

    crossing = [pair for pair in pairs_of(rows, swapped) if pair[0] != pair[1]]
    stays = lax.axis_index("rows") % 2 == lax.axis_index("heads") % 2
    return jnp.where(stays, value, lax.ppermute(value, AXES, crossing))


def fast_body(
    rows,
    tokens,
    memory,
    cotangent,
    dec_seg,
    mem_seg,
    w_self,
    w_self_out,
    w_cross_q,
    w_cross_kv,
    w_cross_out,
    fc_in,
    fc_out,
    ad_down,
    ad_up,
    prefix,
    ln_gain,
    ln_bias,
):
    count = prefix.shape[1]
    held = forward_call(
        tokens,
        memory,
        dec_seg.reshape(2, 1, SEQ),
        mem_seg.reshape(2, 1, MLEN),
        jnp.pad(prefix, ((0, 0), (0, 32 - count), (0, 0))),
        w_self,
        w_self_out,
        w_cross_q,
        w_cross_kv,
        w_cross_out,
        fc_in,
        fc_out,
        ad_down,
        ad_up,
        ln_gain,
        ln_bias,
    )
    out_own, grad_two, unit_sum, cross_dctx = feed_call(
        held.resid2, cotangent, ln_gain, ln_bias, held.wco_m, held.wco_o,
        fc_in, held.fin, fc_out, held.fout, held.ad, held.fad,
    )
    output = swapped_rows(rows, out_own)
    cross_dq, cross_dkv = backward_call(
        False, (held.q, held.kv), held.bounds, held.cctx, cross_dctx, held.clse
    )
    grad_one, self_dctx, memory_sum = query_call(
        cross_dq, cross_dkv, held.wkv, held.wq_m, held.wq_o, grad_two, held.resid1, held.wso_m, held.wso_o, ln_gain
    )
    grad_memory = swapped_rows(rows, memory_sum).astype(jnp.float32)
    self_dqkv, prefix_blocks = backward_call(
        True, (held.qkv,), held.bounds, held.sctx, self_dctx, held.slse, held.pre
    )
    grad_input, prefix_grad, down_grad, up_grad = last_call(
        rows // 2, self_dqkv, held.wself, grad_one, prefix_blocks, unit_sum
    )
    return (output, grad_input.astype(jnp.float32), grad_memory, prefix_grad[:, :count], down_grad, up_grad)


def solution(mesh):
    in_specs = (
        P(("rows", "heads"), None),
        P(("rows", "heads"), None),
        P(("rows", "heads"), None),
        P("rows"),
        P("rows"),
        P(None, None, "heads"),
        P("heads", None),
        P(None, "heads"),
        P(None, None, "heads"),
        P("heads", None),
        P(None, "heads"),
        P("heads", None),
        P(None, "heads"),
        P("heads", None),
        P(None, None, "heads"),
        P(),
        P(),
    )
    out_specs = (
        P(("rows", "heads"), None),
        P(("rows", "heads"), None),
        P(("rows", "heads"), None),
        P(None, None, "heads"),
        P(None, "heads"),
        P("heads", None),
    )
    chosen = functools.partial(fast_body, mesh.shape["rows"]) if fast_fits(mesh) else body
    return jax.shard_map(chosen, mesh=mesh, in_specs=in_specs, out_specs=out_specs, check_vma=False)
```
